32 devices in a mesh: row: 8 (over y, x, core), rep: 4 (over z).
Axes of the slice: x: 2, y: 2, z: 4, core: 2. Of those that a mesh axis runs over, the one named last changes fastest.
Arguments:
- features: bfloat16 [32768, 1024], P('row', 'rep'), may hold values from -6 to 6
- tiles: bfloat16 [256, 16, 128, 128], P('row'), may hold values from -0.1875 to 0.1875
- columns: int32 [256, 16], P('row'), may hold values from 0 to 255
- counts: int32 [256], P('row'), may hold values from 1 to 16, as said below
- weight: bfloat16 [1024, 1024], P(None, 'rep'), may hold values from -0.1875 to 0.1875
- cotangent: bfloat16 [32768, 1024], P('row', 'rep'), may hold values from -6 to 6
Outputs:
- activations: bfloat16 [32768, 1024], P('row', 'rep')
- feature_grad: bfloat16 [32768, 1024], P('row', 'rep')
- weight_grad: float32 [1024, 1024], P('rep', 'row')
The draws below stay inside these ranges and needn't reach their ends.
Inputs may be any that keep to these rules, and one draw needn't show every extreme that they name: `counts`: in every draw some row block has all 16 slots in use.
All inputs are finite; a program needn't handle non-finite values.
Results may differ from the reference program's by a relative error of at most 0.014.
Values may be sent and summed in bfloat16 or wider, within the bound.
No kernel may reach another device: no remote copies, remote signals or barrier semaphores. Data moves between devices by JAX's collectives and lax.ppermute only.
A program may use at most 192 MiB of HBM per device.

```python
import math
import jax
import jax.numpy as jnp
import numpy as np
from jax import lax

F = 1024
H = 1024
TILE = 128
KMAX = 16
BLK_DEV = 32
NBLK = 256
NODES = 32768
N_ROW = 8


def draw_counts(key, part):
    first_key, second_key = jax.random.split(jax.random.fold_in(key, 17))
    drawn = jax.random.randint(first_key, (NBLK,), 1, KMAX + 1)
    chosen = jax.random.randint(second_key, (), 0, NBLK)
    return jnp.where(jnp.arange(NBLK) == chosen, KMAX, drawn).astype(jnp.int32)


def plant(result, rng, low, top_value):
    index_at = [jax.random.randint(jax.random.fold_in(rng, axis), (), 0, length) for axis, length in enumerate(result.shape)]
    widest = result.shape.index(max(result.shape))
    next_to = index_at[:widest] + [(index_at[widest] + 1) % result.shape[widest]] + index_at[widest + 1:]
    return result.at[tuple(index_at)].set(low).at[tuple(next_to)].set(top_value)


def block_scale(key, extent, shards, least, high):
    def one(position, parts):
        draws = jax.random.uniform(jax.random.fold_in(jax.random.fold_in(key, 6), position), (parts,), jnp.float32, least / len(shards), high / len(shards))
        return jnp.repeat(jnp.exp(draws), extent[position] // parts).reshape((-1,) + (1,) * (len(extent) - position - 1))

    factor_of = one(*shards[0])
    for cut in shards[1:]:
        factor_of = factor_of * one(*cut)
    return factor_of


def rank_table(number_of, skew):
    weights = [(1 << 20) // math.isqrt(rank ** skew) + 1 for rank in range(1, number_of + 1)]
    width = 1 + sum(weights) // (1 << 30)
    return np.cumsum(np.array([max(1, weight // width) for weight in weights]))


def ranked_ids(key, shape, amount, skew):
    table = rank_table(amount, skew)
    ticket = jax.random.randint(jax.random.fold_in(key, 1), shape, 0, int(table[amount - 1]))
    grade = jnp.searchsorted(jnp.asarray(table, jnp.int32), ticket, side="right")
    return jax.random.permutation(jax.random.fold_in(key, 2), amount)[grade].astype(jnp.int32)


def bell_draw(key, extent, spread, most, shards=(), dtype=jnp.bfloat16):
    array = spread * jax.random.normal(key, extent, jnp.float32)
    if shards:
        array = array * block_scale(key, extent, shards, -0.22, 0.18)
    return jnp.clip(array, -most, most).astype(dtype)


def setup_inputs(seed: int = 0) -> dict:
    key_of = jax.random.split(jax.random.key(seed), 7)
    features = bell_draw(key_of[0], (NODES, F), 1.0, 6.0, ((0, 8), (1, 4)))
    tiles = bell_draw(key_of[1], (NBLK, KMAX, TILE, TILE), (KMAX * TILE // 2) ** -0.5, 0.1875, ((0, 8),))
    columns = plant(ranked_ids(key_of[2], (NBLK, KMAX), NBLK, 2), jax.random.fold_in(key_of[2], 3), 0, NBLK - 1).astype(jnp.int32)
    counts = draw_counts(jax.random.fold_in(key_of[6], 71), 0)
    weight = bell_draw(key_of[4], (F, H), F ** -0.5, 0.1875, ((1, 4),))
    cotangent = bell_draw(key_of[5], (NODES, H), 1.0, 6.0, ((0, 8), (1, 4)))
    return dict(features=features, tiles=tiles, columns=columns, counts=counts, weight=weight, cotangent=cotangent)


def reference(features, tiles, columns, counts, weight, cotangent):
    alive_mask = jnp.arange(KMAX)[None, :] < counts[:, None]
    masked_tiles = jnp.where(alive_mask[:, :, None, None], tiles.astype(jnp.float32), jnp.float32(0.0))
    source_blocks = features.reshape(NBLK, TILE, F)

    def one_block(packed):
        tile_block, column_block = packed
        operand = jnp.take(source_blocks, column_block, axis=0).astype(jnp.float32)
        return jnp.einsum("kij,kjf->if", tile_block, operand)

    mixed = lax.map(one_block, (masked_tiles, columns)).reshape(NODES, F).astype(jnp.bfloat16)
    preact = jnp.dot(mixed, weight, preferred_element_type=jnp.float32)
    sigmoid_pre = jax.nn.sigmoid(preact)
    activations = (preact * sigmoid_pre).astype(jnp.bfloat16)
    grad_out = (cotangent.astype(jnp.float32) * sigmoid_pre * (1.0 + preact * (1.0 - sigmoid_pre))).astype(jnp.bfloat16)
    weight_grad = jnp.dot(mixed.T, grad_out, preferred_element_type=jnp.float32)
    mixed_grad = jnp.dot(grad_out, weight.T, preferred_element_type=jnp.float32).astype(jnp.bfloat16)
    grad_blocks = mixed_grad.reshape(N_ROW, BLK_DEV, TILE, F).astype(jnp.float32)
    tiles_dev = masked_tiles.reshape(N_ROW, BLK_DEV, KMAX, TILE, TILE)
    columns_dev = columns.reshape(N_ROW, BLK_DEV * KMAX).astype(jnp.int32)

    def one_device(accum, packed):
        tile_group, column_group, grad_group = packed
        contrib = jnp.einsum("bkij,bif->bkjf", tile_group, grad_group)
        term = jax.ops.segment_sum(contrib.reshape(BLK_DEV * KMAX, TILE, F), column_group, num_segments=NBLK)
        rounded = lax.optimization_barrier(term.astype(jnp.bfloat16))
        return accum + rounded.astype(jnp.float32), None

    total, unused = lax.scan(one_device, jnp.zeros((NBLK, TILE, F), jnp.float32), (tiles_dev, columns_dev, grad_blocks))
    feature_grad = total.reshape(NODES, F).astype(jnp.bfloat16)
    return activations, feature_grad, weight_grad
```

```python
import functools
import jax
import jax.numpy as jnp
from jax import lax
from jax.experimental import pallas as pl
from jax.experimental.pallas import tpu as pltpu
from jax.sharding import PartitionSpec as P

BF16, F32 = jnp.bfloat16, jnp.float32
VMEM_LIMIT = 56 * 1024 * 1024
LANES = 128
CORES = 2


def params():
    return pltpu.CompilerParams(vmem_limit_bytes=VMEM_LIMIT)


def any_spec():
    return pl.BlockSpec(memory_space=pl.ANY)


class Ring:
    def __init__(self, devices):
        self.chips = devices // CORES
        half = self.chips // 2
        self.order = list(range(half)) + list(range(self.chips - 1, half - 1, -1))
        self.devices = devices

    def perm(self, step):
        pairs = []
        for place, chip in enumerate(self.order):
            to = self.order[(place + step) % self.chips]
            pairs += [(chip * CORES + core, to * CORES + core) for core in range(CORES)]
        return pairs

    def hop(self, value, step):
        return lax.ppermute(value, "row", self.perm(step))

    def sibling(self, value):
        return lax.ppermute(value, "row", [(d, d ^ 1) for d in range(self.devices)])

    def device_at(self, offset, other_core):
        me = lax.axis_index("row")
        order = jnp.array(self.order, jnp.int32)
        place_of = jnp.array([self.order.index(c) for c in range(self.chips)], jnp.int32)
        chip = order[(place_of[me // CORES] + offset) % self.chips]
        core = me % CORES
        return chip * CORES + (1 - core if other_core else core)


def gather_pieces(ring, x):
    rows = x.shape[0]
    half = rows // 2
    middle = ring.chips // 2
    got = [(0, 0, x)]
    up = down = x
    for step in range(1, middle):
        up, down = ring.hop(up, 1), ring.hop(down, -1)
        got += [(-step, 0, up), (step, 0, down)]
    got += [(middle, 0, ring.hop(up[:half], 1)), (middle, half, ring.hop(down[half:], -1))]
    pieces = []
    for offset, start, value in got:
        pieces.append((ring.device_at(offset, False) * rows + start, value))
        pieces.append((ring.device_at(offset, True) * rows + start, ring.sibling(value)))
    return pieces


def add(*values):
    return functools.reduce(lambda a, b: a + b, [v.astype(F32) for v in values])


def reduce_pieces(ring, own, other):
    half = own[0].shape[0] // 2
    middle = ring.chips // 2
    total = [add(own[o], ring.sibling(other[o])) for o in range(ring.chips)]
    up = ring.hop(total[middle][:half].astype(BF16), 1)
    down = ring.hop(total[middle][half:].astype(BF16), -1)
    for step in range(middle - 1, 0, -1):
        to_up, to_down = total[step], total[ring.chips - step]
        if step == middle - 1:
            to_up = jnp.concatenate([to_up[:half] + up.astype(F32), to_up[half:]])
            to_down = jnp.concatenate([to_down[:half], to_down[half:] + down.astype(F32)])
        else:
            to_up, to_down = add(to_up, up), add(to_down, down)
        up, down = ring.hop(to_up.astype(BF16), 1), ring.hop(to_down.astype(BF16), -1)
    if middle == 1:
        return (total[0] + jnp.concatenate([up, down]).astype(F32)).astype(BF16)
    return add(total[0], up, down).astype(BF16)


def exchange(blocks):
    size = len(blocks)
    got = [blocks[0]] + [None] * (size - 1)
    for u in range(1, size):
        got[(size - u) % size] = lax.ppermute(blocks[u], "rep", [(i, (i + u) % size) for i in range(size)])
    return got


def row_block(t, me, per_part, parts):
    return lax.rem(me + t // per_part, parts) * per_part + lax.rem(t, per_part)


def spmm_kernel(n_pieces, parts, group, cols, counts, meta, tiles, *refs):
    pieces, outs = refs[:n_pieces], refs[n_pieces : n_pieces + parts]
    source, acc, sems = refs[n_pieces + parts :]
    t = pl.program_id(0)
    tile_size = tiles.shape[2]
    slots = tiles.shape[1]
    per_part = pl.num_programs(0) // parts

    @pl.when(t == 0)
    def _():
        copies = []
        for p, piece in enumerate(pieces):
            start = pl.multiple_of(meta[1 + p], tile_size)
            copies.append(pltpu.make_async_copy(piece, source.at[pl.ds(start, piece.shape[0])], sems.at[p]))
            copies[-1].start()
        for copy in copies:
            copy.wait()

    b = row_block(t, meta[0], per_part, parts)
    count = counts[b]
    for first in range(0, slots, group):

        @pl.when(count > first)
        def _():
            left, right = [], []
            for k in range(first, first + group):
                tile = tiles[0, k]
                left.append(jnp.where(k < count, tile, jnp.zeros_like(tile)))
                right.append(source[pl.ds(pl.multiple_of(cols[b, k] * tile_size, tile_size), tile_size), :])
            part = jnp.dot(
                jnp.concatenate(left, axis=1), jnp.concatenate(right, axis=0), preferred_element_type=F32
            )
            if first:
                acc[...] += part
            else:
                acc[...] = part

    for u in range(parts):

        @pl.when(t // per_part == u)
        def _():
            outs[u][...] = acc[...].astype(BF16)


def spmm(tiles, columns, counts, me, pieces, parts):
    blocks, slots, tile_size, _ = tiles.shape
    width = pieces[0][1].shape[1]
    total_rows = sum(v.shape[0] for _, v in pieces)
    per_part = blocks // parts
    meta = jnp.stack([me] + [start for start, _ in pieces]).astype(jnp.int32)

    def out_spec(u):
        return pl.BlockSpec(
            (tile_size, width), lambda t, cols, cnt, meta: (jnp.clip(t - u * per_part, 0, per_part - 1), 0)
        )

    return pl.pallas_call(
        functools.partial(spmm_kernel, len(pieces), parts, min(slots, 8)),
        grid_spec=pltpu.PrefetchScalarGridSpec(
            num_scalar_prefetch=3,
            grid=(blocks,),
            in_specs=[
                pl.BlockSpec(
                    (1, slots, tile_size, tile_size),
                    lambda t, cols, cnt, meta: (row_block(t, meta[0], per_part, parts), 0, 0, 0),
                )
            ]
            + [any_spec()] * len(pieces),
            out_specs=[out_spec(u) for u in range(parts)],
            scratch_shapes=[
                pltpu.VMEM((total_rows, width), BF16),
                pltpu.VMEM((tile_size, width), F32),
                pltpu.SemaphoreType.DMA((len(pieces),)),
            ],
        ),
        out_shape=[jax.ShapeDtypeStruct((per_part * tile_size, width), BF16) for _ in range(parts)],
        compiler_params=params(),
        cost_estimate=pl.CostEstimate(
            flops=2 * blocks * slots * tile_size * tile_size * width,
            bytes_accessed=2 * (tiles.size + total_rows * width),
            transcendentals=0,
        ),
        name="spmm",
    )(columns, counts, meta, tiles, *[v for _, v in pieces])


def spmm_t_kernel(parts, n_outs, group, cols, counts, meta, tiles, *refs):
    grads, outs = refs[:parts], refs[parts : parts + n_outs]
    total, grad, stage, in_sems, out_sems = refs[parts + n_outs :]
    t = pl.program_id(0)
    slots, tile_size = tiles.shape[1], tiles.shape[2]
    per_part = pl.num_programs(0) // parts
    part_rows = per_part * tile_size
    width = grad.shape[1]

    @pl.when(t == 0)
    def _():
        copies = []
        for u in range(parts):
            copies.append(pltpu.make_async_copy(grads[u], grad.at[pl.ds(u * part_rows, part_rows)], in_sems.at[u]))
            copies[-1].start()

        @pl.loop(0, total.shape[0] // tile_size)
        def _(i):
            total[pl.ds(pl.multiple_of(i * tile_size, tile_size), tile_size), :] = jnp.zeros((tile_size, width), F32)

        for copy in copies:
            copy.wait()

    b = row_block(t, meta[0], per_part, parts)
    count = counts[b]
    block_grad = grad[pl.ds(pl.multiple_of(t * tile_size, tile_size), tile_size), :]
    for first in range(0, slots, group):

        @pl.when(count > first)
        def _():
            left = tiles[0, first : first + group].reshape(group * tile_size, tile_size)
            part = jnp.dot(left, block_grad, preferred_element_type=F32)
            for k in range(group):
                at = pl.ds(pl.multiple_of(cols[b, first + k] * tile_size, tile_size), tile_size)
                total[at, :] += part[k * tile_size : (k + 1) * tile_size]

    @pl.when(t == pl.num_programs(0) - 1)
    def _():
        copies = []
        for o in range(n_outs):
            slot = o % 2
            rows = outs[o].shape[0]
            if o >= 2:
                copies[o - 2].wait()

            @pl.loop(0, rows // tile_size)
            def _(i):
                start = pl.multiple_of(meta[1 + o] + i * tile_size, tile_size)
                to = pl.multiple_of(i * tile_size, tile_size)
                stage[slot, pl.ds(to, tile_size), :] = total[pl.ds(start, tile_size), :].astype(BF16)

            copies.append(pltpu.make_async_copy(stage.at[slot, pl.ds(0, rows)], outs[o], out_sems.at[o]))
            copies[o].start()
        for copy in copies[-2:]:
            copy.wait()


def spmm_t(tiles_t, columns, counts, me, grads, starts, rows, total_rows):
    blocks, slots, tile_size, _ = tiles_t.shape
    parts = len(grads)
    part_rows, width = grads[0].shape
    per_part = blocks // parts
    meta = jnp.stack([me] + starts).astype(jnp.int32)
    return pl.pallas_call(
        functools.partial(spmm_t_kernel, parts, len(starts), min(slots, 4)),
        grid_spec=pltpu.PrefetchScalarGridSpec(
            num_scalar_prefetch=3,
            grid=(blocks,),
            in_specs=[
                pl.BlockSpec(
                    (1, slots, tile_size, tile_size),
                    lambda t, cols, cnt, meta: (row_block(t, meta[0], per_part, parts), 0, 0, 0),
                )
            ]
            + [any_spec()] * parts,
            out_specs=[any_spec()] * len(starts),
            scratch_shapes=[
                pltpu.VMEM((total_rows, width), F32),
                pltpu.VMEM((parts * part_rows, width), BF16),
                pltpu.VMEM((2, rows, width), BF16),
                pltpu.SemaphoreType.DMA((parts,)),
                pltpu.SemaphoreType.DMA((len(starts),)),
            ],
        ),
        out_shape=[jax.ShapeDtypeStruct((rows, width), BF16) for _ in starts],
        compiler_params=params(),
        cost_estimate=pl.CostEstimate(
            flops=2 * blocks * slots * tile_size * tile_size * width,
            bytes_accessed=2 * (tiles_t.size + total_rows * width),
            transcendentals=0,
        ),
        name="spmm_t",
    )(columns, counts, meta, tiles_t, *grads)


def dense_kernel(parts, chunks, meta, *refs):
    n_mixed = parts * chunks
    mixed_refs, cot_refs, w_hbm = refs[:n_mixed], refs[n_mixed : n_mixed + parts], refs[n_mixed + parts]
    outs = refs[n_mixed + parts + 1 :]
    act_outs, mg_outs = outs[:parts], outs[parts : parts + n_mixed]
    mixed_out, grad_out, weight, sems = outs[parts + n_mixed :]
    f_wide, h_wide = weight.shape[0] // parts, weight.shape[1] // parts
    width = f_wide // chunks
    me = meta[0]

    def place(u):
        return lax.rem(me + u, parts)

    @pl.when(pl.program_id(0) == 0)
    def _():
        copies = []
        for i in range(parts):
            for j in range(parts):
                src = w_hbm.at[
                    pl.ds(pl.multiple_of(place(i) * f_wide, f_wide), f_wide),
                    pl.ds(pl.multiple_of(place(j) * h_wide, h_wide), h_wide),
                ]
                dst = weight.at[pl.ds(i * f_wide, f_wide), pl.ds(j * h_wide, h_wide)]
                copies.append(pltpu.make_async_copy(src, dst, sems.at[i * parts + j]))
                copies[-1].start()
        for copy in copies:
            copy.wait()

    mixed = jnp.concatenate([ref[...] for ref in mixed_refs], axis=1)
    for u in range(parts):
        at = pl.ds(pl.multiple_of(place(u) * f_wide, f_wide), f_wide)
        mixed_out[:, at] = mixed[:, u * f_wide : (u + 1) * f_wide]
    grads = []
    for u in range(parts):
        preact = jnp.dot(mixed, weight[:, u * h_wide : (u + 1) * h_wide], preferred_element_type=F32)
        sig = jax.nn.sigmoid(preact)
        act_outs[u][...] = (preact * sig).astype(BF16)
        grads.append((cot_refs[u][...].astype(F32) * sig * (1.0 + preact * (1.0 - sig))).astype(BF16))
        at = pl.ds(pl.multiple_of(place(u) * h_wide, h_wide), h_wide)
        grad_out[:, at] = grads[u]
    grad = jnp.concatenate(grads, axis=1)
    back = lax.dot_general(grad, weight[...], (((1,), (1,)), ((), ())), preferred_element_type=F32).astype(BF16)
    for i in range(n_mixed):
        mg_outs[i][...] = back[:, i * width : (i + 1) * width]


def dense(me, mixed, cot, weight):
    parts, chunks = len(mixed), len(mixed[0])
    rows, width = mixed[0][0].shape
    features, hidden = weight.shape
    h_wide = hidden // parts
    step = min(rows, 256)

    def spec(w):
        return pl.BlockSpec((step, w), lambda t, meta: (t, 0))

    outs = pl.pallas_call(
        functools.partial(dense_kernel, parts, chunks),
        grid_spec=pltpu.PrefetchScalarGridSpec(
            num_scalar_prefetch=1,
            grid=(rows // step,),
            in_specs=[spec(width)] * (parts * chunks) + [spec(h_wide)] * parts + [any_spec()],
            out_specs=[spec(h_wide)] * parts + [spec(width)] * (parts * chunks) + [spec(features), spec(hidden)],
            scratch_shapes=[pltpu.VMEM((features, hidden), BF16), pltpu.SemaphoreType.DMA((parts * parts,))],
        ),
        out_shape=[jax.ShapeDtypeStruct((rows, h_wide), BF16)] * parts
        + [jax.ShapeDtypeStruct((rows, width), BF16)] * (parts * chunks)
        + [jax.ShapeDtypeStruct((rows, features), BF16), jax.ShapeDtypeStruct((rows, hidden), BF16)],
        compiler_params=params(),
        cost_estimate=pl.CostEstimate(
            flops=4 * rows * features * hidden,
            bytes_accessed=2 * (features * hidden + 6 * rows * hidden),
            transcendentals=rows * hidden,
        ),
        name="dense",
    )(me[None].astype(jnp.int32), *[m for row in mixed for m in row], *cot, weight)
    n = parts * chunks
    act, back = outs[:parts], outs[parts : parts + n]
    return act, [back[u * chunks : (u + 1) * chunks] for u in range(parts)], outs[-2], outs[-1]


def local(features, tiles, columns, counts, weight, cotangent):
    rows, f_wide = features.shape
    blocks, slots, tile_size, _ = tiles.shape
    row_size, parts = lax.axis_size("row"), lax.axis_size("rep")
    ring = Ring(row_size)
    rep = lax.axis_index("rep")
    chunks = f_wide // LANES if f_wide % LANES == 0 else 1
    width = f_wide // chunks
    part_rows = rows // parts

    def part_of(x, u):
        return lax.dynamic_slice_in_dim(x, lax.rem(rep + u, parts) * part_rows, part_rows, 0)

    share = weight.shape[0] // row_size
    w_share = lax.dynamic_slice_in_dim(weight, lax.axis_index("row") * share, share, 0)
    w_full = lax.all_gather(lax.all_gather(w_share, "rep", axis=1, tiled=True), "row", axis=0, tiled=True)

    cot = exchange([part_of(cotangent, u) for u in range(parts)])

    alive = jnp.arange(slots)[None, :] < counts[:, None]
    tiles_t = jnp.swapaxes(jnp.where(alive[:, :, None, None], tiles, jnp.zeros((), tiles.dtype)), 2, 3)

    mixed = []
    for c in range(chunks):
        x = features[:, c * width : (c + 1) * width]
        if c:
            x, *_ = lax.optimization_barrier((x, *[v for _, v in pieces]))
        pieces = gather_pieces(ring, x)
        mixed.append(exchange(spmm(tiles, columns, counts, rep, pieces, parts)))
    mixed = [[mixed[c][u] for c in range(chunks)] for u in range(parts)]

    act, back, mixed_rows, grad_rows = dense(rep, mixed, cot, w_full)

    weight_terms = lax.dot_general(mixed_rows, grad_rows, (((0,), (0,)), ((), ())), preferred_element_type=F32)
    weight_terms = lax.psum_scatter(weight_terms.astype(BF16), "row", scatter_dimension=1, tiled=True)
    weight_grad = lax.psum_scatter(weight_terms, "rep", scatter_dimension=0, tiled=True).astype(F32)

    starts = [ring.device_at(o, other) * rows for other in (False, True) for o in range(ring.chips)]
    feature_grad = []
    for c in range(chunks):
        grads = exchange([back[u][c] for u in range(parts)])
        terms = spmm_t(tiles_t, columns, counts, rep, grads, starts, rows, rows * row_size)
        feature_grad.append(reduce_pieces(ring, terms[: ring.chips], terms[ring.chips :]))
    feature_grad = jnp.concatenate(feature_grad, axis=1)

    act, _ = lax.optimization_barrier((act, grads))
    act = exchange(act)
    activations = jnp.zeros((rows, cotangent.shape[1]), BF16)
    for u in range(parts):
        activations = lax.dynamic_update_slice_in_dim(activations, act[u], lax.rem(rep + u, parts) * part_rows, 0)
    return (activations, feature_grad, weight_grad)


def solution(mesh):
    in_specs = (
        P("row", "rep"),
        P("row", None, None, None),
        P("row", None),
        P("row"),
        P(None, "rep"),
        P("row", "rep"),
    )
    out_specs = (P("row", "rep"), P("row", "rep"), P("rep", "row"))
    return jax.shard_map(local, mesh=mesh, in_specs=in_specs, out_specs=out_specs, check_vma=False)
```

```python
import functools
import jax
import jax.numpy as jnp
from jax import lax
from jax.experimental import pallas as pl
from jax.experimental.pallas import tpu as pltpu
from jax.sharding import PartitionSpec as P

BF16, F32 = jnp.bfloat16, jnp.float32
VMEM_LIMIT = 56 * 1024 * 1024
LANES = 128
CORES = 2


def params():
    return pltpu.CompilerParams(vmem_limit_bytes=VMEM_LIMIT)


def any_spec():
    return pl.BlockSpec(memory_space=pl.ANY)


class Ring:
    def __init__(self, devices):
        self.chips = devices // CORES
        half = self.chips // 2
        self.order = list(range(half)) + list(range(self.chips - 1, half - 1, -1))
        self.devices = devices

    def perm(self, step):
        pairs = []
        for place, chip in enumerate(self.order):
            to = self.order[(place + step) % self.chips]
            pairs += [(chip * CORES + core, to * CORES + core) for core in range(CORES)]
        return pairs

    def hop(self, value, step):
        return lax.ppermute(value, "row", self.perm(step))

    def sibling(self, value):
        return lax.ppermute(value, "row", [(d, d ^ 1) for d in range(self.devices)])

    def device_at(self, offset, other_core):
        me = lax.axis_index("row")
        order = jnp.array(self.order, jnp.int32)
        place_of = jnp.array([self.order.index(c) for c in range(self.chips)], jnp.int32)
        chip = order[(place_of[me // CORES] + offset) % self.chips]
        core = me % CORES
        return chip * CORES + (1 - core if other_core else core)


def after(value, *others):
    return lax.optimization_barrier((value, *others))[0]


def gather_chunks(ring, chunks):
    rows = chunks[0].shape[0]
    half = rows // 2
    middle = ring.chips // 2
    gate = ()
    pieces = []
    for x in chunks:
        low, high = after(x[:half], *gate), after(x[half:], *gate)
        got = [(0, 0, x)]
        up, down = (low, high), (high, low)
        for step in range(1, middle):
            up = tuple(ring.hop(v, 1) for v in up)
            down = tuple(ring.hop(v, -1) for v in down)
            got += [(-step, 0, up[0]), (step, half, down[0]), (-step, half, up[1]), (step, 0, down[1])]
        gate = (up[1], down[1]) if middle > 1 else ()
        got += [(middle, 0, ring.hop(up[0], 1)), (middle, half, ring.hop(down[0], -1))]
        pieces.append([])
        for offset, start, value in got:
            pieces[-1].append((ring.device_at(offset, False) * rows + start, value))
            pieces[-1].append((ring.device_at(offset, True) * rows + start, ring.sibling(value)))
    return pieces


def reduce_pieces(ring, own_far, own_near, other_far, other_near):
    rows = own_far.shape[0]
    half = rows // 2
    middle = ring.chips // 2
    got_far = ring.sibling(other_far)
    got_near = ring.sibling(other_near)

    def far(start):
        return own_far[start : start + half].astype(F32) + got_far[start : start + half].astype(F32)

    def near(offset):
        offset %= ring.chips
        at = offset - (offset > middle)
        return own_near[at].astype(F32) + got_near[at * rows : (at + 1) * rows].astype(F32)

    up = ring.hop(far(0).astype(BF16), 1)
    down = ring.hop(far(half).astype(BF16), -1)
    for step in range(middle - 1, 0, -1):
        to_up, to_down = near(step), near(-step)
        if step == middle - 1:
            to_up = jnp.concatenate([to_up[:half] + up.astype(F32), to_up[half:]])
            to_down = jnp.concatenate([to_down[:half], to_down[half:] + down.astype(F32)])
        else:
            to_up, to_down = to_up + up.astype(F32), to_down + down.astype(F32)
        up, down = ring.hop(to_up.astype(BF16), 1), ring.hop(to_down.astype(BF16), -1)
    if middle == 1:
        return (near(0) + jnp.concatenate([up, down]).astype(F32)).astype(BF16)
    return (near(0) + up.astype(F32) + down.astype(F32)).astype(BF16)


def exchange(blocks):
    size = len(blocks)
    got = [blocks[0]] + [None] * (size - 1)
    for u in range(1, size):
        got[(size - u) % size] = lax.ppermute(blocks[u], "rep", [(i, (i + u) % size) for i in range(size)])
    return got


def masked_tiles(tiles, i, count):
    found = []
    for k in range(tiles.shape[1]):
        tile = tiles[i, k]
        found.append(jnp.where(k < count, tile, jnp.zeros_like(tile)))
    return jnp.concatenate(found, axis=1)


def step_spec(blocks, slots, tile_size, parts, per_step, skip):
    def index(t, cols, cnt, meta):
        return (lax.rem(meta[0] + t, parts) * (blocks // parts // per_step) + skip, 0, 0, 0)

    return pl.BlockSpec((per_step, slots, tile_size, tile_size), index)


def aligned(start, size, unit):
    return pl.ds(pl.multiple_of(start, unit), size)


def spmm_kernel(n_pieces, per_part, skip, cols, counts, meta, tiles, *refs):
    parts = pl.num_programs(0)
    n_outs = len(refs) - n_pieces - 3
    pieces, outs = refs[:n_pieces], refs[n_pieces : n_pieces + n_outs]
    source, result, sems = refs[n_pieces + n_outs :]
    t = pl.program_id(0)
    per_step, slots, tile_size, _ = tiles.shape

    @pl.when(t == 0)
    def _():
        copies = []
        for p, piece in enumerate(pieces):
            copies.append(
                pltpu.make_async_copy(piece, source.at[aligned(meta[1 + p], piece.shape[0], tile_size)], sems.at[p])
            )
            copies[-1].start()
        for copy in copies:
            copy.wait()

    for i in range(per_step):
        b = lax.rem(meta[0] + t, parts) * per_part + skip * per_step + i
        right = [source[aligned(cols[b, k] * tile_size, tile_size, tile_size), :] for k in range(slots)]
        product = jnp.dot(
            masked_tiles(tiles, i, counts[b]), jnp.concatenate(right, axis=0), preferred_element_type=F32
        )
        result[i * tile_size : (i + 1) * tile_size, :] = product.astype(BF16)

    for u in range(n_outs):

        @pl.when(t == u)
        def _():
            outs[u][...] = result[...]


def spmm(tiles, columns, counts, me, pieces, parts, cut, skip):
    blocks, slots, tile_size, _ = tiles.shape
    width = pieces[0][1].shape[1]
    total_rows = sum(v.shape[0] for _, v in pieces)
    per_part = blocks // parts
    per_step = per_part // cut
    rows = per_step * tile_size
    meta = jnp.stack([me] + [start for start, _ in pieces]).astype(jnp.int32)
    return pl.pallas_call(
        functools.partial(spmm_kernel, len(pieces), per_part, skip),
        grid_spec=pltpu.PrefetchScalarGridSpec(
            num_scalar_prefetch=3,
            grid=(parts,),
            in_specs=[step_spec(blocks, slots, tile_size, parts, per_step, skip)] + [any_spec()] * len(pieces),
            out_specs=[pl.BlockSpec((rows, width), lambda t, cols, cnt, meta: (0, 0))] * parts,
            scratch_shapes=[
                pltpu.VMEM((total_rows, width), BF16),
                pltpu.VMEM((rows, width), BF16),
                pltpu.SemaphoreType.DMA((len(pieces),)),
            ],
        ),
        out_shape=[jax.ShapeDtypeStruct((rows, width), BF16)] * parts,
        compiler_params=params(),
        cost_estimate=pl.CostEstimate(
            flops=2 * parts * rows * slots * tile_size * width,
            bytes_accessed=2 * (tiles.size // cut + total_rows * width),
            transcendentals=0,
        ),
        name="spmm",
    )(columns, counts, meta, tiles, *[v for _, v in pieces])


def spmm_t_kernel(n_grads, per_part, n_outs, terms, cols, counts, meta, tiles, *refs):
    parts = pl.num_programs(0)
    grads, outs = refs[:n_grads], refs[n_grads : n_grads + n_outs]
    total, grad, stage, in_sems, out_sems = refs[n_grads + n_outs :]
    t = pl.program_id(0)
    per_step, slots, tile_size, _ = tiles.shape
    width = grad.shape[1]
    rows = stage.shape[1]

    @pl.when(t == 0)
    def _():
        copies, start = [], 0
        for g, ref in enumerate(grads):
            copies.append(pltpu.make_async_copy(ref, grad.at[pl.ds(start, ref.shape[0])], in_sems.at[g]))
            copies[-1].start()
            start += ref.shape[0]

        @pl.loop(0, total.shape[0] // tile_size, unroll=8)
        def _(i):
            total[aligned(i * tile_size, tile_size, tile_size), :] = jnp.zeros((tile_size, width), F32)

        for copy in copies:
            copy.wait()

    for i in range(per_step):
        b = lax.rem(meta[0] + t, parts) * per_part + i
        block = grad[aligned((t * per_step + i) * tile_size, tile_size, tile_size), :]
        part = lax.dot_general(
            masked_tiles(tiles, i, counts[b]), block, (((0,), (0,)), ((), ())), preferred_element_type=F32
        )
        for k in range(slots):
            total[aligned(cols[b, k] * tile_size, tile_size, tile_size), :] += part[k * tile_size : (k + 1) * tile_size]

    @pl.when(t == parts - 1)
    def _():
        copies = []
        for o, (out, at) in enumerate(terms):
            slot = o % 2
            if o >= 2:
                copies[o - 2].wait()

            @pl.loop(0, rows // tile_size, unroll=4)
            def _(i):
                start = aligned(meta[1 + o] + i * tile_size, tile_size, tile_size)
                stage[slot, aligned(i * tile_size, tile_size, tile_size), :] = total[start, :].astype(BF16)

            copies.append(
                pltpu.make_async_copy(stage.at[slot], outs[out].at[pl.ds(at * rows, rows)], out_sems.at[o])
            )
            copies[o].start()
        for copy in copies[-2:]:
            copy.wait()


def spmm_t(tiles, columns, counts, me, grads, parts, wanted, rows, total_rows):
    blocks, slots, tile_size, _ = tiles.shape
    width = grads[0].shape[1]
    per_part = blocks // parts
    flat = [(out, at) for out, starts in enumerate(wanted) for at in range(len(starts))]
    meta = jnp.stack([me] + [start for starts in wanted for start in starts]).astype(jnp.int32)
    return pl.pallas_call(
        functools.partial(spmm_t_kernel, len(grads), per_part, len(wanted), flat),
        grid_spec=pltpu.PrefetchScalarGridSpec(
            num_scalar_prefetch=3,
            grid=(parts,),
            in_specs=[step_spec(blocks, slots, tile_size, parts, per_part, 0)] + [any_spec()] * len(grads),
            out_specs=[any_spec()] * len(wanted),
            scratch_shapes=[
                pltpu.VMEM((total_rows, width), F32),
                pltpu.VMEM((rows, width), BF16),
                pltpu.VMEM((2, rows, width), BF16),
                pltpu.SemaphoreType.DMA((len(grads),)),
                pltpu.SemaphoreType.DMA((len(flat),)),
            ],
        ),
        out_shape=[jax.ShapeDtypeStruct((len(starts) * rows, width), BF16) for starts in wanted],
        compiler_params=params(),
        cost_estimate=pl.CostEstimate(
            flops=2 * blocks * slots * tile_size * tile_size * width,
            bytes_accessed=2 * (tiles.size + total_rows * width),
            transcendentals=0,
        ),
        name="spmm_t",
    )(columns, counts, meta, tiles, *grads)


def dense_kernel(parts, chunks, meta, *refs):
    n_mixed = parts * chunks
    mixed_refs, cot_refs, w_hbm = refs[:n_mixed], refs[n_mixed : n_mixed + parts], refs[n_mixed + parts]
    outs = refs[n_mixed + parts + 1 :]
    act_outs, mg_outs = outs[:parts], outs[parts : parts + n_mixed]
    mixed_out, grad_out, weight, sems = outs[parts + n_mixed :]
    f_wide, h_wide = weight.shape[0] // parts, weight.shape[1] // parts
    width = f_wide // chunks
    me = meta[0]

    def place(u):
        return lax.rem(me + u, parts)

    @pl.when(pl.program_id(0) == 0)
    def _():
        copies = []
        for i in range(parts):
            src = w_hbm.at[aligned(place(i) * f_wide, f_wide, f_wide)]
            copies.append(pltpu.make_async_copy(src, weight.at[pl.ds(i * f_wide, f_wide)], sems.at[i]))
            copies[-1].start()
        for copy in copies:
            copy.wait()

    mixed = jnp.concatenate([ref[...] for ref in mixed_refs], axis=1)
    for u in range(parts):
        at = pl.ds(pl.multiple_of(place(u) * f_wide, f_wide), f_wide)
        mixed_out[:, at] = mixed[:, u * f_wide : (u + 1) * f_wide]
    grads = []
    for u in range(parts):
        preact = jnp.dot(mixed, weight[:, u * h_wide : (u + 1) * h_wide], preferred_element_type=F32)
        sig = jax.nn.sigmoid(preact)
        act_outs[u][...] = (preact * sig).astype(BF16)
        grads.append((cot_refs[u][...].astype(F32) * sig * (1.0 + preact * (1.0 - sig))).astype(BF16))
        at = pl.ds(pl.multiple_of(place(u) * h_wide, h_wide), h_wide)
        grad_out[:, at] = grads[u]
    grad = jnp.concatenate(grads, axis=1)
    back = lax.dot_general(grad, weight[...], (((1,), (1,)), ((), ())), preferred_element_type=F32).astype(BF16)
    for i in range(n_mixed):
        mg_outs[i][...] = back[:, i * width : (i + 1) * width]


def dense(me, mixed, cot, weight, rows, first):
    parts, chunks = len(mixed), len(mixed[0])
    width = mixed[0][0][0].shape[1]
    features, hidden = weight.shape
    h_wide = hidden // parts
    step = min(rows, 256)

    def spec(w, start=0):
        return pl.BlockSpec((step, w), lambda t, meta: (t + start // step, 0))

    flat = [m for row in mixed for m in row]
    outs = pl.pallas_call(
        functools.partial(dense_kernel, parts, chunks),
        grid_spec=pltpu.PrefetchScalarGridSpec(
            num_scalar_prefetch=1,
            grid=(rows // step,),
            in_specs=[spec(width, at) for _, at in flat] + [spec(h_wide, first)] * parts + [any_spec()],
            out_specs=[spec(h_wide)] * parts + [spec(width)] * (parts * chunks) + [spec(features), spec(hidden)],
            scratch_shapes=[pltpu.VMEM((features, hidden), BF16), pltpu.SemaphoreType.DMA((parts,))],
        ),
        out_shape=[jax.ShapeDtypeStruct((rows, h_wide), BF16)] * parts
        + [jax.ShapeDtypeStruct((rows, width), BF16)] * (parts * chunks)
        + [jax.ShapeDtypeStruct((rows, features), BF16), jax.ShapeDtypeStruct((rows, hidden), BF16)],
        compiler_params=params(),
        cost_estimate=pl.CostEstimate(
            flops=4 * rows * features * hidden,
            bytes_accessed=2 * (features * hidden + 6 * rows * hidden),
            transcendentals=rows * hidden,
        ),
        name="dense",
    )(me[None].astype(jnp.int32), *[m for m, _ in flat], *cot, weight)
    n = parts * chunks
    act, back = outs[:parts], outs[parts : parts + n]
    return act, [back[u * chunks : (u + 1) * chunks] for u in range(parts)], outs[-2], outs[-1]


def local(features, tiles, columns, counts, weight, cotangent):
    rows, f_wide = features.shape
    h_wide = cotangent.shape[1]
    row_size, parts = lax.axis_size("row"), lax.axis_size("rep")
    ring = Ring(row_size)
    rep = lax.axis_index("rep")
    chunks = f_wide // LANES if f_wide % LANES == 0 else 1
    width = f_wide // chunks
    part_rows = rows // parts
    halves = 2
    half_rows = part_rows // halves

    def part_of(x, u):
        return lax.dynamic_slice_in_dim(x, lax.rem(rep + u, parts) * part_rows, part_rows, 0)

    share = weight.shape[0] // row_size
    w_share = lax.dynamic_slice_in_dim(weight, lax.axis_index("row") * share, share, 0)
    w_share = exchange([w_share] * parts)
    cot = exchange([after(part_of(cotangent, u), *w_share[1:2]) for u in range(parts)])

    pieces = gather_chunks(ring, [features[:, c * width : (c + 1) * width] for c in range(chunks)])
    w_share = after(jnp.concatenate(w_share, axis=1), pieces[-1][2][1])
    w_full = lax.all_gather(w_share, "row", axis=0, tiled=True)

    mixed = []
    for c in range(chunks):
        if c < chunks - 1:
            got = exchange(spmm(tiles, columns, counts, rep, pieces[c], parts, 1, 0))
            mixed.append([[(v, h * half_rows) for v in got] for h in range(halves)])
        else:
            got = [exchange(spmm(tiles, columns, counts, rep, pieces[c], parts, halves, h)) for h in range(halves)]
            mixed.append([[(v, 0) for v in got[h]] for h in range(halves)])

    act, back, weight_terms = [], [], 0.0
    for h in range(halves):
        blocks = [[mixed[c][h][u] for c in range(chunks)] for u in range(parts)]
        act_h, back_h, mixed_h, grad_h = dense(rep, blocks, cot, w_full, half_rows, h * half_rows)
        act.append(act_h)
        back.append(back_h)
        weight_terms += lax.dot_general(mixed_h, grad_h, (((0,), (0,)), ((), ())), preferred_element_type=F32)

    weight_terms = lax.psum_scatter(weight_terms.astype(BF16), "row", scatter_dimension=1, tiled=True)
    weight_grad = lax.psum_scatter(weight_terms, "rep", scatter_dimension=0, tiled=True).astype(F32)

    middle = ring.chips // 2
    near = [o for o in range(ring.chips) if o != middle]
    wanted = [
        [ring.device_at(o, other) * rows for o in offsets]
        for other in (False, True)
        for offsets in [[middle]] + ([[o] for o in near] if not other else [near])
    ]
    gate = ()
    feature_grad = []
    for c in range(chunks):
        got = []
        for h in range(halves):
            got.append(exchange([after(back[h][u][c], *gate) for u in range(parts)]))
        gate = got[0][1:]
        grads = [got[h][u] for u in range(parts) for h in range(halves)]
        terms = spmm_t(tiles, columns, counts, rep, grads, parts, wanted, rows, rows * row_size)
        feature_grad.append(reduce_pieces(ring, terms[0], terms[1 : 1 + len(near)], terms[-2], terms[-1]))
    feature_grad = jnp.concatenate(feature_grad, axis=1)

    activations = jnp.zeros((rows, h_wide), BF16)
    for h in range(halves):
        for u, value in enumerate(exchange([after(a, *gate) for a in act[h]])):
            start = lax.rem(rep + u, parts) * part_rows + h * half_rows
            activations = lax.dynamic_update_slice_in_dim(activations, value, start, 0)
    return (activations, feature_grad, weight_grad)


def solution(mesh):
    in_specs = (
        P("row", "rep"),
        P("row", None, None, None),
        P("row", None),
        P("row"),
        P(None, "rep"),
        P("row", "rep"),
    )
    out_specs = (P("row", "rep"), P("row", "rep"), P("rep", "row"))
    return jax.shard_map(local, mesh=mesh, in_specs=in_specs, out_specs=out_specs, check_vma=False)
```

```python
import functools
import jax
import jax.numpy as jnp
from jax import lax
from jax.experimental import pallas as pl
from jax.experimental.pallas import tpu as pltpu
from jax.sharding import PartitionSpec as P

BF16, F32 = jnp.bfloat16, jnp.float32
VMEM_LIMIT = 56 * 1024 * 1024
LANES = 128
CORES = 2


def params():
    return pltpu.CompilerParams(vmem_limit_bytes=VMEM_LIMIT)


def any_spec():
    return pl.BlockSpec(memory_space=pl.ANY)


class Ring:
    def __init__(self, devices):
        self.chips = devices // CORES
        half = self.chips // 2
        self.order = list(range(half)) + list(range(self.chips - 1, half - 1, -1))
        self.devices = devices

    def perm(self, step):
        pairs = []
        for place, chip in enumerate(self.order):
            to = self.order[(place + step) % self.chips]
            pairs += [(chip * CORES + core, to * CORES + core) for core in range(CORES)]
        return pairs

    def hop(self, value, step):
        return lax.ppermute(value, "row", self.perm(step))

    def sibling(self, value):
        return lax.ppermute(value, "row", [(d, d ^ 1) for d in range(self.devices)])

    def device_at(self, offset, other_core):
        me = lax.axis_index("row")
        order = jnp.array(self.order, jnp.int32)
        place_of = jnp.array([self.order.index(c) for c in range(self.chips)], jnp.int32)
        chip = order[(place_of[me // CORES] + offset) % self.chips]
        core = me % CORES
        return chip * CORES + (1 - core if other_core else core)


class Waves:
    def __init__(self):
        self.pending = {}
        self.done = {}
        self.token = None

    def go(self, **values):
        assert not set(values) & (set(self.pending) | set(self.done))
        self.pending.update(values)

    def close(self):
        names, values = list(self.pending), list(self.pending.values())
        flat, tree = jax.tree.flatten(values)
        flat = lax.optimization_barrier(flat)
        self.token = flat[0]
        self.done.update(zip(names, jax.tree.unflatten(tree, flat)))
        self.pending = {}

    def gate(self, value):
        if self.token is None:
            return value
        return lax.optimization_barrier((value, self.token))[0]

    def __getitem__(self, name):
        return self.done[name]


def shift_groups(size):
    ends = sorted({1, size - 1})
    return ends, [s for s in range(2, size - 1)]


def send(blocks, shifts):
    size = len(blocks)
    return {
        (size - s) % size: lax.ppermute(blocks[s], "rep", [(i, (i + s) % size) for i in range(size)]) for s in shifts
    }


def ordered(own, *groups):
    got = {0: own}
    for group in groups:
        got.update(group)
    return [got[u] for u in range(len(got))]


def masked_tiles(tiles, i, count):
    found = []
    for k in range(tiles.shape[1]):
        tile = tiles[i, k]
        found.append(jnp.where(k < count, tile, jnp.zeros_like(tile)))
    return jnp.concatenate(found, axis=1)


def step_spec(blocks, slots, tile_size, parts, per_step, skip):
    def index(t, cols, cnt, meta):
        return (lax.rem(meta[0] + t, parts) * (blocks // parts // per_step) + skip, 0, 0, 0)

    return pl.BlockSpec((per_step, slots, tile_size, tile_size), index)


def aligned(start, size, unit):
    return pl.ds(pl.multiple_of(start, unit), size)


def spmm_kernel(n_pieces, per_part, skip, cols, counts, meta, tiles, *refs):
    parts = pl.num_programs(0)
    n_outs = len(refs) - n_pieces - 3
    pieces, outs = refs[:n_pieces], refs[n_pieces : n_pieces + n_outs]
    source, result, sems = refs[n_pieces + n_outs :]
    t = pl.program_id(0)
    per_step, slots, tile_size, _ = tiles.shape

    @pl.when(t == 0)
    def _():
        copies = []
        for p, piece in enumerate(pieces):
            copies.append(
                pltpu.make_async_copy(piece, source.at[aligned(meta[1 + p], piece.shape[0], tile_size)], sems.at[p])
            )
            copies[-1].start()
        for copy in copies:
            copy.wait()

    for i in range(per_step):
        b = lax.rem(meta[0] + t, parts) * per_part + skip * per_step + i
        right = [source[aligned(cols[b, k] * tile_size, tile_size, tile_size), :] for k in range(slots)]
        product = jnp.dot(
            masked_tiles(tiles, i, counts[b]), jnp.concatenate(right, axis=0), preferred_element_type=F32
        )
        result[i * tile_size : (i + 1) * tile_size, :] = product.astype(BF16)

    for u in range(n_outs):

        @pl.when(t == u)
        def _():
            outs[u][...] = result[...]


def spmm(tiles, columns, counts, meta, pieces, parts, cut, skip):
    blocks, slots, tile_size, _ = tiles.shape
    width = pieces[0].shape[1]
    total_rows = sum(v.shape[0] for v in pieces)
    per_part = blocks // parts
    per_step = per_part // cut
    rows = per_step * tile_size
    return pl.pallas_call(
        functools.partial(spmm_kernel, len(pieces), per_part, skip),
        grid_spec=pltpu.PrefetchScalarGridSpec(
            num_scalar_prefetch=3,
            grid=(parts,),
            in_specs=[step_spec(blocks, slots, tile_size, parts, per_step, skip)] + [any_spec()] * len(pieces),
            out_specs=[pl.BlockSpec((rows, width), lambda t, cols, cnt, meta: (0, 0))] * parts,
            scratch_shapes=[
                pltpu.VMEM((total_rows, width), BF16),
                pltpu.VMEM((rows, width), BF16),
                pltpu.SemaphoreType.DMA((len(pieces),)),
            ],
        ),
        out_shape=[jax.ShapeDtypeStruct((rows, width), BF16)] * parts,
        compiler_params=params(),
        cost_estimate=pl.CostEstimate(
            flops=2 * parts * rows * slots * tile_size * width,
            bytes_accessed=2 * (tiles.size // cut + total_rows * width),
            transcendentals=0,
        ),
        name="spmm",
    )(columns, counts, meta, tiles, *pieces)


def spmm_t_kernel(n_grads, per_part, n_outs, terms, cols, counts, meta, tiles, *refs):
    parts = pl.num_programs(0)
    grads, outs = refs[:n_grads], refs[n_grads : n_grads + n_outs]
    total, grad, stage, in_sems, out_sems = refs[n_grads + n_outs :]
    t = pl.program_id(0)
    per_step, slots, tile_size, _ = tiles.shape
    width = grad.shape[1]
    rows = stage.shape[1]

    @pl.when(t == 0)
    def _():
        copies, start = [], 0
        for g, ref in enumerate(grads):
            copies.append(pltpu.make_async_copy(ref, grad.at[pl.ds(start, ref.shape[0])], in_sems.at[g]))
            copies[-1].start()
            start += ref.shape[0]

        @pl.loop(0, total.shape[0] // tile_size, unroll=8)
        def _(i):
            total[aligned(i * tile_size, tile_size, tile_size), :] = jnp.zeros((tile_size, width), F32)

        for copy in copies:
            copy.wait()

    for i in range(per_step):
        b = lax.rem(meta[0] + t, parts) * per_part + i
        block = grad[aligned((t * per_step + i) * tile_size, tile_size, tile_size), :]
        part = lax.dot_general(
            masked_tiles(tiles, i, counts[b]), block, (((0,), (0,)), ((), ())), preferred_element_type=F32
        )
        for k in range(slots):
            total[aligned(cols[b, k] * tile_size, tile_size, tile_size), :] += part[k * tile_size : (k + 1) * tile_size]

    @pl.when(t == parts - 1)
    def _():
        copies = []
        for o, (out, at) in enumerate(terms):
            slot = o % 2
            if o >= 2:
                copies[o - 2].wait()

            @pl.loop(0, rows // tile_size, unroll=4)
            def _(i):
                start = aligned(meta[1 + o] + i * tile_size, tile_size, tile_size)
                stage[slot, aligned(i * tile_size, tile_size, tile_size), :] = total[start, :].astype(BF16)

            copies.append(
                pltpu.make_async_copy(stage.at[slot], outs[out].at[pl.ds(at * rows, rows)], out_sems.at[o])
            )
            copies[o].start()
        for copy in copies[-2:]:
            copy.wait()


def spmm_t(tiles, columns, counts, meta, grads, parts, held, rows, total_rows):
    blocks, slots, tile_size, _ = tiles.shape
    width = grads[0].shape[1]
    per_part = blocks // parts
    flat = [(out, at) for out, many in enumerate(held) for at in range(many)]
    return pl.pallas_call(
        functools.partial(spmm_t_kernel, len(grads), per_part, len(held), flat),
        grid_spec=pltpu.PrefetchScalarGridSpec(
            num_scalar_prefetch=3,
            grid=(parts,),
            in_specs=[step_spec(blocks, slots, tile_size, parts, per_part, 0)] + [any_spec()] * len(grads),
            out_specs=[any_spec()] * len(held),
            scratch_shapes=[
                pltpu.VMEM((total_rows, width), F32),
                pltpu.VMEM((rows, width), BF16),
                pltpu.VMEM((2, rows, width), BF16),
                pltpu.SemaphoreType.DMA((len(grads),)),
                pltpu.SemaphoreType.DMA((len(flat),)),
            ],
        ),
        out_shape=[jax.ShapeDtypeStruct((many * rows, width), BF16) for many in held],
        compiler_params=params(),
        cost_estimate=pl.CostEstimate(
            flops=2 * blocks * slots * tile_size * tile_size * width,
            bytes_accessed=2 * (tiles.size + total_rows * width),
            transcendentals=0,
        ),
        name="spmm_t",
    )(columns, counts, meta, tiles, *grads)


def dense_kernel(parts, chunks, meta, *refs):
    n_mixed = parts * chunks
    mixed_refs, cot_refs, w_hbm = refs[:n_mixed], refs[n_mixed : n_mixed + parts], refs[n_mixed + parts]
    outs = refs[n_mixed + parts + 1 :]
    act_outs, mg_outs = outs[:parts], outs[parts : parts + n_mixed]
    mixed_out, grad_out, weight, sems = outs[parts + n_mixed :]
    f_wide, h_wide = weight.shape[0] // parts, weight.shape[1] // parts
    width = f_wide // chunks
    me = meta[0]

    def place(u):
        return lax.rem(me + u, parts)

    @pl.when(pl.program_id(0) == 0)
    def _():
        copies = []
        for i in range(parts):
            for j in range(parts):
                src = w_hbm.at[aligned(place(i) * f_wide, f_wide, f_wide), aligned(place(j) * h_wide, h_wide, h_wide)]
                dst = weight.at[pl.ds(i * f_wide, f_wide), pl.ds(j * h_wide, h_wide)]
                copies.append(pltpu.make_async_copy(src, dst, sems.at[i * parts + j]))
                copies[-1].start()
        for copy in copies:
            copy.wait()

    mixed = jnp.concatenate([ref[...] for ref in mixed_refs], axis=1)
    for u in range(parts):
        at = pl.ds(pl.multiple_of(place(u) * f_wide, f_wide), f_wide)
        mixed_out[:, at] = mixed[:, u * f_wide : (u + 1) * f_wide]
    grads = []
    for u in range(parts):
        preact = jnp.dot(mixed, weight[:, u * h_wide : (u + 1) * h_wide], preferred_element_type=F32)
        sig = jax.nn.sigmoid(preact)
        act_outs[u][...] = (preact * sig).astype(BF16)
        grads.append((cot_refs[u][...].astype(F32) * sig * (1.0 + preact * (1.0 - sig))).astype(BF16))
        at = pl.ds(pl.multiple_of(place(u) * h_wide, h_wide), h_wide)
        grad_out[:, at] = grads[u]
    grad = jnp.concatenate(grads, axis=1)
    back = lax.dot_general(grad, weight[...], (((1,), (1,)), ((), ())), preferred_element_type=F32).astype(BF16)
    for i in range(n_mixed):
        mg_outs[i][...] = back[:, i * width : (i + 1) * width]


def dense(meta, mixed, cot, weight, rows, first):
    parts, chunks = len(mixed), len(mixed[0])
    width = mixed[0][0][0].shape[1]
    features, hidden = weight.shape
    h_wide = hidden // parts
    step = min(rows, 256)

    def spec(w, start=0):
        return pl.BlockSpec((step, w), lambda t, meta: (t + start // step, 0))

    flat = [m for row in mixed for m in row]
    outs = pl.pallas_call(
        functools.partial(dense_kernel, parts, chunks),
        grid_spec=pltpu.PrefetchScalarGridSpec(
            num_scalar_prefetch=1,
            grid=(rows // step,),
            in_specs=[spec(width, at) for _, at in flat] + [spec(h_wide, first)] * parts + [any_spec()],
            out_specs=[spec(h_wide)] * parts + [spec(width)] * (parts * chunks) + [spec(features), spec(hidden)],
            scratch_shapes=[pltpu.VMEM((features, hidden), BF16), pltpu.SemaphoreType.DMA((parts * parts,))],
        ),
        out_shape=[jax.ShapeDtypeStruct((rows, h_wide), BF16)] * parts
        + [jax.ShapeDtypeStruct((rows, width), BF16)] * (parts * chunks)
        + [jax.ShapeDtypeStruct((rows, features), BF16), jax.ShapeDtypeStruct((rows, hidden), BF16)],
        compiler_params=params(),
        cost_estimate=pl.CostEstimate(
            flops=4 * rows * features * hidden,
            bytes_accessed=2 * (features * hidden + 6 * rows * hidden),
            transcendentals=rows * hidden,
        ),
        name="dense",
    )(meta, *[m for m, _ in flat], *cot, weight)
    n = parts * chunks
    act, back = outs[:parts], outs[parts : parts + n]
    return act, [back[u * chunks : (u + 1) * chunks] for u in range(parts)], outs[-2], outs[-1]


def local(features, tiles, columns, counts, weight, cotangent):
    rows, f_wide = features.shape
    h_wide = cotangent.shape[1]
    row_size, parts = lax.axis_size("row"), lax.axis_size("rep")
    ring = Ring(row_size)
    rep = lax.axis_index("rep")
    chunks = f_wide // LANES if f_wide % LANES == 0 else 1
    width = f_wide // chunks
    half = rows // 2
    part_rows = rows // parts
    halves = 2
    half_rows = part_rows // halves
    middle = ring.chips // 2
    near = [o for o in range(ring.chips) if o != middle]
    ends, inner = shift_groups(parts)
    last = chunks - 1
    w = Waves()

    offsets = [(0, 0)] + [(o, 0) for step in range(1, middle) for o in (-step, step)] + [(middle, 0), (middle, half)]
    own_meta = [ring.device_at(o, False) * rows + at for o, at in offsets]
    other_meta = [ring.device_at(o, True) * rows + at for o, at in offsets]
    spmm_meta = jnp.stack([rep] + own_meta + other_meta).astype(jnp.int32)
    held = [1] + [1] * len(near) + [1, len(near)]
    order = [middle] + near
    terms_at = [ring.device_at(o, other) * rows for other in (False, True) for o in order]
    spmm_t_meta = jnp.stack([rep] + terms_at).astype(jnp.int32)
    dense_meta = rep[None].astype(jnp.int32)

    def part_of(x, u):
        return lax.dynamic_slice_in_dim(x, lax.rem(rep + u, parts) * part_rows, part_rows, 0)

    share = weight.shape[0] // row_size
    w_share = lax.dynamic_slice_in_dim(weight, lax.axis_index("row") * share, share, 0)
    w_share = lax.all_gather(w_share, "rep", axis=1, tiled=True)

    cot_blocks = [part_of(cotangent, u) for u in range(parts)]
    xs = [features[:, c * width : (c + 1) * width] for c in range(chunks)]
    up = down = xs[0]
    got_own = {}
    got_other = {}
    mixed = {}

    def run_spmm(c, cut, skip):
        own = [got_own[c, i] for i in range(len(offsets))]
        other = [got_other[c, i] for i in range(len(offsets))]
        return spmm(tiles, columns, counts, spmm_meta, own + other, parts, cut, skip)

    w.go(metas=(spmm_meta, spmm_t_meta, dense_meta))
    for c in range(chunks):
        if c == 0:
            w.go(own=ring.sibling(features), cot_ends=send(cot_blocks, ends))
        got_own[c, 0] = xs[c]
        for step in range(1, middle):
            name = f"{c}_{step}"
            w.go(**{"up" + name: ring.hop(up, 1), "down" + name: ring.hop(down, -1)})
            if c and step == 1:
                for i in (-2, -1):
                    got_other[c - 1, len(offsets) + i] = ring.sibling(got_own[c - 1, len(offsets) + i])
                w.go(**{f"mixed{c - 1}": run_spmm(c - 1, 1, 0)})
            w.close()
            up, down = w["up" + name], w["down" + name]
            got_own[c, 2 * step - 1], got_own[c, 2 * step] = up, down
            w.go(**{"other_up" + name: ring.sibling(up), "other_down" + name: ring.sibling(down)})
        w.go(**{f"far_up{c}": ring.hop(up[:half], 1), f"far_down{c}": ring.hop(down[half:], -1)})
        if c:
            mixed[c - 1] = w[f"mixed{c - 1}"]
            w.go(**{f"mixed_ends{c - 1}": send(mixed[c - 1], ends)})
        w.close()
        if c == 0:
            spmm_meta, spmm_t_meta, dense_meta = w["metas"]
        if c == 0:
            w.go(cot_inner=send([w.gate(b) for b in cot_blocks], inner))
            w_full = lax.all_gather(w.gate(w_share), "row", axis=0, tiled=True)
        else:
            w.go(**{f"mixed_inner{c - 1}": send(mixed[c - 1], inner)})
        got_own[c, len(offsets) - 2], got_own[c, len(offsets) - 1] = w[f"far_up{c}"], w[f"far_down{c}"]
        got_other[c, 0] = w["own"][:, c * width : (c + 1) * width]
        for step in range(1, middle):
            name = f"{c}_{step}"
            got_other[c, 2 * step - 1], got_other[c, 2 * step] = w["other_up" + name], w["other_down" + name]
        if c < last:
            up = down = w.gate(xs[c + 1])
    for i in (-2, -1):
        got_other[last, len(offsets) + i] = ring.sibling(got_own[last, len(offsets) + i])

    for h in range(halves):
        w.go(**{f"half{h}": run_spmm(last, halves, h)})
        w.close()
        w.go(**{f"half_got{h}": send(w[f"half{h}"], ends + inner)})

    cot = ordered(cot_blocks[0], w["cot_ends"], w["cot_inner"])
    whole = [ordered(mixed[c][0], w[f"mixed_ends{c}"], w[f"mixed_inner{c}"]) for c in range(last)]
    sums = 0.0
    for h in range(halves):
        part = ordered(w[f"half{h}"][0], w[f"half_got{h}"])
        blocks = [[(whole[c][u], h * half_rows) for c in range(last)] + [(part[u], 0)] for u in range(parts)]
        act, back, mixed_rows, grad_rows = dense(dense_meta, blocks, cot, w_full, half_rows, h * half_rows)
        sums += lax.dot_general(mixed_rows, grad_rows, (((0,), (0,)), ((), ())), preferred_element_type=F32)
        w.go(**{f"act{h}": act, f"back{h}": back})
        w.close()
        w.go(**{f"back_got0_{h}": send([b[0] for b in w[f"back{h}"]], ends + inner)})
    w.close()

    weight_terms = lax.psum_scatter(sums.astype(BF16), "row", scatter_dimension=1, tiled=True)
    weight_grad = lax.psum_scatter(weight_terms, "rep", scatter_dimension=0, tiled=True).astype(F32)

    act_blocks = [jnp.concatenate([w[f"act{h}"][u] for h in range(halves)]) for u in range(parts)]
    feature_grad = []
    for c in range(chunks):
        grads = [
            ordered(w[f"back{h}"][0][c], w[f"back_got{c}_{h}"])[u] for u in range(parts) for h in range(halves)
        ]
        if c:
            grads = [w.gate(g) for g in grads]
        w.go(**{f"terms{c}": spmm_t(tiles, columns, counts, spmm_t_meta, grads, parts, held, rows, rows * row_size)})
        if c < last:
            for h in range(halves):
                w.go(**{f"back_got{c + 1}_{h}": send([w.gate(b[c + 1]) for b in w[f"back{h}"]], ends + inner)})
        w.close()
        terms = w[f"terms{c}"]
        own_far, own_near, other_far, other_near = terms[0], terms[1:-2], terms[-2], terms[-1]
        got_far = ring.sibling(other_far)
        w.go(**{f"got_near{c}": ring.sibling(other_near)})

        def far(start):
            return own_far[start : start + half].astype(F32) + got_far[start : start + half].astype(F32)

        up = ring.hop(far(0).astype(BF16), 1)
        down = ring.hop(far(half).astype(BF16), -1)
        w.go(**{f"sum{c}_{middle}": (up, down)})
        if c == last:
            w.go(act_inner=send(act_blocks, inner))
        w.close()
        got_near = w[f"got_near{c}"]

        def near_sum(offset):
            at = near.index(offset % ring.chips)
            return own_near[at].astype(F32) + got_near[at * rows : (at + 1) * rows].astype(F32)

        for step in range(middle - 1, 0, -1):
            up, down = w[f"sum{c}_{step + 1}"]
            to_up, to_down = near_sum(step), near_sum(-step)
            if step == middle - 1:
                to_up = jnp.concatenate([to_up[:half] + up.astype(F32), to_up[half:]])
                to_down = jnp.concatenate([to_down[:half], to_down[half:] + down.astype(F32)])
            else:
                to_up, to_down = to_up + up.astype(F32), to_down + down.astype(F32)
            to_up, to_down = to_up.astype(BF16), to_down.astype(BF16)
            w.go(**{f"sum{c}_{step}": (ring.hop(to_up, 1), ring.hop(to_down, -1))})
            if c == 0 and step == middle - 1:
                w.go(act_ends=send([w.gate(a) for a in act_blocks], ends))
            if step > 1:
                w.close()
            elif c < last:
                w.token = to_up[:8]
        up, down = (w.pending if f"sum{c}_1" in w.pending else w.done)[f"sum{c}_1"]
        if middle == 1:
            feature_grad.append((near_sum(0) + jnp.concatenate([up, down]).astype(F32)).astype(BF16))
        else:
            feature_grad.append((near_sum(0) + up.astype(F32) + down.astype(F32)).astype(BF16))
    act = {**w.pending, **w.done}
    act = ordered(act_blocks[0], act["act_ends"], act["act_inner"])
    feature_grad = jnp.concatenate(feature_grad, axis=1)
    activations = jnp.zeros((rows, h_wide), BF16)
    for u in range(parts):
        activations = lax.dynamic_update_slice_in_dim(activations, act[u], lax.rem(rep + u, parts) * part_rows, 0)
    return (activations, feature_grad, weight_grad)


def solution(mesh):
    in_specs = (
        P("row", "rep"),
        P("row", None, None, None),
        P("row", None),
        P("row"),
        P(None, "rep"),
        P("row", "rep"),
    )
    out_specs = (P("row", "rep"), P("row", "rep"), P("rep", "row"))
    return jax.shard_map(local, mesh=mesh, in_specs=in_specs, out_specs=out_specs, check_vma=False)
```

```python
import functools
import jax
import jax.numpy as jnp
from jax import lax
from jax.experimental import pallas as pl
from jax.experimental.pallas import tpu as pltpu
from jax.sharding import PartitionSpec as P

BF16, F32 = jnp.bfloat16, jnp.float32
VMEM_LIMIT = 56 * 1024 * 1024
LANES = 128
CORES = 2


def params():
    return pltpu.CompilerParams(vmem_limit_bytes=VMEM_LIMIT)


def any_spec():
    return pl.BlockSpec(memory_space=pl.ANY)


class Ring:
    def __init__(self, devices):
        self.chips = devices // CORES
        half = self.chips // 2
        self.order = list(range(half)) + list(range(self.chips - 1, half - 1, -1))
        self.devices = devices

    def perm(self, step):
        pairs = []
        for place, chip in enumerate(self.order):
            to = self.order[(place + step) % self.chips]
            pairs += [(chip * CORES + core, to * CORES + core) for core in range(CORES)]
        return pairs

    def hop(self, value, step):
        return lax.ppermute(value, "row", self.perm(step))

    def sibling(self, value):
        return lax.ppermute(value, "row", [(d, d ^ 1) for d in range(self.devices)])

    def device_at(self, offset, other_core):
        me = lax.axis_index("row")
        order = jnp.array(self.order, jnp.int32)
        place_of = jnp.array([self.order.index(c) for c in range(self.chips)], jnp.int32)
        chip = order[(place_of[me // CORES] + offset) % self.chips]
        core = me % CORES
        return chip * CORES + (1 - core if other_core else core)


class Waves:
    def __init__(self):
        self.pending = {}
        self.done = {}
        self.token = None

    def go(self, **values):
        assert not set(values) & (set(self.pending) | set(self.done))
        self.pending.update(values)

    def close(self):
        names, values = list(self.pending), list(self.pending.values())
        flat, tree = jax.tree.flatten(values)
        flat = lax.optimization_barrier(flat)
        self.token = flat[0]
        self.done.update(zip(names, jax.tree.unflatten(tree, flat)))
        self.pending = {}

    def gate(self, value):
        if self.token is None:
            return value
        return lax.optimization_barrier((value, self.token))[0]

    def __getitem__(self, name):
        return self.done[name]


def shift_groups(size):
    ends = sorted({1, size - 1})
    return ends, [s for s in range(2, size - 1)]


def send(blocks, shifts):
    size = len(blocks)
    return {
        (size - s) % size: lax.ppermute(blocks[s], "rep", [(i, (i + s) % size) for i in range(size)]) for s in shifts
    }


def ordered(own, *groups):
    got = {0: own}
    for group in groups:
        got.update(group)
    return [got[u] for u in range(len(got))]


def masked_tiles(tiles, i, count):
    found = []
    for k in range(tiles.shape[1]):
        tile = tiles[i, k]
        found.append(jnp.where(k < count, tile, jnp.zeros_like(tile)))
    return jnp.concatenate(found, axis=1)


def step_spec(blocks, slots, tile_size, parts, per_step, skip):
    def index(t, cols, cnt, meta):
        return (lax.rem(meta[0] + t, parts) * (blocks // parts // per_step) + skip, 0, 0, 0)

    return pl.BlockSpec((per_step, slots, tile_size, tile_size), index)


def aligned(start, size, unit):
    return pl.ds(pl.multiple_of(start, unit), size)


def spmm_kernel(n_pieces, per_part, skip, cols, counts, meta, tiles, *refs):
    parts = pl.num_programs(0)
    n_outs = len(refs) - n_pieces - 3
    pieces, outs = refs[:n_pieces], refs[n_pieces : n_pieces + n_outs]
    source, result, sems = refs[n_pieces + n_outs :]
    t = pl.program_id(0)
    per_step, slots, tile_size, _ = tiles.shape

    @pl.when(t == 0)
    def _():
        copies = []
        for p, piece in enumerate(pieces):
            copies.append(
                pltpu.make_async_copy(piece, source.at[aligned(meta[1 + p], piece.shape[0], tile_size)], sems.at[p])
            )
            copies[-1].start()
        for copy in copies:
            copy.wait()

    for i in range(per_step):
        b = lax.rem(meta[0] + t, parts) * per_part + skip * per_step + i
        right = [source[aligned(cols[b, k] * tile_size, tile_size, tile_size), :] for k in range(slots)]
        product = jnp.dot(
            masked_tiles(tiles, i, counts[b]), jnp.concatenate(right, axis=0), preferred_element_type=F32
        )
        result[i * tile_size : (i + 1) * tile_size, :] = product.astype(BF16)

    for u in range(n_outs):

        @pl.when(t == u)
        def _():
            outs[u][...] = result[...]


def spmm(tiles, columns, counts, meta, pieces, parts, cut, skip):
    blocks, slots, tile_size, _ = tiles.shape
    width = pieces[0].shape[1]
    total_rows = sum(v.shape[0] for v in pieces)
    per_part = blocks // parts
    per_step = per_part // cut
    rows = per_step * tile_size
    return pl.pallas_call(
        functools.partial(spmm_kernel, len(pieces), per_part, skip),
        grid_spec=pltpu.PrefetchScalarGridSpec(
            num_scalar_prefetch=3,
            grid=(parts,),
            in_specs=[step_spec(blocks, slots, tile_size, parts, per_step, skip)] + [any_spec()] * len(pieces),
            out_specs=[pl.BlockSpec((rows, width), lambda t, cols, cnt, meta: (0, 0))] * parts,
            scratch_shapes=[
                pltpu.VMEM((total_rows, width), BF16),
                pltpu.VMEM((rows, width), BF16),
                pltpu.SemaphoreType.DMA((len(pieces),)),
            ],
        ),
        out_shape=[jax.ShapeDtypeStruct((rows, width), BF16)] * parts,
        compiler_params=params(),
        cost_estimate=pl.CostEstimate(
            flops=2 * parts * rows * slots * tile_size * width,
            bytes_accessed=2 * (tiles.size // cut + total_rows * width),
            transcendentals=0,
        ),
        name="spmm",
    )(columns, counts, meta, tiles, *pieces)


def spmm_t_kernel(n_grads, per_part, n_outs, terms, cols, counts, meta, tiles, *refs):
    parts = pl.num_programs(0)
    grads, outs = refs[:n_grads], refs[n_grads : n_grads + n_outs]
    total, grad, stage, in_sems, out_sems = refs[n_grads + n_outs :]
    t = pl.program_id(0)
    per_step, slots, tile_size, _ = tiles.shape
    width = grad.shape[1]
    rows = stage.shape[1]

    @pl.when(t == 0)
    def _():
        copies, start = [], 0
        for g, ref in enumerate(grads):
            copies.append(pltpu.make_async_copy(ref, grad.at[pl.ds(start, ref.shape[0])], in_sems.at[g]))
            copies[-1].start()
            start += ref.shape[0]

        @pl.loop(0, total.shape[0] // tile_size, unroll=8)
        def _(i):
            total[aligned(i * tile_size, tile_size, tile_size), :] = jnp.zeros((tile_size, width), F32)

        for copy in copies:
            copy.wait()

    for i in range(per_step):
        b = lax.rem(meta[0] + t, parts) * per_part + i
        block = grad[aligned((t * per_step + i) * tile_size, tile_size, tile_size), :]
        part = lax.dot_general(
            masked_tiles(tiles, i, counts[b]), block, (((0,), (0,)), ((), ())), preferred_element_type=F32
        )
        for k in range(slots):
            total[aligned(cols[b, k] * tile_size, tile_size, tile_size), :] += part[k * tile_size : (k + 1) * tile_size]

    @pl.when(t == parts - 1)
    def _():
        copies = []
        for o, (out, at) in enumerate(terms):
            slot = o % 2
            if o >= 2:
                copies[o - 2].wait()

            @pl.loop(0, rows // tile_size, unroll=4)
            def _(i):
                start = aligned(meta[1 + o] + i * tile_size, tile_size, tile_size)
                stage[slot, aligned(i * tile_size, tile_size, tile_size), :] = total[start, :].astype(BF16)

            copies.append(
                pltpu.make_async_copy(stage.at[slot], outs[out].at[pl.ds(at * rows, rows)], out_sems.at[o])
            )
            copies[o].start()
        for copy in copies[-2:]:
            copy.wait()


def spmm_t(tiles, columns, counts, meta, grads, parts, held, rows, total_rows):
    blocks, slots, tile_size, _ = tiles.shape
    width = grads[0].shape[1]
    per_part = blocks // parts
    flat = [(out, at) for out, many in enumerate(held) for at in range(many)]
    return pl.pallas_call(
        functools.partial(spmm_t_kernel, len(grads), per_part, len(held), flat),
        grid_spec=pltpu.PrefetchScalarGridSpec(
            num_scalar_prefetch=3,
            grid=(parts,),
            in_specs=[step_spec(blocks, slots, tile_size, parts, per_part, 0)] + [any_spec()] * len(grads),
            out_specs=[any_spec()] * len(held),
            scratch_shapes=[
                pltpu.VMEM((total_rows, width), F32),
                pltpu.VMEM((rows, width), BF16),
                pltpu.VMEM((2, rows, width), BF16),
                pltpu.SemaphoreType.DMA((len(grads),)),
                pltpu.SemaphoreType.DMA((len(flat),)),
            ],
        ),
        out_shape=[jax.ShapeDtypeStruct((many * rows, width), BF16) for many in held],
        compiler_params=params(),
        cost_estimate=pl.CostEstimate(
            flops=2 * blocks * slots * tile_size * tile_size * width,
            bytes_accessed=2 * (tiles.size + total_rows * width),
            transcendentals=0,
        ),
        name="spmm_t",
    )(columns, counts, meta, tiles, *grads)


def dense_kernel(parts, chunks, n_earlier, meta, *refs):
    n_mixed = parts * chunks
    mixed_refs, cot_refs, w_hbm = refs[:n_mixed], refs[n_mixed : n_mixed + parts], refs[n_mixed + parts]
    outs = refs[n_mixed + parts + 1 + n_earlier :]
    act_outs, mg_outs = outs[:parts], outs[parts : parts + n_mixed]
    mixed_out, grad_out, weight, sems = outs[parts + n_mixed :]
    f_wide, h_wide = weight.shape[0] // parts, weight.shape[1] // parts
    width = f_wide // chunks
    me = meta[0]

    def place(u):
        return lax.rem(me + u, parts)

    @pl.when(pl.program_id(0) == 0)
    def _():
        copies = []
        for i in range(parts):
            for j in range(parts):
                src = w_hbm.at[aligned(place(i) * f_wide, f_wide, f_wide), aligned(place(j) * h_wide, h_wide, h_wide)]
                dst = weight.at[pl.ds(i * f_wide, f_wide), pl.ds(j * h_wide, h_wide)]
                copies.append(pltpu.make_async_copy(src, dst, sems.at[i * parts + j]))
                copies[-1].start()
        for copy in copies:
            copy.wait()

    mixed = jnp.concatenate([ref[...] for ref in mixed_refs], axis=1)
    for u in range(parts):
        at = pl.ds(pl.multiple_of(place(u) * f_wide, f_wide), f_wide)
        mixed_out[:, at] = mixed[:, u * f_wide : (u + 1) * f_wide]
    grads = []
    for u in range(parts):
        preact = jnp.dot(mixed, weight[:, u * h_wide : (u + 1) * h_wide], preferred_element_type=F32)
        sig = jax.nn.sigmoid(preact)
        act_outs[u][...] = (preact * sig).astype(BF16)
        grads.append((cot_refs[u][...].astype(F32) * sig * (1.0 + preact * (1.0 - sig))).astype(BF16))
        at = pl.ds(pl.multiple_of(place(u) * h_wide, h_wide), h_wide)
        grad_out[:, at] = grads[u]
    grad = jnp.concatenate(grads, axis=1)
    back = lax.dot_general(grad, weight[...], (((1,), (1,)), ((), ())), preferred_element_type=F32).astype(BF16)
    for i in range(n_mixed):
        mg_outs[i][...] = back[:, i * width : (i + 1) * width]


def dense(meta, mixed, cot, weight, rows, first, earlier):
    parts, chunks = len(mixed), len(mixed[0])
    width = mixed[0][0][0].shape[1]
    features, hidden = weight.shape
    h_wide = hidden // parts
    all_rows = cot[0].shape[0]
    step = min(rows, 256)
    flat = [m for row in mixed for m in row]
    earlier = list(earlier)

    def spec(w, start=0):
        return pl.BlockSpec((step, w), lambda t, meta: (t + start // step, 0))

    kinds = [(h_wide, True)] * parts + [(width, c > 0) for _ in range(parts) for c in range(chunks)]
    kinds += [(features, True), (hidden, True)]
    whole_at = [i for i, (_, whole) in enumerate(kinds) if whole]
    n_inputs = 1 + len(flat) + parts + 1
    outs = pl.pallas_call(
        functools.partial(dense_kernel, parts, chunks, len(earlier)),
        grid_spec=pltpu.PrefetchScalarGridSpec(
            num_scalar_prefetch=1,
            grid=(rows // step,),
            in_specs=[spec(width, at) for _, at in flat]
            + [spec(h_wide, first)] * parts
            + [any_spec()]
            + [any_spec()] * len(earlier),
            out_specs=[spec(w, first if whole else 0) for w, whole in kinds],
            scratch_shapes=[pltpu.VMEM((features, hidden), BF16), pltpu.SemaphoreType.DMA((parts * parts,))],
        ),
        out_shape=[jax.ShapeDtypeStruct((all_rows if whole else rows, w), BF16) for w, whole in kinds],
        input_output_aliases={n_inputs + i: at for i, at in enumerate(whole_at)} if earlier else {},
        compiler_params=params(),
        cost_estimate=pl.CostEstimate(
            flops=4 * rows * features * hidden,
            bytes_accessed=2 * (features * hidden + 6 * rows * hidden),
            transcendentals=rows * hidden,
        ),
        name="dense",
    )(meta, *[m for m, _ in flat], *cot, weight, *earlier)
    n = parts * chunks
    act, back = outs[:parts], outs[parts : parts + n]
    return (
        act,
        [back[u * chunks : (u + 1) * chunks] for u in range(parts)],
        outs[-2],
        outs[-1],
        [outs[i] for i in whole_at],
    )


def local(features, tiles, columns, counts, weight, cotangent):
    rows, f_wide = features.shape
    h_wide = cotangent.shape[1]
    row_size, parts = lax.axis_size("row"), lax.axis_size("rep")
    ring = Ring(row_size)
    rep = lax.axis_index("rep")
    chunks = f_wide // LANES if f_wide % LANES == 0 else 1
    width = f_wide // chunks
    half = rows // 2
    part_rows = rows // parts
    halves = 2
    half_rows = part_rows // halves
    middle = ring.chips // 2
    near = [o for o in range(ring.chips) if o != middle]
    ends, inner = shift_groups(parts)
    last = chunks - 1
    w = Waves()

    offsets = [(0, 0)] + [(o, 0) for step in range(1, middle) for o in (-step, step)] + [(middle, 0), (middle, half)]
    own_meta = [ring.device_at(o, False) * rows + at for o, at in offsets]
    other_meta = [ring.device_at(o, True) * rows + at for o, at in offsets]
    spmm_meta = jnp.stack([rep] + own_meta + other_meta).astype(jnp.int32)
    held = [1] + [1] * len(near) + [1, len(near)]
    order = [middle] + near
    terms_at = [ring.device_at(o, other) * rows for other in (False, True) for o in order]
    spmm_t_meta = jnp.stack([rep] + terms_at).astype(jnp.int32)
    dense_meta = rep[None].astype(jnp.int32)

    def part_of(x, u):
        return lax.dynamic_slice_in_dim(x, lax.rem(rep + u, parts) * part_rows, part_rows, 0)

    share = weight.shape[0] // row_size
    w_share = lax.dynamic_slice_in_dim(weight, lax.axis_index("row") * share, share, 0)
    w_share = lax.all_gather(w_share, "rep", axis=1, tiled=True)

    cot_blocks = [part_of(cotangent, u) for u in range(parts)]
    xs = [features[:, c * width : (c + 1) * width] for c in range(chunks)]
    up = down = xs[0]
    got_own = {}
    got_other = {}
    mixed = {}

    def run_spmm(c, cut, skip):
        own = [got_own[c, i] for i in range(len(offsets))]
        other = [got_other[c, i] for i in range(len(offsets))]
        return spmm(tiles, columns, counts, spmm_meta, own + other, parts, cut, skip)

    cot_ends = send(cot_blocks, ends)
    own_other = ring.sibling(features)
    for c in range(chunks):
        got_own[c, 0] = xs[c]
        got_other[c, 0] = own_other[:, c * width : (c + 1) * width]
        for step in range(1, middle):
            name = f"{c}_{step}"
            w.go(**{"up" + name: ring.hop(up, 1), "down" + name: ring.hop(down, -1)})
            if c and step == 1:
                for i in range(1, len(offsets)):
                    got_other[c - 1, i] = ring.sibling(got_own[c - 1, i])
                w.go(**{f"mixed{c - 1}": run_spmm(c - 1, 1, 0)})
            w.close()
            up, down = w["up" + name], w["down" + name]
            got_own[c, 2 * step - 1], got_own[c, 2 * step] = up, down
        w.go(**{f"far_up{c}": ring.hop(up[:half], 1), f"far_down{c}": ring.hop(down[half:], -1)})
        if c == 0:
            w.go(cot_ends=cot_ends, own_other=own_other, metas=(spmm_meta, spmm_t_meta, dense_meta))
        else:
            mixed[c - 1] = w[f"mixed{c - 1}"]
        if c == last:
            for step in range(1, middle):
                for i in (2 * step - 1, 2 * step):
                    got_other[c, i] = ring.sibling(got_own[c, i])
                    w.go(**{f"other{c}_{i}": got_other[c, i]})
        w.close()
        if c == 0:
            spmm_meta, spmm_t_meta, dense_meta = w["metas"]
            w.go(cot_inner=send([w.gate(b) for b in cot_blocks], inner))
        else:
            w.go(**{f"mixed_got{c - 1}": send(mixed[c - 1], ends + inner)})
        got_own[c, len(offsets) - 2], got_own[c, len(offsets) - 1] = w[f"far_up{c}"], w[f"far_down{c}"]
        if c < last:
            up = down = w.gate(xs[c + 1])
    w_full = lax.all_gather(w.gate(w_share), "row", axis=0, tiled=True)
    for i in (-2, -1):
        got_other[last, len(offsets) + i] = ring.sibling(got_own[last, len(offsets) + i])

    for h in range(halves):
        w.go(**{f"half{h}": run_spmm(last, halves, h)})
        w.close()
        w.go(**{f"half_got{h}": send(w[f"half{h}"], ends + inner)})

    cot = ordered(cot_blocks[0], w["cot_ends"], w["cot_inner"])
    whole = [ordered(mixed[c][0], w[f"mixed_got{c}"]) for c in range(last)]
    earlier = ()
    for h in range(halves):
        part = ordered(w[f"half{h}"][0], w[f"half_got{h}"])
        blocks = [[(whole[c][u], h * half_rows) for c in range(last)] + [(part[u], 0)] for u in range(parts)]
        act, back, mixed_rows, grad_rows, earlier = dense(
            dense_meta, blocks, cot, w_full, half_rows, h * half_rows, earlier
        )
        w.go(**{f"back{h}": [b[0] for b in back]})
        if h == halves - 1:
            w.go(whole=(act, back, mixed_rows, grad_rows))
        w.close()
        w.go(**{f"back_got{h}": send(w[f"back{h}"], ends + inner)})
    act, back, mixed_rows, grad_rows = w["whole"]
    sums = lax.dot_general(mixed_rows, grad_rows, (((0,), (0,)), ((), ())), preferred_element_type=F32)
    w.go(sums=sums.astype(BF16))
    w.close()
    weight_terms = lax.psum_scatter(w["sums"], "row", scatter_dimension=1, tiled=True)

    feature_grad = []
    for c in range(chunks):
        if c:
            grads = [w.gate(g) for g in ordered(back[0][c], w[f"rest_ends{c}"], w[f"rest_inner{c}"])]
        else:
            parts_got = [ordered(w[f"back{h}"][0], w[f"back_got{h}"]) for h in range(halves)]
            grads = [parts_got[h][u] for u in range(parts) for h in range(halves)]
        w.go(**{f"terms{c}": spmm_t(tiles, columns, counts, spmm_t_meta, grads, parts, held, rows, rows * row_size)})
        if c < last:
            rest = [w.gate(b[c + 1]) for b in back]
            w.go(**{f"rest_ends{c + 1}": send(rest, ends)})
        w.close()
        if c < last:
            w.go(**{f"rest_inner{c + 1}": send(rest, inner)})
        terms = w[f"terms{c}"]
        own_far, own_near, other_far, other_near = terms[0], terms[1:-2], terms[-2], terms[-1]
        got_far = ring.sibling(other_far)
        other_near = lax.optimization_barrier((other_near, got_far))[0]
        w.go(**{f"got_near{c}": ring.sibling(other_near)})

        def far(start):
            return own_far[start : start + half].astype(F32) + got_far[start : start + half].astype(F32)

        up = ring.hop(far(0).astype(BF16), 1)
        down = ring.hop(far(half).astype(BF16), -1)
        w.go(**{f"sum{c}_{middle}": (up, down)})
        if c == last:
            w.go(act_inner=send(act, inner))
        w.close()
        got_near = w[f"got_near{c}"]

        def near_sum(offset):
            at = near.index(offset % ring.chips)
            return own_near[at].astype(F32) + got_near[at * rows : (at + 1) * rows].astype(F32)

        for step in range(middle - 1, 0, -1):
            up, down = w[f"sum{c}_{step + 1}"]
            to_up, to_down = near_sum(step), near_sum(-step)
            if step == middle - 1:
                to_up = jnp.concatenate([to_up[:half] + up.astype(F32), to_up[half:]])
                to_down = jnp.concatenate([to_down[:half], to_down[half:] + down.astype(F32)])
            else:
                to_up, to_down = to_up + up.astype(F32), to_down + down.astype(F32)
            to_up, to_down = to_up.astype(BF16), to_down.astype(BF16)
            w.go(**{f"sum{c}_{step}": (ring.hop(to_up, 1), ring.hop(to_down, -1))})
            if c == 0 and step == middle - 1:
                w.go(act_ends=send([w.gate(a) for a in act], ends))
            if step > 1:
                w.close()
            else:
                w.token = to_up[:8]
        up, down = (w.pending if f"sum{c}_1" in w.pending else w.done)[f"sum{c}_1"]
        if middle == 1:
            feature_grad.append((near_sum(0) + jnp.concatenate([up, down]).astype(F32)).astype(BF16))
        else:
            feature_grad.append((near_sum(0) + up.astype(F32) + down.astype(F32)).astype(BF16))
    weight_grad = lax.psum_scatter(w.gate(weight_terms), "rep", scatter_dimension=0, tiled=True).astype(F32)
    got = {**w.pending, **w.done}
    act = ordered(act[0], got["act_ends"], got["act_inner"])
    feature_grad = jnp.concatenate(feature_grad, axis=1)
    activations = jnp.zeros((rows, h_wide), BF16)
    for u in range(parts):
        activations = lax.dynamic_update_slice_in_dim(activations, act[u], lax.rem(rep + u, parts) * part_rows, 0)
    return (activations, feature_grad, weight_grad)


def solution(mesh):
    in_specs = (
        P("row", "rep"),
        P("row", None, None, None),
        P("row", None),
        P("row"),
        P(None, "rep"),
        P("row", "rep"),
    )
    out_specs = (P("row", "rep"), P("row", "rep"), P("rep", "row"))
    return jax.shard_map(local, mesh=mesh, in_specs=in_specs, out_specs=out_specs, check_vma=False)
```

```python
import functools
import jax
import jax.numpy as jnp
from jax import lax
from jax.experimental import pallas as pl
from jax.experimental.pallas import tpu as pltpu
from jax.sharding import PartitionSpec as P

BF16, F32 = jnp.bfloat16, jnp.float32
VMEM_LIMIT = 56 * 1024 * 1024
LANES = 128
CORES = 2


def params():
    return pltpu.CompilerParams(vmem_limit_bytes=VMEM_LIMIT)


def any_spec():
    return pl.BlockSpec(memory_space=pl.ANY)


class Ring:
    def __init__(self, devices):
        self.chips = devices // CORES
        half = self.chips // 2
        self.order = list(range(half)) + list(range(self.chips - 1, half - 1, -1))
        self.devices = devices

    def perm(self, step):
        pairs = []
        for place, chip in enumerate(self.order):
            to = self.order[(place + step) % self.chips]
            pairs += [(chip * CORES + core, to * CORES + core) for core in range(CORES)]
        return pairs

    def hop(self, value, step):
        return lax.ppermute(value, "row", self.perm(step))

    def sibling(self, value):
        return lax.ppermute(value, "row", [(d, d ^ 1) for d in range(self.devices)])

    def device_at(self, offset, other_core):
        me = lax.axis_index("row")
        order = jnp.array(self.order, jnp.int32)
        place_of = jnp.array([self.order.index(c) for c in range(self.chips)], jnp.int32)
        chip = order[(place_of[me // CORES] + offset) % self.chips]
        core = me % CORES
        return chip * CORES + (1 - core if other_core else core)


class Waves:
    def __init__(self):
        self.pending = {}
        self.done = {}
        self.token = None

    def go(self, **values):
        assert not set(values) & (set(self.pending) | set(self.done))
        self.pending.update(values)

    def close(self):
        names, values = list(self.pending), list(self.pending.values())
        flat, tree = jax.tree.flatten(values)
        flat = lax.optimization_barrier(flat)
        self.token = flat[0]
        self.done.update(zip(names, jax.tree.unflatten(tree, flat)))
        self.pending = {}

    def gate(self, value):
        if self.token is None:
            return value
        return lax.optimization_barrier((value, self.token))[0]

    def __getitem__(self, name):
        return self.done[name]


def shift_groups(size):
    ends = sorted({1, size - 1})
    return ends, [s for s in range(2, size - 1)]


def send(blocks, shifts):
    size = len(blocks)
    return {
        (size - s) % size: lax.ppermute(blocks[s], "rep", [(i, (i + s) % size) for i in range(size)]) for s in shifts
    }


def ordered(own, *groups):
    got = {0: own}
    for group in groups:
        got.update(group)
    return [got[u] for u in range(len(got))]


def masked_tiles(tiles, i, count):
    found = []
    for k in range(tiles.shape[1]):
        tile = tiles[i, k]
        found.append(jnp.where(k < count, tile, jnp.zeros_like(tile)))
    return jnp.concatenate(found, axis=1)


def step_spec(blocks, slots, tile_size, parts, per_step, skip):
    def index(t, cols, cnt, meta):
        return (lax.rem(meta[0] + t, parts) * (blocks // parts // per_step) + skip, 0, 0, 0)

    return pl.BlockSpec((per_step, slots, tile_size, tile_size), index)


def aligned(start, size, unit):
    return pl.ds(pl.multiple_of(start, unit), size)


def spmm_kernel(n_pieces, per_part, skip, cols, counts, meta, tiles, *refs):
    parts = pl.num_programs(0)
    n_outs = len(refs) - n_pieces - 3
    pieces, outs = refs[:n_pieces], refs[n_pieces : n_pieces + n_outs]
    source, result, sems = refs[n_pieces + n_outs :]
    t = pl.program_id(0)
    per_step, slots, tile_size, _ = tiles.shape

    @pl.when(t == 0)
    def _():
        copies = []
        for p, piece in enumerate(pieces):
            copies.append(
                pltpu.make_async_copy(piece, source.at[aligned(meta[1 + p], piece.shape[0], tile_size)], sems.at[p])
            )
            copies[-1].start()
        for copy in copies:
            copy.wait()

    for i in range(per_step):
        b = lax.rem(meta[0] + t, parts) * per_part + skip * per_step + i
        right = [source[aligned(cols[b, k] * tile_size, tile_size, tile_size), :] for k in range(slots)]
        product = jnp.dot(
            masked_tiles(tiles, i, counts[b]), jnp.concatenate(right, axis=0), preferred_element_type=F32
        )
        result[i * tile_size : (i + 1) * tile_size, :] = product.astype(BF16)

    for u in range(n_outs):

        @pl.when(t == u)
        def _():
            outs[u][...] = result[...]


def spmm(tiles, columns, counts, meta, pieces, parts, cut, skip):
    blocks, slots, tile_size, _ = tiles.shape
    width = pieces[0].shape[1]
    total_rows = sum(v.shape[0] for v in pieces)
    per_part = blocks // parts
    per_step = per_part // cut
    rows = per_step * tile_size
    return pl.pallas_call(
        functools.partial(spmm_kernel, len(pieces), per_part, skip),
        grid_spec=pltpu.PrefetchScalarGridSpec(
            num_scalar_prefetch=3,
            grid=(parts,),
            in_specs=[step_spec(blocks, slots, tile_size, parts, per_step, skip)] + [any_spec()] * len(pieces),
            out_specs=[pl.BlockSpec((rows, width), lambda t, cols, cnt, meta: (0, 0))] * parts,
            scratch_shapes=[
                pltpu.VMEM((total_rows, width), BF16),
                pltpu.VMEM((rows, width), BF16),
                pltpu.SemaphoreType.DMA((len(pieces),)),
            ],
        ),
        out_shape=[jax.ShapeDtypeStruct((rows, width), BF16)] * parts,
        compiler_params=params(),
        cost_estimate=pl.CostEstimate(
            flops=2 * parts * rows * slots * tile_size * width,
            bytes_accessed=2 * (tiles.size // cut + total_rows * width),
            transcendentals=0,
        ),
        name="spmm",
    )(columns, counts, meta, tiles, *pieces)


def spmm_t_kernel(n_grads, per_part, n_outs, terms, cols, counts, meta, tiles, *refs):
    parts = pl.num_programs(0)
    grads, outs = refs[:n_grads], refs[n_grads : n_grads + n_outs]
    total, grad, stage, in_sems, out_sems = refs[n_grads + n_outs :]
    t = pl.program_id(0)
    per_step, slots, tile_size, _ = tiles.shape
    width = grad.shape[1]
    rows = stage.shape[1]

    @pl.when(t == 0)
    def _():
        copies, start = [], 0
        for g, ref in enumerate(grads):
            copies.append(pltpu.make_async_copy(ref, grad.at[pl.ds(start, ref.shape[0])], in_sems.at[g]))
            copies[-1].start()
            start += ref.shape[0]

        @pl.loop(0, total.shape[0] // tile_size, unroll=8)
        def _(i):
            total[aligned(i * tile_size, tile_size, tile_size), :] = jnp.zeros((tile_size, width), F32)

        for copy in copies:
            copy.wait()

    for i in range(per_step):
        b = lax.rem(meta[0] + t, parts) * per_part + i
        block = grad[aligned((t * per_step + i) * tile_size, tile_size, tile_size), :]
        part = lax.dot_general(
            masked_tiles(tiles, i, counts[b]), block, (((0,), (0,)), ((), ())), preferred_element_type=F32
        )
        for k in range(slots):
            total[aligned(cols[b, k] * tile_size, tile_size, tile_size), :] += part[k * tile_size : (k + 1) * tile_size]

    @pl.when(t == parts - 1)
    def _():
        copies = []
        for o, (out, at) in enumerate(terms):
            slot = o % 2
            if o >= 2:
                copies[o - 2].wait()

            @pl.loop(0, rows // tile_size, unroll=4)
            def _(i):
                start = aligned(meta[1 + o] + i * tile_size, tile_size, tile_size)
                stage[slot, aligned(i * tile_size, tile_size, tile_size), :] = total[start, :].astype(BF16)

            copies.append(
                pltpu.make_async_copy(stage.at[slot], outs[out].at[pl.ds(at * rows, rows)], out_sems.at[o])
            )
            copies[o].start()
        for copy in copies[-2:]:
            copy.wait()


def spmm_t(tiles, columns, counts, meta, grads, parts, held, rows, total_rows):
    blocks, slots, tile_size, _ = tiles.shape
    width = grads[0].shape[1]
    per_part = blocks // parts
    flat = [(out, at) for out, many in enumerate(held) for at in range(many)]
    return pl.pallas_call(
        functools.partial(spmm_t_kernel, len(grads), per_part, len(held), flat),
        grid_spec=pltpu.PrefetchScalarGridSpec(
            num_scalar_prefetch=3,
            grid=(parts,),
            in_specs=[step_spec(blocks, slots, tile_size, parts, per_part, 0)] + [any_spec()] * len(grads),
            out_specs=[any_spec()] * len(held),
            scratch_shapes=[
                pltpu.VMEM((total_rows, width), F32),
                pltpu.VMEM((rows, width), BF16),
                pltpu.VMEM((2, rows, width), BF16),
                pltpu.SemaphoreType.DMA((len(grads),)),
                pltpu.SemaphoreType.DMA((len(flat),)),
            ],
        ),
        out_shape=[jax.ShapeDtypeStruct((many * rows, width), BF16) for many in held],
        compiler_params=params(),
        cost_estimate=pl.CostEstimate(
            flops=2 * blocks * slots * tile_size * tile_size * width,
            bytes_accessed=2 * (tiles.size + total_rows * width),
            transcendentals=0,
        ),
        name="spmm_t",
    )(columns, counts, meta, tiles, *grads)


def dense_kernel(parts, chunks, n_earlier, meta, *refs):
    n_mixed = parts * chunks
    mixed_refs, cot_refs, w_hbm = refs[:n_mixed], refs[n_mixed : n_mixed + parts], refs[n_mixed + parts]
    outs = refs[n_mixed + parts + 1 + n_earlier :]
    act_outs, mg_outs = outs[:parts], outs[parts : parts + n_mixed]
    mixed_out, grad_out, weight, sems = outs[parts + n_mixed :]
    f_wide, h_wide = weight.shape[0] // parts, weight.shape[1] // parts
    width = f_wide // chunks
    me = meta[0]

    def place(u):
        return lax.rem(me + u, parts)

    @pl.when(pl.program_id(0) == 0)
    def _():
        copies = []
        for i in range(parts):
            for j in range(parts):
                src = w_hbm.at[aligned(place(i) * f_wide, f_wide, f_wide), aligned(place(j) * h_wide, h_wide, h_wide)]
                dst = weight.at[pl.ds(i * f_wide, f_wide), pl.ds(j * h_wide, h_wide)]
                copies.append(pltpu.make_async_copy(src, dst, sems.at[i * parts + j]))
                copies[-1].start()
        for copy in copies:
            copy.wait()

    mixed = jnp.concatenate([ref[...] for ref in mixed_refs], axis=1)
    for u in range(parts):
        at = pl.ds(pl.multiple_of(place(u) * f_wide, f_wide), f_wide)
        mixed_out[:, at] = mixed[:, u * f_wide : (u + 1) * f_wide]
    grads = []
    for u in range(parts):
        preact = jnp.dot(mixed, weight[:, u * h_wide : (u + 1) * h_wide], preferred_element_type=F32)
        sig = jax.nn.sigmoid(preact)
        act_outs[u][...] = (preact * sig).astype(BF16)
        grads.append((cot_refs[u][...].astype(F32) * sig * (1.0 + preact * (1.0 - sig))).astype(BF16))
        at = pl.ds(pl.multiple_of(place(u) * h_wide, h_wide), h_wide)
        grad_out[:, at] = grads[u]
    grad = jnp.concatenate(grads, axis=1)
    back = lax.dot_general(grad, weight[...], (((1,), (1,)), ((), ())), preferred_element_type=F32).astype(BF16)
    for i in range(n_mixed):
        mg_outs[i][...] = back[:, i * width : (i + 1) * width]


def dense(meta, mixed, cot, weight, rows, first, earlier):
    parts, chunks = len(mixed), len(mixed[0])
    width = mixed[0][0][0].shape[1]
    features, hidden = weight.shape
    h_wide = hidden // parts
    all_rows = cot[0].shape[0]
    step = min(rows, 256)
    flat = [m for row in mixed for m in row]
    earlier = list(earlier)

    def spec(w, start=0):
        return pl.BlockSpec((step, w), lambda t, meta: (t + start // step, 0))

    kinds = [(h_wide, True)] * parts + [(width, c > 0) for _ in range(parts) for c in range(chunks)]
    kinds += [(features, True), (hidden, True)]
    whole_at = [i for i, (_, whole) in enumerate(kinds) if whole]
    n_inputs = 1 + len(flat) + parts + 1
    outs = pl.pallas_call(
        functools.partial(dense_kernel, parts, chunks, len(earlier)),
        grid_spec=pltpu.PrefetchScalarGridSpec(
            num_scalar_prefetch=1,
            grid=(rows // step,),
            in_specs=[spec(width, at) for _, at in flat]
            + [spec(h_wide, first)] * parts
            + [any_spec()]
            + [any_spec()] * len(earlier),
            out_specs=[spec(w, first if whole else 0) for w, whole in kinds],
            scratch_shapes=[pltpu.VMEM((features, hidden), BF16), pltpu.SemaphoreType.DMA((parts * parts,))],
        ),
        out_shape=[jax.ShapeDtypeStruct((all_rows if whole else rows, w), BF16) for w, whole in kinds],
        input_output_aliases={n_inputs + i: at for i, at in enumerate(whole_at)} if earlier else {},
        compiler_params=params(),
        cost_estimate=pl.CostEstimate(
            flops=4 * rows * features * hidden,
            bytes_accessed=2 * (features * hidden + 6 * rows * hidden),
            transcendentals=rows * hidden,
        ),
        name="dense",
    )(meta, *[m for m, _ in flat], *cot, weight, *earlier)
    n = parts * chunks
    act, back = outs[:parts], outs[parts : parts + n]
    return (
        act,
        [back[u * chunks : (u + 1) * chunks] for u in range(parts)],
        outs[-2],
        outs[-1],
        [outs[i] for i in whole_at],
    )


def local(features, tiles, columns, counts, weight, cotangent):
    rows, f_wide = features.shape
    h_wide = cotangent.shape[1]
    row_size, parts = lax.axis_size("row"), lax.axis_size("rep")
    ring = Ring(row_size)
    rep = lax.axis_index("rep")
    chunks = f_wide // LANES if f_wide % LANES == 0 else 1
    width = f_wide // chunks
    half = rows // 2
    part_rows = rows // parts
    halves = 2
    half_rows = part_rows // halves
    middle = ring.chips // 2
    near = [o for o in range(ring.chips) if o != middle]
    ends, inner = shift_groups(parts)
    last = chunks - 1
    w = Waves()

    offsets = [(0, 0)] + [(o, 0) for step in range(1, middle) for o in (-step, step)] + [(middle, 0), (middle, half)]
    own_meta = [ring.device_at(o, False) * rows + at for o, at in offsets]
    other_meta = [ring.device_at(o, True) * rows + at for o, at in offsets]
    spmm_meta = jnp.stack([rep] + own_meta + other_meta).astype(jnp.int32)
    held = [1] + [1] * len(near) + [1, len(near)]
    order = [middle] + near
    terms_at = [ring.device_at(o, other) * rows for other in (False, True) for o in order]
    spmm_t_meta = jnp.stack([rep] + terms_at).astype(jnp.int32)
    dense_meta = rep[None].astype(jnp.int32)

    def part_of(x, u):
        return lax.dynamic_slice_in_dim(x, lax.rem(rep + u, parts) * part_rows, part_rows, 0)

    share = weight.shape[0] // row_size
    w_share = lax.dynamic_slice_in_dim(weight, lax.axis_index("row") * share, share, 0)
    w_share = lax.all_gather(w_share, "rep", axis=1, tiled=True)

    cot_blocks = [part_of(cotangent, u) for u in range(parts)]
    xs = [features[:, c * width : (c + 1) * width] for c in range(chunks)]
    up = down = xs[0]
    got_own = {}
    got_other = {}
    mixed = {}

    def run_spmm(c, cut, skip):
        own = [got_own[c, i] for i in range(len(offsets))]
        other = [got_other[c, i] for i in range(len(offsets))]
        return spmm(tiles, columns, counts, spmm_meta, own + other, parts, cut, skip)

    cot_ends = send(cot_blocks, ends)
    own_other = ring.sibling(features)
    for c in range(chunks):
        got_own[c, 0] = xs[c]
        got_other[c, 0] = own_other[:, c * width : (c + 1) * width]
        for step in range(1, middle):
            name = f"{c}_{step}"
            w.go(**{"up" + name: ring.hop(up, 1), "down" + name: ring.hop(down, -1)})
            if c and step == 1:
                for i in range(1, len(offsets)):
                    got_other[c - 1, i] = ring.sibling(got_own[c - 1, i])
                w.go(**{f"mixed{c - 1}": run_spmm(c - 1, 1, 0)})
            w.close()
            up, down = w["up" + name], w["down" + name]
            got_own[c, 2 * step - 1], got_own[c, 2 * step] = up, down
        w.go(**{f"far_up{c}": ring.hop(up[:half], 1), f"far_down{c}": ring.hop(down[half:], -1)})
        if c == 0:
            w.go(cot_ends=cot_ends, own_other=own_other, metas=(spmm_meta, spmm_t_meta, dense_meta))
        seen = []
        if c == last:
            for step in range(1, middle):
                for i in (2 * step - 1, 2 * step):
                    got_other[c, i] = ring.sibling(got_own[c, i])
                    w.go(**{f"other{c}_{i}": got_other[c, i]})
                    seen.append(got_other[c, i])
        if c:
            mixed[c - 1] = w[f"mixed{c - 1}"]
            ready = [lax.optimization_barrier((b, *seen))[0] for b in mixed[c - 1]]
            w.go(**{f"mixed_ends{c - 1}": send(ready, ends)})
        w.close()
        if c == 0:
            spmm_meta, spmm_t_meta, dense_meta = w["metas"]
            w.go(cot_inner=send([w.gate(b) for b in cot_blocks], inner))
        else:
            w.go(**{f"mixed_inner{c - 1}": send([w.gate(b) for b in mixed[c - 1]], inner)})
        got_own[c, len(offsets) - 2], got_own[c, len(offsets) - 1] = w[f"far_up{c}"], w[f"far_down{c}"]
        if c < last:
            up = down = w.gate(xs[c + 1])
    w_full = lax.all_gather(w.gate(w_share), "row", axis=0, tiled=True)
    for i in (-2, -1):
        got_other[last, len(offsets) + i] = ring.sibling(got_own[last, len(offsets) + i])

    for h in range(halves):
        w.go(**{f"half{h}": run_spmm(last, halves, h)})
        w.close()
        w.go(**{f"half_got{h}": send(w[f"half{h}"], ends + inner)})

    cot = ordered(cot_blocks[0], w["cot_ends"], w["cot_inner"])
    whole = [ordered(mixed[c][0], w[f"mixed_ends{c}"], w[f"mixed_inner{c}"]) for c in range(last)]
    earlier = ()
    for h in range(halves):
        part = ordered(w[f"half{h}"][0], w[f"half_got{h}"])
        blocks = [[(whole[c][u], h * half_rows) for c in range(last)] + [(part[u], 0)] for u in range(parts)]
        act, back, mixed_rows, grad_rows, earlier = dense(
            dense_meta, blocks, cot, w_full, half_rows, h * half_rows, earlier
        )
        w.go(**{f"back{h}": [b[0] for b in back]})
        if h == halves - 1:
            w.go(whole=(act, back, mixed_rows, grad_rows))
        w.close()
        w.go(**{f"back_got{h}": send(w[f"back{h}"], ends + inner)})
    act, back, mixed_rows, grad_rows = w["whole"]
    by_row = grad_rows.reshape(part_rows, row_size, -1)
    sums = jnp.einsum("nf,nrh->rfh", mixed_rows, by_row, preferred_element_type=F32).astype(BF16)
    w.go(sums=sums)
    w.close()
    weight_terms = lax.psum_scatter(w["sums"], "row", scatter_dimension=0, tiled=True)[0]

    def run_spmm_t(c, grads):
        return spmm_t(tiles, columns, counts, spmm_t_meta, grads, parts, held, rows, rows * row_size)

    parts_got = [ordered(w[f"back{h}"][0], w[f"back_got{h}"]) for h in range(halves)]
    w.go(terms0=run_spmm_t(0, [parts_got[h][u] for u in range(parts) for h in range(halves)]))
    for c in range(1, chunks):
        w.go(**{f"rest_got{c}": send([w.gate(b[c]) for b in back], ends + inner)})
    w.close()

    near_sums = []
    for c in range(chunks):
        terms = w[f"terms{c}"]
        own_far, own_near, other_far, other_near = terms[0], terms[1:-2], terms[-2], terms[-1]
        got_far = ring.sibling(other_far)
        got_near = ring.sibling(lax.optimization_barrier((other_near, got_far))[0])
        far = [
            (own_far[at : at + half].astype(F32) + got_far[at : at + half].astype(F32)).astype(BF16)
            for at in (0, half)
        ]
        w.go(**{f"got_near{c}": got_near, f"sum{c}_{middle}": (ring.hop(far[0], 1), ring.hop(far[1], -1))})
        if c < last:
            grads = ordered(back[0][c + 1], w[f"rest_got{c + 1}"])
            grads = lax.optimization_barrier((grads, far[0][:8], far[1][:8]))[0]
            w.go(**{f"terms{c + 1}": run_spmm_t(c + 1, grads)})
        if c == 0:
            w.go(weight_terms=weight_terms)
        w.close()
        if c == 0:
            weight_terms = lax.psum_scatter(w["weight_terms"], "rep", scatter_dimension=0, tiled=True)
            w.go(act_ends=send([w.gate(a) for a in act], ends))

        def near_sum(offset, got=w[f"got_near{c}"], own=own_near):
            at = near.index(offset % ring.chips)
            return own[at].astype(F32) + got[at * rows : (at + 1) * rows].astype(F32)

        near_sums.append(near_sum)
        for step in range(middle - 1, 0, -1):
            up, down = w[f"sum{c}_{step + 1}"]
            to_up, to_down = near_sum(step), near_sum(-step)
            if step == middle - 1:
                to_up = jnp.concatenate([to_up[:half] + up.astype(F32), to_up[half:]])
                to_down = jnp.concatenate([to_down[:half], to_down[half:] + down.astype(F32)])
            else:
                to_up, to_down = to_up + up.astype(F32), to_down + down.astype(F32)
            to_up, to_down = to_up.astype(BF16), to_down.astype(BF16)
            w.go(**{f"sum{c}_{step}": (ring.hop(to_up, 1), ring.hop(to_down, -1))})
            if step > 1:
                w.close()
            else:
                w.token = to_up[:8]
    got = {**w.done, **w.pending, "act_inner": send([w.gate(a) for a in act], inner)}
    feature_grad = []
    for c, near_sum in enumerate(near_sums):
        up, down = got[f"sum{c}_1"]
        if middle == 1:
            feature_grad.append((near_sum(0) + jnp.concatenate([up, down]).astype(F32)).astype(BF16))
        else:
            feature_grad.append((near_sum(0) + up.astype(F32) + down.astype(F32)).astype(BF16))
    weight_grad = w.gate(weight_terms).astype(F32)
    act = ordered(act[0], got["act_ends"], got["act_inner"])
    feature_grad = jnp.concatenate(feature_grad, axis=1)
    activations = jnp.zeros((rows, h_wide), BF16)
    for u in range(parts):
        activations = lax.dynamic_update_slice_in_dim(activations, act[u], lax.rem(rep + u, parts) * part_rows, 0)
    return (activations, feature_grad, weight_grad)


def solution(mesh):
    in_specs = (
        P("row", "rep"),
        P("row", None, None, None),
        P("row", None),
        P("row"),
        P(None, "rep"),
        P("row", "rep"),
    )
    out_specs = (P("row", "rep"), P("row", "rep"), P("rep", "row"))
    return jax.shard_map(local, mesh=mesh, in_specs=in_specs, out_specs=out_specs, check_vma=False)
```

```python
import functools
import jax
import jax.numpy as jnp
from jax import lax
from jax.experimental import pallas as pl
from jax.experimental.pallas import tpu as pltpu
from jax.sharding import PartitionSpec as P

BF16, F32 = jnp.bfloat16, jnp.float32
VMEM_LIMIT = 56 * 1024 * 1024
LANES = 128
CORES = 2


def params():
    return pltpu.CompilerParams(vmem_limit_bytes=VMEM_LIMIT)


def any_spec():
    return pl.BlockSpec(memory_space=pl.ANY)


class Ring:
    def __init__(self, devices):
        self.chips = devices // CORES
        half = self.chips // 2
        self.order = list(range(half)) + list(range(self.chips - 1, half - 1, -1))
        self.devices = devices

    def perm(self, step):
        pairs = []
        for place, chip in enumerate(self.order):
            to = self.order[(place + step) % self.chips]
            pairs += [(chip * CORES + core, to * CORES + core) for core in range(CORES)]
        return pairs

    def hop(self, value, step):
        return lax.ppermute(value, "row", self.perm(step))

    def sibling(self, value):
        return lax.ppermute(value, "row", [(d, d ^ 1) for d in range(self.devices)])

    def device_at(self, offset, other_core):
        me = lax.axis_index("row")
        order = jnp.array(self.order, jnp.int32)
        place_of = jnp.array([self.order.index(c) for c in range(self.chips)], jnp.int32)
        chip = order[(place_of[me // CORES] + offset) % self.chips]
        core = me % CORES
        return chip * CORES + (1 - core if other_core else core)


class Waves:
    def __init__(self):
        self.pending = {}
        self.done = {}
        self.token = None

    def go(self, **values):
        assert not set(values) & (set(self.pending) | set(self.done))
        self.pending.update(values)

    def close(self):
        names, values = list(self.pending), list(self.pending.values())
        flat, tree = jax.tree.flatten(values)
        flat = lax.optimization_barrier(flat)
        self.token = flat[0]
        self.done.update(zip(names, jax.tree.unflatten(tree, flat)))
        self.pending = {}

    def gate(self, value):
        if self.token is None:
            return value
        return lax.optimization_barrier((value, self.token))[0]

    def __getitem__(self, name):
        return self.done[name]


def shift_groups(size):
    ends = sorted({1, size - 1})
    return ends, [s for s in range(2, size - 1)]


def send(blocks, shifts):
    size = len(blocks)
    return {
        (size - s) % size: lax.ppermute(blocks[s], "rep", [(i, (i + s) % size) for i in range(size)]) for s in shifts
    }


def ordered(own, *groups):
    got = {0: own}
    for group in groups:
        got.update(group)
    return [got[u] for u in range(len(got))]


def masked_tiles(tiles, i, count):
    found = []
    for k in range(tiles.shape[1]):
        tile = tiles[i, k]
        found.append(jnp.where(k < count, tile, jnp.zeros_like(tile)))
    return jnp.concatenate(found, axis=1)


def step_spec(blocks, slots, tile_size, parts, per_step, skip):
    def index(t, cols, cnt, meta):
        return (lax.rem(meta[0] + t, parts) * (blocks // parts // per_step) + skip, 0, 0, 0)

    return pl.BlockSpec((per_step, slots, tile_size, tile_size), index)


def aligned(start, size, unit):
    return pl.ds(pl.multiple_of(start, unit), size)


def spmm_kernel(n_pieces, per_part, skip, cols, counts, meta, tiles, *refs):
    parts = pl.num_programs(0)
    n_outs = len(refs) - n_pieces - 3
    pieces, outs = refs[:n_pieces], refs[n_pieces : n_pieces + n_outs]
    source, result, sems = refs[n_pieces + n_outs :]
    t = pl.program_id(0)
    per_step, slots, tile_size, _ = tiles.shape

    @pl.when(t == 0)
    def _():
        copies = []
        for p, piece in enumerate(pieces):
            copies.append(
                pltpu.make_async_copy(piece, source.at[aligned(meta[1 + p], piece.shape[0], tile_size)], sems.at[p])
            )
            copies[-1].start()
        for copy in copies:
            copy.wait()

    for i in range(per_step):
        b = lax.rem(meta[0] + t, parts) * per_part + skip * per_step + i
        right = [source[aligned(cols[b, k] * tile_size, tile_size, tile_size), :] for k in range(slots)]
        product = jnp.dot(
            masked_tiles(tiles, i, counts[b]), jnp.concatenate(right, axis=0), preferred_element_type=F32
        )
        result[i * tile_size : (i + 1) * tile_size, :] = product.astype(BF16)

    for u in range(n_outs):

        @pl.when(t == u)
        def _():
            outs[u][...] = result[...]


def spmm(tiles, columns, counts, meta, pieces, parts, cut, skip):
    blocks, slots, tile_size, _ = tiles.shape
    width = pieces[0].shape[1]
    total_rows = sum(v.shape[0] for v in pieces)
    per_part = blocks // parts
    per_step = per_part // cut
    rows = per_step * tile_size
    return pl.pallas_call(
        functools.partial(spmm_kernel, len(pieces), per_part, skip),
        grid_spec=pltpu.PrefetchScalarGridSpec(
            num_scalar_prefetch=3,
            grid=(parts,),
            in_specs=[step_spec(blocks, slots, tile_size, parts, per_step, skip)] + [any_spec()] * len(pieces),
            out_specs=[pl.BlockSpec((rows, width), lambda t, cols, cnt, meta: (0, 0))] * parts,
            scratch_shapes=[
                pltpu.VMEM((total_rows, width), BF16),
                pltpu.VMEM((rows, width), BF16),
                pltpu.SemaphoreType.DMA((len(pieces),)),
            ],
        ),
        out_shape=[jax.ShapeDtypeStruct((rows, width), BF16)] * parts,
        compiler_params=params(),
        cost_estimate=pl.CostEstimate(
            flops=2 * parts * rows * slots * tile_size * width,
            bytes_accessed=2 * (tiles.size // cut + total_rows * width),
            transcendentals=0,
        ),
        name="spmm",
    )(columns, counts, meta, tiles, *pieces)


def spmm_t_kernel(n_grads, per_part, n_outs, terms, cols, counts, meta, tiles, *refs):
    parts = pl.num_programs(0)
    grads, outs = refs[:n_grads], refs[n_grads : n_grads + n_outs]
    total, grad, stage, in_sems, out_sems = refs[n_grads + n_outs :]
    t = pl.program_id(0)
    per_step, slots, tile_size, _ = tiles.shape
    width = grad.shape[1]
    rows = stage.shape[1]

    @pl.when(t == 0)
    def _():
        copies, start = [], 0
        for g, ref in enumerate(grads):
            copies.append(pltpu.make_async_copy(ref, grad.at[pl.ds(start, ref.shape[0])], in_sems.at[g]))
            copies[-1].start()
            start += ref.shape[0]

        @pl.loop(0, total.shape[0] // tile_size, unroll=8)
        def _(i):
            total[aligned(i * tile_size, tile_size, tile_size), :] = jnp.zeros((tile_size, width), F32)

        for copy in copies:
            copy.wait()

    for i in range(per_step):
        b = lax.rem(meta[0] + t, parts) * per_part + i
        block = grad[aligned((t * per_step + i) * tile_size, tile_size, tile_size), :]
        part = lax.dot_general(
            masked_tiles(tiles, i, counts[b]), block, (((0,), (0,)), ((), ())), preferred_element_type=F32
        )
        for k in range(slots):
            total[aligned(cols[b, k] * tile_size, tile_size, tile_size), :] += part[k * tile_size : (k + 1) * tile_size]

    @pl.when(t == parts - 1)
    def _():
        copies = []
        for o, (out, at) in enumerate(terms):
            slot = o % 2
            if o >= 2:
                copies[o - 2].wait()

            @pl.loop(0, rows // tile_size, unroll=4)
            def _(i):
                start = aligned(meta[1 + o] + i * tile_size, tile_size, tile_size)
                stage[slot, aligned(i * tile_size, tile_size, tile_size), :] = total[start, :].astype(BF16)

            copies.append(
                pltpu.make_async_copy(stage.at[slot], outs[out].at[pl.ds(at * rows, rows)], out_sems.at[o])
            )
            copies[o].start()
        for copy in copies[-2:]:
            copy.wait()


def spmm_t(tiles, columns, counts, meta, grads, parts, held, rows, total_rows):
    blocks, slots, tile_size, _ = tiles.shape
    width = grads[0].shape[1]
    per_part = blocks // parts
    flat = [(out, at) for out, many in enumerate(held) for at in range(many)]
    return pl.pallas_call(
        functools.partial(spmm_t_kernel, len(grads), per_part, len(held), flat),
        grid_spec=pltpu.PrefetchScalarGridSpec(
            num_scalar_prefetch=3,
            grid=(parts,),
            in_specs=[step_spec(blocks, slots, tile_size, parts, per_part, 0)] + [any_spec()] * len(grads),
            out_specs=[any_spec()] * len(held),
            scratch_shapes=[
                pltpu.VMEM((total_rows, width), F32),
                pltpu.VMEM((rows, width), BF16),
                pltpu.VMEM((2, rows, width), BF16),
                pltpu.SemaphoreType.DMA((len(grads),)),
                pltpu.SemaphoreType.DMA((len(flat),)),
            ],
        ),
        out_shape=[jax.ShapeDtypeStruct((many * rows, width), BF16) for many in held],
        compiler_params=params(),
        cost_estimate=pl.CostEstimate(
            flops=2 * blocks * slots * tile_size * tile_size * width,
            bytes_accessed=2 * (tiles.size + total_rows * width),
            transcendentals=0,
        ),
        name="spmm_t",
    )(columns, counts, meta, tiles, *grads)


def dense_kernel(parts, chunks, n_earlier, meta, *refs):
    n_mixed = parts * chunks
    mixed_refs, cot_refs, w_hbm = refs[:n_mixed], refs[n_mixed : n_mixed + parts], refs[n_mixed + parts]
    outs = refs[n_mixed + parts + 1 + n_earlier :]
    act_outs, mg_outs = outs[:parts], outs[parts : parts + n_mixed]
    mixed_out, grad_out, weight, sems = outs[parts + n_mixed :]
    f_wide, h_wide = weight.shape[0] // parts, weight.shape[1] // parts
    width = f_wide // chunks
    me = meta[0]

    def place(u):
        return lax.rem(me + u, parts)

    @pl.when(pl.program_id(0) == 0)
    def _():
        copies = []
        for i in range(parts):
            src = w_hbm.at[aligned(place(i) * f_wide, f_wide, f_wide)]
            copies.append(pltpu.make_async_copy(src, weight.at[pl.ds(i * f_wide, f_wide)], sems.at[i]))
            copies[-1].start()
        for copy in copies:
            copy.wait()

    mixed = jnp.concatenate([ref[...] for ref in mixed_refs], axis=1)
    for u in range(parts):
        at = pl.ds(pl.multiple_of(place(u) * f_wide, f_wide), f_wide)
        mixed_out[:, at] = mixed[:, u * f_wide : (u + 1) * f_wide]
    grads = []
    for u in range(parts):
        preact = jnp.dot(mixed, weight[:, u * h_wide : (u + 1) * h_wide], preferred_element_type=F32)
        sig = jax.nn.sigmoid(preact)
        act_outs[u][...] = (preact * sig).astype(BF16)
        grads.append((cot_refs[u][...].astype(F32) * sig * (1.0 + preact * (1.0 - sig))).astype(BF16))
        at = pl.ds(pl.multiple_of(place(u) * h_wide, h_wide), h_wide)
        grad_out[:, at] = grads[u]
    grad = jnp.concatenate(grads, axis=1)
    back = lax.dot_general(grad, weight[...], (((1,), (1,)), ((), ())), preferred_element_type=F32).astype(BF16)
    for i in range(n_mixed):
        mg_outs[i][...] = back[:, i * width : (i + 1) * width]


def dense(meta, mixed, cot, weight, rows, first, earlier):
    parts, chunks = len(mixed), len(mixed[0])
    width = mixed[0][0][0].shape[1]
    features, hidden = weight.shape
    h_wide = hidden // parts
    all_rows = cot[0].shape[0]
    step = min(rows, 256)
    flat = [m for row in mixed for m in row]
    earlier = list(earlier)

    def spec(w, start=0):
        return pl.BlockSpec((step, w), lambda t, meta: (t + start // step, 0))

    kinds = [(h_wide, True)] * parts + [(width, c > 0) for _ in range(parts) for c in range(chunks)]
    kinds += [(features, True), (hidden, True)]
    whole_at = [i for i, (_, whole) in enumerate(kinds) if whole]
    n_inputs = 1 + len(flat) + parts + 1
    outs = pl.pallas_call(
        functools.partial(dense_kernel, parts, chunks, len(earlier)),
        grid_spec=pltpu.PrefetchScalarGridSpec(
            num_scalar_prefetch=1,
            grid=(rows // step,),
            in_specs=[spec(width, at) for _, at in flat]
            + [spec(h_wide, first)] * parts
            + [any_spec()]
            + [any_spec()] * len(earlier),
            out_specs=[spec(w, first if whole else 0) for w, whole in kinds],
            scratch_shapes=[pltpu.VMEM((features, hidden), BF16), pltpu.SemaphoreType.DMA((parts,))],
        ),
        out_shape=[jax.ShapeDtypeStruct((all_rows if whole else rows, w), BF16) for w, whole in kinds],
        input_output_aliases={n_inputs + i: at for i, at in enumerate(whole_at)} if earlier else {},
        compiler_params=params(),
        cost_estimate=pl.CostEstimate(
            flops=4 * rows * features * hidden,
            bytes_accessed=2 * (features * hidden + 6 * rows * hidden),
            transcendentals=rows * hidden,
        ),
        name="dense",
    )(meta, *[m for m, _ in flat], *cot, weight, *earlier)
    n = parts * chunks
    act, back = outs[:parts], outs[parts : parts + n]
    return (
        act,
        [back[u * chunks : (u + 1) * chunks] for u in range(parts)],
        outs[-2],
        outs[-1],
        [outs[i] for i in whole_at],
    )


def total_of(*values):
    return functools.reduce(lambda a, b: a + b, [v.astype(F32) for v in values]).astype(BF16)


def step_kernel(low_blocks, own_up, got_up, up, own_down, got_down, down, to_up, to_down):
    low = pl.program_id(0) < low_blocks

    def put(out, own, got, more, with_more):
        both = own[...].astype(F32) + got[...].astype(F32)

        @pl.when(with_more)
        def _():
            out[...] = (both + more[...].astype(F32)).astype(BF16)

        @pl.when(jnp.logical_not(with_more))
        def _():
            out[...] = both.astype(BF16)

    put(to_up, own_up, got_up, up, low)
    put(to_down, own_down, got_down, down, jnp.logical_not(low))


def step_sums(own_up, at_up, up, own_down, at_down, down, got):
    rows, width = own_up.shape
    step = min(rows // 2, 512)
    blocks = rows // step
    low = blocks // 2

    def spec(index):
        return pl.BlockSpec((step, width), lambda t: (index(t), 0))

    here = spec(lambda t: t)
    return pl.pallas_call(
        functools.partial(step_kernel, low),
        grid=(blocks,),
        in_specs=[
            here,
            spec(lambda t: t + at_up * blocks),
            spec(lambda t: jnp.minimum(t, low - 1)),
            here,
            spec(lambda t: t + at_down * blocks),
            spec(lambda t: jnp.maximum(t - low, 0)),
        ],
        out_specs=[here, here],
        out_shape=[jax.ShapeDtypeStruct((rows, width), BF16)] * 2,
        compiler_params=params(),
        cost_estimate=pl.CostEstimate(flops=4 * rows * width, bytes_accessed=14 * rows * width, transcendentals=0),
        name="step_sums",
    )(own_up, got, up, own_down, got, down)


def result_kernel(n_ready, *refs):
    ready, (own, got, up, down, out) = refs[:n_ready], refs[n_ready:]
    width = own.shape[1]
    for c, ref in enumerate(ready):
        out[:, c * width : (c + 1) * width] = ref[...]
    out[:, n_ready * width :] = (
        own[...].astype(F32) + got[...].astype(F32) + up[...].astype(F32) + down[...].astype(F32)
    ).astype(BF16)


def result_of(ready, own, got, at, up, down):
    rows, width = own.shape
    step = min(rows, 512)
    blocks = rows // step
    here = pl.BlockSpec((step, width), lambda t: (t, 0))
    there = pl.BlockSpec((step, width), lambda t: (t + at * blocks, 0))
    wide = width * (len(ready) + 1)
    return pl.pallas_call(
        functools.partial(result_kernel, len(ready)),
        grid=(blocks,),
        in_specs=[here] * (len(ready) + 1) + [there, here, here],
        out_specs=pl.BlockSpec((step, wide), lambda t: (t, 0)),
        out_shape=jax.ShapeDtypeStruct((rows, wide), BF16),
        compiler_params=params(),
        cost_estimate=pl.CostEstimate(flops=4 * rows * width, bytes_accessed=14 * rows * width, transcendentals=0),
        name="feature_grad",
    )(*ready, own, got, up, down)


class Reduction:
    def __init__(self, ring, own_far, own_near, other_far, other_near):
        self.ring, self.middle = ring, ring.chips // 2
        self.near = [o for o in range(ring.chips) if o != self.middle]
        self.own_far, self.own_near, self.other_far, self.other_near = own_far, own_near, other_far, other_near
        self.rows = own_far.shape[0]

    def far_swap(self):
        return self.ring.sibling(self.other_far)

    def near_swap(self, after):
        return self.ring.sibling(lax.optimization_barrier((self.other_near, after))[0])

    def far_sums(self, got):
        half = self.rows // 2
        return [total_of(self.own_far[at : at + half], got[at : at + half]) for at in (0, half)]

    def hops(self, up, down):
        return self.ring.hop(up, 1), self.ring.hop(down, -1)

    def place(self, offset):
        return self.near.index(offset % self.ring.chips)

    def near_terms(self, offset, got):
        at = self.place(offset)
        return self.own_near[at], got[at * self.rows : (at + 1) * self.rows]

    def sums(self, step, got, up, down, kernel):
        if step < self.middle - 1:
            return total_of(*self.near_terms(step, got), up), total_of(*self.near_terms(-step, got), down)
        at_up, at_down = self.place(step), self.place(-step)
        if kernel:
            return step_sums(self.own_near[at_up], at_up, up, self.own_near[at_down], at_down, down, got)
        zeros = jnp.zeros_like(up)
        return (
            total_of(*self.near_terms(step, got), jnp.concatenate([up, zeros])),
            total_of(*self.near_terms(-step, got), jnp.concatenate([zeros, down])),
        )

    def last(self, up, down):
        if self.middle > 1:
            return up, down
        return jnp.concatenate([up, jnp.zeros_like(up)]), jnp.concatenate([jnp.zeros_like(down), down])


def local(features, tiles, columns, counts, weight, cotangent):
    rows, f_wide = features.shape
    h_wide = cotangent.shape[1]
    row_size, parts = lax.axis_size("row"), lax.axis_size("rep")
    ring = Ring(row_size)
    rep = lax.axis_index("rep")
    chunks = f_wide // LANES if f_wide % LANES == 0 else 1
    width = f_wide // chunks
    half = rows // 2
    part_rows = rows // parts
    halves = 2
    half_rows = part_rows // halves
    middle = ring.chips // 2
    near = [o for o in range(ring.chips) if o != middle]
    ends, inner = shift_groups(parts)
    last = chunks - 1
    w = Waves()

    offsets = [(0, 0)] + [(o, 0) for step in range(1, middle) for o in (-step, step)] + [(middle, 0), (middle, half)]
    own_meta = [ring.device_at(o, False) * rows + at for o, at in offsets]
    other_meta = [ring.device_at(o, True) * rows + at for o, at in offsets]
    spmm_meta = jnp.stack([rep] + own_meta + other_meta).astype(jnp.int32)
    held = [1] + [1] * len(near) + [1, len(near)]
    order = [middle] + near
    terms_at = [ring.device_at(o, other) * rows for other in (False, True) for o in order]
    spmm_t_meta = jnp.stack([rep] + terms_at).astype(jnp.int32)
    dense_meta = rep[None].astype(jnp.int32)

    def part_of(x, u):
        return lax.dynamic_slice_in_dim(x, lax.rem(rep + u, parts) * part_rows, part_rows, 0)

    share = weight.shape[0] // row_size
    w_share = lax.dynamic_slice_in_dim(weight, lax.axis_index("row") * share, share, 0)

    cot_blocks = [part_of(cotangent, u) for u in range(parts)]
    xs = [features[:, c * width : (c + 1) * width] for c in range(chunks)]
    up = down = xs[0]
    got_own = {}
    got_other = {}
    mixed = {}

    def run_spmm(c, cut, skip):
        own = [got_own[c, i] for i in range(len(offsets))]
        other = [got_other[c, i] for i in range(len(offsets))]
        return spmm(tiles, columns, counts, spmm_meta, own + other, parts, cut, skip)

    cot_ends = send(cot_blocks, ends)
    own_other = ring.sibling(features)
    for c in range(chunks):
        got_own[c, 0] = xs[c]
        got_other[c, 0] = own_other[:, c * width : (c + 1) * width]
        for step in range(1, middle):
            name = f"{c}_{step}"
            w.go(**{"up" + name: ring.hop(up, 1), "down" + name: ring.hop(down, -1)})
            if c and step == 1:
                for i in range(1, len(offsets)):
                    got_other[c - 1, i] = ring.sibling(got_own[c - 1, i])
                w.go(**{f"mixed{c - 1}": run_spmm(c - 1, 1, 0)})
            w.close()
            up, down = w["up" + name], w["down" + name]
            got_own[c, 2 * step - 1], got_own[c, 2 * step] = up, down
        w.go(**{f"far_up{c}": ring.hop(up[:half], 1), f"far_down{c}": ring.hop(down[half:], -1)})
        if c == 0:
            w.go(cot_ends=cot_ends, own_other=own_other, metas=(spmm_meta, spmm_t_meta, dense_meta))
            w.go(shares=send([w.gate(w_share)] * parts, ends + inner))
        seen = []
        if c == last:
            for step in range(1, middle):
                for i in (2 * step - 1, 2 * step):
                    got_other[c, i] = ring.sibling(got_own[c, i])
                    w.go(**{f"other{c}_{i}": got_other[c, i]})
                    seen.append(got_other[c, i])
        if c:
            mixed[c - 1] = w[f"mixed{c - 1}"]
            ready = [lax.optimization_barrier((b, *seen))[0] for b in mixed[c - 1]]
            w.go(**{f"mixed_ends{c - 1}": send(ready, ends)})
        w.close()
        if c == 0:
            spmm_meta, spmm_t_meta, dense_meta = w["metas"]
            w.go(cot_inner=send([w.gate(b) for b in cot_blocks], inner))
        else:
            w.go(**{f"mixed_inner{c - 1}": send([w.gate(b) for b in mixed[c - 1]], inner)})
        got_own[c, len(offsets) - 2], got_own[c, len(offsets) - 1] = w[f"far_up{c}"], w[f"far_down{c}"]
        if c < last:
            up = down = w.gate(xs[c + 1])
    w_rows = jnp.concatenate(ordered(w_share, w["shares"]), axis=1)
    w_full = lax.all_gather(w.gate(w_rows), "row", axis=0, tiled=True)
    for i in (-2, -1):
        got_other[last, len(offsets) + i] = ring.sibling(got_own[last, len(offsets) + i])

    for h in range(halves):
        w.go(**{f"half{h}": run_spmm(last, halves, h)})
        w.close()
        w.go(**{f"half_got{h}": send(w[f"half{h}"], ends + inner)})

    cot = ordered(cot_blocks[0], w["cot_ends"], w["cot_inner"])
    whole = [ordered(mixed[c][0], w[f"mixed_ends{c}"], w[f"mixed_inner{c}"]) for c in range(last)]
    earlier = ()
    for h in range(halves):
        part = ordered(w[f"half{h}"][0], w[f"half_got{h}"])
        blocks = [[(whole[c][u], h * half_rows) for c in range(last)] + [(part[u], 0)] for u in range(parts)]
        act, back, mixed_rows, grad_rows, earlier = dense(
            dense_meta, blocks, cot, w_full, half_rows, h * half_rows, earlier
        )
        w.go(**{f"back{h}": [b[0] for b in back]})
        if h == halves - 1:
            w.go(whole=(act, back, mixed_rows, grad_rows))
        w.close()
        w.go(**{f"back_got{h}": send(w[f"back{h}"], ends + inner)})
    act, back, mixed_rows, grad_rows = w["whole"]
    sums = lax.dot_general(grad_rows, mixed_rows, (((0,), (0,)), ((), ())), preferred_element_type=F32).astype(BF16)
    share = sums.shape[0] // row_size

    def sums_for(offset, other):
        return lax.dynamic_slice_in_dim(sums, ring.device_at(offset, other) * share, share, 0)

    wg = Reduction(
        ring,
        sums_for(middle, False),
        [sums_for(o, False) for o in near],
        sums_for(middle, True),
        jnp.concatenate([sums_for(o, True) for o in near]),
    )
    wg_far = wg.far_swap()
    w.go(wg_own=(wg.own_far, wg.own_near), wg_far=wg_far, wg_near=wg.near_swap(wg_far))
    w.close()
    wg.own_far, wg.own_near = w["wg_own"]
    w.go(wg_up_down=wg.hops(*wg.far_sums(w["wg_far"])))

    def run_spmm_t(c, grads):
        return spmm_t(tiles, columns, counts, spmm_t_meta, grads, parts, held, rows, rows * row_size)

    parts_got = [ordered(w[f"back{h}"][0], w[f"back_got{h}"]) for h in range(halves)]
    w.go(terms0=run_spmm_t(0, [parts_got[h][u] for u in range(parts) for h in range(halves)]))
    for c in range(1, chunks):
        w.go(**{f"rest_got{c}": send([w.gate(b[c]) for b in back], ends + inner)})
    w.close()

    def wg_steps(first, until):
        up, down = w["wg_up_down"]
        for step in range(first, until, -1):
            up, down = wg.hops(*wg.sums(step, w["wg_near"], up, down, False))
        return up, down

    reductions = []
    for c in range(chunks):
        terms = w[f"terms{c}"]
        red = Reduction(ring, terms[0], terms[1:-2], terms[-2], terms[-1])
        reductions.append(red)
        got_far = red.far_swap()
        got_near = red.near_swap(got_far)
        far = red.far_sums(got_far)
        w.go(**{f"got_near{c}": got_near, f"sum{c}_{middle}": red.hops(*far)})
        if c < last:
            grads = ordered(back[0][c + 1], w[f"rest_got{c + 1}"])
            grads = lax.optimization_barrier((grads, far[0][:8], far[1][:8]))[0]
            w.go(**{f"terms{c + 1}": run_spmm_t(c + 1, grads)})
        if c == 0:
            w.go(wg_last=wg_steps(middle - 1, 0))
        if c == last:
            w.go(act_inner=send([lax.optimization_barrier((a, got_near))[0] for a in act], inner))
        w.close()
        if c == 0:
            block = total_of(*wg.near_terms(0, w["wg_near"]), *wg.last(*w["wg_last"]))
            cuts = [
                lax.dynamic_slice_in_dim(block, lax.rem(rep + u, parts) * f_wide, f_wide, 1) for u in range(parts)
            ]
            wg_got = send(cuts, ends + inner)
            w.go(weight_grad=functools.reduce(lambda a, b: a + b, [v.astype(F32) for v in [cuts[0], *wg_got.values()]]))
        for step in range(middle - 1, 0, -1):
            to_up, to_down = red.sums(step, w[f"got_near{c}"], *w[f"sum{c}_{step + 1}"], True)
            w.go(**{f"sum{c}_{step}": red.hops(to_up, to_down)})
            if step > 1:
                w.close()
            else:
                w.token = to_up[:8]
    got = {**w.done, **w.pending, "act_ends": send([w.gate(a) for a in act], ends)}
    ready = [
        total_of(*red.near_terms(0, got[f"got_near{c}"]), *red.last(*got[f"sum{c}_1"]))
        for c, red in enumerate(reductions[:-1])
    ]
    red = reductions[-1]
    at = red.place(0)
    feature_grad = result_of(ready, red.own_near[at], got[f"got_near{last}"], at, *red.last(*got[f"sum{last}_1"]))
    weight_grad = got["weight_grad"].T
    act = ordered(act[0], got["act_ends"], got["act_inner"])
    activations = jnp.zeros((rows, h_wide), BF16)
    for u in range(parts):
        activations = lax.dynamic_update_slice_in_dim(activations, act[u], lax.rem(rep + u, parts) * part_rows, 0)
    return (activations, feature_grad, weight_grad)


def solution(mesh):
    in_specs = (
        P("row", "rep"),
        P("row", None, None, None),
        P("row", None),
        P("row"),
        P(None, "rep"),
        P("row", "rep"),
    )
    out_specs = (P("row", "rep"), P("row", "rep"), P("rep", "row"))
    return jax.shard_map(local, mesh=mesh, in_specs=in_specs, out_specs=out_specs, check_vma=False)
```

```python
import functools
import jax
import jax.numpy as jnp
from jax import lax
from jax.experimental import pallas as pl
from jax.experimental.pallas import tpu as pltpu
from jax.sharding import PartitionSpec as P

BF16, F32 = jnp.bfloat16, jnp.float32
VMEM_LIMIT = 56 * 1024 * 1024
LANES = 128
CORES = 2


def params():
    return pltpu.CompilerParams(vmem_limit_bytes=VMEM_LIMIT)


def any_spec():
    return pl.BlockSpec(memory_space=pl.ANY)


class Ring:
    def __init__(self, devices):
        self.chips = devices // CORES
        half = self.chips // 2
        self.order = list(range(half)) + list(range(self.chips - 1, half - 1, -1))
        self.devices = devices

    def perm(self, step):
        pairs = []
        for place, chip in enumerate(self.order):
            to = self.order[(place + step) % self.chips]
            pairs += [(chip * CORES + core, to * CORES + core) for core in range(CORES)]
        return pairs

    def hop(self, value, step):
        return lax.ppermute(value, "row", self.perm(step))

    def sibling(self, value):
        return lax.ppermute(value, "row", [(d, d ^ 1) for d in range(self.devices)])

    def device_at(self, offset, other_core):
        me = lax.axis_index("row")
        order = jnp.array(self.order, jnp.int32)
        place_of = jnp.array([self.order.index(c) for c in range(self.chips)], jnp.int32)
        chip = order[(place_of[me // CORES] + offset) % self.chips]
        core = me % CORES
        return chip * CORES + (1 - core if other_core else core)


class Waves:
    def __init__(self):
        self.pending = {}
        self.done = {}
        self.token = None

    def go(self, **values):
        assert not set(values) & (set(self.pending) | set(self.done))
        self.pending.update(values)

    def close(self):
        names, values = list(self.pending), list(self.pending.values())
        flat, tree = jax.tree.flatten(values)
        flat = lax.optimization_barrier(flat)
        self.token = flat[0]
        self.done.update(zip(names, jax.tree.unflatten(tree, flat)))
        self.pending = {}

    def gate(self, value):
        if self.token is None:
            return value
        return lax.optimization_barrier((value, self.token))[0]

    def __getitem__(self, name):
        return self.done[name]


def shift_groups(size):
    ends = sorted({1, size - 1})
    return ends, [s for s in range(2, size - 1)]


def send(blocks, shifts):
    size = len(blocks)
    return {
        (size - s) % size: lax.ppermute(blocks[s], "rep", [(i, (i + s) % size) for i in range(size)]) for s in shifts
    }


def ordered(own, *groups):
    got = {0: own}
    for group in groups:
        got.update(group)
    return [got[u] for u in range(len(got))]


def masked_tiles(tiles, i, count):
    found = []
    for k in range(tiles.shape[1]):
        tile = tiles[i, k]
        found.append(jnp.where(k < count, tile, jnp.zeros_like(tile)))
    return jnp.concatenate(found, axis=1)


def step_spec(blocks, slots, tile_size, parts, per_step, skip):
    def index(t, cols, cnt, meta):
        return (lax.rem(meta[0] + t, parts) * (blocks // parts // per_step) + skip, 0, 0, 0)

    return pl.BlockSpec((per_step, slots, tile_size, tile_size), index)


def aligned(start, size, unit):
    return pl.ds(pl.multiple_of(start, unit), size)


def spmm_kernel(n_pieces, per_part, skip, cols, counts, meta, tiles, *refs):
    parts = pl.num_programs(0)
    n_outs = len(refs) - n_pieces - 3
    pieces, outs = refs[:n_pieces], refs[n_pieces : n_pieces + n_outs]
    source, result, sems = refs[n_pieces + n_outs :]
    t = pl.program_id(0)
    per_step, slots, tile_size, _ = tiles.shape

    @pl.when(t == 0)
    def _():
        copies = []
        for p, piece in enumerate(pieces):
            copies.append(
                pltpu.make_async_copy(piece, source.at[aligned(meta[1 + p], piece.shape[0], tile_size)], sems.at[p])
            )
            copies[-1].start()
        for copy in copies:
            copy.wait()

    for i in range(per_step):
        b = lax.rem(meta[0] + t, parts) * per_part + skip * per_step + i
        right = [source[aligned(cols[b, k] * tile_size, tile_size, tile_size), :] for k in range(slots)]
        product = jnp.dot(
            masked_tiles(tiles, i, counts[b]), jnp.concatenate(right, axis=0), preferred_element_type=F32
        )
        result[i * tile_size : (i + 1) * tile_size, :] = product.astype(BF16)

    for u in range(n_outs):

        @pl.when(t == u)
        def _():
            outs[u][...] = result[...]


def spmm(tiles, columns, counts, meta, pieces, parts, cut, skip):
    blocks, slots, tile_size, _ = tiles.shape
    width = pieces[0].shape[1]
    total_rows = sum(v.shape[0] for v in pieces)
    per_part = blocks // parts
    per_step = per_part // cut
    rows = per_step * tile_size
    return pl.pallas_call(
        functools.partial(spmm_kernel, len(pieces), per_part, skip),
        grid_spec=pltpu.PrefetchScalarGridSpec(
            num_scalar_prefetch=3,
            grid=(parts,),
            in_specs=[step_spec(blocks, slots, tile_size, parts, per_step, skip)] + [any_spec()] * len(pieces),
            out_specs=[pl.BlockSpec((rows, width), lambda t, cols, cnt, meta: (0, 0))] * parts,
            scratch_shapes=[
                pltpu.VMEM((total_rows, width), BF16),
                pltpu.VMEM((rows, width), BF16),
                pltpu.SemaphoreType.DMA((len(pieces),)),
            ],
        ),
        out_shape=[jax.ShapeDtypeStruct((rows, width), BF16)] * parts,
        compiler_params=params(),
        cost_estimate=pl.CostEstimate(
            flops=2 * parts * rows * slots * tile_size * width,
            bytes_accessed=2 * (tiles.size // cut + total_rows * width),
            transcendentals=0,
        ),
        name="spmm",
    )(columns, counts, meta, tiles, *pieces)


def spmm_t_kernel(n_grads, per_part, n_outs, terms, cols, counts, meta, tiles, *refs):
    parts = pl.num_programs(0)
    grads, outs = refs[:n_grads], refs[n_grads : n_grads + n_outs]
    total, grad, stage, in_sems, out_sems = refs[n_grads + n_outs :]
    t = pl.program_id(0)
    per_step, slots, tile_size, _ = tiles.shape
    width = grad.shape[1]
    rows = stage.shape[1]

    @pl.when(t == 0)
    def _():
        copies, start = [], 0
        for g, ref in enumerate(grads):
            copies.append(pltpu.make_async_copy(ref, grad.at[pl.ds(start, ref.shape[0])], in_sems.at[g]))
            copies[-1].start()
            start += ref.shape[0]

        @pl.loop(0, total.shape[0] // tile_size, unroll=8)
        def _(i):
            total[aligned(i * tile_size, tile_size, tile_size), :] = jnp.zeros((tile_size, width), F32)

        for copy in copies:
            copy.wait()

    for i in range(per_step):
        b = lax.rem(meta[0] + t, parts) * per_part + i
        block = grad[aligned((t * per_step + i) * tile_size, tile_size, tile_size), :]
        part = lax.dot_general(
            masked_tiles(tiles, i, counts[b]), block, (((0,), (0,)), ((), ())), preferred_element_type=F32
        )
        for k in range(slots):
            total[aligned(cols[b, k] * tile_size, tile_size, tile_size), :] += part[k * tile_size : (k + 1) * tile_size]

    @pl.when(t == parts - 1)
    def _():
        copies = []
        for o, (out, at) in enumerate(terms):
            slot = o % 2
            if o >= 2:
                copies[o - 2].wait()

            @pl.loop(0, rows // tile_size, unroll=4)
            def _(i):
                start = aligned(meta[1 + o] + i * tile_size, tile_size, tile_size)
                stage[slot, aligned(i * tile_size, tile_size, tile_size), :] = total[start, :].astype(BF16)

            copies.append(
                pltpu.make_async_copy(stage.at[slot], outs[out].at[pl.ds(at * rows, rows)], out_sems.at[o])
            )
            copies[o].start()
        for copy in copies[-2:]:
            copy.wait()


def spmm_t(tiles, columns, counts, meta, grads, parts, held, rows, total_rows):
    blocks, slots, tile_size, _ = tiles.shape
    width = grads[0].shape[1]
    per_part = blocks // parts
    flat = [(out, at) for out, many in enumerate(held) for at in range(many)]
    return pl.pallas_call(
        functools.partial(spmm_t_kernel, len(grads), per_part, len(held), flat),
        grid_spec=pltpu.PrefetchScalarGridSpec(
            num_scalar_prefetch=3,
            grid=(parts,),
            in_specs=[step_spec(blocks, slots, tile_size, parts, per_part, 0)] + [any_spec()] * len(grads),
            out_specs=[any_spec()] * len(held),
            scratch_shapes=[
                pltpu.VMEM((total_rows, width), F32),
                pltpu.VMEM((rows, width), BF16),
                pltpu.VMEM((2, rows, width), BF16),
                pltpu.SemaphoreType.DMA((len(grads),)),
                pltpu.SemaphoreType.DMA((len(flat),)),
            ],
        ),
        out_shape=[jax.ShapeDtypeStruct((many * rows, width), BF16) for many in held],
        compiler_params=params(),
        cost_estimate=pl.CostEstimate(
            flops=2 * blocks * slots * tile_size * tile_size * width,
            bytes_accessed=2 * (tiles.size + total_rows * width),
            transcendentals=0,
        ),
        name="spmm_t",
    )(columns, counts, meta, tiles, *grads)


def dense_kernel(parts, chunks, n_earlier, is_first, is_last, meta, *refs):
    n_mixed = parts * chunks
    mixed_refs, cot_refs, w_hbm = refs[:n_mixed], refs[n_mixed : n_mixed + parts], refs[n_mixed + parts]
    refs = refs[n_mixed + parts + 1 :]
    if not is_first:
        sums_hbm, refs = refs[0], refs[1:]
    outs = refs[n_earlier:]
    act_outs, mg_outs = outs[:parts], outs[parts : parts + n_mixed]
    sums_out, weight, sums, sems, sums_sem = outs[parts + n_mixed :]
    f_wide, h_wide = weight.shape[0] // parts, weight.shape[1] // parts
    width = f_wide // chunks
    me = meta[0]
    t = pl.program_id(0)

    def place(u):
        return lax.rem(me + u, parts)

    @pl.when(t == 0)
    def _():
        copies = []
        for i in range(parts):
            for j in range(parts):
                src = w_hbm.at[place(j), aligned(place(i) * f_wide, f_wide, f_wide)]
                dst = weight.at[pl.ds(i * f_wide, f_wide), pl.ds(j * h_wide, h_wide)]
                copies.append(pltpu.make_async_copy(src, dst, sems.at[i * parts + j]))
                copies[-1].start()
        for copy in copies:
            copy.wait()
        if is_first:
            sums[...] = jnp.zeros_like(sums)
        else:
            load = pltpu.make_async_copy(sums_hbm, sums, sums_sem)
            load.start()
            load.wait()

    mixed = jnp.concatenate([ref[...] for ref in mixed_refs], axis=1)
    grads = []
    for u in range(parts):
        preact = jnp.dot(mixed, weight[:, u * h_wide : (u + 1) * h_wide], preferred_element_type=F32)
        sig = jax.nn.sigmoid(preact)
        act_outs[u][...] = (preact * sig).astype(BF16)
        grads.append((cot_refs[u][...].astype(F32) * sig * (1.0 + preact * (1.0 - sig))).astype(BF16))
    grad = jnp.concatenate(grads, axis=1)
    back = lax.dot_general(grad, weight[...], (((1,), (1,)), ((), ())), preferred_element_type=F32).astype(BF16)
    for i in range(n_mixed):
        mg_outs[i][...] = back[:, i * width : (i + 1) * width]
    for u in range(parts):
        sums[u * h_wide : (u + 1) * h_wide, :] += lax.dot_general(
            grads[u], mixed, (((0,), (0,)), ((), ())), preferred_element_type=F32
        )

    @pl.when(t == pl.num_programs(0) - 1)
    def _():
        if is_last:
            for u in range(parts):
                to = aligned(place(u) * h_wide, h_wide, h_wide)
                sums_out[to, :] = sums[u * h_wide : (u + 1) * h_wide, :].astype(BF16)
        else:
            store = pltpu.make_async_copy(sums, sums_out, sums_sem)
            store.start()
            store.wait()


def dense(meta, mixed, cot, weight, rows, first, earlier):
    parts, chunks = len(mixed), len(mixed[0])
    width = mixed[0][0][0].shape[1]
    _, features, h_wide = weight.shape
    hidden = parts * h_wide
    all_rows = cot[0].shape[0]
    step = min(rows, 256)
    flat = [m for row in mixed for m in row]
    earlier_whole, earlier_sums = earlier if earlier else ([], [])
    is_first, is_last = not earlier, first + rows == all_rows

    def spec(w, start=0):
        return pl.BlockSpec((step, w), lambda t, meta: (t + start // step, 0))

    kinds = [(h_wide, True)] * parts + [(width, c > 0) for _ in range(parts) for c in range(chunks)]
    whole_at = [i for i, (_, whole) in enumerate(kinds) if whole]
    n_inputs = 1 + len(flat) + parts + 1 + len(earlier_sums)
    sums_spec = pl.BlockSpec((hidden, features), lambda t, meta: (0, 0)) if is_last else any_spec()
    outs = pl.pallas_call(
        functools.partial(dense_kernel, parts, chunks, len(earlier_whole), is_first, is_last),
        grid_spec=pltpu.PrefetchScalarGridSpec(
            num_scalar_prefetch=1,
            grid=(rows // step,),
            in_specs=[spec(width, at) for _, at in flat]
            + [spec(h_wide, first)] * parts
            + [any_spec()] * (1 + len(earlier_sums) + len(earlier_whole)),
            out_specs=[spec(w, first if whole else 0) for w, whole in kinds] + [sums_spec],
            scratch_shapes=[
                pltpu.VMEM((features, hidden), BF16),
                pltpu.VMEM((hidden, features), F32),
                pltpu.SemaphoreType.DMA((parts * parts,)),
                pltpu.SemaphoreType.DMA,
            ],
        ),
        out_shape=[jax.ShapeDtypeStruct((all_rows if whole else rows, w), BF16) for w, whole in kinds]
        + [jax.ShapeDtypeStruct((hidden, features), BF16 if is_last else F32)],
        input_output_aliases={n_inputs + i: at for i, at in enumerate(whole_at)} if earlier else {},
        compiler_params=params(),
        cost_estimate=pl.CostEstimate(
            flops=6 * rows * features * hidden,
            bytes_accessed=2 * (3 * features * hidden + 4 * rows * hidden),
            transcendentals=rows * hidden,
        ),
        name="dense",
    )(meta, *[m for m, _ in flat], *cot, weight, *earlier_sums, *earlier_whole)
    n = parts * chunks
    act, back = outs[:parts], outs[parts : parts + n]
    return (
        act,
        [back[u * chunks : (u + 1) * chunks] for u in range(parts)],
        outs[-1],
        ([outs[i] for i in whole_at], [outs[-1]]),
    )


def total_of(*values):
    return functools.reduce(lambda a, b: a + b, [v.astype(F32) for v in values]).astype(BF16)


def result_kernel(n_ready, low_blocks, *refs):
    ready, (own, got, up_low, up_high, down_low, down_high, out) = refs[:n_ready], refs[n_ready:]
    width = own.shape[1]
    low = pl.program_id(0) < low_blocks
    for c, ref in enumerate(ready):
        out[:, c * width : (c + 1) * width] = ref[...]

    def put(up, down):
        total = own[...].astype(F32) + got[...].astype(F32) + up[...].astype(F32) + down[...].astype(F32)
        out[:, n_ready * width :] = total.astype(BF16)

    @pl.when(low)
    def _():
        put(up_low, down_low)

    @pl.when(jnp.logical_not(low))
    def _():
        put(up_high, down_high)


def result_of(ready, own, got, up, down):
    rows, width = own.shape
    step = min(rows // 2, 1024)
    blocks = rows // step
    low = blocks // 2
    here = pl.BlockSpec((step, width), lambda t: (t, 0))
    lower = pl.BlockSpec((step, width), lambda t: (jnp.minimum(t, low - 1), 0))
    upper = pl.BlockSpec((step, width), lambda t: (jnp.maximum(t - low, 0), 0))
    wide = width * (len(ready) + 1)
    return pl.pallas_call(
        functools.partial(result_kernel, len(ready), low),
        grid=(blocks,),
        in_specs=[here] * (len(ready) + 2) + [lower, upper] * 2,
        out_specs=pl.BlockSpec((step, wide), lambda t: (t, 0)),
        out_shape=jax.ShapeDtypeStruct((rows, wide), BF16),
        compiler_params=params(),
        cost_estimate=pl.CostEstimate(flops=4 * rows * width, bytes_accessed=14 * rows * width, transcendentals=0),
        name="feature_grad",
    )(*ready, own, got, *up, *down)


class Reduction:
    def __init__(self, ring, own_far, own_zero, own_near, other_far, other_zero, other_near):
        self.ring, self.middle = ring, ring.chips // 2
        self.near = near_places(ring)
        self.own_far, self.own_zero, self.own_near = own_far, own_zero, own_near
        self.other_far, self.other_zero, self.other_near = other_far, other_zero, other_near
        self.rows = own_far.shape[0]
        self.half = self.rows // 2

    def swaps(self):
        far = self.ring.sibling(self.other_far)
        self.got_near = self.ring.sibling(lax.optimization_barrier((self.other_near, far))[0])
        self.got_zero = self.ring.sibling(lax.optimization_barrier((self.other_zero, self.got_near))[0])
        return far

    def far_sums(self, got):
        return [total_of(self.own_far[at : at + self.half], got[at : at + self.half]) for at in (0, self.half)]

    def near_sum(self, offset, upper, *more):
        at = self.near.index(offset % self.ring.chips)
        start = upper * self.half
        own = self.own_near[at][start : start + self.half]
        start += at * self.rows
        return total_of(own, self.got_near[start : start + self.half], *more)

    def hops(self, up, down):
        return self.ring.hop(up, 1), self.ring.hop(down, -1)

    def free_sums(self):
        return self.near_sum(self.middle - 1, 1), self.near_sum(1 - self.middle, 0)

    def bound_sums(self, far):
        return self.near_sum(self.middle - 1, 0, far[0]), self.near_sum(1 - self.middle, 1, far[1])

    def finish(self, free, bound):
        for step in range(self.middle - 2, 0, -1):
            free = self.hops(self.near_sum(step, 1, free[0]), self.near_sum(-step, 0, free[1]))
            bound = self.hops(self.near_sum(step, 0, bound[0]), self.near_sum(-step, 1, bound[1]))
        return (bound[0], free[0]), (free[1], bound[1])


def near_places(ring):
    return [o for o in range(1, ring.chips) if o != ring.chips // 2]


def local(features, tiles, columns, counts, weight, cotangent):
    rows, f_wide = features.shape
    h_wide = cotangent.shape[1]
    row_size, parts = lax.axis_size("row"), lax.axis_size("rep")
    ring = Ring(row_size)
    rep = lax.axis_index("rep")
    chunks = f_wide // LANES if f_wide % LANES == 0 else 1
    width = f_wide // chunks
    half = rows // 2
    part_rows = rows // parts
    halves = 2
    half_rows = part_rows // halves
    middle = ring.chips // 2
    near = near_places(ring)
    ends, inner = shift_groups(parts)
    last = chunks - 1
    w = Waves()

    offsets = [(0, 0)] + [(o, 0) for step in range(1, middle) for o in (-step, step)] + [(middle, 0), (middle, half)]
    own_meta = [ring.device_at(o, False) * rows + at for o, at in offsets]
    other_meta = [ring.device_at(o, True) * rows + at for o, at in offsets]
    spmm_meta = jnp.stack([rep] + own_meta + other_meta).astype(jnp.int32)
    held = [1, 1] + [1] * len(near) + [1, 1, len(near)]
    order = [middle, 0] + near
    terms_at = [ring.device_at(o, other) * rows for other in (False, True) for o in order]
    spmm_t_meta = jnp.stack([rep] + terms_at).astype(jnp.int32)
    dense_meta = rep[None].astype(jnp.int32)

    def part_of(x, u):
        return lax.dynamic_slice_in_dim(x, lax.rem(rep + u, parts) * part_rows, part_rows, 0)

    w_full = lax.all_gather(weight, "rep", axis=0, tiled=False)

    cot_blocks = [part_of(cotangent, u) for u in range(parts)]
    xs = [features[:, c * width : (c + 1) * width] for c in range(chunks)]
    up = down = xs[0]
    got_own = {}
    got_other = {}
    mixed = {}

    def run_spmm(c, cut, skip):
        own = [got_own[c, i] for i in range(len(offsets))]
        other = [got_other[c, i] for i in range(len(offsets))]
        return spmm(tiles, columns, counts, spmm_meta, own + other, parts, cut, skip)

    cot_ends = send(cot_blocks, ends)
    own_other = ring.sibling(features)
    for c in range(chunks):
        got_own[c, 0] = xs[c]
        got_other[c, 0] = own_other[:, c * width : (c + 1) * width]
        for step in range(1, middle):
            name = f"{c}_{step}"
            w.go(**{"up" + name: ring.hop(up, 1), "down" + name: ring.hop(down, -1)})
            if c and step == 1:
                for i in range(1, len(offsets)):
                    got_other[c - 1, i] = ring.sibling(got_own[c - 1, i])
                w.go(**{f"mixed{c - 1}": run_spmm(c - 1, 1, 0)})
            if c == 0 and step == 1:
                w.go(metas=(spmm_meta, spmm_t_meta, dense_meta))
            w.close()
            up, down = w["up" + name], w["down" + name]
            got_own[c, 2 * step - 1], got_own[c, 2 * step] = up, down
        w.go(**{f"far_up{c}": ring.hop(up[:half], 1), f"far_down{c}": ring.hop(down[half:], -1)})
        if c == 0:
            w.go(cot_ends=cot_ends, own_other=own_other)
        seen = []
        if c == last:
            for step in range(1, middle):
                for i in (2 * step - 1, 2 * step):
                    got_other[c, i] = ring.sibling(got_own[c, i])
                    w.go(**{f"other{c}_{i}": got_other[c, i]})
                    seen.append(got_other[c, i])
        if c:
            mixed[c - 1] = w[f"mixed{c - 1}"]
            ready = [lax.optimization_barrier((b, *seen))[0] for b in mixed[c - 1]]
            w.go(**{f"mixed_ends{c - 1}": send(ready, ends)})
        w.close()
        if c == 0:
            spmm_meta, spmm_t_meta, dense_meta = w["metas"]
            w.go(cot_inner=send([w.gate(b) for b in cot_blocks], inner))
        else:
            w.go(**{f"mixed_inner{c - 1}": send([w.gate(b) for b in mixed[c - 1]], inner)})
        got_own[c, len(offsets) - 2], got_own[c, len(offsets) - 1] = w[f"far_up{c}"], w[f"far_down{c}"]
        if c < last:
            up = down = w.gate(xs[c + 1])
    for i in (-2, -1):
        got_other[last, len(offsets) + i] = ring.sibling(got_own[last, len(offsets) + i])

    for h in range(halves):
        w.go(**{f"half{h}": run_spmm(last, halves, h)})
        w.close()
        w.go(**{f"half_got{h}": send(w[f"half{h}"], ends + inner)})

    cot = ordered(cot_blocks[0], w["cot_ends"], w["cot_inner"])
    whole = [ordered(mixed[c][0], w[f"mixed_ends{c}"], w[f"mixed_inner{c}"]) for c in range(last)]
    earlier = ()
    for h in range(halves):
        part = ordered(w[f"half{h}"][0], w[f"half_got{h}"])
        blocks = [[(whole[c][u], h * half_rows) for c in range(last)] + [(part[u], 0)] for u in range(parts)]
        act, back, sums, earlier = dense(dense_meta, blocks, cot, w_full, half_rows, h * half_rows, earlier)
        w.go(**{f"back{h}": [b[0] for b in back]})
        if h == halves - 1:
            w.go(whole=(act, back, sums))
        w.close()
        w.go(**{f"back_got{h}": send(w[f"back{h}"], ends + inner)})
    act, back, sums = w["whole"]

    share = sums.shape[0] // row_size

    def sums_for(offset, other):
        return lax.dynamic_slice_in_dim(sums, ring.device_at(offset, other) * share, share, 0)

    wg = Reduction(
        ring,
        sums_for(middle, False),
        sums_for(0, False),
        [sums_for(o, False) for o in near],
        sums_for(middle, True),
        sums_for(0, True),
        jnp.concatenate([sums_for(o, True) for o in near]),
    )
    wg_far = wg.swaps()
    w.go(wg=(wg.own_zero, wg.own_near, wg.got_near, wg.got_zero, wg.far_sums(wg_far)))
    w.close()
    wg.own_zero, wg.own_near, wg.got_near, wg.got_zero, wg_far = w["wg"]
    w.go(wg_far=wg.hops(*wg_far))

    def run_spmm_t(c, grads):
        return spmm_t(tiles, columns, counts, spmm_t_meta, grads, parts, held, rows, rows * row_size)

    parts_got = [ordered(w[f"back{h}"][0], w[f"back_got{h}"]) for h in range(halves)]
    w.go(terms0=run_spmm_t(0, [parts_got[h][u] for u in range(parts) for h in range(halves)]))
    for c in range(1, chunks):
        w.go(**{f"rest_got{c}": send([w.gate(b[c]) for b in back], ends + inner)})
    w.close()
    wg_bound = wg.bound_sums(w["wg_far"])
    wg_free = wg.free_sums()
    wg_got = wg.hops(jnp.concatenate([wg_bound[0], wg_free[0]]), jnp.concatenate([wg_free[1], wg_bound[1]]))
    wg_got = wg.finish(
        (wg_got[0][wg.half :], wg_got[1][: wg.half]), (wg_got[0][: wg.half], wg_got[1][wg.half :])
    )

    reductions = []
    for c in range(chunks):
        terms = w[f"terms{c}"]
        red = Reduction(ring, terms[0], terms[1], terms[2:-3], terms[-3], terms[-2], terms[-1])
        reductions.append(red)
        far = red.far_sums(red.swaps())
        free = red.free_sums()
        if c == 0:
            free = lax.optimization_barrier((free, wg_got))[0]
        far_hops, free_hops = red.hops(*far), red.hops(*free)
        w.go(**{f"far{c}": far_hops, f"zero{c}": red.got_zero})
        if c < last:
            grads = ordered(back[0][c + 1], w[f"rest_got{c + 1}"])
            grads = lax.optimization_barrier((grads, free[0][:8], free[1][:8]))[0]
            w.go(**{f"terms{c + 1}": run_spmm_t(c + 1, grads), f"free{c}": free_hops})
        if c == 0:
            act_inner = send([lax.optimization_barrier((a, free[0][:8]))[0] for a in act], inner)
        if c == last:
            w.go(act_inner=act_inner)
            low_end = send([lax.optimization_barrier((a, *act_inner.values()))[0] for a in act], ends[:1])
            w.go(low_end=low_end)
        w.close()
        if c == 0:
            up, down = (jnp.concatenate(halves_of) for halves_of in wg_got)
            block = total_of(wg.own_zero, wg.got_zero, up, down)
            cuts = [w.gate(block[:, u * f_wide : (u + 1) * f_wide]) for u in range(parts)]
            cuts_got = send(cuts, ends + inner)
            weight_grad = functools.reduce(
                lambda a, b: a + b, [v.astype(F32) for v in [cuts[0], *cuts_got.values()]]
            )
        red.free_hops = w[f"free{c}"] if c < last else free_hops
        bound = red.bound_sums(w[f"far{c}"])
        red.bound_hops = red.hops(*bound)
        if c < last:
            w.go(**{f"bound{c}": red.bound_hops})
    high_end = send([lax.optimization_barrier((a, bound[0][:8]))[0] for a in act], ends[1:])

    feature_grad = ()
    for c, red in enumerate(reductions):
        bound_hops = w[f"bound{c}"] if c < last else red.bound_hops
        up, down = red.finish(red.free_hops, bound_hops)
        feature_grad = (result_of(feature_grad, red.own_zero, w[f"zero{c}"], up, down),)
    feature_grad = feature_grad[0]
    weight_grad = weight_grad.T
    got = {"act_ends": {**w["low_end"], **high_end}, "act_inner": w["act_inner"]}
    act = ordered(act[0], got["act_ends"], got["act_inner"])
    activations = jnp.zeros((rows, h_wide), BF16)
    for u in range(parts):
        activations = lax.dynamic_update_slice_in_dim(activations, act[u], lax.rem(rep + u, parts) * part_rows, 0)
    return (activations, feature_grad, weight_grad)


def solution(mesh):
    in_specs = (
        P("row", "rep"),
        P("row", None, None, None),
        P("row", None),
        P("row"),
        P(None, "rep"),
        P("row", "rep"),
    )
    out_specs = (P("row", "rep"), P("row", "rep"), P("rep", "row"))
    return jax.shard_map(local, mesh=mesh, in_specs=in_specs, out_specs=out_specs, check_vma=False)
```

```python
import functools
import jax
import jax.numpy as jnp
from jax import lax
from jax.experimental import pallas as pl
from jax.experimental.pallas import tpu as pltpu
from jax.sharding import PartitionSpec as P

BF16, F32 = jnp.bfloat16, jnp.float32
VMEM_LIMIT = 56 * 1024 * 1024
LANES = 128
CORES = 2


def params():
    return pltpu.CompilerParams(vmem_limit_bytes=VMEM_LIMIT)


def any_spec():
    return pl.BlockSpec(memory_space=pl.ANY)


class Ring:
    def __init__(self, devices):
        self.chips = devices // CORES
        half = self.chips // 2
        self.order = list(range(half)) + list(range(self.chips - 1, half - 1, -1))
        self.devices = devices

    def perm(self, step):
        pairs = []
        for place, chip in enumerate(self.order):
            to = self.order[(place + step) % self.chips]
            pairs += [(chip * CORES + core, to * CORES + core) for core in range(CORES)]
        return pairs

    def hop(self, value, step):
        return lax.ppermute(value, "row", self.perm(step))

    def sibling(self, value):
        return lax.ppermute(value, "row", [(d, d ^ 1) for d in range(self.devices)])

    def device_at(self, offset, other_core):
        me = lax.axis_index("row")
        order = jnp.array(self.order, jnp.int32)
        place_of = jnp.array([self.order.index(c) for c in range(self.chips)], jnp.int32)
        chip = order[(place_of[me // CORES] + offset) % self.chips]
        core = me % CORES
        return chip * CORES + (1 - core if other_core else core)


class Waves:
    def __init__(self):
        self.pending = {}
        self.done = {}
        self.token = None

    def go(self, **values):
        assert not set(values) & (set(self.pending) | set(self.done))
        self.pending.update(values)

    def close(self):
        names, values = list(self.pending), list(self.pending.values())
        flat, tree = jax.tree.flatten(values)
        flat = lax.optimization_barrier(flat)
        self.token = flat[0]
        self.done.update(zip(names, jax.tree.unflatten(tree, flat)))
        self.pending = {}

    def gate(self, value):
        if self.token is None:
            return value
        return lax.optimization_barrier((value, self.token))[0]

    def __getitem__(self, name):
        return self.done[name]


def shift_groups(size):
    ends = sorted({1, size - 1})
    return ends, [s for s in range(2, size - 1)]


def send(blocks, shifts):
    size = len(blocks)
    return {
        (size - s) % size: lax.ppermute(blocks[s], "rep", [(i, (i + s) % size) for i in range(size)]) for s in shifts
    }


def ordered(own, *groups):
    got = {0: own}
    for group in groups:
        got.update(group)
    return [got[u] for u in range(len(got))]


def masked_tiles(tiles, i, count):
    found = []
    for k in range(tiles.shape[1]):
        tile = tiles[i, k]
        found.append(jnp.where(k < count, tile, jnp.zeros_like(tile)))
    return jnp.concatenate(found, axis=1)


def step_spec(blocks, slots, tile_size, parts, per_step, skip):
    def index(t, cols, cnt, meta):
        return (lax.rem(meta[0] + t, parts) * (blocks // parts // per_step) + skip, 0, 0, 0)

    return pl.BlockSpec((per_step, slots, tile_size, tile_size), index)


def aligned(start, size, unit):
    return pl.ds(pl.multiple_of(start, unit), size)


def spmm_kernel(n_pieces, per_part, skip, cols, counts, meta, tiles, *refs):
    parts = pl.num_programs(0)
    n_outs = len(refs) - n_pieces - 3
    pieces, outs = refs[:n_pieces], refs[n_pieces : n_pieces + n_outs]
    source, result, sems = refs[n_pieces + n_outs :]
    t = pl.program_id(0)
    per_step, slots, tile_size, _ = tiles.shape

    @pl.when(t == 0)
    def _():
        copies = []
        for p, piece in enumerate(pieces):
            copies.append(
                pltpu.make_async_copy(piece, source.at[aligned(meta[1 + p], piece.shape[0], tile_size)], sems.at[p])
            )
            copies[-1].start()
        for copy in copies:
            copy.wait()

    for i in range(per_step):
        b = lax.rem(meta[0] + t, parts) * per_part + skip * per_step + i
        right = [source[aligned(cols[b, k] * tile_size, tile_size, tile_size), :] for k in range(slots)]
        product = jnp.dot(
            masked_tiles(tiles, i, counts[b]), jnp.concatenate(right, axis=0), preferred_element_type=F32
        )
        result[i * tile_size : (i + 1) * tile_size, :] = product.astype(BF16)

    for u in range(n_outs):

        @pl.when(t == u)
        def _():
            outs[u][...] = result[...]


def spmm(tiles, columns, counts, meta, pieces, parts, cut, skip):
    blocks, slots, tile_size, _ = tiles.shape
    width = pieces[0].shape[1]
    total_rows = sum(v.shape[0] for v in pieces)
    per_part = blocks // parts
    per_step = per_part // cut
    rows = per_step * tile_size
    return pl.pallas_call(
        functools.partial(spmm_kernel, len(pieces), per_part, skip),
        grid_spec=pltpu.PrefetchScalarGridSpec(
            num_scalar_prefetch=3,
            grid=(parts,),
            in_specs=[step_spec(blocks, slots, tile_size, parts, per_step, skip)] + [any_spec()] * len(pieces),
            out_specs=[pl.BlockSpec((rows, width), lambda t, cols, cnt, meta: (0, 0))] * parts,
            scratch_shapes=[
                pltpu.VMEM((total_rows, width), BF16),
                pltpu.VMEM((rows, width), BF16),
                pltpu.SemaphoreType.DMA((len(pieces),)),
            ],
        ),
        out_shape=[jax.ShapeDtypeStruct((rows, width), BF16)] * parts,
        compiler_params=params(),
        cost_estimate=pl.CostEstimate(
            flops=2 * parts * rows * slots * tile_size * width,
            bytes_accessed=2 * (tiles.size // cut + total_rows * width),
            transcendentals=0,
        ),
        name="spmm",
    )(columns, counts, meta, tiles, *pieces)


def spmm_t_kernel(n_grads, per_part, n_outs, terms, cols, counts, meta, tiles, *refs):
    parts = pl.num_programs(0)
    grads, outs = refs[:n_grads], refs[n_grads : n_grads + n_outs]
    total, grad, stage, in_sems, out_sems = refs[n_grads + n_outs :]
    t = pl.program_id(0)
    per_step, slots, tile_size, _ = tiles.shape
    width = grad.shape[1]
    rows = stage.shape[1]

    @pl.when(t == 0)
    def _():
        copies, start = [], 0
        for g, ref in enumerate(grads):
            copies.append(pltpu.make_async_copy(ref, grad.at[pl.ds(start, ref.shape[0])], in_sems.at[g]))
            copies[-1].start()
            start += ref.shape[0]

        @pl.loop(0, total.shape[0] // tile_size, unroll=8)
        def _(i):
            total[aligned(i * tile_size, tile_size, tile_size), :] = jnp.zeros((tile_size, width), F32)

        for copy in copies:
            copy.wait()

    for i in range(per_step):
        b = lax.rem(meta[0] + t, parts) * per_part + i
        block = grad[aligned((t * per_step + i) * tile_size, tile_size, tile_size), :]
        part = lax.dot_general(
            masked_tiles(tiles, i, counts[b]), block, (((0,), (0,)), ((), ())), preferred_element_type=F32
        )
        for k in range(slots):
            total[aligned(cols[b, k] * tile_size, tile_size, tile_size), :] += part[k * tile_size : (k + 1) * tile_size]

    @pl.when(t == parts - 1)
    def _():
        copies = []
        for o, (out, at) in enumerate(terms):
            slot = o % 2
            if o >= 2:
                copies[o - 2].wait()

            @pl.loop(0, rows // tile_size, unroll=4)
            def _(i):
                start = aligned(meta[1 + o] + i * tile_size, tile_size, tile_size)
                stage[slot, aligned(i * tile_size, tile_size, tile_size), :] = total[start, :].astype(BF16)

            copies.append(
                pltpu.make_async_copy(stage.at[slot], outs[out].at[pl.ds(at * rows, rows)], out_sems.at[o])
            )
            copies[o].start()
        for copy in copies[-2:]:
            copy.wait()


def spmm_t(tiles, columns, counts, meta, grads, parts, held, rows, total_rows):
    blocks, slots, tile_size, _ = tiles.shape
    width = grads[0].shape[1]
    per_part = blocks // parts
    flat = [(out, at) for out, many in enumerate(held) for at in range(many)]
    return pl.pallas_call(
        functools.partial(spmm_t_kernel, len(grads), per_part, len(held), flat),
        grid_spec=pltpu.PrefetchScalarGridSpec(
            num_scalar_prefetch=3,
            grid=(parts,),
            in_specs=[step_spec(blocks, slots, tile_size, parts, per_part, 0)] + [any_spec()] * len(grads),
            out_specs=[any_spec()] * len(held),
            scratch_shapes=[
                pltpu.VMEM((total_rows, width), F32),
                pltpu.VMEM((rows, width), BF16),
                pltpu.VMEM((2, rows, width), BF16),
                pltpu.SemaphoreType.DMA((len(grads),)),
                pltpu.SemaphoreType.DMA((len(flat),)),
            ],
        ),
        out_shape=[jax.ShapeDtypeStruct((many * rows, width), BF16) for many in held],
        compiler_params=params(),
        cost_estimate=pl.CostEstimate(
            flops=2 * blocks * slots * tile_size * tile_size * width,
            bytes_accessed=2 * (tiles.size + total_rows * width),
            transcendentals=0,
        ),
        name="spmm_t",
    )(columns, counts, meta, tiles, *grads)


def dense_kernel(parts, chunks, n_earlier, is_first, is_last, meta, *refs):
    n_mixed = parts * chunks
    mixed_refs, cot_refs = refs[:n_mixed], refs[n_mixed : n_mixed + parts]
    w_halves = refs[n_mixed + parts : n_mixed + parts + CORES]
    refs = refs[n_mixed + parts + CORES :]
    if not is_first:
        sums_hbm, refs = refs[0], refs[1:]
    outs = refs[n_earlier:]
    act_outs, mg_outs = outs[:parts], outs[parts : parts + n_mixed]
    sums_out, weight, sums, sems, sums_sem = outs[parts + n_mixed :]
    f_wide, h_wide = weight.shape[0] // parts, weight.shape[1] // parts
    width = f_wide // chunks
    me = meta[0]
    t = pl.program_id(0)

    def place(u):
        return lax.rem(me + u, parts)

    @pl.when(t == 0)
    def _():
        copies = []
        for i in range(parts):
            half, at = i // (parts // CORES), i % (parts // CORES)
            whole_at = lax.rem(meta[1] + half, CORES) * (parts // CORES) + at
            to = aligned(lax.rem(whole_at + parts - me, parts) * f_wide, f_wide, f_wide)
            for j in range(parts):
                src = w_halves[half].at[place(j), pl.ds(at * f_wide, f_wide)]
                dst = weight.at[to, pl.ds(j * h_wide, h_wide)]
                copies.append(pltpu.make_async_copy(src, dst, sems.at[i * parts + j]))
                copies[-1].start()
        for copy in copies:
            copy.wait()
        if is_first:
            sums[...] = jnp.zeros_like(sums)
        else:
            load = pltpu.make_async_copy(sums_hbm, sums, sums_sem)
            load.start()
            load.wait()

    mixed = jnp.concatenate([ref[...] for ref in mixed_refs], axis=1)
    grads = []
    for u in range(parts):
        preact = jnp.dot(mixed, weight[:, u * h_wide : (u + 1) * h_wide], preferred_element_type=F32)
        sig = jax.nn.sigmoid(preact)
        act_outs[u][...] = (preact * sig).astype(BF16)
        grads.append((cot_refs[u][...].astype(F32) * sig * (1.0 + preact * (1.0 - sig))).astype(BF16))
    grad = jnp.concatenate(grads, axis=1)
    back = lax.dot_general(grad, weight[...], (((1,), (1,)), ((), ())), preferred_element_type=F32).astype(BF16)
    for i in range(n_mixed):
        mg_outs[i][...] = back[:, i * width : (i + 1) * width]
    for u in range(parts):
        sums[u * h_wide : (u + 1) * h_wide, :] += lax.dot_general(
            grads[u], mixed, (((0,), (0,)), ((), ())), preferred_element_type=F32
        )

    @pl.when(t == pl.num_programs(0) - 1)
    def _():
        if is_last:
            for u in range(parts):
                to = aligned(place(u) * h_wide, h_wide, h_wide)
                sums_out[to, :] = sums[u * h_wide : (u + 1) * h_wide, :].astype(BF16)
        else:
            store = pltpu.make_async_copy(sums, sums_out, sums_sem)
            store.start()
            store.wait()


def dense(meta, mixed, cot, weight, rows, first, earlier):
    parts, chunks = len(mixed), len(mixed[0])
    width = mixed[0][0][0].shape[1]
    features, h_wide = CORES * weight[0].shape[1], weight[0].shape[2]
    hidden = parts * h_wide
    all_rows = cot[0].shape[0]
    step = min(rows, 256)
    flat = [m for row in mixed for m in row]
    earlier_whole, earlier_sums = earlier if earlier else ([], [])
    is_first, is_last = not earlier, first + rows == all_rows

    def spec(w, start=0):
        return pl.BlockSpec((step, w), lambda t, meta: (t + start // step, 0))

    kinds = [(h_wide, True)] * parts + [(width, c > 0) for _ in range(parts) for c in range(chunks)]
    whole_at = [i for i, (_, whole) in enumerate(kinds) if whole]
    n_inputs = 1 + len(flat) + parts + CORES + len(earlier_sums)
    sums_spec = pl.BlockSpec((hidden, features), lambda t, meta: (0, 0)) if is_last else any_spec()
    outs = pl.pallas_call(
        functools.partial(dense_kernel, parts, chunks, len(earlier_whole), is_first, is_last),
        grid_spec=pltpu.PrefetchScalarGridSpec(
            num_scalar_prefetch=1,
            grid=(rows // step,),
            in_specs=[spec(width, at) for _, at in flat]
            + [spec(h_wide, first)] * parts
            + [any_spec()] * (CORES + len(earlier_sums) + len(earlier_whole)),
            out_specs=[spec(w, first if whole else 0) for w, whole in kinds] + [sums_spec],
            scratch_shapes=[
                pltpu.VMEM((features, hidden), BF16),
                pltpu.VMEM((hidden, features), F32),
                pltpu.SemaphoreType.DMA((parts * parts,)),
                pltpu.SemaphoreType.DMA,
            ],
        ),
        out_shape=[jax.ShapeDtypeStruct((all_rows if whole else rows, w), BF16) for w, whole in kinds]
        + [jax.ShapeDtypeStruct((hidden, features), BF16 if is_last else F32)],
        input_output_aliases={n_inputs + i: at for i, at in enumerate(whole_at)} if earlier else {},
        compiler_params=params(),
        cost_estimate=pl.CostEstimate(
            flops=6 * rows * features * hidden,
            bytes_accessed=2 * (3 * features * hidden + 4 * rows * hidden),
            transcendentals=rows * hidden,
        ),
        name="dense",
    )(meta, *[m for m, _ in flat], *cot, *weight, *earlier_sums, *earlier_whole)
    n = parts * chunks
    act, back = outs[:parts], outs[parts : parts + n]
    return (
        act,
        [back[u * chunks : (u + 1) * chunks] for u in range(parts)],
        outs[-1],
        ([outs[i] for i in whole_at], [outs[-1]]),
    )


def total_of(*values):
    return functools.reduce(lambda a, b: a + b, [v.astype(F32) for v in values]).astype(BF16)


def result_kernel(n_ready, low_blocks, *refs):
    ready, (own, got, up_low, up_high, down_low, down_high, out) = refs[:n_ready], refs[n_ready:]
    width = own.shape[1]
    low = pl.program_id(0) < low_blocks
    for c, ref in enumerate(ready):
        out[:, c * width : (c + 1) * width] = ref[...]

    def put(up, down):
        total = own[...].astype(F32) + got[...].astype(F32) + up[...].astype(F32) + down[...].astype(F32)
        out[:, n_ready * width :] = total.astype(BF16)

    @pl.when(low)
    def _():
        put(up_low, down_low)

    @pl.when(jnp.logical_not(low))
    def _():
        put(up_high, down_high)


def result_of(ready, own, got, up, down):
    rows, width = own.shape
    step = min(rows // 2, 1024)
    blocks = rows // step
    low = blocks // 2
    here = pl.BlockSpec((step, width), lambda t: (t, 0))
    lower = pl.BlockSpec((step, width), lambda t: (jnp.minimum(t, low - 1), 0))
    upper = pl.BlockSpec((step, width), lambda t: (jnp.maximum(t - low, 0), 0))
    wide = width * (len(ready) + 1)
    return pl.pallas_call(
        functools.partial(result_kernel, len(ready), low),
        grid=(blocks,),
        in_specs=[here] * (len(ready) + 2) + [lower, upper] * 2,
        out_specs=pl.BlockSpec((step, wide), lambda t: (t, 0)),
        out_shape=jax.ShapeDtypeStruct((rows, wide), BF16),
        compiler_params=params(),
        cost_estimate=pl.CostEstimate(flops=4 * rows * width, bytes_accessed=14 * rows * width, transcendentals=0),
        name="feature_grad",
    )(*ready, own, got, *up, *down)


class Reduction:
    def __init__(self, ring, own_far, own_zero, own_near, other_far, other_zero, other_near):
        self.ring, self.middle = ring, ring.chips // 2
        self.near = near_places(ring)
        self.own_far, self.own_zero, self.own_near = own_far, own_zero, own_near
        self.other_far, self.other_zero, self.other_near = other_far, other_zero, other_near
        self.rows = own_far.shape[0]
        self.half = self.rows // 2

    def start(self):
        got = self.ring.sibling(self.other_far)
        far = [total_of(self.own_far[at : at + self.half], got[at : at + self.half]) for at in (0, self.half)]
        far = lax.optimization_barrier(far)
        self.got_near = self.ring.sibling(lax.optimization_barrier((self.other_near, *far))[0])
        self.got_zero = self.ring.sibling(lax.optimization_barrier((self.other_zero, self.got_near))[0])
        return far

    def near_sum(self, offset, upper, *more):
        at = self.near.index(offset % self.ring.chips)
        start = upper * self.half
        own = self.own_near[at][start : start + self.half]
        start += at * self.rows
        return total_of(own, self.got_near[start : start + self.half], *more)

    def hops(self, up, down):
        return self.ring.hop(up, 1), self.ring.hop(down, -1)

    def free_sums(self):
        return self.near_sum(self.middle - 1, 1), self.near_sum(1 - self.middle, 0)

    def bound_sums(self, far):
        return self.near_sum(self.middle - 1, 0, far[0]), self.near_sum(1 - self.middle, 1, far[1])

    def finish(self, free, bound):
        for step in range(self.middle - 2, 0, -1):
            free = self.hops(self.near_sum(step, 1, free[0]), self.near_sum(-step, 0, free[1]))
            bound = self.hops(self.near_sum(step, 0, bound[0]), self.near_sum(-step, 1, bound[1]))
        return (bound[0], free[0]), (free[1], bound[1])


def near_places(ring):
    return [o for o in range(1, ring.chips) if o != ring.chips // 2]


def local(features, tiles, columns, counts, weight, cotangent):
    rows, f_wide = features.shape
    h_wide = cotangent.shape[1]
    row_size, parts = lax.axis_size("row"), lax.axis_size("rep")
    ring = Ring(row_size)
    rep = lax.axis_index("rep")
    chunks = f_wide // LANES if f_wide % LANES == 0 else 1
    width = f_wide // chunks
    half = rows // 2
    part_rows = rows // parts
    halves = 2
    half_rows = part_rows // halves
    middle = ring.chips // 2
    near = near_places(ring)
    ends, inner = shift_groups(parts)
    last = chunks - 1
    w = Waves()

    offsets = [(0, 0)] + [(o, 0) for step in range(1, middle) for o in (-step, step)] + [(middle, 0), (middle, half)]
    own_meta = [ring.device_at(o, False) * rows + at for o, at in offsets]
    other_meta = [ring.device_at(o, True) * rows + at for o, at in offsets]
    spmm_meta = jnp.stack([rep] + own_meta + other_meta).astype(jnp.int32)
    held = [1, 1] + [1] * len(near) + [1, 1, len(near)]
    order = [middle, 0] + near
    terms_at = [ring.device_at(o, other) * rows for other in (False, True) for o in order]
    spmm_t_meta = jnp.stack([rep] + terms_at).astype(jnp.int32)
    dense_meta = jnp.stack([rep, lax.rem(lax.axis_index("row"), CORES)]).astype(jnp.int32)

    def part_of(x, u):
        return lax.dynamic_slice_in_dim(x, lax.rem(rep + u, parts) * part_rows, part_rows, 0)

    w_rows = weight.shape[0] // CORES
    core = lax.rem(lax.axis_index("row"), CORES)
    w_half = lax.all_gather(lax.dynamic_slice_in_dim(weight, core * w_rows, w_rows, 0), "rep", axis=0, tiled=False)

    cot_blocks = [part_of(cotangent, u) for u in range(parts)]
    xs = [features[:, c * width : (c + 1) * width] for c in range(chunks)]
    up = down = xs[0]
    got_own = {}
    got_other = {}
    mixed = {}

    def run_spmm(c, cut, skip):
        own = [got_own[c, i] for i in range(len(offsets))]
        other = [got_other[c, i] for i in range(len(offsets))]
        return spmm(tiles, columns, counts, spmm_meta, own + other, parts, cut, skip)

    cot_ends = send(cot_blocks, ends)
    own_other = ring.sibling(features)
    for c in range(chunks):
        got_own[c, 0] = xs[c]
        got_other[c, 0] = own_other[:, c * width : (c + 1) * width]
        for step in range(1, middle):
            name = f"{c}_{step}"
            w.go(**{"up" + name: ring.hop(up, 1), "down" + name: ring.hop(down, -1)})
            if c and step == 1:
                for i in range(1, len(offsets)):
                    got_other[c - 1, i] = ring.sibling(got_own[c - 1, i])
                w.go(**{f"mixed{c - 1}": run_spmm(c - 1, 1, 0)})
            if c == 0 and step == 1:
                w.go(metas=(spmm_meta, spmm_t_meta, dense_meta))
            w.close()
            up, down = w["up" + name], w["down" + name]
            got_own[c, 2 * step - 1], got_own[c, 2 * step] = up, down
        w.go(**{f"far_up{c}": ring.hop(up[:half], 1), f"far_down{c}": ring.hop(down[half:], -1)})
        if c == 0:
            w.go(cot_ends=cot_ends, own_other=own_other)
        seen = []
        if c == last:
            for step in range(1, middle):
                for i in (2 * step - 1, 2 * step):
                    got_other[c, i] = ring.sibling(got_own[c, i])
                    w.go(**{f"other{c}_{i}": got_other[c, i]})
                    seen.append(got_other[c, i])
        if c:
            mixed[c - 1] = w[f"mixed{c - 1}"]
            ready = [lax.optimization_barrier((b, *seen))[0] for b in mixed[c - 1]]
            w.go(**{f"mixed_ends{c - 1}": send(ready, ends)})
        w.close()
        if c == 0:
            spmm_meta, spmm_t_meta, dense_meta = w["metas"]
            w.go(cot_inner=send([w.gate(b) for b in cot_blocks], inner))
        else:
            w.go(**{f"mixed_inner{c - 1}": send([w.gate(b) for b in mixed[c - 1]], inner)})
        got_own[c, len(offsets) - 2], got_own[c, len(offsets) - 1] = w[f"far_up{c}"], w[f"far_down{c}"]
        if c < last:
            up = down = w.gate(xs[c + 1])
    for i in (-2, -1):
        got_other[last, len(offsets) + i] = ring.sibling(got_own[last, len(offsets) + i])

    w.go(w_other=ring.sibling(w.gate(w_half)))
    for h in range(halves):
        w.go(**{f"half{h}": run_spmm(last, halves, h)})
        w.close()
        w.go(**{f"half_got{h}": send(w[f"half{h}"], ends + inner)})

    cot = ordered(cot_blocks[0], w["cot_ends"], w["cot_inner"])
    whole = [ordered(mixed[c][0], w[f"mixed_ends{c}"], w[f"mixed_inner{c}"]) for c in range(last)]
    earlier = ()
    for h in range(halves):
        part = ordered(w[f"half{h}"][0], w[f"half_got{h}"])
        blocks = [[(whole[c][u], h * half_rows) for c in range(last)] + [(part[u], 0)] for u in range(parts)]
        act, back, sums, earlier = dense(dense_meta, blocks, cot, (w_half, w["w_other"]), half_rows, h * half_rows, earlier)
        w.go(**{f"back{h}": [b[0] for b in back]})
        if h == halves - 1:
            w.go(whole=(act, back, sums))
        w.close()
        w.go(**{f"back_got{h}": send(w[f"back{h}"], ends + inner)})
    act, back, sums = w["whole"]

    share = sums.shape[0] // row_size
    first_got = w.pending[f"back_got{halves - 1}"][1]
    sums = lax.optimization_barrier((sums, first_got))[0]

    def sums_for(offset, other):
        return lax.dynamic_slice_in_dim(sums, ring.device_at(offset, other) * share, share, 0)

    wg = Reduction(
        ring,
        sums_for(middle, False),
        sums_for(0, False),
        [sums_for(o, False) for o in near],
        sums_for(middle, True),
        sums_for(0, True),
        jnp.concatenate([sums_for(o, True) for o in near]),
    )
    wg_far = wg.hops(*wg.start())
    w.go(wg=(wg.own_zero, wg.own_near, wg.got_near, wg.got_zero, wg_far))
    w.close()
    wg.own_zero, wg.own_near, wg.got_near, wg.got_zero, wg_far = w["wg"]
    wg_bound, wg_free = wg.bound_sums(wg_far), wg.free_sums()
    w.go(wg_got=wg.hops(jnp.concatenate([wg_bound[0], wg_free[0]]), jnp.concatenate([wg_free[1], wg_bound[1]])))

    def run_spmm_t(c, grads):
        return spmm_t(tiles, columns, counts, spmm_t_meta, grads, parts, held, rows, rows * row_size)

    parts_got = [ordered(w[f"back{h}"][0], w[f"back_got{h}"]) for h in range(halves)]
    w.go(terms0=run_spmm_t(0, [parts_got[h][u] for u in range(parts) for h in range(halves)]))
    for c in range(1, chunks):
        w.go(**{f"rest_got{c}": send([w.gate(b[c]) for b in back], ends + inner)})
    w.close()
    wg_got = w["wg_got"]
    wg_got = wg.finish(
        (wg_got[0][wg.half :], wg_got[1][: wg.half]), (wg_got[0][: wg.half], wg_got[1][wg.half :])
    )

    def send_act(shifts, *after):
        return send([lax.optimization_barrier((a, *after))[0] for a in act], shifts)

    reductions = []
    for c in range(chunks):
        terms = w[f"terms{c}"]
        red = Reduction(ring, terms[0], terms[1], terms[2:-3], terms[-3], terms[-2], terms[-1])
        reductions.append(red)
        far = red.start()
        w.go(**{f"far{c}": red.hops(*far), f"zero{c}": red.got_zero})
        free = red.free_sums()
        if c < last:
            grads = ordered(back[0][c + 1], w[f"rest_got{c + 1}"])
            grads = lax.optimization_barrier((grads, free[0][:8], free[1][:8]))[0]
            w.go(**{f"terms{c + 1}": run_spmm_t(c + 1, grads), f"free{c}": red.hops(*free)})
        if c == 0:
            w.go(act_inner=send_act(inner, free[0][:8]))
        if c == last:
            w.go(low_end=send_act(ends[:1], far[0][:8]))
        w.close()
        if c == last:
            free = [w.gate(f) for f in free]
        red.free_hops = w[f"free{c}"] if c < last else red.hops(*free)
        bound = red.bound_sums(w[f"far{c}"])
        red.bound_hops = red.hops(*bound)
        if c < last:
            w.go(**{f"bound{c}": red.bound_hops})
    high_end = send_act(ends[1:], bound[0][:8])

    up, down = (jnp.concatenate(halves_of) for halves_of in wg_got)
    block = total_of(wg.own_zero, wg.got_zero, up, down)
    cuts = [lax.optimization_barrier((block, bound[0][:8]))[0][:, u * f_wide : (u + 1) * f_wide] for u in range(parts)]
    cuts_got = send(cuts, ends + inner)
    weight_grad = functools.reduce(lambda a, b: a + b, [v.astype(F32) for v in [cuts[0], *cuts_got.values()]])

    feature_grad = ()
    for c, red in enumerate(reductions):
        bound_hops = w[f"bound{c}"] if c < last else red.bound_hops
        up, down = red.finish(red.free_hops, bound_hops)
        feature_grad = (result_of(feature_grad, red.own_zero, w[f"zero{c}"], up, down),)
    feature_grad = feature_grad[0]
    weight_grad = weight_grad.T
    got = {"act_ends": {**w["low_end"], **high_end}, "act_inner": w["act_inner"]}
    act = ordered(act[0], got["act_ends"], got["act_inner"])
    activations = jnp.zeros((rows, h_wide), BF16)
    for u in range(parts):
        activations = lax.dynamic_update_slice_in_dim(activations, act[u], lax.rem(rep + u, parts) * part_rows, 0)
    return (activations, feature_grad, weight_grad)


def solution(mesh):
    in_specs = (
        P("row", "rep"),
        P("row", None, None, None),
        P("row", None),
        P("row"),
        P(None, "rep"),
        P("row", "rep"),
    )
    out_specs = (P("row", "rep"), P("row", "rep"), P("rep", "row"))
    return jax.shard_map(local, mesh=mesh, in_specs=in_specs, out_specs=out_specs, check_vma=False)
```

```python
import functools
import jax
import jax.numpy as jnp
from jax import lax
from jax.experimental import pallas as pl
from jax.experimental.pallas import tpu as pltpu
from jax.sharding import PartitionSpec as P

BF16, F32 = jnp.bfloat16, jnp.float32
VMEM_LIMIT = 56 * 1024 * 1024
LANES = 128
CORES = 2


def params():
    return pltpu.CompilerParams(vmem_limit_bytes=VMEM_LIMIT)


def any_spec():
    return pl.BlockSpec(memory_space=pl.ANY)


class Ring:
    def __init__(self, devices):
        self.chips = devices // CORES
        half = self.chips // 2
        self.order = list(range(half)) + list(range(self.chips - 1, half - 1, -1))
        self.devices = devices

    def perm(self, step):
        pairs = []
        for place, chip in enumerate(self.order):
            to = self.order[(place + step) % self.chips]
            pairs += [(chip * CORES + core, to * CORES + core) for core in range(CORES)]
        return pairs

    def hop(self, value, step):
        return lax.ppermute(value, "row", self.perm(step))

    def sibling(self, value):
        return lax.ppermute(value, "row", [(d, d ^ 1) for d in range(self.devices)])

    def device_at(self, offset, other_core):
        me = lax.axis_index("row")
        order = jnp.array(self.order, jnp.int32)
        place_of = jnp.array([self.order.index(c) for c in range(self.chips)], jnp.int32)
        chip = order[(place_of[me // CORES] + offset) % self.chips]
        core = me % CORES
        return chip * CORES + (1 - core if other_core else core)


class Waves:
    def __init__(self):
        self.pending = {}
        self.done = {}
        self.token = None

    def go(self, **values):
        assert not set(values) & (set(self.pending) | set(self.done))
        self.pending.update(values)

    def close(self):
        names, values = list(self.pending), list(self.pending.values())
        flat, tree = jax.tree.flatten(values)
        flat = lax.optimization_barrier(flat)
        self.token = flat[0]
        self.done.update(zip(names, jax.tree.unflatten(tree, flat)))
        self.pending = {}

    def gate(self, value):
        if self.token is None:
            return value
        return lax.optimization_barrier((value, self.token))[0]

    def __getitem__(self, name):
        return self.done[name]


def shift_groups(size):
    ends = sorted({1, size - 1})
    return ends, [s for s in range(2, size - 1)]


def send(blocks, shifts):
    size = len(blocks)
    return {
        (size - s) % size: lax.ppermute(blocks[s], "rep", [(i, (i + s) % size) for i in range(size)]) for s in shifts
    }


def ordered(own, *groups):
    got = {0: own}
    for group in groups:
        got.update(group)
    return [got[u] for u in range(len(got))]


def masked_tiles(tiles, i, count):
    found = []
    for k in range(tiles.shape[1]):
        tile = tiles[i, k]
        found.append(jnp.where(k < count, tile, jnp.zeros_like(tile)))
    return jnp.concatenate(found, axis=1)


def step_spec(blocks, slots, tile_size, parts, per_step, skip):
    def index(t, cols, cnt, meta):
        return (lax.rem(meta[0] + t, parts) * (blocks // parts // per_step) + skip, 0, 0, 0)

    return pl.BlockSpec((per_step, slots, tile_size, tile_size), index)


def aligned(start, size, unit):
    return pl.ds(pl.multiple_of(start, unit), size)


def spmm_kernel(n_pieces, per_part, skip, cols, counts, meta, tiles, *refs):
    parts = pl.num_programs(0)
    n_outs = len(refs) - n_pieces - 3
    pieces, outs = refs[:n_pieces], refs[n_pieces : n_pieces + n_outs]
    source, result, sems = refs[n_pieces + n_outs :]
    t = pl.program_id(0)
    per_step, slots, tile_size, _ = tiles.shape

    @pl.when(t == 0)
    def _():
        copies = []
        for p, piece in enumerate(pieces):
            copies.append(
                pltpu.make_async_copy(piece, source.at[aligned(meta[1 + p], piece.shape[0], tile_size)], sems.at[p])
            )
            copies[-1].start()
        for copy in copies:
            copy.wait()

    for i in range(per_step):
        b = lax.rem(meta[0] + t, parts) * per_part + skip * per_step + i
        right = [source[aligned(cols[b, k] * tile_size, tile_size, tile_size), :] for k in range(slots)]
        product = jnp.dot(
            masked_tiles(tiles, i, counts[b]), jnp.concatenate(right, axis=0), preferred_element_type=F32
        )
        result[i * tile_size : (i + 1) * tile_size, :] = product.astype(BF16)

    for u in range(n_outs):

        @pl.when(t == u)
        def _():
            outs[u][...] = result[...]


def spmm(tiles, columns, counts, meta, pieces, parts, cut, skip):
    blocks, slots, tile_size, _ = tiles.shape
    width = pieces[0].shape[1]
    total_rows = sum(v.shape[0] for v in pieces)
    per_part = blocks // parts
    per_step = per_part // cut
    rows = per_step * tile_size
    return pl.pallas_call(
        functools.partial(spmm_kernel, len(pieces), per_part, skip),
        grid_spec=pltpu.PrefetchScalarGridSpec(
            num_scalar_prefetch=3,
            grid=(parts,),
            in_specs=[step_spec(blocks, slots, tile_size, parts, per_step, skip)] + [any_spec()] * len(pieces),
            out_specs=[pl.BlockSpec((rows, width), lambda t, cols, cnt, meta: (0, 0))] * parts,
            scratch_shapes=[
                pltpu.VMEM((total_rows, width), BF16),
                pltpu.VMEM((rows, width), BF16),
                pltpu.SemaphoreType.DMA((len(pieces),)),
            ],
        ),
        out_shape=[jax.ShapeDtypeStruct((rows, width), BF16)] * parts,
        compiler_params=params(),
        cost_estimate=pl.CostEstimate(
            flops=2 * parts * rows * slots * tile_size * width,
            bytes_accessed=2 * (tiles.size // cut + total_rows * width),
            transcendentals=0,
        ),
        name="spmm",
    )(columns, counts, meta, tiles, *pieces)


def spmm_t_kernel(n_grads, per_part, n_outs, terms, cols, counts, meta, tiles, *refs):
    parts = pl.num_programs(0)
    grads, outs = refs[:n_grads], refs[n_grads : n_grads + n_outs]
    total, grad, stage, in_sems, out_sems = refs[n_grads + n_outs :]
    t = pl.program_id(0)
    per_step, slots, tile_size, _ = tiles.shape
    width = grad.shape[1]
    rows = stage.shape[1]

    @pl.when(t == 0)
    def _():
        copies, start = [], 0
        for g, ref in enumerate(grads):
            copies.append(pltpu.make_async_copy(ref, grad.at[pl.ds(start, ref.shape[0])], in_sems.at[g]))
            copies[-1].start()
            start += ref.shape[0]

        @pl.loop(0, total.shape[0] // tile_size, unroll=8)
        def _(i):
            total[aligned(i * tile_size, tile_size, tile_size), :] = jnp.zeros((tile_size, width), F32)

        for copy in copies:
            copy.wait()

    for i in range(per_step):
        b = lax.rem(meta[0] + t, parts) * per_part + i
        block = grad[aligned((t * per_step + i) * tile_size, tile_size, tile_size), :]
        part = lax.dot_general(
            masked_tiles(tiles, i, counts[b]), block, (((0,), (0,)), ((), ())), preferred_element_type=F32
        )
        for k in range(slots):
            total[aligned(cols[b, k] * tile_size, tile_size, tile_size), :] += part[k * tile_size : (k + 1) * tile_size]

    @pl.when(t == parts - 1)
    def _():
        copies = []
        for o, (out, at) in enumerate(terms):
            slot = o % 2
            if o >= 2:
                copies[o - 2].wait()

            @pl.loop(0, rows // tile_size, unroll=4)
            def _(i):
                start = aligned(meta[1 + o] + i * tile_size, tile_size, tile_size)
                stage[slot, aligned(i * tile_size, tile_size, tile_size), :] = total[start, :].astype(BF16)

            copies.append(
                pltpu.make_async_copy(stage.at[slot], outs[out].at[pl.ds(at * rows, rows)], out_sems.at[o])
            )
            copies[o].start()
        for copy in copies[-2:]:
            copy.wait()


def spmm_t(tiles, columns, counts, meta, grads, parts, held, rows, total_rows):
    blocks, slots, tile_size, _ = tiles.shape
    width = grads[0].shape[1]
    per_part = blocks // parts
    flat = [(out, at) for out, many in enumerate(held) for at in range(many)]
    return pl.pallas_call(
        functools.partial(spmm_t_kernel, len(grads), per_part, len(held), flat),
        grid_spec=pltpu.PrefetchScalarGridSpec(
            num_scalar_prefetch=3,
            grid=(parts,),
            in_specs=[step_spec(blocks, slots, tile_size, parts, per_part, 0)] + [any_spec()] * len(grads),
            out_specs=[any_spec()] * len(held),
            scratch_shapes=[
                pltpu.VMEM((total_rows, width), F32),
                pltpu.VMEM((rows, width), BF16),
                pltpu.VMEM((2, rows, width), BF16),
                pltpu.SemaphoreType.DMA((len(grads),)),
                pltpu.SemaphoreType.DMA((len(flat),)),
            ],
        ),
        out_shape=[jax.ShapeDtypeStruct((many * rows, width), BF16) for many in held],
        compiler_params=params(),
        cost_estimate=pl.CostEstimate(
            flops=2 * blocks * slots * tile_size * tile_size * width,
            bytes_accessed=2 * (tiles.size + total_rows * width),
            transcendentals=0,
        ),
        name="spmm_t",
    )(columns, counts, meta, tiles, *grads)


def dense_kernel(parts, chunks, n_earlier, is_first, is_last, meta, *refs):
    n_mixed = parts * chunks
    mixed_refs, cot_refs = refs[:n_mixed], refs[n_mixed : n_mixed + parts]
    w_halves = refs[n_mixed + parts : n_mixed + parts + CORES]
    refs = refs[n_mixed + parts + CORES :]
    if not is_first:
        sums_hbm, refs = refs[0], refs[1:]
    outs = refs[n_earlier:]
    act_outs, mg_outs = outs[:parts], outs[parts : parts + n_mixed]
    sums_out, weight, sums, sems, sums_sem = outs[parts + n_mixed :]
    f_wide, h_wide = weight.shape[0] // parts, weight.shape[1] // parts
    width = f_wide // chunks
    me = meta[0]
    t = pl.program_id(0)

    def place(u):
        return lax.rem(me + u, parts)

    @pl.when(t == 0)
    def _():
        copies = []
        for i in range(parts):
            half, at = i // (parts // CORES), i % (parts // CORES)
            whole_at = lax.rem(meta[1] + half, CORES) * (parts // CORES) + at
            to = aligned(lax.rem(whole_at + parts - me, parts) * f_wide, f_wide, f_wide)
            for j in range(parts):
                src = w_halves[half].at[place(j), pl.ds(at * f_wide, f_wide)]
                dst = weight.at[to, pl.ds(j * h_wide, h_wide)]
                copies.append(pltpu.make_async_copy(src, dst, sems.at[i * parts + j]))
                copies[-1].start()
        for copy in copies:
            copy.wait()
        if is_first:
            sums[...] = jnp.zeros_like(sums)
        else:
            load = pltpu.make_async_copy(sums_hbm, sums, sums_sem)
            load.start()
            load.wait()

    mixed = jnp.concatenate([ref[...] for ref in mixed_refs], axis=1)
    grads = []
    for u in range(parts):
        preact = jnp.dot(mixed, weight[:, u * h_wide : (u + 1) * h_wide], preferred_element_type=F32)
        sig = jax.nn.sigmoid(preact)
        act_outs[u][...] = (preact * sig).astype(BF16)
        grads.append((cot_refs[u][...].astype(F32) * sig * (1.0 + preact * (1.0 - sig))).astype(BF16))
    grad = jnp.concatenate(grads, axis=1)
    back = lax.dot_general(grad, weight[...], (((1,), (1,)), ((), ())), preferred_element_type=F32).astype(BF16)
    for i in range(n_mixed):
        mg_outs[i][...] = back[:, i * width : (i + 1) * width]
    for u in range(parts):
        sums[u * h_wide : (u + 1) * h_wide, :] += lax.dot_general(
            grads[u], mixed, (((0,), (0,)), ((), ())), preferred_element_type=F32
        )

    @pl.when(t == pl.num_programs(0) - 1)
    def _():
        if is_last:
            for u in range(parts):
                to = aligned(place(u) * h_wide, h_wide, h_wide)
                sums_out[to, :] = sums[u * h_wide : (u + 1) * h_wide, :].astype(BF16)
        else:
            store = pltpu.make_async_copy(sums, sums_out, sums_sem)
            store.start()
            store.wait()


def dense(meta, mixed, cot, weight, rows, first, earlier):
    parts, chunks = len(mixed), len(mixed[0])
    width = mixed[0][0][0].shape[1]
    features, h_wide = CORES * weight[0].shape[1], weight[0].shape[2]
    hidden = parts * h_wide
    all_rows = cot[0].shape[0]
    step = min(rows, 256)
    flat = [m for row in mixed for m in row]
    earlier_whole, earlier_sums = earlier if earlier else ([], [])
    is_first, is_last = not earlier, first + rows == all_rows

    def spec(w, start=0):
        return pl.BlockSpec((step, w), lambda t, meta: (t + start // step, 0))

    kinds = [(h_wide, True)] * parts + [(width, c > 0) for _ in range(parts) for c in range(chunks)]
    whole_at = [i for i, (_, whole) in enumerate(kinds) if whole]
    n_inputs = 1 + len(flat) + parts + CORES + len(earlier_sums)
    sums_spec = pl.BlockSpec((hidden, features), lambda t, meta: (0, 0)) if is_last else any_spec()
    outs = pl.pallas_call(
        functools.partial(dense_kernel, parts, chunks, len(earlier_whole), is_first, is_last),
        grid_spec=pltpu.PrefetchScalarGridSpec(
            num_scalar_prefetch=1,
            grid=(rows // step,),
            in_specs=[spec(width, at) for _, at in flat]
            + [spec(h_wide, first)] * parts
            + [any_spec()] * (CORES + len(earlier_sums) + len(earlier_whole)),
            out_specs=[spec(w, first if whole else 0) for w, whole in kinds] + [sums_spec],
            scratch_shapes=[
                pltpu.VMEM((features, hidden), BF16),
                pltpu.VMEM((hidden, features), F32),
                pltpu.SemaphoreType.DMA((parts * parts,)),
                pltpu.SemaphoreType.DMA,
            ],
        ),
        out_shape=[jax.ShapeDtypeStruct((all_rows if whole else rows, w), BF16) for w, whole in kinds]
        + [jax.ShapeDtypeStruct((hidden, features), BF16 if is_last else F32)],
        input_output_aliases={n_inputs + i: at for i, at in enumerate(whole_at)} if earlier else {},
        compiler_params=params(),
        cost_estimate=pl.CostEstimate(
            flops=6 * rows * features * hidden,
            bytes_accessed=2 * (3 * features * hidden + 4 * rows * hidden),
            transcendentals=rows * hidden,
        ),
        name="dense",
    )(meta, *[m for m, _ in flat], *cot, *weight, *earlier_sums, *earlier_whole)
    n = parts * chunks
    act, back = outs[:parts], outs[parts : parts + n]
    return (
        act,
        [back[u * chunks : (u + 1) * chunks] for u in range(parts)],
        outs[-1],
        ([outs[i] for i in whole_at], [outs[-1]]),
    )


def total_of(*values):
    return functools.reduce(lambda a, b: a + b, [v.astype(F32) for v in values]).astype(BF16)


def first_kernel(low_blocks, own_far, got_far, own_up, got_up, own_down, got_down, to_up, to_down):
    low = pl.program_id(0) < low_blocks

    def put(out, own, got):
        out[...] = (own[...].astype(F32) + got[...].astype(F32)).astype(BF16)

    @pl.when(low)
    def _():
        put(to_up, own_far, got_far)
        put(to_down, own_down, got_down)

    @pl.when(jnp.logical_not(low))
    def _():
        put(to_up, own_up, got_up)
        put(to_down, own_far, got_far)


def first_sums(own_far, own_up, own_down, got, at_far, at_up, at_down):
    rows, width = own_far.shape
    step = min(rows // 2, 1024)
    blocks = rows // step
    low = blocks // 2

    def spec(index):
        return pl.BlockSpec((step, width), lambda t: (index(t), 0))

    def upper(t):
        return jnp.maximum(t, low)

    def lower(t):
        return jnp.minimum(t, low - 1)

    here = spec(lambda t: t)
    return pl.pallas_call(
        functools.partial(first_kernel, low),
        grid=(blocks,),
        in_specs=[
            here,
            spec(lambda t: t + at_far * blocks),
            spec(upper),
            spec(lambda t: upper(t) + at_up * blocks),
            spec(lower),
            spec(lambda t: lower(t) + at_down * blocks),
        ],
        out_specs=[here, here],
        out_shape=[jax.ShapeDtypeStruct((rows, width), BF16)] * 2,
        compiler_params=params(),
        cost_estimate=pl.CostEstimate(flops=2 * rows * width, bytes_accessed=12 * rows * width, transcendentals=0),
        name="first_sums",
    )(own_far, got, own_up, got, own_down, got)


def result_kernel(n_ready, low_blocks, *refs):
    ready, (own, got, up_low, up_high, down_low, down_high, out) = refs[:n_ready], refs[n_ready:]
    width = own.shape[1]
    low = pl.program_id(0) < low_blocks
    for c, ref in enumerate(ready):
        out[:, c * width : (c + 1) * width] = ref[...]

    def put(up, down):
        total = own[...].astype(F32) + got[...].astype(F32) + up[...].astype(F32) + down[...].astype(F32)
        out[:, n_ready * width :] = total.astype(BF16)

    @pl.when(low)
    def _():
        put(up_low, down_low)

    @pl.when(jnp.logical_not(low))
    def _():
        put(up_high, down_high)


def result_of(ready, own, got, up, down):
    rows, width = own.shape
    step = min(rows // 2, 1024)
    blocks = rows // step
    low = blocks // 2
    here = pl.BlockSpec((step, width), lambda t: (t, 0))
    lower = pl.BlockSpec((step, width), lambda t: (jnp.minimum(t, low - 1), 0))

    def upper(value):
        skip = low if value.shape[0] < rows else 0
        return pl.BlockSpec((step, width), lambda t: (jnp.maximum(t, low) - skip, 0))

    wide = width * (len(ready) + 1)
    return pl.pallas_call(
        functools.partial(result_kernel, len(ready), low),
        grid=(blocks,),
        in_specs=[here] * (len(ready) + 2) + [lower, upper(up[1]), lower, upper(down[1])],
        out_specs=pl.BlockSpec((step, wide), lambda t: (t, 0)),
        out_shape=jax.ShapeDtypeStruct((rows, wide), BF16),
        compiler_params=params(),
        cost_estimate=pl.CostEstimate(flops=4 * rows * width, bytes_accessed=14 * rows * width, transcendentals=0),
        name="feature_grad",
    )(*ready, own, got, *up, *down)


class Reduction:
    def __init__(self, ring, own_far, own_zero, own_near, other, other_zero):
        self.ring, self.middle = ring, ring.chips // 2
        self.near = near_places(ring)
        self.own_far, self.own_zero, self.own_near = own_far, own_zero, own_near
        self.other, self.other_zero = other, other_zero
        self.rows = own_far.shape[0]
        self.half = self.rows // 2

    def place(self, offset):
        return self.near.index(offset % self.ring.chips)

    def near_sum(self, offset, upper, *more):
        at = self.place(offset)
        start = upper * self.half
        own = self.own_near[at][start : start + self.half]
        start += (1 + at) * self.rows
        return total_of(own, self.got[start : start + self.half], *more)

    def hops(self, up, down):
        return self.ring.hop(up, 1), self.ring.hop(down, -1)

    def first(self, kernel):
        at_up, at_down = self.place(self.middle - 1), self.place(1 - self.middle)
        if kernel:
            own_up, own_down = self.own_near[at_up], self.own_near[at_down]
            return first_sums(self.own_far, own_up, own_down, self.got, 0, 1 + at_up, 1 + at_down)
        far = total_of(self.own_far, self.got[: self.rows])
        return (
            jnp.concatenate([far[: self.half], self.near_sum(self.middle - 1, 1)]),
            jnp.concatenate([self.near_sum(1 - self.middle, 0), far[self.half :]]),
        )

    def second(self, got_first):
        up, down = got_first
        return (
            self.near_sum(self.middle - 1, 0, up[: self.half]),
            self.near_sum(1 - self.middle, 1, down[self.half :]),
        )

    def finish(self, got_first, bound):
        if self.middle == 2:
            return (bound[0], got_first[0]), (got_first[1], bound[1])
        free = got_first[0][self.half :], got_first[1][: self.half]
        for step in range(self.middle - 2, 0, -1):
            free = self.hops(self.near_sum(step, 1, free[0]), self.near_sum(-step, 0, free[1]))
            bound = self.hops(self.near_sum(step, 0, bound[0]), self.near_sum(-step, 1, bound[1]))
        return (bound[0], free[0]), (free[1], bound[1])


def near_places(ring):
    return [o for o in range(1, ring.chips) if o != ring.chips // 2]


def local(features, tiles, columns, counts, weight, cotangent):
    rows, f_wide = features.shape
    h_wide = cotangent.shape[1]
    row_size, parts = lax.axis_size("row"), lax.axis_size("rep")
    ring = Ring(row_size)
    rep = lax.axis_index("rep")
    chunks = f_wide // LANES if f_wide % LANES == 0 else 1
    width = f_wide // chunks
    half = rows // 2
    part_rows = rows // parts
    halves = 2
    half_rows = part_rows // halves
    middle = ring.chips // 2
    near = near_places(ring)
    ends, inner = shift_groups(parts)
    last = chunks - 1
    w = Waves()

    offsets = [(0, 0)] + [(o, 0) for step in range(1, middle) for o in (-step, step)] + [(middle, 0), (middle, half)]
    own_meta = [ring.device_at(o, False) * rows + at for o, at in offsets]
    other_meta = [ring.device_at(o, True) * rows + at for o, at in offsets]
    spmm_meta = jnp.stack([rep] + own_meta + other_meta).astype(jnp.int32)
    held = [1] * (2 + len(near)) + [1 + len(near), 1]
    terms_at = [ring.device_at(o, False) * rows for o in [middle, 0] + near]
    terms_at += [ring.device_at(o, True) * rows for o in [middle] + near + [0]]
    spmm_t_meta = jnp.stack([rep] + terms_at).astype(jnp.int32)
    dense_meta = jnp.stack([rep, lax.rem(lax.axis_index("row"), CORES)]).astype(jnp.int32)

    def part_of(x, u):
        return lax.dynamic_slice_in_dim(x, lax.rem(rep + u, parts) * part_rows, part_rows, 0)

    w_rows = weight.shape[0] // CORES
    core = lax.rem(lax.axis_index("row"), CORES)
    w_half = lax.all_gather(lax.dynamic_slice_in_dim(weight, core * w_rows, w_rows, 0), "rep", axis=0, tiled=False)

    cot_blocks = [part_of(cotangent, u) for u in range(parts)]
    xs = [features[:, c * width : (c + 1) * width] for c in range(chunks)]
    up = down = xs[0]
    got_own = {}
    got_other = {}
    mixed = {}

    def run_spmm(c, cut, skip):
        own = [got_own[c, i] for i in range(len(offsets))]
        other = [got_other[c, i] for i in range(len(offsets))]
        return spmm(tiles, columns, counts, spmm_meta, own + other, parts, cut, skip)

    cot_ends = send(cot_blocks, ends)
    later = {}
    own_other = ring.sibling(features)
    for c in range(chunks):
        got_own[c, 0] = xs[c]
        got_other[c, 0] = own_other[:, c * width : (c + 1) * width]
        for step in range(1, middle):
            name = f"{c}_{step}"
            w.go(**{"up" + name: ring.hop(up, 1), "down" + name: ring.hop(down, -1)})
            if c and step == 1:
                for i in range(1, len(offsets)):
                    got_other[c - 1, i] = ring.sibling(got_own[c - 1, i])
                w.go(**{f"mixed{c - 1}": run_spmm(c - 1, 1, 0)})
            if c == 0 and step == 1:
                w.go(metas=(spmm_meta, spmm_t_meta, dense_meta))
            w.close()
            up, down = w["up" + name], w["down" + name]
            got_own[c, 2 * step - 1], got_own[c, 2 * step] = up, down
        w.go(**{f"far_up{c}": ring.hop(up[:half], 1), f"far_down{c}": ring.hop(down[half:], -1)})
        if c == 0:
            w.go(cot_ends=cot_ends, own_other=own_other)
        seen = []
        if c == last:
            for step in range(1, middle):
                for i in (2 * step - 1, 2 * step):
                    got_other[c, i] = ring.sibling(got_own[c, i])
                    w.go(**{f"other{c}_{i}": got_other[c, i]})
                    seen.append(got_other[c, i])
        if c:
            mixed[c - 1] = w[f"mixed{c - 1}"]
            ready = [lax.optimization_barrier((b, *seen))[0] for b in mixed[c - 1]]
            later[f"mixed_ends{c - 1}"] = send(ready, ends)
        w.close()
        if c == 0:
            spmm_meta, spmm_t_meta, dense_meta = w["metas"]
            later["cot_inner"] = send([w.gate(b) for b in cot_blocks], inner)
        else:
            later[f"mixed_inner{c - 1}"] = send([w.gate(b) for b in mixed[c - 1]], inner)
        got_own[c, len(offsets) - 2], got_own[c, len(offsets) - 1] = w[f"far_up{c}"], w[f"far_down{c}"]
        if c < last:
            up = down = w.gate(xs[c + 1])
    for i in (-2, -1):
        got_other[last, len(offsets) + i] = ring.sibling(got_own[last, len(offsets) + i])

    w.go(w_other=ring.sibling(w.gate(w_half)), **later)
    for h in range(halves):
        w.go(**{f"half{h}": run_spmm(last, halves, h)})
        w.close()
        w.go(**{f"half_got{h}": send(w[f"half{h}"], ends + inner)})

    cot = ordered(cot_blocks[0], w["cot_ends"], w["cot_inner"])
    whole = [ordered(mixed[c][0], w[f"mixed_ends{c}"], w[f"mixed_inner{c}"]) for c in range(last)]
    earlier = ()
    for h in range(halves):
        part = ordered(w[f"half{h}"][0], w[f"half_got{h}"])
        blocks = [[(whole[c][u], h * half_rows) for c in range(last)] + [(part[u], 0)] for u in range(parts)]
        act, back, sums, earlier = dense(dense_meta, blocks, cot, (w_half, w["w_other"]), half_rows, h * half_rows, earlier)
        w.go(**{f"back{h}": [b[0] for b in back]})
        if h == halves - 1:
            w.go(whole=(act, back, sums))
        w.close()
        w.go(**{f"back_got{h}": send(w[f"back{h}"], ends + inner)})
    act, back, sums = w["whole"]

    share = sums.shape[0] // row_size

    def sums_for(offset, other):
        return lax.dynamic_slice_in_dim(sums, ring.device_at(offset, other) * share, share, 0)

    wg_other = jnp.concatenate([sums_for(o, True) for o in [middle] + near + [0]])
    w.go(wg_got=ring.sibling(wg_other))
    w.close()
    wg_got = w["wg_got"]
    wg = Reduction(
        ring, sums_for(middle, False), sums_for(0, False), [sums_for(o, False) for o in near], None, None
    )
    wg.got, wg.got_zero = wg_got[:-share], wg_got[-share:]

    def run_spmm_t(c, grads):
        return spmm_t(tiles, columns, counts, spmm_t_meta, grads, parts, held, rows, rows * row_size)

    parts_got = [ordered(w[f"back{h}"][0], w[f"back_got{h}"]) for h in range(halves)]
    w.go(wg_first=wg.hops(*wg.first(False)))
    w.go(terms0=run_spmm_t(0, [parts_got[h][u] for u in range(parts) for h in range(halves)]))
    for c in range(1, chunks):
        w.go(**{f"rest_got{c}": send([w.gate(b[c]) for b in back], ends + inner)})
    w.close()
    wg_second = wg.hops(*wg.second(w["wg_first"]))

    def send_act(shifts, *after):
        return send([lax.optimization_barrier((a, *after))[0] for a in act], shifts)

    reductions = []
    for c in range(chunks):
        terms = w[f"terms{c}"]
        red = Reduction(ring, terms[0], terms[1], terms[2:-2], terms[-2], terms[-1])
        reductions.append(red)
        red.got = ring.sibling(red.other)
        if c == 0:
            red.got = lax.optimization_barrier((red.got, wg_second))[0]
        first = red.first(True)
        red.got_zero = ring.sibling(lax.optimization_barrier((red.other_zero, first[0]))[0])
        w.go(**{f"first{c}": red.hops(*first)})
        if c < last:
            grads = ordered(back[0][c + 1], w[f"rest_got{c + 1}"])
            grads = lax.optimization_barrier((grads, first[0][:8], first[1][:8]))[0]
            w.go(**{f"terms{c + 1}": run_spmm_t(c + 1, grads), f"zero{c}": red.got_zero})
        if c == 0:
            w.go(act_ends=send_act(ends, first[0][:8]))
        if c == last:
            w.go(act_inner=send_act(inner, first[0][:8]))
        w.close()
        second = red.second(w[f"first{c}"])
        red.second_hops = red.hops(*second)
        if c < last:
            w.go(**{f"second{c}": red.second_hops})

    up, down = wg.finish(w["wg_first"], wg_second)
    if middle == 2:
        up, down = (up[0], up[1][wg.half :]), (down[0][: wg.half], down[1])
    block = total_of(wg.own_zero, wg.got_zero, jnp.concatenate(up), jnp.concatenate(down))
    block = lax.optimization_barrier((block, second[0][:8]))[0]
    cuts = [block[:, u * f_wide : (u + 1) * f_wide] for u in range(parts)]
    cuts_got = send(cuts, ends + inner)
    weight_grad = functools.reduce(lambda a, b: a + b, [v.astype(F32) for v in [cuts[0], *cuts_got.values()]])

    feature_grad = ()
    for c, red in enumerate(reductions):
        second_hops = w[f"second{c}"] if c < last else red.second_hops
        got_zero = w[f"zero{c}"] if c < last else red.got_zero
        up, down = red.finish(w[f"first{c}"], second_hops)
        feature_grad = (result_of(feature_grad, red.own_zero, got_zero, up, down),)
    feature_grad = feature_grad[0]
    weight_grad = weight_grad.T
    act = ordered(act[0], w["act_ends"], w["act_inner"])
    activations = jnp.zeros((rows, h_wide), BF16)
    for u in range(parts):
        activations = lax.dynamic_update_slice_in_dim(activations, act[u], lax.rem(rep + u, parts) * part_rows, 0)
    return (activations, feature_grad, weight_grad)


def solution(mesh):
    in_specs = (
        P("row", "rep"),
        P("row", None, None, None),
        P("row", None),
        P("row"),
        P(None, "rep"),
        P("row", "rep"),
    )
    out_specs = (P("row", "rep"), P("row", "rep"), P("rep", "row"))
    return jax.shard_map(local, mesh=mesh, in_specs=in_specs, out_specs=out_specs, check_vma=False)
```

```python
import functools
import jax
import jax.numpy as jnp
from jax import lax
from jax.experimental import pallas as pl
from jax.experimental.pallas import tpu as pltpu
from jax.sharding import PartitionSpec as P

BF16, F32 = jnp.bfloat16, jnp.float32
VMEM_LIMIT = 56 * 1024 * 1024
LANES = 128
CORES = 2


def params():
    return pltpu.CompilerParams(vmem_limit_bytes=VMEM_LIMIT)


def any_spec():
    return pl.BlockSpec(memory_space=pl.ANY)


class Ring:
    def __init__(self, devices):
        self.chips = devices // CORES
        half = self.chips // 2
        self.order = list(range(half)) + list(range(self.chips - 1, half - 1, -1))
        self.devices = devices

    def perm(self, step):
        pairs = []
        for place, chip in enumerate(self.order):
            to = self.order[(place + step) % self.chips]
            pairs += [(chip * CORES + core, to * CORES + core) for core in range(CORES)]
        return pairs

    def hop(self, value, step):
        return lax.ppermute(value, "row", self.perm(step))

    def sibling(self, value):
        return lax.ppermute(value, "row", [(d, d ^ 1) for d in range(self.devices)])

    def device_at(self, offset, other_core):
        me = lax.axis_index("row")
        order = jnp.array(self.order, jnp.int32)
        place_of = jnp.array([self.order.index(c) for c in range(self.chips)], jnp.int32)
        chip = order[(place_of[me // CORES] + offset) % self.chips]
        core = me % CORES
        return chip * CORES + (1 - core if other_core else core)


class Waves:
    def __init__(self):
        self.pending = {}
        self.done = {}
        self.token = None

    def go(self, **values):
        assert not set(values) & (set(self.pending) | set(self.done))
        self.pending.update(values)

    def close(self):
        names, values = list(self.pending), list(self.pending.values())
        flat, tree = jax.tree.flatten(values)
        flat = lax.optimization_barrier(flat)
        self.token = flat[0]
        self.done.update(zip(names, jax.tree.unflatten(tree, flat)))
        self.pending = {}

    def gate(self, value):
        if self.token is None:
            return value
        return lax.optimization_barrier((value, self.token))[0]

    def __getitem__(self, name):
        return self.done[name]


def shift_groups(size):
    ends = sorted({1, size - 1})
    return ends, [s for s in range(2, size - 1)]


def send(blocks, shifts):
    size = len(blocks)
    return {
        (size - s) % size: lax.ppermute(blocks[s], "rep", [(i, (i + s) % size) for i in range(size)]) for s in shifts
    }


def ordered(own, *groups):
    got = {0: own}
    for group in groups:
        got.update(group)
    return [got[u] for u in range(len(got))]


def masked_tiles(tiles, i, count):
    found = []
    for k in range(tiles.shape[1]):
        tile = tiles[i, k]
        found.append(jnp.where(k < count, tile, jnp.zeros_like(tile)))
    return jnp.concatenate(found, axis=1)


def step_spec(blocks, slots, tile_size, parts, per_step, skip):
    def index(t, cols, cnt, meta):
        return (lax.rem(meta[0] + t, parts) * (blocks // parts // per_step) + skip, 0, 0, 0)

    return pl.BlockSpec((per_step, slots, tile_size, tile_size), index)


def aligned(start, size, unit):
    return pl.ds(pl.multiple_of(start, unit), size)


def spmm_kernel(n_pieces, per_part, skip, cols, counts, meta, tiles, *refs):
    parts = pl.num_programs(0)
    n_outs = len(refs) - n_pieces - 3
    pieces, outs = refs[:n_pieces], refs[n_pieces : n_pieces + n_outs]
    source, result, sems = refs[n_pieces + n_outs :]
    t = pl.program_id(0)
    per_step, slots, tile_size, _ = tiles.shape

    @pl.when(t == 0)
    def _():
        copies = []
        for p, piece in enumerate(pieces):
            copies.append(
                pltpu.make_async_copy(piece, source.at[aligned(meta[1 + p], piece.shape[0], tile_size)], sems.at[p])
            )
            copies[-1].start()
        for copy in copies:
            copy.wait()

    for i in range(per_step):
        b = lax.rem(meta[0] + t, parts) * per_part + skip * per_step + i
        right = [source[aligned(cols[b, k] * tile_size, tile_size, tile_size), :] for k in range(slots)]
        product = jnp.dot(
            masked_tiles(tiles, i, counts[b]), jnp.concatenate(right, axis=0), preferred_element_type=F32
        )
        result[i * tile_size : (i + 1) * tile_size, :] = product.astype(BF16)

    for u in range(n_outs):

        @pl.when(t == u)
        def _():
            outs[u][...] = result[...]


def spmm(tiles, columns, counts, meta, pieces, parts, cut, skip):
    blocks, slots, tile_size, _ = tiles.shape
    width = pieces[0].shape[1]
    total_rows = sum(v.shape[0] for v in pieces)
    per_part = blocks // parts
    per_step = per_part // cut
    rows = per_step * tile_size
    return pl.pallas_call(
        functools.partial(spmm_kernel, len(pieces), per_part, skip),
        grid_spec=pltpu.PrefetchScalarGridSpec(
            num_scalar_prefetch=3,
            grid=(parts,),
            in_specs=[step_spec(blocks, slots, tile_size, parts, per_step, skip)] + [any_spec()] * len(pieces),
            out_specs=[pl.BlockSpec((rows, width), lambda t, cols, cnt, meta: (0, 0))] * parts,
            scratch_shapes=[
                pltpu.VMEM((total_rows, width), BF16),
                pltpu.VMEM((rows, width), BF16),
                pltpu.SemaphoreType.DMA((len(pieces),)),
            ],
        ),
        out_shape=[jax.ShapeDtypeStruct((rows, width), BF16)] * parts,
        compiler_params=params(),
        cost_estimate=pl.CostEstimate(
            flops=2 * parts * rows * slots * tile_size * width,
            bytes_accessed=2 * (tiles.size // cut + total_rows * width),
            transcendentals=0,
        ),
        name="spmm",
    )(columns, counts, meta, tiles, *pieces)


def spmm_t_kernel(n_grads, per_part, n_outs, terms, cols, counts, meta, tiles, *refs):
    parts = pl.num_programs(0)
    grads, outs = refs[:n_grads], refs[n_grads : n_grads + n_outs]
    total, grad, stage, in_sems, out_sems = refs[n_grads + n_outs :]
    t = pl.program_id(0)
    per_step, slots, tile_size, _ = tiles.shape
    width = grad.shape[1]
    rows = stage.shape[1]

    @pl.when(t == 0)
    def _():
        copies, start = [], 0
        for g, ref in enumerate(grads):
            copies.append(pltpu.make_async_copy(ref, grad.at[pl.ds(start, ref.shape[0])], in_sems.at[g]))
            copies[-1].start()
            start += ref.shape[0]

        @pl.loop(0, total.shape[0] // tile_size, unroll=8)
        def _(i):
            total[aligned(i * tile_size, tile_size, tile_size), :] = jnp.zeros((tile_size, width), F32)

        for copy in copies:
            copy.wait()

    for i in range(per_step):
        b = lax.rem(meta[0] + t, parts) * per_part + i
        block = grad[aligned((t * per_step + i) * tile_size, tile_size, tile_size), :]
        part = lax.dot_general(
            masked_tiles(tiles, i, counts[b]), block, (((0,), (0,)), ((), ())), preferred_element_type=F32
        )
        for k in range(slots):
            total[aligned(cols[b, k] * tile_size, tile_size, tile_size), :] += part[k * tile_size : (k + 1) * tile_size]

    @pl.when(t == parts - 1)
    def _():
        copies = []
        for o, (out, at) in enumerate(terms):
            slot = o % 2
            if o >= 2:
                copies[o - 2].wait()

            @pl.loop(0, rows // tile_size, unroll=4)
            def _(i):
                start = aligned(meta[1 + o] + i * tile_size, tile_size, tile_size)
                stage[slot, aligned(i * tile_size, tile_size, tile_size), :] = total[start, :].astype(BF16)

            copies.append(
                pltpu.make_async_copy(stage.at[slot], outs[out].at[pl.ds(at * rows, rows)], out_sems.at[o])
            )
            copies[o].start()
        for copy in copies[-2:]:
            copy.wait()


def spmm_t(tiles, columns, counts, meta, grads, parts, held, rows, total_rows):
    blocks, slots, tile_size, _ = tiles.shape
    width = grads[0].shape[1]
    per_part = blocks // parts
    flat = [(out, at) for out, many in enumerate(held) for at in range(many)]
    return pl.pallas_call(
        functools.partial(spmm_t_kernel, len(grads), per_part, len(held), flat),
        grid_spec=pltpu.PrefetchScalarGridSpec(
            num_scalar_prefetch=3,
            grid=(parts,),
            in_specs=[step_spec(blocks, slots, tile_size, parts, per_part, 0)] + [any_spec()] * len(grads),
            out_specs=[any_spec()] * len(held),
            scratch_shapes=[
                pltpu.VMEM((total_rows, width), F32),
                pltpu.VMEM((rows, width), BF16),
                pltpu.VMEM((2, rows, width), BF16),
                pltpu.SemaphoreType.DMA((len(grads),)),
                pltpu.SemaphoreType.DMA((len(flat),)),
            ],
        ),
        out_shape=[jax.ShapeDtypeStruct((many * rows, width), BF16) for many in held],
        compiler_params=params(),
        cost_estimate=pl.CostEstimate(
            flops=2 * blocks * slots * tile_size * tile_size * width,
            bytes_accessed=2 * (tiles.size + total_rows * width),
            transcendentals=0,
        ),
        name="spmm_t",
    )(columns, counts, meta, tiles, *grads)


def dense_kernel(parts, chunks, n_earlier, is_first, is_last, meta, *refs):
    n_mixed = parts * chunks
    mixed_refs, cot_refs = refs[:n_mixed], refs[n_mixed : n_mixed + parts]
    w_hbm, refs = refs[n_mixed + parts], refs[n_mixed + parts + 1 :]
    if not is_first:
        sums_hbm, refs = refs[0], refs[1:]
    outs = refs[n_earlier:]
    act_outs, mg_outs = outs[:parts], outs[parts : parts + n_mixed]
    sums_out, weight, sums, sems, sums_sem = outs[parts + n_mixed :]
    f_wide, h_wide = weight.shape[0] // parts, weight.shape[1] // parts
    width = f_wide // chunks
    me = meta[0]
    t = pl.program_id(0)

    def place(u):
        return lax.rem(me + u, parts)

    @pl.when(t == 0)
    def _():
        copies = []
        for i in range(parts):
            src = w_hbm.at[aligned(place(i) * f_wide, f_wide, f_wide)]
            copies.append(pltpu.make_async_copy(src, weight.at[pl.ds(i * f_wide, f_wide)], sems.at[i]))
            copies[-1].start()
        for copy in copies:
            copy.wait()
        if is_first:
            sums[...] = jnp.zeros_like(sums)
        else:
            load = pltpu.make_async_copy(sums_hbm, sums, sums_sem)
            load.start()
            load.wait()

    mixed = jnp.concatenate([ref[...] for ref in mixed_refs], axis=1)
    grads = []
    for u in range(parts):
        preact = jnp.dot(mixed, weight[:, u * h_wide : (u + 1) * h_wide], preferred_element_type=F32)
        sig = jax.nn.sigmoid(preact)
        act_outs[u][...] = (preact * sig).astype(BF16)
        grads.append((cot_refs[u][...].astype(F32) * sig * (1.0 + preact * (1.0 - sig))).astype(BF16))
    grad = jnp.concatenate(grads, axis=1)
    back = lax.dot_general(grad, weight[...], (((1,), (1,)), ((), ())), preferred_element_type=F32).astype(BF16)
    for i in range(n_mixed):
        mg_outs[i][...] = back[:, i * width : (i + 1) * width]
    for u in range(parts):
        sums[u * h_wide : (u + 1) * h_wide, :] += lax.dot_general(
            grads[u], mixed, (((0,), (0,)), ((), ())), preferred_element_type=F32
        )

    @pl.when(t == pl.num_programs(0) - 1)
    def _():
        if is_last:
            for u in range(parts):
                to = aligned(place(u) * h_wide, h_wide, h_wide)
                sums_out[to, :] = sums[u * h_wide : (u + 1) * h_wide, :].astype(BF16)
        else:
            store = pltpu.make_async_copy(sums, sums_out, sums_sem)
            store.start()
            store.wait()


def dense(meta, mixed, cot, weight, rows, first, earlier):
    parts, chunks = len(mixed), len(mixed[0])
    width = mixed[0][0][0].shape[1]
    features, hidden = weight.shape
    h_wide = hidden // parts
    all_rows = cot[0].shape[0]
    step = min(rows, 256)
    flat = [m for row in mixed for m in row]
    earlier_whole, earlier_sums = earlier if earlier else ([], [])
    is_first, is_last = not earlier, first + rows == all_rows

    def spec(w, start=0):
        return pl.BlockSpec((step, w), lambda t, meta: (t + start // step, 0))

    kinds = [(h_wide, True)] * parts + [(width, c > 0) for _ in range(parts) for c in range(chunks)]
    whole_at = [i for i, (_, whole) in enumerate(kinds) if whole]
    n_inputs = 1 + len(flat) + parts + 1 + len(earlier_sums)
    sums_spec = pl.BlockSpec((hidden, features), lambda t, meta: (0, 0)) if is_last else any_spec()
    outs = pl.pallas_call(
        functools.partial(dense_kernel, parts, chunks, len(earlier_whole), is_first, is_last),
        grid_spec=pltpu.PrefetchScalarGridSpec(
            num_scalar_prefetch=1,
            grid=(rows // step,),
            in_specs=[spec(width, at) for _, at in flat]
            + [spec(h_wide, first)] * parts
            + [any_spec()] * (1 + len(earlier_sums) + len(earlier_whole)),
            out_specs=[spec(w, first if whole else 0) for w, whole in kinds] + [sums_spec],
            scratch_shapes=[
                pltpu.VMEM((features, hidden), BF16),
                pltpu.VMEM((hidden, features), F32),
                pltpu.SemaphoreType.DMA((parts,)),
                pltpu.SemaphoreType.DMA,
            ],
        ),
        out_shape=[jax.ShapeDtypeStruct((all_rows if whole else rows, w), BF16) for w, whole in kinds]
        + [jax.ShapeDtypeStruct((hidden, features), BF16 if is_last else F32)],
        input_output_aliases={n_inputs + i: at for i, at in enumerate(whole_at)} if earlier else {},
        compiler_params=params(),
        cost_estimate=pl.CostEstimate(
            flops=6 * rows * features * hidden,
            bytes_accessed=2 * (3 * features * hidden + 4 * rows * hidden),
            transcendentals=rows * hidden,
        ),
        name="dense",
    )(meta, *[m for m, _ in flat], *cot, weight, *earlier_sums, *earlier_whole)
    n = parts * chunks
    act, back = outs[:parts], outs[parts : parts + n]
    return (
        act,
        [back[u * chunks : (u + 1) * chunks] for u in range(parts)],
        outs[-1],
        ([outs[i] for i in whole_at], [outs[-1]]),
    )


def total_of(*values):
    return functools.reduce(lambda a, b: a + b, [v.astype(F32) for v in values]).astype(BF16)


def result_kernel(n_ready, low_blocks, *refs):
    ready, (own, got, up_low, up_high, down_low, down_high, out) = refs[:n_ready], refs[n_ready:]
    width = own.shape[1]
    low = pl.program_id(0) < low_blocks
    for c, ref in enumerate(ready):
        out[:, c * width : (c + 1) * width] = ref[...]

    def put(up, down):
        total = own[...].astype(F32) + got[...].astype(F32) + up[...].astype(F32) + down[...].astype(F32)
        out[:, n_ready * width :] = total.astype(BF16)

    @pl.when(low)
    def _():
        put(up_low, down_low)

    @pl.when(jnp.logical_not(low))
    def _():
        put(up_high, down_high)


def result_of(ready, own, got, at, up, down):
    rows, width = own.shape
    step = min(rows // 2, 1024)
    blocks = rows // step
    low = blocks // 2
    here = pl.BlockSpec((step, width), lambda t: (t, 0))
    lower = pl.BlockSpec((step, width), lambda t: (jnp.minimum(t, low - 1), 0))
    upper = pl.BlockSpec((step, width), lambda t: (jnp.maximum(t - low, 0), 0))
    there = pl.BlockSpec((step, width), lambda t: (t + at * blocks, 0))
    wide = width * (len(ready) + 1)
    return pl.pallas_call(
        functools.partial(result_kernel, len(ready), low),
        grid=(blocks,),
        in_specs=[here] * (len(ready) + 1) + [there] + [lower, upper] * 2,
        out_specs=pl.BlockSpec((step, wide), lambda t: (t, 0)),
        out_shape=jax.ShapeDtypeStruct((rows, wide), BF16),
        compiler_params=params(),
        cost_estimate=pl.CostEstimate(flops=4 * rows * width, bytes_accessed=14 * rows * width, transcendentals=0),
        name="feature_grad",
    )(*ready, own, got, *up, *down)


class Reduction:
    def __init__(self, ring, own_far, own_zero, own_near, other_far, other_rest):
        self.ring, self.middle = ring, ring.chips // 2
        self.near = near_places(ring)
        self.own_far, self.own_zero, self.own_near = own_far, own_zero, own_near
        self.other_far, self.other_rest = other_far, other_rest
        self.rows = own_far.shape[0]
        self.half = self.rows // 2

    def far_sums(self, got):
        return [total_of(self.own_far[at : at + self.half], got[at : at + self.half]) for at in (0, self.half)]

    def start(self):
        far = lax.optimization_barrier(self.far_sums(self.ring.sibling(self.other_far)))
        self.got = self.ring.sibling(lax.optimization_barrier((self.other_rest, *far))[0])
        return far

    def near_sum(self, offset, upper, *more):
        at = self.near.index(offset % self.ring.chips)
        start = upper * self.half
        own = self.own_near[at][start : start + self.half]
        start += at * self.rows
        return total_of(own, self.got[start : start + self.half], *more)

    def hops(self, up, down):
        return self.ring.hop(up, 1), self.ring.hop(down, -1)

    def free_sums(self):
        return self.near_sum(self.middle - 1, 1), self.near_sum(1 - self.middle, 0)

    def bound_sums(self, far):
        return self.near_sum(self.middle - 1, 0, far[0]), self.near_sum(1 - self.middle, 1, far[1])

    def finish(self, free, bound):
        for step in range(self.middle - 2, 0, -1):
            free = self.hops(self.near_sum(step, 1, free[0]), self.near_sum(-step, 0, free[1]))
            bound = self.hops(self.near_sum(step, 0, bound[0]), self.near_sum(-step, 1, bound[1]))
        return (bound[0], free[0]), (free[1], bound[1])


def near_places(ring):
    return [o for o in range(1, ring.chips) if o != ring.chips // 2]


def local(features, tiles, columns, counts, weight, cotangent):
    rows, f_wide = features.shape
    h_wide = cotangent.shape[1]
    row_size, parts = lax.axis_size("row"), lax.axis_size("rep")
    ring = Ring(row_size)
    rep = lax.axis_index("rep")
    chunks = f_wide // LANES if f_wide % LANES == 0 else 1
    width = f_wide // chunks
    half = rows // 2
    part_rows = rows // parts
    halves = 2
    half_rows = part_rows // halves
    middle = ring.chips // 2
    near = near_places(ring)
    ends, inner = shift_groups(parts)
    last = chunks - 1
    w = Waves()

    offsets = [(0, 0)] + [(o, 0) for step in range(1, middle) for o in (-step, step)] + [(middle, 0), (middle, half)]
    own_meta = [ring.device_at(o, False) * rows + at for o, at in offsets]
    other_meta = [ring.device_at(o, True) * rows + at for o, at in offsets]
    spmm_meta = jnp.stack([rep] + own_meta + other_meta).astype(jnp.int32)
    held = [1] * (2 + len(near)) + [1, len(near) + 1]
    terms_at = [ring.device_at(o, False) * rows for o in [middle, 0] + near]
    terms_at += [ring.device_at(o, True) * rows for o in [middle] + near + [0]]
    spmm_t_meta = jnp.stack([rep] + terms_at).astype(jnp.int32)
    dense_meta = rep[None].astype(jnp.int32)

    def part_of(x, u):
        return lax.dynamic_slice_in_dim(x, lax.rem(rep + u, parts) * part_rows, part_rows, 0)

    w_rows = weight.shape[0] // row_size
    w_share = lax.dynamic_slice_in_dim(weight, lax.axis_index("row") * w_rows, w_rows, 0)

    cot_blocks = [part_of(cotangent, u) for u in range(parts)]
    xs = [features[:, c * width : (c + 1) * width] for c in range(chunks)]
    up = down = xs[0]
    got_own = {}
    got_other = {}
    mixed = {}

    def run_spmm(c, cut, skip):
        own = [got_own[c, i] for i in range(len(offsets))]
        other = [got_other[c, i] for i in range(len(offsets))]
        return spmm(tiles, columns, counts, spmm_meta, own + other, parts, cut, skip)

    cot_ends = send(cot_blocks, ends)
    own_other = ring.sibling(features)
    for c in range(chunks):
        got_own[c, 0] = xs[c]
        got_other[c, 0] = own_other[:, c * width : (c + 1) * width]
        for step in range(1, middle):
            name = f"{c}_{step}"
            w.go(**{"up" + name: ring.hop(up, 1), "down" + name: ring.hop(down, -1)})
            if c and step == 1:
                for i in range(1, len(offsets)):
                    got_other[c - 1, i] = ring.sibling(got_own[c - 1, i])
                w.go(**{f"mixed{c - 1}": run_spmm(c - 1, 1, 0)})
            if c == 0 and step == 1:
                w.go(metas=(spmm_meta, spmm_t_meta, dense_meta))
            w.close()
            up, down = w["up" + name], w["down" + name]
            got_own[c, 2 * step - 1], got_own[c, 2 * step] = up, down
        far_up, far_down = up[:half], down[half:]
        w.go(**{f"far_up{c}": ring.hop(far_up, 1), f"far_down{c}": ring.hop(far_down, -1)})
        if c == 0:
            w.go(cot_ends=cot_ends, own_other=own_other)
            w_ready = lax.optimization_barrier((w_share, far_up[:8], far_down[:8]))[0]
            w.go(shares=send([w_ready] * parts, ends + inner))
        seen = []
        if c == last:
            for step in range(1, middle):
                for i in (2 * step - 1, 2 * step):
                    got_other[c, i] = ring.sibling(got_own[c, i])
                    w.go(**{f"other{c}_{i}": got_other[c, i]})
                    seen.append(got_other[c, i])
        if c:
            mixed[c - 1] = w[f"mixed{c - 1}"]
            ready = [lax.optimization_barrier((b, *seen))[0] for b in mixed[c - 1]]
            w.go(**{f"mixed_ends{c - 1}": send(ready, ends)})
        w.close()
        if c == 0:
            spmm_meta, spmm_t_meta, dense_meta = w["metas"]
            w.go(cot_inner=send([w.gate(b) for b in cot_blocks], inner))
        else:
            w.go(**{f"mixed_inner{c - 1}": send([w.gate(b) for b in mixed[c - 1]], inner)})
        got_own[c, len(offsets) - 2], got_own[c, len(offsets) - 1] = w[f"far_up{c}"], w[f"far_down{c}"]
        if c < last:
            up = down = w.gate(xs[c + 1])
    for i in (-2, -1):
        got_other[last, len(offsets) + i] = ring.sibling(got_own[last, len(offsets) + i])

    w_full = jnp.concatenate(ordered(w_share, w["shares"]), axis=1)
    w_full = lax.all_gather(w.gate(w_full), "row", axis=0, tiled=True)
    for h in range(halves):
        w.go(**{f"half{h}": run_spmm(last, halves, h)})
        w.close()
        w.go(**{f"half_got{h}": send(w[f"half{h}"], ends + inner)})

    cot = ordered(cot_blocks[0], w["cot_ends"], w["cot_inner"])
    whole = [ordered(mixed[c][0], w[f"mixed_ends{c}"], w[f"mixed_inner{c}"]) for c in range(last)]
    earlier = ()
    for h in range(halves):
        part = ordered(w[f"half{h}"][0], w[f"half_got{h}"])
        blocks = [[(whole[c][u], h * half_rows) for c in range(last)] + [(part[u], 0)] for u in range(parts)]
        act, back, sums, earlier = dense(dense_meta, blocks, cot, w_full, half_rows, h * half_rows, earlier)
        w.go(**{f"back{h}": [b[0] for b in back]})
        if h == halves - 1:
            w.go(whole=(act, back, sums))
        w.close()
        w.go(**{f"back_got{h}": send(w[f"back{h}"], ends + inner)})
    act, back, sums = w["whole"]

    share = sums.shape[0] // row_size

    def sums_for(offset, other):
        return lax.dynamic_slice_in_dim(sums, ring.device_at(offset, other) * share, share, 0)

    w.go(wg_got=ring.sibling(jnp.concatenate([sums_for(o, True) for o in [middle] + near + [0]])))
    w.close()
    wg_got = w["wg_got"]
    wg = Reduction(ring, sums_for(middle, False), sums_for(0, False), [sums_for(o, False) for o in near], None, None)
    wg.got = wg_got[share:]
    wg_far, wg_free = wg.far_sums(wg_got[:share]), wg.free_sums()
    w.go(wg_first=wg.hops(jnp.concatenate([wg_far[0], wg_free[0]]), jnp.concatenate([wg_free[1], wg_far[1]])))

    def run_spmm_t(c, grads):
        return spmm_t(tiles, columns, counts, spmm_t_meta, grads, parts, held, rows, rows * row_size)

    parts_got = [ordered(w[f"back{h}"][0], w[f"back_got{h}"]) for h in range(halves)]
    w.go(terms0=run_spmm_t(0, [parts_got[h][u] for u in range(parts) for h in range(halves)]))
    for c in range(1, chunks):
        w.go(**{f"rest_got{c}": send([w.gate(b[c]) for b in back], ends + inner)})
    w.close()
    up, down = w["wg_first"]
    wg_free = up[wg.half :], down[: wg.half]
    wg_bound = wg.bound_sums((up[: wg.half], down[wg.half :]))

    def send_act(shifts, *after):
        return send([lax.optimization_barrier((a, *after))[0] for a in act], shifts)

    reductions = []
    for c in range(chunks):
        terms = w[f"terms{c}"]
        red = Reduction(ring, terms[0], terms[1], terms[2:-2], terms[-2], terms[-1])
        reductions.append(red)
        far = red.start()
        w.go(**{f"far{c}": red.hops(*far)})
        free = red.free_sums()
        if c < last:
            grads = ordered(back[0][c + 1], w[f"rest_got{c + 1}"])
            grads = lax.optimization_barrier((grads, free[0][:8], free[1][:8]))[0]
            w.go(**{f"terms{c + 1}": run_spmm_t(c + 1, grads), f"free{c}": red.hops(*free)})
        if c == 0:
            w.go(act_inner=send_act(inner, free[0][:8]))
        if c == last:
            w.go(low_end=send_act(ends[:1], far[0][:8]))
        w.close()
        if c == last:
            free = [w.gate(f) for f in free]
        red.free_hops = w[f"free{c}"] if c < last else red.hops(*free)
        bound = red.bound_sums(w[f"far{c}"])
        if c == 0:
            bound = [jnp.concatenate([b, v.reshape(-1, width)]) for b, v in zip(bound, wg_bound)]
        red.bound_hops = red.hops(*bound)
        if c < last:
            w.go(**{f"bound{c}": red.bound_hops})

    feature_grad = ()
    for c, red in enumerate(reductions):
        bound_hops = w[f"bound{c}"] if c < last else red.bound_hops
        if c == 0:
            wg_bound = [v[red.half :].reshape(wg.half, -1) for v in bound_hops]
            if middle > 2:
                bound_hops = [v[: red.half] for v in bound_hops]
        up, down = red.finish(red.free_hops, bound_hops)
        at = len(near)
        feature_grad = (result_of(feature_grad, red.own_zero, red.got, at, up, down),)
        if c == 0:
            early = feature_grad[0][:8]
    feature_grad = feature_grad[0]

    up, down = (jnp.concatenate(halves_of) for halves_of in wg.finish(wg_free, wg_bound))
    block = total_of(wg.own_zero, wg.got[len(near) * share :], up, down)
    if chunks > 1:
        block, early = lax.optimization_barrier((block, early))
    cuts = [block[:, u * f_wide : (u + 1) * f_wide] for u in range(parts)]
    cuts_got = send(cuts, ends + inner)
    weight_grad = functools.reduce(lambda a, b: a + b, [v.astype(F32) for v in [cuts[0], *cuts_got.values()]])
    high_end = send_act(ends[1:], early if chunks > 1 else bound[0][:8])
    weight_grad = weight_grad.T
    got = {"act_ends": {**w["low_end"], **high_end}, "act_inner": w["act_inner"]}
    act = ordered(act[0], got["act_ends"], got["act_inner"])
    activations = jnp.zeros((rows, h_wide), BF16)
    for u in range(parts):
        activations = lax.dynamic_update_slice_in_dim(activations, act[u], lax.rem(rep + u, parts) * part_rows, 0)
    return (activations, feature_grad, weight_grad)


def solution(mesh):
    in_specs = (
        P("row", "rep"),
        P("row", None, None, None),
        P("row", None),
        P("row"),
        P(None, "rep"),
        P("row", "rep"),
    )
    out_specs = (P("row", "rep"), P("row", "rep"), P("rep", "row"))
    return jax.shard_map(local, mesh=mesh, in_specs=in_specs, out_specs=out_specs, check_vma=False)
```

```python
import functools
import jax
import jax.numpy as jnp
from jax import lax
from jax.experimental import pallas as pl
from jax.experimental.pallas import tpu as pltpu
from jax.sharding import PartitionSpec as P

BF16, F32 = jnp.bfloat16, jnp.float32
VMEM_LIMIT = 56 * 1024 * 1024
LANES = 128
CORES = 2


def params():
    return pltpu.CompilerParams(vmem_limit_bytes=VMEM_LIMIT)


def any_spec():
    return pl.BlockSpec(memory_space=pl.ANY)


class Ring:
    def __init__(self, devices):
        self.chips = devices // CORES
        half = self.chips // 2
        self.order = list(range(half)) + list(range(self.chips - 1, half - 1, -1))
        self.devices = devices

    def perm(self, step):
        pairs = []
        for place, chip in enumerate(self.order):
            to = self.order[(place + step) % self.chips]
            pairs += [(chip * CORES + core, to * CORES + core) for core in range(CORES)]
        return pairs

    def hop(self, value, step):
        return lax.ppermute(value, "row", self.perm(step))

    def sibling(self, value):
        return lax.ppermute(value, "row", [(d, d ^ 1) for d in range(self.devices)])

    def device_at(self, offset, other_core):
        me = lax.axis_index("row")
        order = jnp.array(self.order, jnp.int32)
        place_of = jnp.array([self.order.index(c) for c in range(self.chips)], jnp.int32)
        chip = order[(place_of[me // CORES] + offset) % self.chips]
        core = me % CORES
        return chip * CORES + (1 - core if other_core else core)


class Waves:
    def __init__(self):
        self.pending = {}
        self.done = {}
        self.token = None

    def go(self, **values):
        assert not set(values) & (set(self.pending) | set(self.done))
        self.pending.update(values)

    def close(self):
        names, values = list(self.pending), list(self.pending.values())
        flat, tree = jax.tree.flatten(values)
        flat = lax.optimization_barrier(flat)
        self.token = flat[0]
        self.done.update(zip(names, jax.tree.unflatten(tree, flat)))
        self.pending = {}

    def gate(self, value):
        if self.token is None:
            return value
        return lax.optimization_barrier((value, self.token))[0]

    def __getitem__(self, name):
        return self.done[name]


def shift_groups(size):
    ends = sorted({1, size - 1})
    return ends, [s for s in range(2, size - 1)]


def send(blocks, shifts):
    size = len(blocks)
    return {
        (size - s) % size: lax.ppermute(blocks[s], "rep", [(i, (i + s) % size) for i in range(size)]) for s in shifts
    }


def ordered(own, *groups):
    got = {0: own}
    for group in groups:
        got.update(group)
    return [got[u] for u in range(len(got))]


def masked_tiles(tiles, i, count):
    found = []
    for k in range(tiles.shape[1]):
        tile = tiles[i, k]
        found.append(jnp.where(k < count, tile, jnp.zeros_like(tile)))
    return jnp.concatenate(found, axis=1)


def step_spec(blocks, slots, tile_size, parts, per_step, skip):
    def index(t, cols, cnt, meta):
        return (lax.rem(meta[0] + t, parts) * (blocks // parts // per_step) + skip, 0, 0, 0)

    return pl.BlockSpec((per_step, slots, tile_size, tile_size), index)


def aligned(start, size, unit):
    return pl.ds(pl.multiple_of(start, unit), size)


def spmm_kernel(n_pieces, per_part, skip, cols, counts, meta, tiles, *refs):
    parts = pl.num_programs(0)
    n_outs = len(refs) - n_pieces - 3
    pieces, outs = refs[:n_pieces], refs[n_pieces : n_pieces + n_outs]
    source, result, sems = refs[n_pieces + n_outs :]
    t = pl.program_id(0)
    per_step, slots, tile_size, _ = tiles.shape

    @pl.when(t == 0)
    def _():
        copies = []
        for p, piece in enumerate(pieces):
            copies.append(
                pltpu.make_async_copy(piece, source.at[aligned(meta[1 + p], piece.shape[0], tile_size)], sems.at[p])
            )
            copies[-1].start()
        for copy in copies:
            copy.wait()

    for i in range(per_step):
        b = lax.rem(meta[0] + t, parts) * per_part + skip * per_step + i
        right = [source[aligned(cols[b, k] * tile_size, tile_size, tile_size), :] for k in range(slots)]
        product = jnp.dot(
            masked_tiles(tiles, i, counts[b]), jnp.concatenate(right, axis=0), preferred_element_type=F32
        )
        result[i * tile_size : (i + 1) * tile_size, :] = product.astype(BF16)

    for u in range(n_outs):

        @pl.when(t == u)
        def _():
            outs[u][...] = result[...]


def spmm(tiles, columns, counts, meta, pieces, parts, cut, skip):
    blocks, slots, tile_size, _ = tiles.shape
    width = pieces[0].shape[1]
    total_rows = sum(v.shape[0] for v in pieces)
    per_part = blocks // parts
    per_step = per_part // cut
    rows = per_step * tile_size
    return pl.pallas_call(
        functools.partial(spmm_kernel, len(pieces), per_part, skip),
        grid_spec=pltpu.PrefetchScalarGridSpec(
            num_scalar_prefetch=3,
            grid=(parts,),
            in_specs=[step_spec(blocks, slots, tile_size, parts, per_step, skip)] + [any_spec()] * len(pieces),
            out_specs=[pl.BlockSpec((rows, width), lambda t, cols, cnt, meta: (0, 0))] * parts,
            scratch_shapes=[
                pltpu.VMEM((total_rows, width), BF16),
                pltpu.VMEM((rows, width), BF16),
                pltpu.SemaphoreType.DMA((len(pieces),)),
            ],
        ),
        out_shape=[jax.ShapeDtypeStruct((rows, width), BF16)] * parts,
        compiler_params=params(),
        cost_estimate=pl.CostEstimate(
            flops=2 * parts * rows * slots * tile_size * width,
            bytes_accessed=2 * (tiles.size // cut + total_rows * width),
            transcendentals=0,
        ),
        name="spmm",
    )(columns, counts, meta, tiles, *pieces)


def spmm_t_kernel(n_grads, per_part, n_outs, terms, cols, counts, meta, tiles, *refs):
    parts = pl.num_programs(0)
    grads, outs = refs[:n_grads], refs[n_grads : n_grads + n_outs]
    total, grad, stage, in_sems, out_sems = refs[n_grads + n_outs :]
    t = pl.program_id(0)
    per_step, slots, tile_size, _ = tiles.shape
    width = grad.shape[1]
    rows = stage.shape[1]

    @pl.when(t == 0)
    def _():
        copies, start = [], 0
        for g, ref in enumerate(grads):
            copies.append(pltpu.make_async_copy(ref, grad.at[pl.ds(start, ref.shape[0])], in_sems.at[g]))
            copies[-1].start()
            start += ref.shape[0]

        @pl.loop(0, total.shape[0] // tile_size, unroll=8)
        def _(i):
            total[aligned(i * tile_size, tile_size, tile_size), :] = jnp.zeros((tile_size, width), F32)

        for copy in copies:
            copy.wait()

    for i in range(per_step):
        b = lax.rem(meta[0] + t, parts) * per_part + i
        block = grad[aligned((t * per_step + i) * tile_size, tile_size, tile_size), :]
        part = lax.dot_general(
            masked_tiles(tiles, i, counts[b]), block, (((0,), (0,)), ((), ())), preferred_element_type=F32
        )
        for k in range(slots):
            total[aligned(cols[b, k] * tile_size, tile_size, tile_size), :] += part[k * tile_size : (k + 1) * tile_size]

    @pl.when(t == parts - 1)
    def _():
        copies = []
        for o, (out, at) in enumerate(terms):
            slot = o % 2
            if o >= 2:
                copies[o - 2].wait()

            @pl.loop(0, rows // tile_size, unroll=4)
            def _(i):
                start = aligned(meta[1 + o] + i * tile_size, tile_size, tile_size)
                stage[slot, aligned(i * tile_size, tile_size, tile_size), :] = total[start, :].astype(BF16)

            copies.append(
                pltpu.make_async_copy(stage.at[slot], outs[out].at[pl.ds(at * rows, rows)], out_sems.at[o])
            )
            copies[o].start()
        for copy in copies[-2:]:
            copy.wait()


def spmm_t(tiles, columns, counts, meta, grads, parts, held, rows, total_rows):
    blocks, slots, tile_size, _ = tiles.shape
    width = grads[0].shape[1]
    per_part = blocks // parts
    flat = [(out, at) for out, many in enumerate(held) for at in range(many)]
    return pl.pallas_call(
        functools.partial(spmm_t_kernel, len(grads), per_part, len(held), flat),
        grid_spec=pltpu.PrefetchScalarGridSpec(
            num_scalar_prefetch=3,
            grid=(parts,),
            in_specs=[step_spec(blocks, slots, tile_size, parts, per_part, 0)] + [any_spec()] * len(grads),
            out_specs=[any_spec()] * len(held),
            scratch_shapes=[
                pltpu.VMEM((total_rows, width), F32),
                pltpu.VMEM((rows, width), BF16),
                pltpu.VMEM((2, rows, width), BF16),
                pltpu.SemaphoreType.DMA((len(grads),)),
                pltpu.SemaphoreType.DMA((len(flat),)),
            ],
        ),
        out_shape=[jax.ShapeDtypeStruct((many * rows, width), BF16) for many in held],
        compiler_params=params(),
        cost_estimate=pl.CostEstimate(
            flops=2 * blocks * slots * tile_size * tile_size * width,
            bytes_accessed=2 * (tiles.size + total_rows * width),
            transcendentals=0,
        ),
        name="spmm_t",
    )(columns, counts, meta, tiles, *grads)


def dense_kernel(parts, chunks, n_earlier, meta, *refs):
    n_mixed = parts * chunks
    mixed_refs, cot_refs, w_hbm = refs[:n_mixed], refs[n_mixed : n_mixed + parts], refs[n_mixed + parts]
    outs = refs[n_mixed + parts + 1 + n_earlier :]
    act_outs, mg_outs = outs[:parts], outs[parts : parts + n_mixed]
    mixed_out, grad_out, weight, sems = outs[parts + n_mixed :]
    f_wide, h_wide = weight.shape[0] // parts, weight.shape[1] // parts
    width = f_wide // chunks
    me = meta[0]

    def place(u):
        return lax.rem(me + u, parts)

    @pl.when(pl.program_id(0) == 0)
    def _():
        copies = []
        for i in range(parts):
            src = w_hbm.at[aligned(place(i) * f_wide, f_wide, f_wide)]
            copies.append(pltpu.make_async_copy(src, weight.at[pl.ds(i * f_wide, f_wide)], sems.at[i]))
            copies[-1].start()
        for copy in copies:
            copy.wait()

    mixed = jnp.concatenate([ref[...] for ref in mixed_refs], axis=1)
    for u in range(parts):
        at = pl.ds(pl.multiple_of(place(u) * f_wide, f_wide), f_wide)
        mixed_out[:, at] = mixed[:, u * f_wide : (u + 1) * f_wide]
    grads = []
    for u in range(parts):
        preact = jnp.dot(mixed, weight[:, u * h_wide : (u + 1) * h_wide], preferred_element_type=F32)
        sig = jax.nn.sigmoid(preact)
        act_outs[u][...] = (preact * sig).astype(BF16)
        grads.append((cot_refs[u][...].astype(F32) * sig * (1.0 + preact * (1.0 - sig))).astype(BF16))
        at = pl.ds(pl.multiple_of(place(u) * h_wide, h_wide), h_wide)
        grad_out[:, at] = grads[u]
    grad = jnp.concatenate(grads, axis=1)
    back = lax.dot_general(grad, weight[...], (((1,), (1,)), ((), ())), preferred_element_type=F32).astype(BF16)
    for i in range(n_mixed):
        mg_outs[i][...] = back[:, i * width : (i + 1) * width]


def dense(meta, mixed, cot, weight, rows, first, earlier):
    parts, chunks = len(mixed), len(mixed[0])
    width = mixed[0][0][0].shape[1]
    features, hidden = weight.shape
    h_wide = hidden // parts
    all_rows = cot[0].shape[0]
    step = min(rows, 256)
    flat = [m for row in mixed for m in row]
    earlier = list(earlier)

    def spec(w, start=0):
        return pl.BlockSpec((step, w), lambda t, meta: (t + start // step, 0))

    kinds = [(h_wide, True)] * parts + [(width, c > 0) for _ in range(parts) for c in range(chunks)]
    kinds += [(features, True), (hidden, True)]
    whole_at = [i for i, (_, whole) in enumerate(kinds) if whole]
    n_inputs = 1 + len(flat) + parts + 1
    outs = pl.pallas_call(
        functools.partial(dense_kernel, parts, chunks, len(earlier)),
        grid_spec=pltpu.PrefetchScalarGridSpec(
            num_scalar_prefetch=1,
            grid=(rows // step,),
            in_specs=[spec(width, at) for _, at in flat]
            + [spec(h_wide, first)] * parts
            + [any_spec()]
            + [any_spec()] * len(earlier),
            out_specs=[spec(w, first if whole else 0) for w, whole in kinds],
            scratch_shapes=[pltpu.VMEM((features, hidden), BF16), pltpu.SemaphoreType.DMA((parts,))],
        ),
        out_shape=[jax.ShapeDtypeStruct((all_rows if whole else rows, w), BF16) for w, whole in kinds],
        input_output_aliases={n_inputs + i: at for i, at in enumerate(whole_at)} if earlier else {},
        compiler_params=params(),
        cost_estimate=pl.CostEstimate(
            flops=4 * rows * features * hidden,
            bytes_accessed=2 * (features * hidden + 6 * rows * hidden),
            transcendentals=rows * hidden,
        ),
        name="dense",
    )(meta, *[m for m, _ in flat], *cot, weight, *earlier)
    n = parts * chunks
    act, back = outs[:parts], outs[parts : parts + n]
    return (
        act,
        [back[u * chunks : (u + 1) * chunks] for u in range(parts)],
        outs[-2],
        outs[-1],
        [outs[i] for i in whole_at],
    )


def total_of(*values):
    return functools.reduce(lambda a, b: a + b, [v.astype(F32) for v in values]).astype(BF16)


def step_kernel(low_blocks, own_up, got_up, up, own_down, got_down, down, to_up, to_down):
    low = pl.program_id(0) < low_blocks

    def put(out, own, got, more, with_more):
        both = own[...].astype(F32) + got[...].astype(F32)

        @pl.when(with_more)
        def _():
            out[...] = (both + more[...].astype(F32)).astype(BF16)

        @pl.when(jnp.logical_not(with_more))
        def _():
            out[...] = both.astype(BF16)

    put(to_up, own_up, got_up, up, low)
    put(to_down, own_down, got_down, down, jnp.logical_not(low))


def step_sums(own_up, at_up, up, own_down, at_down, down, got):
    rows, width = own_up.shape
    step = min(rows // 2, 1024)
    blocks = rows // step
    low = blocks // 2

    def spec(index):
        return pl.BlockSpec((step, width), lambda t: (index(t), 0))

    here = spec(lambda t: t)
    return pl.pallas_call(
        functools.partial(step_kernel, low),
        grid=(blocks,),
        in_specs=[
            here,
            spec(lambda t: t + at_up * blocks),
            spec(lambda t: jnp.minimum(t, low - 1)),
            here,
            spec(lambda t: t + at_down * blocks),
            spec(lambda t: jnp.maximum(t - low, 0)),
        ],
        out_specs=[here, here],
        out_shape=[jax.ShapeDtypeStruct((rows, width), BF16)] * 2,
        compiler_params=params(),
        cost_estimate=pl.CostEstimate(flops=4 * rows * width, bytes_accessed=14 * rows * width, transcendentals=0),
        name="step_sums",
    )(own_up, got, up, own_down, got, down)


def result_kernel(n_ready, *refs):
    ready, (own, got, up, down, out) = refs[:n_ready], refs[n_ready:]
    width = own.shape[1]
    for c, ref in enumerate(ready):
        out[:, c * width : (c + 1) * width] = ref[...]
    out[:, n_ready * width :] = (
        own[...].astype(F32) + got[...].astype(F32) + up[...].astype(F32) + down[...].astype(F32)
    ).astype(BF16)


def result_of(ready, own, got, at, up, down):
    rows, width = own.shape
    step = min(rows // 2, 1024)
    blocks = rows // step
    here = pl.BlockSpec((step, width), lambda t: (t, 0))
    there = pl.BlockSpec((step, width), lambda t: (t + at * blocks, 0))
    wide = width * (len(ready) + 1)
    return pl.pallas_call(
        functools.partial(result_kernel, len(ready)),
        grid=(blocks,),
        in_specs=[here] * (len(ready) + 1) + [there, here, here],
        out_specs=pl.BlockSpec((step, wide), lambda t: (t, 0)),
        out_shape=jax.ShapeDtypeStruct((rows, wide), BF16),
        compiler_params=params(),
        cost_estimate=pl.CostEstimate(flops=4 * rows * width, bytes_accessed=14 * rows * width, transcendentals=0),
        name="feature_grad",
    )(*ready, own, got, up, down)


def halves_kernel(low_blocks, own_far, got_far, own_up, got_up, own_down, got_down, to_up, to_down):
    low = pl.program_id(0) < low_blocks

    def put(out, own, got):
        out[...] = (own[...].astype(F32) + got[...].astype(F32)).astype(BF16)

    @pl.when(low)
    def _():
        put(to_up, own_far, got_far)
        put(to_down, own_down, got_down)

    @pl.when(jnp.logical_not(low))
    def _():
        put(to_up, own_up, got_up)
        put(to_down, own_far, got_far)


def halves_sums(own_far, got_far, own_up, at_up, own_down, at_down, got):
    rows, width = own_far.shape
    step = min(rows // 2, 1024)
    blocks = rows // step
    low = blocks // 2

    def spec(index):
        return pl.BlockSpec((step, width), lambda t: (index(t), 0))

    here = spec(lambda t: t)
    return pl.pallas_call(
        functools.partial(halves_kernel, low),
        grid=(blocks,),
        in_specs=[
            here,
            here,
            spec(lambda t: jnp.maximum(t, low)),
            spec(lambda t: jnp.maximum(t, low) + at_up * blocks),
            spec(lambda t: jnp.minimum(t, low - 1)),
            spec(lambda t: jnp.minimum(t, low - 1) + at_down * blocks),
        ],
        out_specs=[here, here],
        out_shape=[jax.ShapeDtypeStruct((rows, width), BF16)] * 2,
        compiler_params=params(),
        cost_estimate=pl.CostEstimate(flops=2 * rows * width, bytes_accessed=12 * rows * width, transcendentals=0),
        name="halves_sums",
    )(own_far, got_far, own_up, got, own_down, got)


def joined_kernel(low_blocks, own, got, up_low, up_high, down_low, down_high, out):
    low = pl.program_id(0) < low_blocks

    def put(up, down):
        total = own[...].astype(F32) + got[...].astype(F32) + up[...].astype(F32) + down[...].astype(F32)
        out[...] = total.astype(BF16)

    @pl.when(low)
    def _():
        put(up_low, down_low)

    @pl.when(jnp.logical_not(low))
    def _():
        put(up_high, down_high)


def joined(own, got, at, up_low, up, down, down_high):
    rows, width = own.shape
    step = min(rows // 2, 1024)
    blocks = rows // step
    low = blocks // 2

    def spec(index):
        return pl.BlockSpec((step, width), lambda t: (index(t), 0))

    return pl.pallas_call(
        functools.partial(joined_kernel, low),
        grid=(blocks,),
        in_specs=[
            spec(lambda t: t),
            spec(lambda t: t + at * blocks),
            spec(lambda t: jnp.minimum(t, low - 1)),
            spec(lambda t: jnp.maximum(t, low)),
            spec(lambda t: jnp.minimum(t, low - 1)),
            spec(lambda t: jnp.maximum(t - low, 0)),
        ],
        out_specs=spec(lambda t: t),
        out_shape=jax.ShapeDtypeStruct((rows, width), BF16),
        compiler_params=params(),
        cost_estimate=pl.CostEstimate(flops=3 * rows * width, bytes_accessed=10 * rows * width, transcendentals=0),
        name="joined",
    )(own, got, up_low, up, down, down_high)


class Reduction:
    def __init__(self, ring, own_far, own_near, other_far, other_near):
        self.ring, self.middle = ring, ring.chips // 2
        self.near = [o for o in range(ring.chips) if o != self.middle]
        self.own_far, self.own_near, self.other_far, self.other_near = own_far, own_near, other_far, other_near
        self.rows = own_far.shape[0]

    def far_swap(self):
        return self.ring.sibling(self.other_far)

    def near_swap(self, after):
        return self.ring.sibling(lax.optimization_barrier((self.other_near, after))[0])

    def far_sums(self, got):
        half = self.rows // 2
        return [total_of(self.own_far[at : at + half], got[at : at + half]) for at in (0, half)]

    def hops(self, up, down):
        return self.ring.hop(up, 1), self.ring.hop(down, -1)

    def place(self, offset):
        return self.near.index(offset % self.ring.chips)

    def near_terms(self, offset, got):
        at = self.place(offset)
        return self.own_near[at], got[at * self.rows : (at + 1) * self.rows]

    def sums(self, step, got, up, down, kernel):
        if step < self.middle - 1:
            return total_of(*self.near_terms(step, got), up), total_of(*self.near_terms(-step, got), down)
        at_up, at_down = self.place(step), self.place(-step)
        if kernel:
            return step_sums(self.own_near[at_up], at_up, up, self.own_near[at_down], at_down, down, got)
        zeros = jnp.zeros_like(up)
        return (
            total_of(*self.near_terms(step, got), jnp.concatenate([up, zeros])),
            total_of(*self.near_terms(-step, got), jnp.concatenate([zeros, down])),
        )

    def halves(self, got_far, got):
        at_up, at_down = self.place(1), self.place(-1)
        return halves_sums(self.own_far, got_far, self.own_near[at_up], at_up, self.own_near[at_down], at_down, got)

    def other_halves(self, got, up, down):
        half = self.rows // 2
        (own_up, got_up), (own_down, got_down) = self.near_terms(1, got), self.near_terms(-1, got)
        return total_of(own_up[:half], got_up[:half], up[:half]), total_of(own_down[half:], got_down[half:], down[half:])

    def last(self, up, down):
        if self.middle > 1:
            return up, down
        return jnp.concatenate([up, jnp.zeros_like(up)]), jnp.concatenate([jnp.zeros_like(down), down])


def local(features, tiles, columns, counts, weight, cotangent):
    rows, f_wide = features.shape
    h_wide = cotangent.shape[1]
    row_size, parts = lax.axis_size("row"), lax.axis_size("rep")
    ring = Ring(row_size)
    rep = lax.axis_index("rep")
    chunks = f_wide // LANES if f_wide % LANES == 0 else 1
    width = f_wide // chunks
    half = rows // 2
    part_rows = rows // parts
    halves = 2
    half_rows = part_rows // halves
    middle = ring.chips // 2
    near = [o for o in range(ring.chips) if o != middle]
    ends, inner = shift_groups(parts)
    last = chunks - 1
    w = Waves()

    offsets = [(0, 0)] + [(o, 0) for step in range(1, middle) for o in (-step, step)] + [(middle, 0), (middle, half)]
    own_meta = [ring.device_at(o, False) * rows + at for o, at in offsets]
    other_meta = [ring.device_at(o, True) * rows + at for o, at in offsets]
    spmm_meta = jnp.stack([rep] + own_meta + other_meta).astype(jnp.int32)
    held = [1] + [1] * len(near) + [1, len(near)]
    order = [middle] + near
    terms_at = [ring.device_at(o, other) * rows for other in (False, True) for o in order]
    spmm_t_meta = jnp.stack([rep] + terms_at).astype(jnp.int32)
    dense_meta = rep[None].astype(jnp.int32)

    def part_of(x, u):
        return lax.dynamic_slice_in_dim(x, lax.rem(rep + u, parts) * part_rows, part_rows, 0)

    share = weight.shape[0] // row_size
    w_share = lax.dynamic_slice_in_dim(weight, lax.axis_index("row") * share, share, 0)

    cot_blocks = [part_of(cotangent, u) for u in range(parts)]
    xs = [features[:, c * width : (c + 1) * width] for c in range(chunks)]
    up = down = xs[0]
    got_own = {}
    got_other = {}
    mixed = {}

    def run_spmm(c, cut, skip):
        own = [got_own[c, i] for i in range(len(offsets))]
        other = [got_other[c, i] for i in range(len(offsets))]
        return spmm(tiles, columns, counts, spmm_meta, own + other, parts, cut, skip)

    cot_ends = send(cot_blocks, ends)
    own_other = ring.sibling(features)
    for c in range(chunks):
        got_own[c, 0] = xs[c]
        got_other[c, 0] = own_other[:, c * width : (c + 1) * width]
        for step in range(1, middle):
            name = f"{c}_{step}"
            w.go(**{"up" + name: ring.hop(up, 1), "down" + name: ring.hop(down, -1)})
            if c and step == 1:
                for i in range(1, len(offsets)):
                    got_other[c - 1, i] = ring.sibling(got_own[c - 1, i])
                w.go(**{f"mixed{c - 1}": run_spmm(c - 1, 1, 0)})
            if c == 0 and step == 1:
                w.go(metas=(spmm_meta, spmm_t_meta, dense_meta))
            w.close()
            up, down = w["up" + name], w["down" + name]
            got_own[c, 2 * step - 1], got_own[c, 2 * step] = up, down
        w.go(**{f"far_up{c}": ring.hop(up[:half], 1), f"far_down{c}": ring.hop(down[half:], -1)})
        if c == 0:
            w.go(cot_ends=cot_ends, own_other=own_other)
        seen = []
        if c == last:
            for step in range(1, middle):
                for i in (2 * step - 1, 2 * step):
                    got_other[c, i] = ring.sibling(got_own[c, i])
                    w.go(**{f"other{c}_{i}": got_other[c, i]})
                    seen.append(got_other[c, i])
        if c:
            mixed[c - 1] = w[f"mixed{c - 1}"]
            ready = [lax.optimization_barrier((b, *seen))[0] for b in mixed[c - 1]]
            w.go(**{f"mixed_ends{c - 1}": send(ready, ends)})
        w.close()
        if c == 0:
            spmm_meta, spmm_t_meta, dense_meta = w["metas"]
            w.go(cot_inner=send([w.gate(b) for b in cot_blocks], inner))
            w.go(shares=send([w.gate(w_share)] * parts, ends + inner))
        else:
            w.go(**{f"mixed_inner{c - 1}": send([w.gate(b) for b in mixed[c - 1]], inner)})
        got_own[c, len(offsets) - 2], got_own[c, len(offsets) - 1] = w[f"far_up{c}"], w[f"far_down{c}"]
        if c < last:
            up = down = w.gate(xs[c + 1])
    w_rows = jnp.concatenate(ordered(w_share, {**w.done, **w.pending}["shares"]), axis=1)
    w_full = lax.all_gather(w.gate(w_rows), "row", axis=0, tiled=True)
    for i in (-2, -1):
        got_other[last, len(offsets) + i] = ring.sibling(got_own[last, len(offsets) + i])

    for h in range(halves):
        w.go(**{f"half{h}": run_spmm(last, halves, h)})
        w.close()
        w.go(**{f"half_got{h}": send(w[f"half{h}"], ends + inner)})

    cot = ordered(cot_blocks[0], w["cot_ends"], w["cot_inner"])
    whole = [ordered(mixed[c][0], w[f"mixed_ends{c}"], w[f"mixed_inner{c}"]) for c in range(last)]
    earlier = ()
    for h in range(halves):
        part = ordered(w[f"half{h}"][0], w[f"half_got{h}"])
        blocks = [[(whole[c][u], h * half_rows) for c in range(last)] + [(part[u], 0)] for u in range(parts)]
        act, back, mixed_rows, grad_rows, earlier = dense(
            dense_meta, blocks, cot, w_full, half_rows, h * half_rows, earlier
        )
        w.go(**{f"back{h}": [b[0] for b in back]})
        if h == halves - 1:
            w.go(whole=(act, back, mixed_rows, grad_rows))
        w.close()
        w.go(**{f"back_got{h}": send(w[f"back{h}"], ends + inner)})
    act, back, mixed_rows, grad_rows = w["whole"]
    sums = lax.dot_general(grad_rows, mixed_rows, (((0,), (0,)), ((), ())), preferred_element_type=F32).astype(BF16)
    share = sums.shape[0] // row_size

    def sums_for(offset, other):
        return lax.dynamic_slice_in_dim(sums, ring.device_at(offset, other) * share, share, 0)

    wg = Reduction(
        ring,
        sums_for(middle, False),
        [sums_for(o, False) for o in near],
        sums_for(middle, True),
        jnp.concatenate([sums_for(o, True) for o in near]),
    )
    wg_far = wg.far_swap()
    w.go(wg_own=(wg.own_far, wg.own_near), wg_far=wg_far, wg_near=wg.near_swap(wg_far))
    w.close()
    wg.own_far, wg.own_near = w["wg_own"]
    w.go(wg_up_down=wg.hops(*wg.far_sums(w["wg_far"])))

    def run_spmm_t(c, grads):
        return spmm_t(tiles, columns, counts, spmm_t_meta, grads, parts, held, rows, rows * row_size)

    parts_got = [ordered(w[f"back{h}"][0], w[f"back_got{h}"]) for h in range(halves)]
    w.go(terms0=run_spmm_t(0, [parts_got[h][u] for u in range(parts) for h in range(halves)]))
    for c in range(1, chunks):
        w.go(**{f"rest_got{c}": send([w.gate(b[c]) for b in back], ends + inner)})
    w.close()

    def wg_steps(first, until):
        up, down = w["wg_up_down"]
        for step in range(first, until, -1):
            up, down = wg.hops(*wg.sums(step, w["wg_near"], up, down, False))
        return up, down

    def send_act(shifts):
        return send([w.gate(a) for a in act], shifts)

    reductions = []
    for c in range(chunks):
        terms = w[f"terms{c}"]
        red = Reduction(ring, terms[0], terms[1:-2], terms[-2], terms[-1])
        reductions.append(red)
        combined = c < last and middle == 2
        got_far = red.far_swap()
        got_near = red.near_swap(got_far)
        if c == 0:
            wg_last = wg_steps(middle - 1, 0)
            w.go(wg_last=wg_last)
        sums = red.halves(got_far, got_near) if combined else red.far_sums(got_far)
        w.go(**{f"got_near{c}": got_near})
        if c < last:
            grads = ordered(back[0][c + 1], w[f"rest_got{c + 1}"])
            grads, sums = lax.optimization_barrier((grads, sums))
            w.go(**{f"terms{c + 1}": run_spmm_t(c + 1, grads)})
        w.go(**{f"sum{c}_{middle}": red.hops(*sums)})
        if c == 0:
            w.go(act_inner=send_act(inner))
        w.close()
        if c == 0:
            block = total_of(*wg.near_terms(0, w["wg_near"]), *wg.last(*w["wg_last"]))
        if c == last:
            cuts = [
                w.gate(lax.dynamic_slice_in_dim(block, lax.rem(rep + u, parts) * f_wide, f_wide, 1))
                for u in range(parts)
            ]
        if combined:
            w.go(**{f"sum{c}_1": red.hops(*red.other_halves(w[f"got_near{c}"], *w[f"sum{c}_{middle}"]))})
            continue
        for step in range(middle - 1, 0, -1):
            to_up, to_down = red.sums(step, w[f"got_near{c}"], *w[f"sum{c}_{step + 1}"], True)
            if step == 1 and c == last:
                cuts, act, to_up, to_down = lax.optimization_barrier((cuts, act, to_up, to_down))
            w.go(**{f"sum{c}_{step}": red.hops(to_up, to_down)})
            if step > 1:
                w.close()
    w.go(act_ends=send(act, ends))
    cuts_got = send(cuts, ends + inner)
    got = {**w.done, **w.pending}
    got["weight_grad"] = functools.reduce(lambda a, b: a + b, [v.astype(F32) for v in [cuts[0], *cuts_got.values()]])
    ready = []
    at = near.index(0)
    for c, red in enumerate(reductions[:-1]):
        up, down = got[f"sum{c}_1"]
        if middle == 2:
            whole_up, whole_down = got[f"sum{c}_2"]
            ready.append(joined(red.own_near[at], got[f"got_near{c}"], at, up, whole_up, whole_down, down))
        else:
            ready.append(total_of(*red.near_terms(0, got[f"got_near{c}"]), *red.last(up, down)))
    red = reductions[-1]
    feature_grad = result_of(ready, red.own_near[at], got[f"got_near{last}"], at, *red.last(*got[f"sum{last}_1"]))
    weight_grad = got["weight_grad"].T
    act = ordered(act[0], got["act_ends"], got["act_inner"])
    activations = jnp.zeros((rows, h_wide), BF16)
    for u in range(parts):
        activations = lax.dynamic_update_slice_in_dim(activations, act[u], lax.rem(rep + u, parts) * part_rows, 0)
    return (activations, feature_grad, weight_grad)


def solution(mesh):
    in_specs = (
        P("row", "rep"),
        P("row", None, None, None),
        P("row", None),
        P("row"),
        P(None, "rep"),
        P("row", "rep"),
    )
    out_specs = (P("row", "rep"), P("row", "rep"), P("rep", "row"))
    return jax.shard_map(local, mesh=mesh, in_specs=in_specs, out_specs=out_specs, check_vma=False)
```

```python
import functools
import jax
import jax.numpy as jnp
from jax import lax
from jax.experimental import pallas as pl
from jax.experimental.pallas import tpu as pltpu
from jax.sharding import PartitionSpec as P

BF16, F32 = jnp.bfloat16, jnp.float32
VMEM_LIMIT = 56 * 1024 * 1024
LANES = 128
CORES = 2


def params():
    return pltpu.CompilerParams(vmem_limit_bytes=VMEM_LIMIT)


def any_spec():
    return pl.BlockSpec(memory_space=pl.ANY)


class Ring:
    def __init__(self, devices):
        self.chips = devices // CORES
        half = self.chips // 2
        self.order = list(range(half)) + list(range(self.chips - 1, half - 1, -1))
        self.devices = devices

    def perm(self, step):
        pairs = []
        for place, chip in enumerate(self.order):
            to = self.order[(place + step) % self.chips]
            pairs += [(chip * CORES + core, to * CORES + core) for core in range(CORES)]
        return pairs

    def hop(self, value, step):
        return lax.ppermute(value, "row", self.perm(step))

    def sibling(self, value):
        return lax.ppermute(value, "row", [(d, d ^ 1) for d in range(self.devices)])

    def device_at(self, offset, other_core):
        me = lax.axis_index("row")
        order = jnp.array(self.order, jnp.int32)
        place_of = jnp.array([self.order.index(c) for c in range(self.chips)], jnp.int32)
        chip = order[(place_of[me // CORES] + offset) % self.chips]
        core = me % CORES
        return chip * CORES + (1 - core if other_core else core)


class Waves:
    def __init__(self):
        self.pending = {}
        self.done = {}
        self.token = None

    def go(self, **values):
        assert not set(values) & (set(self.pending) | set(self.done))
        self.pending.update(values)

    def close(self):
        names, values = list(self.pending), list(self.pending.values())
        flat, tree = jax.tree.flatten(values)
        flat = lax.optimization_barrier(flat)
        self.token = flat[0]
        self.done.update(zip(names, jax.tree.unflatten(tree, flat)))
        self.pending = {}

    def gate(self, value):
        if self.token is None:
            return value
        return lax.optimization_barrier((value, self.token))[0]

    def __getitem__(self, name):
        return self.done[name]


def shift_groups(size):
    ends = sorted({1, size - 1})
    return ends, [s for s in range(2, size - 1)]


def send(blocks, shifts):
    size = len(blocks)
    return {
        (size - s) % size: lax.ppermute(blocks[s], "rep", [(i, (i + s) % size) for i in range(size)]) for s in shifts
    }


def ordered(own, *groups):
    got = {0: own}
    for group in groups:
        got.update(group)
    return [got[u] for u in range(len(got))]


def masked_tiles(tiles, i, count):
    found = []
    for k in range(tiles.shape[1]):
        tile = tiles[i, k]
        found.append(jnp.where(k < count, tile, jnp.zeros_like(tile)))
    return jnp.concatenate(found, axis=1)


def step_spec(blocks, slots, tile_size, parts, per_step, skip):
    def index(t, cols, cnt, meta):
        return (lax.rem(meta[0] + t, parts) * (blocks // parts // per_step) + skip, 0, 0, 0)

    return pl.BlockSpec((per_step, slots, tile_size, tile_size), index)


def aligned(start, size, unit):
    return pl.ds(pl.multiple_of(start, unit), size)


def spmm_kernel(n_pieces, per_part, skip, cols, counts, meta, tiles, *refs):
    parts = pl.num_programs(0)
    n_outs = len(refs) - n_pieces - 3
    pieces, outs = refs[:n_pieces], refs[n_pieces : n_pieces + n_outs]
    source, result, sems = refs[n_pieces + n_outs :]
    t = pl.program_id(0)
    per_step, slots, tile_size, _ = tiles.shape

    @pl.when(t == 0)
    def _():
        copies = []
        for p, piece in enumerate(pieces):
            copies.append(
                pltpu.make_async_copy(piece, source.at[aligned(meta[1 + p], piece.shape[0], tile_size)], sems.at[p])
            )
            copies[-1].start()
        for copy in copies:
            copy.wait()

    for i in range(per_step):
        b = lax.rem(meta[0] + t, parts) * per_part + skip * per_step + i
        right = [source[aligned(cols[b, k] * tile_size, tile_size, tile_size), :] for k in range(slots)]
        product = jnp.dot(
            masked_tiles(tiles, i, counts[b]), jnp.concatenate(right, axis=0), preferred_element_type=F32
        )
        result[i * tile_size : (i + 1) * tile_size, :] = product.astype(BF16)

    for u in range(n_outs):

        @pl.when(t == u)
        def _():
            outs[u][...] = result[...]


def spmm(tiles, columns, counts, meta, pieces, parts, cut, skip):
    blocks, slots, tile_size, _ = tiles.shape
    width = pieces[0].shape[1]
    total_rows = sum(v.shape[0] for v in pieces)
    per_part = blocks // parts
    per_step = per_part // cut
    rows = per_step * tile_size
    return pl.pallas_call(
        functools.partial(spmm_kernel, len(pieces), per_part, skip),
        grid_spec=pltpu.PrefetchScalarGridSpec(
            num_scalar_prefetch=3,
            grid=(parts,),
            in_specs=[step_spec(blocks, slots, tile_size, parts, per_step, skip)] + [any_spec()] * len(pieces),
            out_specs=[pl.BlockSpec((rows, width), lambda t, cols, cnt, meta: (0, 0))] * parts,
            scratch_shapes=[
                pltpu.VMEM((total_rows, width), BF16),
                pltpu.VMEM((rows, width), BF16),
                pltpu.SemaphoreType.DMA((len(pieces),)),
            ],
        ),
        out_shape=[jax.ShapeDtypeStruct((rows, width), BF16)] * parts,
        compiler_params=params(),
        cost_estimate=pl.CostEstimate(
            flops=2 * parts * rows * slots * tile_size * width,
            bytes_accessed=2 * (tiles.size // cut + total_rows * width),
            transcendentals=0,
        ),
        name="spmm",
    )(columns, counts, meta, tiles, *pieces)


def spmm_t_kernel(n_grads, per_part, n_outs, terms, cols, counts, meta, tiles, *refs):
    parts = pl.num_programs(0)
    grads, outs = refs[:n_grads], refs[n_grads : n_grads + n_outs]
    total, grad, stage, in_sems, out_sems = refs[n_grads + n_outs :]
    t = pl.program_id(0)
    per_step, slots, tile_size, _ = tiles.shape
    width = grad.shape[1]
    rows = stage.shape[1]

    @pl.when(t == 0)
    def _():
        copies, start = [], 0
        for g, ref in enumerate(grads):
            copies.append(pltpu.make_async_copy(ref, grad.at[pl.ds(start, ref.shape[0])], in_sems.at[g]))
            copies[-1].start()
            start += ref.shape[0]

        @pl.loop(0, total.shape[0] // tile_size, unroll=8)
        def _(i):
            total[aligned(i * tile_size, tile_size, tile_size), :] = jnp.zeros((tile_size, width), F32)

        for copy in copies:
            copy.wait()

    for i in range(per_step):
        b = lax.rem(meta[0] + t, parts) * per_part + i
        block = grad[aligned((t * per_step + i) * tile_size, tile_size, tile_size), :]
        part = lax.dot_general(
            masked_tiles(tiles, i, counts[b]), block, (((0,), (0,)), ((), ())), preferred_element_type=F32
        )
        for k in range(slots):
            total[aligned(cols[b, k] * tile_size, tile_size, tile_size), :] += part[k * tile_size : (k + 1) * tile_size]

    @pl.when(t == parts - 1)
    def _():
        copies = []
        for o, (out, at) in enumerate(terms):
            slot = o % 2
            if o >= 2:
                copies[o - 2].wait()

            @pl.loop(0, rows // tile_size, unroll=4)
            def _(i):
                start = aligned(meta[1 + o] + i * tile_size, tile_size, tile_size)
                stage[slot, aligned(i * tile_size, tile_size, tile_size), :] = total[start, :].astype(BF16)

            copies.append(
                pltpu.make_async_copy(stage.at[slot], outs[out].at[pl.ds(at * rows, rows)], out_sems.at[o])
            )
            copies[o].start()
        for copy in copies[-2:]:
            copy.wait()


def spmm_t(tiles, columns, counts, meta, grads, parts, held, rows, total_rows):
    blocks, slots, tile_size, _ = tiles.shape
    width = grads[0].shape[1]
    per_part = blocks // parts
    flat = [(out, at) for out, many in enumerate(held) for at in range(many)]
    return pl.pallas_call(
        functools.partial(spmm_t_kernel, len(grads), per_part, len(held), flat),
        grid_spec=pltpu.PrefetchScalarGridSpec(
            num_scalar_prefetch=3,
            grid=(parts,),
            in_specs=[step_spec(blocks, slots, tile_size, parts, per_part, 0)] + [any_spec()] * len(grads),
            out_specs=[any_spec()] * len(held),
            scratch_shapes=[
                pltpu.VMEM((total_rows, width), F32),
                pltpu.VMEM((rows, width), BF16),
                pltpu.VMEM((2, rows, width), BF16),
                pltpu.SemaphoreType.DMA((len(grads),)),
                pltpu.SemaphoreType.DMA((len(flat),)),
            ],
        ),
        out_shape=[jax.ShapeDtypeStruct((many * rows, width), BF16) for many in held],
        compiler_params=params(),
        cost_estimate=pl.CostEstimate(
            flops=2 * blocks * slots * tile_size * tile_size * width,
            bytes_accessed=2 * (tiles.size + total_rows * width),
            transcendentals=0,
        ),
        name="spmm_t",
    )(columns, counts, meta, tiles, *grads)


def dense_kernel(parts, chunks, n_earlier, meta, *refs):
    n_mixed = parts * chunks
    mixed_refs, cot_refs, w_hbm = refs[:n_mixed], refs[n_mixed : n_mixed + parts], refs[n_mixed + parts]
    outs = refs[n_mixed + parts + 1 + n_earlier :]
    act_outs, mg_outs = outs[:parts], outs[parts : parts + n_mixed]
    mixed_out, grad_out, weight, sems = outs[parts + n_mixed :]
    f_wide, h_wide = weight.shape[0] // parts, weight.shape[1] // parts
    width = f_wide // chunks
    me = meta[0]

    def place(u):
        return lax.rem(me + u, parts)

    @pl.when(pl.program_id(0) == 0)
    def _():
        copies = []
        for i in range(parts):
            src = w_hbm.at[aligned(place(i) * f_wide, f_wide, f_wide)]
            copies.append(pltpu.make_async_copy(src, weight.at[pl.ds(i * f_wide, f_wide)], sems.at[i]))
            copies[-1].start()
        for copy in copies:
            copy.wait()

    mixed = jnp.concatenate([ref[...] for ref in mixed_refs], axis=1)
    for u in range(parts):
        at = pl.ds(pl.multiple_of(place(u) * f_wide, f_wide), f_wide)
        mixed_out[:, at] = mixed[:, u * f_wide : (u + 1) * f_wide]
    grads = []
    for u in range(parts):
        preact = jnp.dot(mixed, weight[:, u * h_wide : (u + 1) * h_wide], preferred_element_type=F32)
        sig = jax.nn.sigmoid(preact)
        act_outs[u][...] = (preact * sig).astype(BF16)
        grads.append((cot_refs[u][...].astype(F32) * sig * (1.0 + preact * (1.0 - sig))).astype(BF16))
        at = pl.ds(pl.multiple_of(place(u) * h_wide, h_wide), h_wide)
        grad_out[:, at] = grads[u]
    grad = jnp.concatenate(grads, axis=1)
    back = lax.dot_general(grad, weight[...], (((1,), (1,)), ((), ())), preferred_element_type=F32).astype(BF16)
    for i in range(n_mixed):
        mg_outs[i][...] = back[:, i * width : (i + 1) * width]


def dense(meta, mixed, cot, weight, rows, first, earlier):
    parts, chunks = len(mixed), len(mixed[0])
    width = mixed[0][0][0].shape[1]
    features, hidden = weight.shape
    h_wide = hidden // parts
    all_rows = cot[0].shape[0]
    step = min(rows, 256)
    flat = [m for row in mixed for m in row]
    earlier = list(earlier)

    def spec(w, start=0):
        return pl.BlockSpec((step, w), lambda t, meta: (t + start // step, 0))

    kinds = [(h_wide, True)] * parts + [(width, c > 0) for _ in range(parts) for c in range(chunks)]
    kinds += [(features, True), (hidden, True)]
    whole_at = [i for i, (_, whole) in enumerate(kinds) if whole]
    n_inputs = 1 + len(flat) + parts + 1
    outs = pl.pallas_call(
        functools.partial(dense_kernel, parts, chunks, len(earlier)),
        grid_spec=pltpu.PrefetchScalarGridSpec(
            num_scalar_prefetch=1,
            grid=(rows // step,),
            in_specs=[spec(width, at) for _, at in flat]
            + [spec(h_wide, first)] * parts
            + [any_spec()]
            + [any_spec()] * len(earlier),
            out_specs=[spec(w, first if whole else 0) for w, whole in kinds],
            scratch_shapes=[pltpu.VMEM((features, hidden), BF16), pltpu.SemaphoreType.DMA((parts,))],
        ),
        out_shape=[jax.ShapeDtypeStruct((all_rows if whole else rows, w), BF16) for w, whole in kinds],
        input_output_aliases={n_inputs + i: at for i, at in enumerate(whole_at)} if earlier else {},
        compiler_params=params(),
        cost_estimate=pl.CostEstimate(
            flops=4 * rows * features * hidden,
            bytes_accessed=2 * (features * hidden + 6 * rows * hidden),
            transcendentals=rows * hidden,
        ),
        name="dense",
    )(meta, *[m for m, _ in flat], *cot, weight, *earlier)
    n = parts * chunks
    act, back = outs[:parts], outs[parts : parts + n]
    return (
        act,
        [back[u * chunks : (u + 1) * chunks] for u in range(parts)],
        outs[-2],
        outs[-1],
        [outs[i] for i in whole_at],
    )


def total_of(*values):
    return functools.reduce(lambda a, b: a + b, [v.astype(F32) for v in values]).astype(BF16)


def step_kernel(low_blocks, own_up, got_up, up, own_down, got_down, down, to_up, to_down):
    low = pl.program_id(0) < low_blocks

    def put(out, own, got, more, with_more):
        both = own[...].astype(F32) + got[...].astype(F32)

        @pl.when(with_more)
        def _():
            out[...] = (both + more[...].astype(F32)).astype(BF16)

        @pl.when(jnp.logical_not(with_more))
        def _():
            out[...] = both.astype(BF16)

    put(to_up, own_up, got_up, up, low)
    put(to_down, own_down, got_down, down, jnp.logical_not(low))


def step_sums(own_up, at_up, up, own_down, at_down, down, got):
    rows, width = own_up.shape
    step = min(rows // 2, 1024)
    blocks = rows // step
    low = blocks // 2

    def spec(index):
        return pl.BlockSpec((step, width), lambda t: (index(t), 0))

    here = spec(lambda t: t)
    return pl.pallas_call(
        functools.partial(step_kernel, low),
        grid=(blocks,),
        in_specs=[
            here,
            spec(lambda t: t + at_up * blocks),
            spec(lambda t: jnp.minimum(t, low - 1)),
            here,
            spec(lambda t: t + at_down * blocks),
            spec(lambda t: jnp.maximum(t - low, 0)),
        ],
        out_specs=[here, here],
        out_shape=[jax.ShapeDtypeStruct((rows, width), BF16)] * 2,
        compiler_params=params(),
        cost_estimate=pl.CostEstimate(flops=4 * rows * width, bytes_accessed=14 * rows * width, transcendentals=0),
        name="step_sums",
    )(own_up, got, up, own_down, got, down)


def result_kernel(n_ready, *refs):
    ready, (own, got, up, down, out) = refs[:n_ready], refs[n_ready:]
    width = own.shape[1]
    for c, ref in enumerate(ready):
        out[:, c * width : (c + 1) * width] = ref[...]
    out[:, n_ready * width :] = (
        own[...].astype(F32) + got[...].astype(F32) + up[...].astype(F32) + down[...].astype(F32)
    ).astype(BF16)


def result_of(ready, own, got, at, up, down):
    rows, width = own.shape
    step = min(rows // 2, 1024)
    blocks = rows // step
    here = pl.BlockSpec((step, width), lambda t: (t, 0))
    there = pl.BlockSpec((step, width), lambda t: (t + at * blocks, 0))
    wide = width * (len(ready) + 1)
    return pl.pallas_call(
        functools.partial(result_kernel, len(ready)),
        grid=(blocks,),
        in_specs=[here] * (len(ready) + 1) + [there, here, here],
        out_specs=pl.BlockSpec((step, wide), lambda t: (t, 0)),
        out_shape=jax.ShapeDtypeStruct((rows, wide), BF16),
        compiler_params=params(),
        cost_estimate=pl.CostEstimate(flops=4 * rows * width, bytes_accessed=14 * rows * width, transcendentals=0),
        name="feature_grad",
    )(*ready, own, got, up, down)


def halves_kernel(low_blocks, own_far, got_far, own_up, got_up, own_down, got_down, to_up, to_down):
    low = pl.program_id(0) < low_blocks

    def put(out, own, got):
        out[...] = (own[...].astype(F32) + got[...].astype(F32)).astype(BF16)

    @pl.when(low)
    def _():
        put(to_up, own_far, got_far)
        put(to_down, own_down, got_down)

    @pl.when(jnp.logical_not(low))
    def _():
        put(to_up, own_up, got_up)
        put(to_down, own_far, got_far)


def halves_sums(own_far, got_far, own_up, at_up, own_down, at_down, got):
    rows, width = own_far.shape
    step = min(rows // 2, 1024)
    blocks = rows // step
    low = blocks // 2

    def spec(index):
        return pl.BlockSpec((step, width), lambda t: (index(t), 0))

    here = spec(lambda t: t)
    return pl.pallas_call(
        functools.partial(halves_kernel, low),
        grid=(blocks,),
        in_specs=[
            here,
            here,
            spec(lambda t: jnp.maximum(t, low)),
            spec(lambda t: jnp.maximum(t, low) + at_up * blocks),
            spec(lambda t: jnp.minimum(t, low - 1)),
            spec(lambda t: jnp.minimum(t, low - 1) + at_down * blocks),
        ],
        out_specs=[here, here],
        out_shape=[jax.ShapeDtypeStruct((rows, width), BF16)] * 2,
        compiler_params=params(),
        cost_estimate=pl.CostEstimate(flops=2 * rows * width, bytes_accessed=12 * rows * width, transcendentals=0),
        name="halves_sums",
    )(own_far, got_far, own_up, got, own_down, got)


def joined_kernel(low_blocks, own, got, up_low, up_high, down_low, down_high, out):
    low = pl.program_id(0) < low_blocks

    def put(up, down):
        total = own[...].astype(F32) + got[...].astype(F32) + up[...].astype(F32) + down[...].astype(F32)
        out[...] = total.astype(BF16)

    @pl.when(low)
    def _():
        put(up_low, down_low)

    @pl.when(jnp.logical_not(low))
    def _():
        put(up_high, down_high)


def joined(own, got, at, up_low, up, down, down_high):
    rows, width = own.shape
    step = min(rows // 2, 1024)
    blocks = rows // step
    low = blocks // 2

    def spec(index):
        return pl.BlockSpec((step, width), lambda t: (index(t), 0))

    return pl.pallas_call(
        functools.partial(joined_kernel, low),
        grid=(blocks,),
        in_specs=[
            spec(lambda t: t),
            spec(lambda t: t + at * blocks),
            spec(lambda t: jnp.minimum(t, low - 1)),
            spec(lambda t: jnp.maximum(t, low)),
            spec(lambda t: jnp.minimum(t, low - 1)),
            spec(lambda t: jnp.maximum(t - low, 0)),
        ],
        out_specs=spec(lambda t: t),
        out_shape=jax.ShapeDtypeStruct((rows, width), BF16),
        compiler_params=params(),
        cost_estimate=pl.CostEstimate(flops=3 * rows * width, bytes_accessed=10 * rows * width, transcendentals=0),
        name="joined",
    )(own, got, up_low, up, down, down_high)


class Reduction:
    def __init__(self, ring, own_far, own_near, other_far, other_near):
        self.ring, self.middle = ring, ring.chips // 2
        self.near = [o for o in range(ring.chips) if o != self.middle]
        self.own_far, self.own_near, self.other_far, self.other_near = own_far, own_near, other_far, other_near
        self.rows = own_far.shape[0]

    def far_swap(self):
        return self.ring.sibling(self.other_far)

    def near_swap(self, after):
        return self.ring.sibling(lax.optimization_barrier((self.other_near, after))[0])

    def far_sums(self, got):
        half = self.rows // 2
        return [total_of(self.own_far[at : at + half], got[at : at + half]) for at in (0, half)]

    def hops(self, up, down):
        return self.ring.hop(up, 1), self.ring.hop(down, -1)

    def place(self, offset):
        return self.near.index(offset % self.ring.chips)

    def near_terms(self, offset, got):
        at = self.place(offset)
        return self.own_near[at], got[at * self.rows : (at + 1) * self.rows]

    def sums(self, step, got, up, down, kernel):
        if step < self.middle - 1:
            return total_of(*self.near_terms(step, got), up), total_of(*self.near_terms(-step, got), down)
        at_up, at_down = self.place(step), self.place(-step)
        if kernel:
            return step_sums(self.own_near[at_up], at_up, up, self.own_near[at_down], at_down, down, got)
        zeros = jnp.zeros_like(up)
        return (
            total_of(*self.near_terms(step, got), jnp.concatenate([up, zeros])),
            total_of(*self.near_terms(-step, got), jnp.concatenate([zeros, down])),
        )

    def halves(self, got_far, got):
        at_up, at_down = self.place(1), self.place(-1)
        return halves_sums(self.own_far, got_far, self.own_near[at_up], at_up, self.own_near[at_down], at_down, got)

    def other_halves(self, got, up, down):
        half = self.rows // 2
        (own_up, got_up), (own_down, got_down) = self.near_terms(1, got), self.near_terms(-1, got)
        return total_of(own_up[:half], got_up[:half], up[:half]), total_of(own_down[half:], got_down[half:], down[half:])

    def last(self, up, down):
        if self.middle > 1:
            return up, down
        return jnp.concatenate([up, jnp.zeros_like(up)]), jnp.concatenate([jnp.zeros_like(down), down])


def local(features, tiles, columns, counts, weight, cotangent):
    rows, f_wide = features.shape
    h_wide = cotangent.shape[1]
    row_size, parts = lax.axis_size("row"), lax.axis_size("rep")
    ring = Ring(row_size)
    rep = lax.axis_index("rep")
    chunks = f_wide // LANES if f_wide % LANES == 0 else 1
    width = f_wide // chunks
    half = rows // 2
    part_rows = rows // parts
    halves = 2
    half_rows = part_rows // halves
    middle = ring.chips // 2
    near = [o for o in range(ring.chips) if o != middle]
    ends, inner = shift_groups(parts)
    last = chunks - 1
    w = Waves()

    offsets = [(0, 0)] + [(o, 0) for step in range(1, middle) for o in (-step, step)] + [(middle, 0), (middle, half)]
    own_meta = [ring.device_at(o, False) * rows + at for o, at in offsets]
    other_meta = [ring.device_at(o, True) * rows + at for o, at in offsets]
    spmm_meta = jnp.stack([rep] + own_meta + other_meta).astype(jnp.int32)
    held = [1] + [1] * len(near) + [1, len(near)]
    order = [middle] + near
    terms_at = [ring.device_at(o, other) * rows for other in (False, True) for o in order]
    spmm_t_meta = jnp.stack([rep] + terms_at).astype(jnp.int32)
    dense_meta = rep[None].astype(jnp.int32)

    def part_of(x, u):
        return lax.dynamic_slice_in_dim(x, lax.rem(rep + u, parts) * part_rows, part_rows, 0)

    share = weight.shape[0] // row_size
    w_share = lax.dynamic_slice_in_dim(weight, lax.axis_index("row") * share, share, 0)

    cot_blocks = [part_of(cotangent, u) for u in range(parts)]
    xs = [features[:, c * width : (c + 1) * width] for c in range(chunks)]
    up = down = xs[0]
    got_own = {}
    got_other = {}
    mixed = {}

    def run_spmm(c, cut, skip):
        own = [got_own[c, i] for i in range(len(offsets))]
        other = [got_other[c, i] for i in range(len(offsets))]
        return spmm(tiles, columns, counts, spmm_meta, own + other, parts, cut, skip)

    cot_ends = send(cot_blocks, ends)
    own_other = ring.sibling(features)
    for c in range(chunks):
        got_own[c, 0] = xs[c]
        got_other[c, 0] = own_other[:, c * width : (c + 1) * width]
        for step in range(1, middle):
            name = f"{c}_{step}"
            w.go(**{"up" + name: ring.hop(up, 1), "down" + name: ring.hop(down, -1)})
            if c and step == 1:
                for i in range(1, len(offsets)):
                    got_other[c - 1, i] = ring.sibling(got_own[c - 1, i])
                w.go(**{f"mixed{c - 1}": run_spmm(c - 1, 1, 0)})
            if c == 0 and step == 1:
                w.go(metas=(spmm_meta, spmm_t_meta, dense_meta))
            w.close()
            up, down = w["up" + name], w["down" + name]
            got_own[c, 2 * step - 1], got_own[c, 2 * step] = up, down
        w.go(**{f"far_up{c}": ring.hop(up[:half], 1), f"far_down{c}": ring.hop(down[half:], -1)})
        if c == 0:
            w.go(cot_ends=cot_ends, own_other=own_other)
        seen = []
        if c == last:
            for step in range(1, middle):
                for i in (2 * step - 1, 2 * step):
                    got_other[c, i] = ring.sibling(got_own[c, i])
                    w.go(**{f"other{c}_{i}": got_other[c, i]})
                    seen.append(got_other[c, i])
        if c:
            mixed[c - 1] = w[f"mixed{c - 1}"]
            ready = [lax.optimization_barrier((b, *seen))[0] for b in mixed[c - 1]]
            w.go(**{f"mixed_ends{c - 1}": send(ready, ends)})
        w.close()
        if c == 0:
            spmm_meta, spmm_t_meta, dense_meta = w["metas"]
            w.go(cot_inner=send([w.gate(b) for b in cot_blocks], inner))
            w.go(shares=send([w.gate(w_share)] * parts, ends + inner))
        else:
            w.go(**{f"mixed_inner{c - 1}": send([w.gate(b) for b in mixed[c - 1]], inner)})
        got_own[c, len(offsets) - 2], got_own[c, len(offsets) - 1] = w[f"far_up{c}"], w[f"far_down{c}"]
        if c < last:
            up = down = w.gate(xs[c + 1])
    w_rows = jnp.concatenate(ordered(w_share, {**w.done, **w.pending}["shares"]), axis=1)
    w_full = lax.all_gather(w.gate(w_rows), "row", axis=0, tiled=True)
    for i in (-2, -1):
        got_other[last, len(offsets) + i] = ring.sibling(got_own[last, len(offsets) + i])

    for h in range(halves):
        w.go(**{f"half{h}": run_spmm(last, halves, h)})
        w.close()
        w.go(**{f"half_got{h}": send(w[f"half{h}"], ends + inner)})

    cot = ordered(cot_blocks[0], w["cot_ends"], w["cot_inner"])
    whole = [ordered(mixed[c][0], w[f"mixed_ends{c}"], w[f"mixed_inner{c}"]) for c in range(last)]
    earlier = ()
    for h in range(halves):
        part = ordered(w[f"half{h}"][0], w[f"half_got{h}"])
        blocks = [[(whole[c][u], h * half_rows) for c in range(last)] + [(part[u], 0)] for u in range(parts)]
        act, back, mixed_rows, grad_rows, earlier = dense(
            dense_meta, blocks, cot, w_full, half_rows, h * half_rows, earlier
        )
        w.go(**{f"back{h}": [b[0] for b in back]})
        if h == halves - 1:
            w.go(whole=(act, back, mixed_rows, grad_rows))
        w.close()
        w.go(**{f"back_got{h}": send(w[f"back{h}"], ends + inner)})
    act, back, mixed_rows, grad_rows = w["whole"]
    sums = lax.dot_general(grad_rows, mixed_rows, (((0,), (0,)), ((), ())), preferred_element_type=F32).astype(BF16)
    share = sums.shape[0] // row_size

    def sums_for(offset, other):
        return lax.dynamic_slice_in_dim(sums, ring.device_at(offset, other) * share, share, 0)

    wg = Reduction(
        ring,
        sums_for(middle, False),
        [sums_for(o, False) for o in near],
        sums_for(middle, True),
        jnp.concatenate([sums_for(o, True) for o in near]),
    )
    wg_far = wg.far_swap()
    w.go(wg_own=(wg.own_far, wg.own_near), wg_far=wg_far, wg_near=wg.near_swap(wg_far))
    w.close()
    wg.own_far, wg.own_near = w["wg_own"]
    w.go(wg_up_down=wg.hops(*wg.far_sums(w["wg_far"])))

    def run_spmm_t(c, grads):
        return spmm_t(tiles, columns, counts, spmm_t_meta, grads, parts, held, rows, rows * row_size)

    parts_got = [ordered(w[f"back{h}"][0], w[f"back_got{h}"]) for h in range(halves)]
    w.go(terms0=run_spmm_t(0, [parts_got[h][u] for u in range(parts) for h in range(halves)]))
    for c in range(1, chunks):
        w.go(**{f"rest_got{c}": send([w.gate(b[c]) for b in back], ends + inner)})
    w.close()

    def wg_steps(first, until):
        up, down = w["wg_up_down"]
        for step in range(first, until, -1):
            up, down = wg.hops(*wg.sums(step, w["wg_near"], up, down, False))
        return up, down

    def send_act(shifts):
        return send([w.gate(a) for a in act], shifts)

    reductions = []
    for c in range(chunks):
        terms = w[f"terms{c}"]
        red = Reduction(ring, terms[0], terms[1:-2], terms[-2], terms[-1])
        reductions.append(red)
        combined = c < last and middle == 2
        got_far = red.far_swap()
        got_near = red.near_swap(got_far)
        if c == last and c:
            got_near, cuts = lax.optimization_barrier((got_near, cuts))
            w.go(cuts_got=send(cuts, ends + inner))
        sums = red.halves(got_far, got_near) if combined else red.far_sums(got_far)
        if c == 0:
            sums, wg_last = lax.optimization_barrier((sums, wg_steps(middle - 1, 0)))
        w.go(**{f"got_near{c}": got_near})
        if c < last:
            grads = ordered(back[0][c + 1], w[f"rest_got{c + 1}"])
            grads, sums = lax.optimization_barrier((grads, sums))
            w.go(**{f"terms{c + 1}": run_spmm_t(c + 1, grads)})
        w.go(**{f"sum{c}_{middle}": red.hops(*sums)})
        if c == 0:
            w.go(act_inner=send_act(inner))
        w.close()
        if c == 0:
            block = total_of(*wg.near_terms(0, w["wg_near"]), *wg.last(*wg_last))
            cuts = [
                w.gate(lax.dynamic_slice_in_dim(block, lax.rem(rep + u, parts) * f_wide, f_wide, 1))
                for u in range(parts)
            ]
        if combined:
            w.go(**{f"sum{c}_1": red.hops(*red.other_halves(w[f"got_near{c}"], *w[f"sum{c}_{middle}"]))})
            continue
        for step in range(middle - 1, 0, -1):
            to_up, to_down = red.sums(step, w[f"got_near{c}"], *w[f"sum{c}_{step + 1}"], True)
            if step == 1 and c == last:
                act, to_up, to_down = lax.optimization_barrier((act, to_up, to_down))
            w.go(**{f"sum{c}_{step}": red.hops(to_up, to_down)})
            if step > 1:
                w.close()
    w.go(act_ends=send(act, ends))
    if last == 0:
        w.go(cuts_got=send(cuts, ends + inner))
    got = {**w.done, **w.pending}
    cuts_got = got["cuts_got"]
    got["weight_grad"] = functools.reduce(lambda a, b: a + b, [v.astype(F32) for v in [cuts[0], *cuts_got.values()]])
    ready = []
    at = near.index(0)
    for c, red in enumerate(reductions[:-1]):
        up, down = got[f"sum{c}_1"]
        if middle == 2:
            whole_up, whole_down = got[f"sum{c}_2"]
            ready.append(joined(red.own_near[at], got[f"got_near{c}"], at, up, whole_up, whole_down, down))
        else:
            ready.append(total_of(*red.near_terms(0, got[f"got_near{c}"]), *red.last(up, down)))
    red = reductions[-1]
    feature_grad = result_of(ready, red.own_near[at], got[f"got_near{last}"], at, *red.last(*got[f"sum{last}_1"]))
    weight_grad = got["weight_grad"].T
    act = ordered(act[0], got["act_ends"], got["act_inner"])
    activations = jnp.zeros((rows, h_wide), BF16)
    for u in range(parts):
        activations = lax.dynamic_update_slice_in_dim(activations, act[u], lax.rem(rep + u, parts) * part_rows, 0)
    return (activations, feature_grad, weight_grad)


def solution(mesh):
    in_specs = (
        P("row", "rep"),
        P("row", None, None, None),
        P("row", None),
        P("row"),
        P(None, "rep"),
        P("row", "rep"),
    )
    out_specs = (P("row", "rep"), P("row", "rep"), P("rep", "row"))
    return jax.shard_map(local, mesh=mesh, in_specs=in_specs, out_specs=out_specs, check_vma=False)
```

```python
import functools
import jax
import jax.numpy as jnp
from jax import lax
from jax.experimental import pallas as pl
from jax.experimental.pallas import tpu as pltpu
from jax.sharding import PartitionSpec as P

BF16, F32 = jnp.bfloat16, jnp.float32
VMEM_LIMIT = 56 * 1024 * 1024
LANES = 128
CORES = 2


def params():
    return pltpu.CompilerParams(vmem_limit_bytes=VMEM_LIMIT)


def any_spec():
    return pl.BlockSpec(memory_space=pl.ANY)


class Ring:
    def __init__(self, devices):
        self.chips = devices // CORES
        half = self.chips // 2
        self.order = list(range(half)) + list(range(self.chips - 1, half - 1, -1))
        self.devices = devices

    def perm(self, step):
        pairs = []
        for place, chip in enumerate(self.order):
            to = self.order[(place + step) % self.chips]
            pairs += [(chip * CORES + core, to * CORES + core) for core in range(CORES)]
        return pairs

    def hop(self, value, step):
        return lax.ppermute(value, "row", self.perm(step))

    def sibling(self, value):
        return lax.ppermute(value, "row", [(d, d ^ 1) for d in range(self.devices)])

    def device_at(self, offset, other_core):
        me = lax.axis_index("row")
        order = jnp.array(self.order, jnp.int32)
        place_of = jnp.array([self.order.index(c) for c in range(self.chips)], jnp.int32)
        chip = order[(place_of[me // CORES] + offset) % self.chips]
        core = me % CORES
        return chip * CORES + (1 - core if other_core else core)


class Waves:
    def __init__(self):
        self.pending = {}
        self.done = {}
        self.token = None

    def go(self, **values):
        assert not set(values) & (set(self.pending) | set(self.done))
        self.pending.update(values)

    def close(self):
        names, values = list(self.pending), list(self.pending.values())
        flat, tree = jax.tree.flatten(values)
        flat = lax.optimization_barrier(flat)
        self.token = flat[0]
        self.done.update(zip(names, jax.tree.unflatten(tree, flat)))
        self.pending = {}

    def gate(self, value):
        if self.token is None:
            return value
        return lax.optimization_barrier((value, self.token))[0]

    def __getitem__(self, name):
        return self.done[name]


def shift_groups(size):
    ends = sorted({1, size - 1})
    return ends, [s for s in range(2, size - 1)]


def send(blocks, shifts):
    size = len(blocks)
    return {
        (size - s) % size: lax.ppermute(blocks[s], "rep", [(i, (i + s) % size) for i in range(size)]) for s in shifts
    }


def ordered(own, *groups):
    got = {0: own}
    for group in groups:
        got.update(group)
    return [got[u] for u in range(len(got))]


def masked_tiles(tiles, i, count):
    found = []
    for k in range(tiles.shape[1]):
        tile = tiles[i, k]
        found.append(jnp.where(k < count, tile, jnp.zeros_like(tile)))
    return jnp.concatenate(found, axis=1)


def step_spec(blocks, slots, tile_size, parts, per_step, skip):
    def index(t, cols, cnt, meta):
        return (lax.rem(meta[0] + t, parts) * (blocks // parts // per_step) + skip, 0, 0, 0)

    return pl.BlockSpec((per_step, slots, tile_size, tile_size), index)


def aligned(start, size, unit):
    return pl.ds(pl.multiple_of(start, unit), size)


def spmm_kernel(n_pieces, per_part, skip, cols, counts, meta, tiles, *refs):
    parts = pl.num_programs(0)
    n_outs = len(refs) - n_pieces - 3
    pieces, outs = refs[:n_pieces], refs[n_pieces : n_pieces + n_outs]
    source, result, sems = refs[n_pieces + n_outs :]
    t = pl.program_id(0)
    per_step, slots, tile_size, _ = tiles.shape

    @pl.when(t == 0)
    def _():
        copies = []
        for p, piece in enumerate(pieces):
            copies.append(
                pltpu.make_async_copy(piece, source.at[aligned(meta[1 + p], piece.shape[0], tile_size)], sems.at[p])
            )
            copies[-1].start()
        for copy in copies:
            copy.wait()

    for i in range(per_step):
        b = lax.rem(meta[0] + t, parts) * per_part + skip * per_step + i
        right = [source[aligned(cols[b, k] * tile_size, tile_size, tile_size), :] for k in range(slots)]
        product = jnp.dot(
            masked_tiles(tiles, i, counts[b]), jnp.concatenate(right, axis=0), preferred_element_type=F32
        )
        result[i * tile_size : (i + 1) * tile_size, :] = product.astype(BF16)

    for u in range(n_outs):

        @pl.when(t == u)
        def _():
            outs[u][...] = result[...]


def spmm(tiles, columns, counts, meta, pieces, parts, cut, skip):
    blocks, slots, tile_size, _ = tiles.shape
    width = pieces[0].shape[1]
    total_rows = sum(v.shape[0] for v in pieces)
    per_part = blocks // parts
    per_step = per_part // cut
    rows = per_step * tile_size
    return pl.pallas_call(
        functools.partial(spmm_kernel, len(pieces), per_part, skip),
        grid_spec=pltpu.PrefetchScalarGridSpec(
            num_scalar_prefetch=3,
            grid=(parts,),
            in_specs=[step_spec(blocks, slots, tile_size, parts, per_step, skip)] + [any_spec()] * len(pieces),
            out_specs=[pl.BlockSpec((rows, width), lambda t, cols, cnt, meta: (0, 0))] * parts,
            scratch_shapes=[
                pltpu.VMEM((total_rows, width), BF16),
                pltpu.VMEM((rows, width), BF16),
                pltpu.SemaphoreType.DMA((len(pieces),)),
            ],
        ),
        out_shape=[jax.ShapeDtypeStruct((rows, width), BF16)] * parts,
        compiler_params=params(),
        cost_estimate=pl.CostEstimate(
            flops=2 * parts * rows * slots * tile_size * width,
            bytes_accessed=2 * (tiles.size // cut + total_rows * width),
            transcendentals=0,
        ),
        name="spmm",
    )(columns, counts, meta, tiles, *pieces)


def spmm_t_kernel(n_grads, per_part, n_outs, terms, cols, counts, meta, tiles, *refs):
    parts = pl.num_programs(0)
    grads, outs = refs[:n_grads], refs[n_grads : n_grads + n_outs]
    total, grad, stage, in_sems, out_sems = refs[n_grads + n_outs :]
    t = pl.program_id(0)
    per_step, slots, tile_size, _ = tiles.shape
    width = grad.shape[1]
    rows = stage.shape[1]

    @pl.when(t == 0)
    def _():
        copies, start = [], 0
        for g, ref in enumerate(grads):
            copies.append(pltpu.make_async_copy(ref, grad.at[pl.ds(start, ref.shape[0])], in_sems.at[g]))
            copies[-1].start()
            start += ref.shape[0]

        @pl.loop(0, total.shape[0] // tile_size, unroll=8)
        def _(i):
            total[aligned(i * tile_size, tile_size, tile_size), :] = jnp.zeros((tile_size, width), F32)

        for copy in copies:
            copy.wait()

    for i in range(per_step):
        b = lax.rem(meta[0] + t, parts) * per_part + i
        block = grad[aligned((t * per_step + i) * tile_size, tile_size, tile_size), :]
        part = lax.dot_general(
            masked_tiles(tiles, i, counts[b]), block, (((0,), (0,)), ((), ())), preferred_element_type=F32
        )
        for k in range(slots):
            total[aligned(cols[b, k] * tile_size, tile_size, tile_size), :] += part[k * tile_size : (k + 1) * tile_size]

    @pl.when(t == parts - 1)
    def _():
        copies = []
        for o, (out, at) in enumerate(terms):
            slot = o % 2
            if o >= 2:
                copies[o - 2].wait()

            @pl.loop(0, rows // tile_size, unroll=4)
            def _(i):
                start = aligned(meta[1 + o] + i * tile_size, tile_size, tile_size)
                stage[slot, aligned(i * tile_size, tile_size, tile_size), :] = total[start, :].astype(BF16)

            copies.append(
                pltpu.make_async_copy(stage.at[slot], outs[out].at[pl.ds(at * rows, rows)], out_sems.at[o])
            )
            copies[o].start()
        for copy in copies[-2:]:
            copy.wait()


def spmm_t(tiles, columns, counts, meta, grads, parts, held, rows, total_rows):
    blocks, slots, tile_size, _ = tiles.shape
    width = grads[0].shape[1]
    per_part = blocks // parts
    flat = [(out, at) for out, many in enumerate(held) for at in range(many)]
    return pl.pallas_call(
        functools.partial(spmm_t_kernel, len(grads), per_part, len(held), flat),
        grid_spec=pltpu.PrefetchScalarGridSpec(
            num_scalar_prefetch=3,
            grid=(parts,),
            in_specs=[step_spec(blocks, slots, tile_size, parts, per_part, 0)] + [any_spec()] * len(grads),
            out_specs=[any_spec()] * len(held),
            scratch_shapes=[
                pltpu.VMEM((total_rows, width), F32),
                pltpu.VMEM((rows, width), BF16),
                pltpu.VMEM((2, rows, width), BF16),
                pltpu.SemaphoreType.DMA((len(grads),)),
                pltpu.SemaphoreType.DMA((len(flat),)),
            ],
        ),
        out_shape=[jax.ShapeDtypeStruct((many * rows, width), BF16) for many in held],
        compiler_params=params(),
        cost_estimate=pl.CostEstimate(
            flops=2 * blocks * slots * tile_size * tile_size * width,
            bytes_accessed=2 * (tiles.size + total_rows * width),
            transcendentals=0,
        ),
        name="spmm_t",
    )(columns, counts, meta, tiles, *grads)


def dense_kernel(parts, chunks, n_earlier, meta, *refs):
    n_mixed = parts * chunks
    mixed_refs, cot_refs, w_hbm = refs[:n_mixed], refs[n_mixed : n_mixed + parts], refs[n_mixed + parts]
    outs = refs[n_mixed + parts + 1 + n_earlier :]
    act_outs, mg_outs = outs[:parts], outs[parts : parts + n_mixed]
    mixed_out, grad_out, weight, sems = outs[parts + n_mixed :]
    f_wide, h_wide = weight.shape[0] // parts, weight.shape[1] // parts
    width = f_wide // chunks
    me = meta[0]

    def place(u):
        return lax.rem(me + u, parts)

    @pl.when(pl.program_id(0) == 0)
    def _():
        copies = []
        for i in range(parts):
            src = w_hbm.at[aligned(place(i) * f_wide, f_wide, f_wide)]
            copies.append(pltpu.make_async_copy(src, weight.at[pl.ds(i * f_wide, f_wide)], sems.at[i]))
            copies[-1].start()
        for copy in copies:
            copy.wait()

    mixed = jnp.concatenate([ref[...] for ref in mixed_refs], axis=1)
    for u in range(parts):
        at = pl.ds(pl.multiple_of(place(u) * f_wide, f_wide), f_wide)
        mixed_out[:, at] = mixed[:, u * f_wide : (u + 1) * f_wide]
    grads = []
    for u in range(parts):
        preact = jnp.dot(mixed, weight[:, u * h_wide : (u + 1) * h_wide], preferred_element_type=F32)
        sig = jax.nn.sigmoid(preact)
        act_outs[u][...] = (preact * sig).astype(BF16)
        grads.append((cot_refs[u][...].astype(F32) * sig * (1.0 + preact * (1.0 - sig))).astype(BF16))
        at = pl.ds(pl.multiple_of(place(u) * h_wide, h_wide), h_wide)
        grad_out[:, at] = grads[u]
    grad = jnp.concatenate(grads, axis=1)
    back = lax.dot_general(grad, weight[...], (((1,), (1,)), ((), ())), preferred_element_type=F32).astype(BF16)
    for i in range(n_mixed):
        mg_outs[i][...] = back[:, i * width : (i + 1) * width]


def dense(meta, mixed, cot, weight, rows, first, earlier):
    parts, chunks = len(mixed), len(mixed[0])
    width = mixed[0][0][0].shape[1]
    features, hidden = weight.shape
    h_wide = hidden // parts
    all_rows = cot[0].shape[0]
    step = min(rows, 256)
    flat = [m for row in mixed for m in row]
    earlier = list(earlier)

    def spec(w, start=0):
        return pl.BlockSpec((step, w), lambda t, meta: (t + start // step, 0))

    kinds = [(h_wide, True)] * parts + [(width, c > 0) for _ in range(parts) for c in range(chunks)]
    kinds += [(features, True), (hidden, True)]
    whole_at = [i for i, (_, whole) in enumerate(kinds) if whole]
    n_inputs = 1 + len(flat) + parts + 1
    outs = pl.pallas_call(
        functools.partial(dense_kernel, parts, chunks, len(earlier)),
        grid_spec=pltpu.PrefetchScalarGridSpec(
            num_scalar_prefetch=1,
            grid=(rows // step,),
            in_specs=[spec(width, at) for _, at in flat]
            + [spec(h_wide, first)] * parts
            + [any_spec()]
            + [any_spec()] * len(earlier),
            out_specs=[spec(w, first if whole else 0) for w, whole in kinds],
            scratch_shapes=[pltpu.VMEM((features, hidden), BF16), pltpu.SemaphoreType.DMA((parts,))],
        ),
        out_shape=[jax.ShapeDtypeStruct((all_rows if whole else rows, w), BF16) for w, whole in kinds],
        input_output_aliases={n_inputs + i: at for i, at in enumerate(whole_at)} if earlier else {},
        compiler_params=params(),
        cost_estimate=pl.CostEstimate(
            flops=4 * rows * features * hidden,
            bytes_accessed=2 * (features * hidden + 6 * rows * hidden),
            transcendentals=rows * hidden,
        ),
        name="dense",
    )(meta, *[m for m, _ in flat], *cot, weight, *earlier)
    n = parts * chunks
    act, back = outs[:parts], outs[parts : parts + n]
    return (
        act,
        [back[u * chunks : (u + 1) * chunks] for u in range(parts)],
        outs[-2],
        outs[-1],
        [outs[i] for i in whole_at],
    )


def total_of(*values):
    return functools.reduce(lambda a, b: a + b, [v.astype(F32) for v in values]).astype(BF16)


def step_kernel(low_blocks, own_up, got_up, up, own_down, got_down, down, to_up, to_down):
    low = pl.program_id(0) < low_blocks

    def put(out, own, got, more, with_more):
        both = own[...].astype(F32) + got[...].astype(F32)

        @pl.when(with_more)
        def _():
            out[...] = (both + more[...].astype(F32)).astype(BF16)

        @pl.when(jnp.logical_not(with_more))
        def _():
            out[...] = both.astype(BF16)

    put(to_up, own_up, got_up, up, low)
    put(to_down, own_down, got_down, down, jnp.logical_not(low))


def step_sums(own_up, at_up, up, own_down, at_down, down, got):
    rows, width = own_up.shape
    step = min(rows // 2, 1024)
    blocks = rows // step
    low = blocks // 2

    def spec(index):
        return pl.BlockSpec((step, width), lambda t: (index(t), 0))

    here = spec(lambda t: t)
    return pl.pallas_call(
        functools.partial(step_kernel, low),
        grid=(blocks,),
        in_specs=[
            here,
            spec(lambda t: t + at_up * blocks),
            spec(lambda t: jnp.minimum(t, low - 1)),
            here,
            spec(lambda t: t + at_down * blocks),
            spec(lambda t: jnp.maximum(t - low, 0)),
        ],
        out_specs=[here, here],
        out_shape=[jax.ShapeDtypeStruct((rows, width), BF16)] * 2,
        compiler_params=params(),
        cost_estimate=pl.CostEstimate(flops=4 * rows * width, bytes_accessed=14 * rows * width, transcendentals=0),
        name="step_sums",
    )(own_up, got, up, own_down, got, down)


def result_kernel(n_ready, *refs):
    ready, (own, got, up, down, out) = refs[:n_ready], refs[n_ready:]
    width = own.shape[1]
    for c, ref in enumerate(ready):
        out[:, c * width : (c + 1) * width] = ref[...]
    out[:, n_ready * width :] = (
        own[...].astype(F32) + got[...].astype(F32) + up[...].astype(F32) + down[...].astype(F32)
    ).astype(BF16)


def result_of(ready, own, got, at, up, down):
    rows, width = own.shape
    step = min(rows // 2, 1024)
    blocks = rows // step
    here = pl.BlockSpec((step, width), lambda t: (t, 0))
    there = pl.BlockSpec((step, width), lambda t: (t + at * blocks, 0))
    wide = width * (len(ready) + 1)
    return pl.pallas_call(
        functools.partial(result_kernel, len(ready)),
        grid=(blocks,),
        in_specs=[here] * (len(ready) + 1) + [there, here, here],
        out_specs=pl.BlockSpec((step, wide), lambda t: (t, 0)),
        out_shape=jax.ShapeDtypeStruct((rows, wide), BF16),
        compiler_params=params(),
        cost_estimate=pl.CostEstimate(flops=4 * rows * width, bytes_accessed=14 * rows * width, transcendentals=0),
        name="feature_grad",
    )(*ready, own, got, up, down)


def halves_kernel(low_blocks, own_far, got_far, own_up, got_up, own_down, got_down, to_up, to_down):
    low = pl.program_id(0) < low_blocks

    def put(out, own, got):
        out[...] = (own[...].astype(F32) + got[...].astype(F32)).astype(BF16)

    @pl.when(low)
    def _():
        put(to_up, own_far, got_far)
        put(to_down, own_down, got_down)

    @pl.when(jnp.logical_not(low))
    def _():
        put(to_up, own_up, got_up)
        put(to_down, own_far, got_far)


def halves_sums(own_far, got_far, own_up, at_up, own_down, at_down, got):
    rows, width = own_far.shape
    step = min(rows // 2, 1024)
    blocks = rows // step
    low = blocks // 2

    def spec(index):
        return pl.BlockSpec((step, width), lambda t: (index(t), 0))

    here = spec(lambda t: t)
    return pl.pallas_call(
        functools.partial(halves_kernel, low),
        grid=(blocks,),
        in_specs=[
            here,
            here,
            spec(lambda t: jnp.maximum(t, low)),
            spec(lambda t: jnp.maximum(t, low) + at_up * blocks),
            spec(lambda t: jnp.minimum(t, low - 1)),
            spec(lambda t: jnp.minimum(t, low - 1) + at_down * blocks),
        ],
        out_specs=[here, here],
        out_shape=[jax.ShapeDtypeStruct((rows, width), BF16)] * 2,
        compiler_params=params(),
        cost_estimate=pl.CostEstimate(flops=2 * rows * width, bytes_accessed=12 * rows * width, transcendentals=0),
        name="halves_sums",
    )(own_far, got_far, own_up, got, own_down, got)


def joined_kernel(low_blocks, own, got, up_low, up_high, down_low, down_high, out):
    low = pl.program_id(0) < low_blocks

    def put(up, down):
        total = own[...].astype(F32) + got[...].astype(F32) + up[...].astype(F32) + down[...].astype(F32)
        out[...] = total.astype(BF16)

    @pl.when(low)
    def _():
        put(up_low, down_low)

    @pl.when(jnp.logical_not(low))
    def _():
        put(up_high, down_high)


def joined(own, got, at, up_low, up, down, down_high):
    rows, width = own.shape
    step = min(rows // 2, 1024)
    blocks = rows // step
    low = blocks // 2

    def spec(index):
        return pl.BlockSpec((step, width), lambda t: (index(t), 0))

    return pl.pallas_call(
        functools.partial(joined_kernel, low),
        grid=(blocks,),
        in_specs=[
            spec(lambda t: t),
            spec(lambda t: t + at * blocks),
            spec(lambda t: jnp.minimum(t, low - 1)),
            spec(lambda t: jnp.maximum(t, low)),
            spec(lambda t: jnp.minimum(t, low - 1)),
            spec(lambda t: jnp.maximum(t - low, 0)),
        ],
        out_specs=spec(lambda t: t),
        out_shape=jax.ShapeDtypeStruct((rows, width), BF16),
        compiler_params=params(),
        cost_estimate=pl.CostEstimate(flops=3 * rows * width, bytes_accessed=10 * rows * width, transcendentals=0),
        name="joined",
    )(own, got, up_low, up, down, down_high)


class Reduction:
    def __init__(self, ring, own_far, own_near, other_far, other_near):
        self.ring, self.middle = ring, ring.chips // 2
        self.near = [o for o in range(ring.chips) if o != self.middle]
        self.own_far, self.own_near, self.other_far, self.other_near = own_far, own_near, other_far, other_near
        self.rows = own_far.shape[0]

    def far_swap(self):
        return self.ring.sibling(self.other_far)

    def near_swap(self, after):
        return self.ring.sibling(lax.optimization_barrier((self.other_near, after))[0])

    def far_sums(self, got):
        half = self.rows // 2
        return [total_of(self.own_far[at : at + half], got[at : at + half]) for at in (0, half)]

    def hops(self, up, down):
        return self.ring.hop(up, 1), self.ring.hop(down, -1)

    def place(self, offset):
        return self.near.index(offset % self.ring.chips)

    def near_terms(self, offset, got):
        at = self.place(offset)
        return self.own_near[at], got[at * self.rows : (at + 1) * self.rows]

    def sums(self, step, got, up, down, kernel):
        if step < self.middle - 1:
            return total_of(*self.near_terms(step, got), up), total_of(*self.near_terms(-step, got), down)
        at_up, at_down = self.place(step), self.place(-step)
        if kernel:
            return step_sums(self.own_near[at_up], at_up, up, self.own_near[at_down], at_down, down, got)
        zeros = jnp.zeros_like(up)
        return (
            total_of(*self.near_terms(step, got), jnp.concatenate([up, zeros])),
            total_of(*self.near_terms(-step, got), jnp.concatenate([zeros, down])),
        )

    def halves(self, got_far, got):
        at_up, at_down = self.place(1), self.place(-1)
        return halves_sums(self.own_far, got_far, self.own_near[at_up], at_up, self.own_near[at_down], at_down, got)

    def other_halves(self, got, up, down):
        half = self.rows // 2
        (own_up, got_up), (own_down, got_down) = self.near_terms(1, got), self.near_terms(-1, got)
        return total_of(own_up[:half], got_up[:half], up[:half]), total_of(own_down[half:], got_down[half:], down[half:])

    def last(self, up, down):
        if self.middle > 1:
            return up, down
        return jnp.concatenate([up, jnp.zeros_like(up)]), jnp.concatenate([jnp.zeros_like(down), down])


def local(features, tiles, columns, counts, weight, cotangent):
    rows, f_wide = features.shape
    h_wide = cotangent.shape[1]
    row_size, parts = lax.axis_size("row"), lax.axis_size("rep")
    ring = Ring(row_size)
    rep = lax.axis_index("rep")
    chunks = f_wide // LANES if f_wide % LANES == 0 else 1
    width = f_wide // chunks
    half = rows // 2
    part_rows = rows // parts
    halves = 2
    half_rows = part_rows // halves
    middle = ring.chips // 2
    near = [o for o in range(ring.chips) if o != middle]
    ends, inner = shift_groups(parts)
    last = chunks - 1
    w = Waves()

    offsets = [(0, 0)] + [(o, 0) for step in range(1, middle) for o in (-step, step)] + [(middle, 0), (middle, half)]
    own_meta = [ring.device_at(o, False) * rows + at for o, at in offsets]
    other_meta = [ring.device_at(o, True) * rows + at for o, at in offsets]
    spmm_meta = jnp.stack([rep] + own_meta + other_meta).astype(jnp.int32)
    held = [1] + [1] * len(near) + [1, len(near)]
    order = [middle] + near
    terms_at = [ring.device_at(o, other) * rows for other in (False, True) for o in order]
    spmm_t_meta = jnp.stack([rep] + terms_at).astype(jnp.int32)
    dense_meta = rep[None].astype(jnp.int32)

    def part_of(x, u):
        return lax.dynamic_slice_in_dim(x, lax.rem(rep + u, parts) * part_rows, part_rows, 0)

    share = weight.shape[0] // row_size
    w_share = lax.dynamic_slice_in_dim(weight, lax.axis_index("row") * share, share, 0)

    cot_blocks = [part_of(cotangent, u) for u in range(parts)]
    xs = [features[:, c * width : (c + 1) * width] for c in range(chunks)]
    up = down = xs[0]
    got_own = {}
    got_other = {}
    mixed = {}

    def run_spmm(c, cut, skip):
        own = [got_own[c, i] for i in range(len(offsets))]
        other = [got_other[c, i] for i in range(len(offsets))]
        return spmm(tiles, columns, counts, spmm_meta, own + other, parts, cut, skip)

    cot_ends = send(cot_blocks, ends)
    own_other = ring.sibling(features)
    for c in range(chunks):
        got_own[c, 0] = xs[c]
        got_other[c, 0] = own_other[:, c * width : (c + 1) * width]
        for step in range(1, middle):
            name = f"{c}_{step}"
            w.go(**{"up" + name: ring.hop(up, 1), "down" + name: ring.hop(down, -1)})
            if c and step == 1:
                for i in range(1, len(offsets)):
                    got_other[c - 1, i] = ring.sibling(got_own[c - 1, i])
                w.go(**{f"mixed{c - 1}": run_spmm(c - 1, 1, 0)})
            if c == 0 and step == 1:
                w.go(metas=(spmm_meta, spmm_t_meta, dense_meta))
            w.close()
            up, down = w["up" + name], w["down" + name]
            got_own[c, 2 * step - 1], got_own[c, 2 * step] = up, down
        w.go(**{f"far_up{c}": ring.hop(up[:half], 1), f"far_down{c}": ring.hop(down[half:], -1)})
        if c == 0:
            w.go(cot_ends=cot_ends, own_other=own_other)
        seen = []
        if c == last:
            for step in range(1, middle):
                for i in (2 * step - 1, 2 * step):
                    got_other[c, i] = ring.sibling(got_own[c, i])
                    w.go(**{f"other{c}_{i}": got_other[c, i]})
                    seen.append(got_other[c, i])
        if c:
            mixed[c - 1] = w[f"mixed{c - 1}"]
            ready = [lax.optimization_barrier((b, *seen))[0] for b in mixed[c - 1]]
            w.go(**{f"mixed_ends{c - 1}": send(ready, ends)})
        w.close()
        if c == 0:
            spmm_meta, spmm_t_meta, dense_meta = w["metas"]
            w.go(cot_inner=send([w.gate(b) for b in cot_blocks], inner))
            w.go(shares=send([w.gate(w_share)] * parts, ends + inner))
        else:
            w.go(**{f"mixed_inner{c - 1}": send([w.gate(b) for b in mixed[c - 1]], inner)})
        got_own[c, len(offsets) - 2], got_own[c, len(offsets) - 1] = w[f"far_up{c}"], w[f"far_down{c}"]
        if c < last:
            up = down = w.gate(xs[c + 1])
    w_rows = jnp.concatenate(ordered(w_share, {**w.done, **w.pending}["shares"]), axis=1)
    w_full = lax.all_gather(w.gate(w_rows), "row", axis=0, tiled=True)
    for i in (-2, -1):
        got_other[last, len(offsets) + i] = ring.sibling(got_own[last, len(offsets) + i])

    for h in range(halves):
        w.go(**{f"half{h}": run_spmm(last, halves, h)})
        w.close()
        w.go(**{f"half_got{h}": send(w[f"half{h}"], ends + inner)})

    cot = ordered(cot_blocks[0], w["cot_ends"], w["cot_inner"])
    whole = [ordered(mixed[c][0], w[f"mixed_ends{c}"], w[f"mixed_inner{c}"]) for c in range(last)]
    earlier = ()
    for h in range(halves):
        part = ordered(w[f"half{h}"][0], w[f"half_got{h}"])
        blocks = [[(whole[c][u], h * half_rows) for c in range(last)] + [(part[u], 0)] for u in range(parts)]
        act, back, mixed_rows, grad_rows, earlier = dense(
            dense_meta, blocks, cot, w_full, half_rows, h * half_rows, earlier
        )
        w.go(**{f"back{h}": [b[0] for b in back]})
        if h == halves - 1:
            w.go(whole=(act, back, mixed_rows, grad_rows))
        w.close()
        w.go(**{f"back_got{h}": send(w[f"back{h}"], ends + inner)})
    act, back, mixed_rows, grad_rows = w["whole"]
    sums = lax.dot_general(grad_rows, mixed_rows, (((0,), (0,)), ((), ())), preferred_element_type=F32).astype(BF16)
    share = sums.shape[0] // row_size

    def sums_for(offset, other):
        return lax.dynamic_slice_in_dim(sums, ring.device_at(offset, other) * share, share, 0)

    wg = Reduction(
        ring,
        sums_for(middle, False),
        [sums_for(o, False) for o in near],
        sums_for(middle, True),
        jnp.concatenate([sums_for(o, True) for o in near]),
    )
    wg_far = wg.far_swap()
    w.go(wg_own=(wg.own_far, wg.own_near), wg_far=wg_far, wg_near=wg.near_swap(wg_far))
    w.close()
    wg.own_far, wg.own_near = w["wg_own"]
    w.go(wg_up_down=wg.hops(*wg.far_sums(w["wg_far"])))

    def run_spmm_t(c, grads):
        return spmm_t(tiles, columns, counts, spmm_t_meta, grads, parts, held, rows, rows * row_size)

    parts_got = [ordered(w[f"back{h}"][0], w[f"back_got{h}"]) for h in range(halves)]
    w.go(terms0=run_spmm_t(0, [parts_got[h][u] for u in range(parts) for h in range(halves)]))
    for c in range(1, chunks):
        w.go(**{f"rest_got{c}": send([w.gate(b[c]) for b in back], ends + inner)})
    w.close()

    def wg_steps(first, until):
        up, down = w["wg_up_down"]
        for step in range(first, until, -1):
            up, down = wg.hops(*wg.sums(step, w["wg_near"], up, down, False))
        return up, down

    def send_act(shifts):
        return send([w.gate(a) for a in act], shifts)

    def reduction(terms):
        red = Reduction(ring, terms[0], terms[1:-2], terms[-2], terms[-1])
        got_far = red.far_swap()
        return red, got_far, red.near_swap(got_far)

    reductions = []
    combined_before = False
    red, got_far, got_near = reduction(w["terms0"])
    for c in range(chunks):
        reductions.append(red)
        combined = c < last and middle == 2
        if c == last and c:
            got_near, cuts = lax.optimization_barrier((got_near, cuts))
            w.go(cuts_got=send(cuts, ends + inner))
        if c == 0 or not combined_before:
            sums = red.halves(got_far, got_near) if combined else red.far_sums(got_far)
        if c == 0:
            sums, wg_last = lax.optimization_barrier((sums, wg_steps(middle - 1, 0)))
        w.go(**{f"got_near{c}": got_near})
        if c < last:
            grads = ordered(back[0][c + 1], w[f"rest_got{c + 1}"])
            grads, sums = lax.optimization_barrier((grads, sums))
            following = reduction(run_spmm_t(c + 1, grads))
            w.go(following=following[1:], following_sums=following[0].far_sums(following[1]) if combined else ())
        first = red.hops(*sums)
        w.go(**{f"sum{c}_{middle}": first})
        if c == 0:
            w.go(act_inner=send_act(inner))
        if c < last or not combined_before:
            w.close()
        if c == 0:
            block = total_of(*wg.near_terms(0, w["wg_near"]), *wg.last(*wg_last))
            cuts = [
                w.gate(lax.dynamic_slice_in_dim(block, lax.rem(rep + u, parts) * f_wide, f_wide, 1))
                for u in range(parts)
            ]
        combined_before = combined
        if combined:
            halves_next = red.other_halves(w[f"got_near{c}"], *w[f"sum{c}_{middle}"])
            red, (got_far, got_near), sums = following[0], w.done.pop("following"), w.done.pop("following_sums")
            w.go(**{f"sum{c}_1": red.hops(*halves_next)})
            continue
        now = {**w.done, **w.pending}
        for step in range(middle - 1, 0, -1):
            to_up, to_down = red.sums(step, now[f"got_near{c}"], *now[f"sum{c}_{step + 1}"], True)
            if step == 1 and c == last:
                act, to_up, to_down = lax.optimization_barrier((act, to_up, to_down))
            w.go(**{f"sum{c}_{step}": red.hops(to_up, to_down)})
            if step > 1:
                w.close()
            now = {**w.done, **w.pending}
        if c < last:
            red, (got_far, got_near) = following[0], w.done.pop("following")
            w.done.pop("following_sums")
    w.go(act_ends=send(act, ends))
    if last == 0:
        w.go(cuts_got=send(cuts, ends + inner))
    got = {**w.done, **w.pending}
    cuts_got = got["cuts_got"]
    got["weight_grad"] = functools.reduce(lambda a, b: a + b, [v.astype(F32) for v in [cuts[0], *cuts_got.values()]])
    ready = []
    at = near.index(0)
    for c, red in enumerate(reductions[:-1]):
        up, down = got[f"sum{c}_1"]
        if middle == 2:
            whole_up, whole_down = got[f"sum{c}_2"]
            ready.append(joined(red.own_near[at], got[f"got_near{c}"], at, up, whole_up, whole_down, down))
        else:
            ready.append(total_of(*red.near_terms(0, got[f"got_near{c}"]), *red.last(up, down)))
    red = reductions[-1]
    feature_grad = result_of(ready, red.own_near[at], got[f"got_near{last}"], at, *red.last(*got[f"sum{last}_1"]))
    weight_grad = got["weight_grad"].T
    act = ordered(act[0], got["act_ends"], got["act_inner"])
    activations = jnp.zeros((rows, h_wide), BF16)
    for u in range(parts):
        activations = lax.dynamic_update_slice_in_dim(activations, act[u], lax.rem(rep + u, parts) * part_rows, 0)
    return (activations, feature_grad, weight_grad)


def solution(mesh):
    in_specs = (
        P("row", "rep"),
        P("row", None, None, None),
        P("row", None),
        P("row"),
        P(None, "rep"),
        P("row", "rep"),
    )
    out_specs = (P("row", "rep"), P("row", "rep"), P("rep", "row"))
    return jax.shard_map(local, mesh=mesh, in_specs=in_specs, out_specs=out_specs, check_vma=False)
```

```python
import functools
import jax
import jax.numpy as jnp
from jax import lax
from jax.experimental import pallas as pl
from jax.experimental.pallas import tpu as pltpu
from jax.sharding import PartitionSpec as P

BF16, F32 = jnp.bfloat16, jnp.float32
VMEM_LIMIT = 56 * 1024 * 1024
LANES = 128
CORES = 2


def params():
    return pltpu.CompilerParams(vmem_limit_bytes=VMEM_LIMIT)


def any_spec():
    return pl.BlockSpec(memory_space=pl.ANY)


class Ring:
    def __init__(self, devices):
        self.chips = devices // CORES
        half = self.chips // 2
        self.order = list(range(half)) + list(range(self.chips - 1, half - 1, -1))
        self.devices = devices

    def perm(self, step):
        pairs = []
        for place, chip in enumerate(self.order):
            to = self.order[(place + step) % self.chips]
            pairs += [(chip * CORES + core, to * CORES + core) for core in range(CORES)]
        return pairs

    def hop(self, value, step):
        return lax.ppermute(value, "row", self.perm(step))

    def sibling(self, value):
        return lax.ppermute(value, "row", [(d, d ^ 1) for d in range(self.devices)])

    def device_at(self, offset, other_core):
        me = lax.axis_index("row")
        order = jnp.array(self.order, jnp.int32)
        place_of = jnp.array([self.order.index(c) for c in range(self.chips)], jnp.int32)
        chip = order[(place_of[me // CORES] + offset) % self.chips]
        core = me % CORES
        return chip * CORES + (1 - core if other_core else core)


class Waves:
    def __init__(self):
        self.pending = {}
        self.done = {}
        self.token = None

    def go(self, **values):
        assert not set(values) & (set(self.pending) | set(self.done))
        self.pending.update(values)

    def close(self):
        names, values = list(self.pending), list(self.pending.values())
        flat, tree = jax.tree.flatten(values)
        flat = lax.optimization_barrier(flat)
        self.token = flat[0]
        self.done.update(zip(names, jax.tree.unflatten(tree, flat)))
        self.pending = {}

    def gate(self, value):
        if self.token is None:
            return value
        return lax.optimization_barrier((value, self.token))[0]

    def __getitem__(self, name):
        return self.done[name]


def shift_groups(size):
    ends = sorted({1, size - 1})
    return ends, [s for s in range(2, size - 1)]


def send(blocks, shifts):
    size = len(blocks)
    return {
        (size - s) % size: lax.ppermute(blocks[s], "rep", [(i, (i + s) % size) for i in range(size)]) for s in shifts
    }


def ordered(own, *groups):
    got = {0: own}
    for group in groups:
        got.update(group)
    return [got[u] for u in range(len(got))]


def masked_tiles(tiles, i, count):
    found = []
    for k in range(tiles.shape[1]):
        tile = tiles[i, k]
        found.append(jnp.where(k < count, tile, jnp.zeros_like(tile)))
    return jnp.concatenate(found, axis=1)


def step_spec(blocks, slots, tile_size, parts, per_step, skip):
    def index(t, cols, cnt, meta):
        return (lax.rem(meta[0] + t, parts) * (blocks // parts // per_step) + skip, 0, 0, 0)

    return pl.BlockSpec((per_step, slots, tile_size, tile_size), index)


def aligned(start, size, unit):
    return pl.ds(pl.multiple_of(start, unit), size)


def spmm_kernel(n_pieces, per_part, skip, cols, counts, meta, tiles, *refs):
    parts = pl.num_programs(0)
    n_outs = len(refs) - n_pieces - 3
    pieces, outs = refs[:n_pieces], refs[n_pieces : n_pieces + n_outs]
    source, result, sems = refs[n_pieces + n_outs :]
    t = pl.program_id(0)
    per_step, slots, tile_size, _ = tiles.shape

    @pl.when(t == 0)
    def _():
        copies = []
        for p, piece in enumerate(pieces):
            copies.append(
                pltpu.make_async_copy(piece, source.at[aligned(meta[1 + p], piece.shape[0], tile_size)], sems.at[p])
            )
            copies[-1].start()
        for copy in copies:
            copy.wait()

    for i in range(per_step):
        b = lax.rem(meta[0] + t, parts) * per_part + skip * per_step + i
        right = [source[aligned(cols[b, k] * tile_size, tile_size, tile_size), :] for k in range(slots)]
        product = jnp.dot(
            masked_tiles(tiles, i, counts[b]), jnp.concatenate(right, axis=0), preferred_element_type=F32
        )
        result[i * tile_size : (i + 1) * tile_size, :] = product.astype(BF16)

    for u in range(n_outs):

        @pl.when(t == u)
        def _():
            outs[u][...] = result[...]


def spmm(tiles, columns, counts, meta, pieces, parts, cut, skip):
    blocks, slots, tile_size, _ = tiles.shape
    width = pieces[0].shape[1]
    total_rows = sum(v.shape[0] for v in pieces)
    per_part = blocks // parts
    per_step = per_part // cut
    rows = per_step * tile_size
    return pl.pallas_call(
        functools.partial(spmm_kernel, len(pieces), per_part, skip),
        grid_spec=pltpu.PrefetchScalarGridSpec(
            num_scalar_prefetch=3,
            grid=(parts,),
            in_specs=[step_spec(blocks, slots, tile_size, parts, per_step, skip)] + [any_spec()] * len(pieces),
            out_specs=[pl.BlockSpec((rows, width), lambda t, cols, cnt, meta: (0, 0))] * parts,
            scratch_shapes=[
                pltpu.VMEM((total_rows, width), BF16),
                pltpu.VMEM((rows, width), BF16),
                pltpu.SemaphoreType.DMA((len(pieces),)),
            ],
        ),
        out_shape=[jax.ShapeDtypeStruct((rows, width), BF16)] * parts,
        compiler_params=params(),
        cost_estimate=pl.CostEstimate(
            flops=2 * parts * rows * slots * tile_size * width,
            bytes_accessed=2 * (tiles.size // cut + total_rows * width),
            transcendentals=0,
        ),
        name="spmm",
    )(columns, counts, meta, tiles, *pieces)


def spmm_t_kernel(n_grads, per_part, n_outs, terms, cols, counts, meta, tiles, *refs):
    parts = pl.num_programs(0)
    grads, outs = refs[:n_grads], refs[n_grads : n_grads + n_outs]
    total, grad, stage, in_sems, out_sems = refs[n_grads + n_outs :]
    t = pl.program_id(0)
    per_step, slots, tile_size, _ = tiles.shape
    width = grad.shape[1]
    rows = stage.shape[1]

    @pl.when(t == 0)
    def _():
        copies, start = [], 0
        for g, ref in enumerate(grads):
            copies.append(pltpu.make_async_copy(ref, grad.at[pl.ds(start, ref.shape[0])], in_sems.at[g]))
            copies[-1].start()
            start += ref.shape[0]

        @pl.loop(0, total.shape[0] // tile_size, unroll=8)
        def _(i):
            total[aligned(i * tile_size, tile_size, tile_size), :] = jnp.zeros((tile_size, width), F32)

        for copy in copies:
            copy.wait()

    for i in range(per_step):
        b = lax.rem(meta[0] + t, parts) * per_part + i
        block = grad[aligned((t * per_step + i) * tile_size, tile_size, tile_size), :]
        part = lax.dot_general(
            masked_tiles(tiles, i, counts[b]), block, (((0,), (0,)), ((), ())), preferred_element_type=F32
        )
        for k in range(slots):
            total[aligned(cols[b, k] * tile_size, tile_size, tile_size), :] += part[k * tile_size : (k + 1) * tile_size]

    @pl.when(t == parts - 1)
    def _():
        copies = []
        for o, (out, at) in enumerate(terms):
            slot = o % 2
            if o >= 2:
                copies[o - 2].wait()

            @pl.loop(0, rows // tile_size, unroll=4)
            def _(i):
                start = aligned(meta[1 + o] + i * tile_size, tile_size, tile_size)
                stage[slot, aligned(i * tile_size, tile_size, tile_size), :] = total[start, :].astype(BF16)

            copies.append(
                pltpu.make_async_copy(stage.at[slot], outs[out].at[pl.ds(at * rows, rows)], out_sems.at[o])
            )
            copies[o].start()
        for copy in copies[-2:]:
            copy.wait()


def spmm_t(tiles, columns, counts, meta, grads, parts, held, rows, total_rows):
    blocks, slots, tile_size, _ = tiles.shape
    width = grads[0].shape[1]
    per_part = blocks // parts
    flat = [(out, at) for out, many in enumerate(held) for at in range(many)]
    return pl.pallas_call(
        functools.partial(spmm_t_kernel, len(grads), per_part, len(held), flat),
        grid_spec=pltpu.PrefetchScalarGridSpec(
            num_scalar_prefetch=3,
            grid=(parts,),
            in_specs=[step_spec(blocks, slots, tile_size, parts, per_part, 0)] + [any_spec()] * len(grads),
            out_specs=[any_spec()] * len(held),
            scratch_shapes=[
                pltpu.VMEM((total_rows, width), F32),
                pltpu.VMEM((rows, width), BF16),
                pltpu.VMEM((2, rows, width), BF16),
                pltpu.SemaphoreType.DMA((len(grads),)),
                pltpu.SemaphoreType.DMA((len(flat),)),
            ],
        ),
        out_shape=[jax.ShapeDtypeStruct((many * rows, width), BF16) for many in held],
        compiler_params=params(),
        cost_estimate=pl.CostEstimate(
            flops=2 * blocks * slots * tile_size * tile_size * width,
            bytes_accessed=2 * (tiles.size + total_rows * width),
            transcendentals=0,
        ),
        name="spmm_t",
    )(columns, counts, meta, tiles, *grads)


def dense_kernel(parts, chunks, n_earlier, meta, *refs):
    n_mixed = parts * chunks
    mixed_refs, cot_refs, w_hbm = refs[:n_mixed], refs[n_mixed : n_mixed + parts], refs[n_mixed + parts]
    outs = refs[n_mixed + parts + 1 + n_earlier :]
    act_outs, mg_outs = outs[:parts], outs[parts : parts + n_mixed]
    mixed_out, grad_out, weight, sems = outs[parts + n_mixed :]
    f_wide, h_wide = weight.shape[0] // parts, weight.shape[1] // parts
    width = f_wide // chunks
    me = meta[0]

    def place(u):
        return lax.rem(me + u, parts)

    @pl.when(pl.program_id(0) == 0)
    def _():
        copies = []
        for i in range(parts):
            src = w_hbm.at[aligned(place(i) * f_wide, f_wide, f_wide)]
            copies.append(pltpu.make_async_copy(src, weight.at[pl.ds(i * f_wide, f_wide)], sems.at[i]))
            copies[-1].start()
        for copy in copies:
            copy.wait()

    mixed = jnp.concatenate([ref[...] for ref in mixed_refs], axis=1)
    for u in range(parts):
        at = pl.ds(pl.multiple_of(place(u) * f_wide, f_wide), f_wide)
        mixed_out[:, at] = mixed[:, u * f_wide : (u + 1) * f_wide]
    grads = []
    for u in range(parts):
        preact = jnp.dot(mixed, weight[:, u * h_wide : (u + 1) * h_wide], preferred_element_type=F32)
        sig = jax.nn.sigmoid(preact)
        act_outs[u][...] = (preact * sig).astype(BF16)
        grads.append((cot_refs[u][...].astype(F32) * sig * (1.0 + preact * (1.0 - sig))).astype(BF16))
        at = pl.ds(pl.multiple_of(place(u) * h_wide, h_wide), h_wide)
        grad_out[:, at] = grads[u]
    grad = jnp.concatenate(grads, axis=1)
    back = lax.dot_general(grad, weight[...], (((1,), (1,)), ((), ())), preferred_element_type=F32).astype(BF16)
    for i in range(n_mixed):
        mg_outs[i][...] = back[:, i * width : (i + 1) * width]


def dense(meta, mixed, cot, weight, rows, first, earlier):
    parts, chunks = len(mixed), len(mixed[0])
    width = mixed[0][0][0].shape[1]
    features, hidden = weight.shape
    h_wide = hidden // parts
    all_rows = cot[0].shape[0]
    step = min(rows, 256)
    flat = [m for row in mixed for m in row]
    earlier = list(earlier)

    def spec(w, start=0):
        return pl.BlockSpec((step, w), lambda t, meta: (t + start // step, 0))

    kinds = [(h_wide, True)] * parts + [(width, c > 0) for _ in range(parts) for c in range(chunks)]
    kinds += [(features, True), (hidden, True)]
    whole_at = [i for i, (_, whole) in enumerate(kinds) if whole]
    n_inputs = 1 + len(flat) + parts + 1
    outs = pl.pallas_call(
        functools.partial(dense_kernel, parts, chunks, len(earlier)),
        grid_spec=pltpu.PrefetchScalarGridSpec(
            num_scalar_prefetch=1,
            grid=(rows // step,),
            in_specs=[spec(width, at) for _, at in flat]
            + [spec(h_wide, first)] * parts
            + [any_spec()]
            + [any_spec()] * len(earlier),
            out_specs=[spec(w, first if whole else 0) for w, whole in kinds],
            scratch_shapes=[pltpu.VMEM((features, hidden), BF16), pltpu.SemaphoreType.DMA((parts,))],
        ),
        out_shape=[jax.ShapeDtypeStruct((all_rows if whole else rows, w), BF16) for w, whole in kinds],
        input_output_aliases={n_inputs + i: at for i, at in enumerate(whole_at)} if earlier else {},
        compiler_params=params(),
        cost_estimate=pl.CostEstimate(
            flops=4 * rows * features * hidden,
            bytes_accessed=2 * (features * hidden + 6 * rows * hidden),
            transcendentals=rows * hidden,
        ),
        name="dense",
    )(meta, *[m for m, _ in flat], *cot, weight, *earlier)
    n = parts * chunks
    act, back = outs[:parts], outs[parts : parts + n]
    return (
        act,
        [back[u * chunks : (u + 1) * chunks] for u in range(parts)],
        outs[-2],
        outs[-1],
        [outs[i] for i in whole_at],
    )


def total_of(*values):
    return functools.reduce(lambda a, b: a + b, [v.astype(F32) for v in values]).astype(BF16)


def step_kernel(low_blocks, own_up, got_up, up, own_down, got_down, down, to_up, to_down):
    low = pl.program_id(0) < low_blocks

    def put(out, own, got, more, with_more):
        both = own[...].astype(F32) + got[...].astype(F32)

        @pl.when(with_more)
        def _():
            out[...] = (both + more[...].astype(F32)).astype(BF16)

        @pl.when(jnp.logical_not(with_more))
        def _():
            out[...] = both.astype(BF16)

    put(to_up, own_up, got_up, up, low)
    put(to_down, own_down, got_down, down, jnp.logical_not(low))


def step_sums(own_up, at_up, up, own_down, at_down, down, got):
    rows, width = own_up.shape
    step = min(rows // 2, 1024)
    blocks = rows // step
    low = blocks // 2

    def spec(index):
        return pl.BlockSpec((step, width), lambda t: (index(t), 0))

    here = spec(lambda t: t)
    return pl.pallas_call(
        functools.partial(step_kernel, low),
        grid=(blocks,),
        in_specs=[
            here,
            spec(lambda t: t + at_up * blocks),
            spec(lambda t: jnp.minimum(t, low - 1)),
            here,
            spec(lambda t: t + at_down * blocks),
            spec(lambda t: jnp.maximum(t - low, 0)),
        ],
        out_specs=[here, here],
        out_shape=[jax.ShapeDtypeStruct((rows, width), BF16)] * 2,
        compiler_params=params(),
        cost_estimate=pl.CostEstimate(flops=4 * rows * width, bytes_accessed=14 * rows * width, transcendentals=0),
        name="step_sums",
    )(own_up, got, up, own_down, got, down)


def result_kernel(n_ready, *refs):
    ready, (own, got, up, down, out) = refs[:n_ready], refs[n_ready:]
    width = own.shape[1]
    for c, ref in enumerate(ready):
        out[:, c * width : (c + 1) * width] = ref[...]
    out[:, n_ready * width :] = (
        own[...].astype(F32) + got[...].astype(F32) + up[...].astype(F32) + down[...].astype(F32)
    ).astype(BF16)


def result_of(ready, own, got, at, up, down):
    rows, width = own.shape
    step = min(rows // 2, 1024)
    blocks = rows // step
    here = pl.BlockSpec((step, width), lambda t: (t, 0))
    there = pl.BlockSpec((step, width), lambda t: (t + at * blocks, 0))
    wide = width * (len(ready) + 1)
    return pl.pallas_call(
        functools.partial(result_kernel, len(ready)),
        grid=(blocks,),
        in_specs=[here] * (len(ready) + 1) + [there, here, here],
        out_specs=pl.BlockSpec((step, wide), lambda t: (t, 0)),
        out_shape=jax.ShapeDtypeStruct((rows, wide), BF16),
        compiler_params=params(),
        cost_estimate=pl.CostEstimate(flops=4 * rows * width, bytes_accessed=14 * rows * width, transcendentals=0),
        name="feature_grad",
    )(*ready, own, got, up, down)


def halves_kernel(low_blocks, own_far, got_far, own_up, got_up, own_down, got_down, to_up, to_down):
    low = pl.program_id(0) < low_blocks

    def put(out, own, got):
        out[...] = (own[...].astype(F32) + got[...].astype(F32)).astype(BF16)

    @pl.when(low)
    def _():
        put(to_up, own_far, got_far)
        put(to_down, own_down, got_down)

    @pl.when(jnp.logical_not(low))
    def _():
        put(to_up, own_up, got_up)
        put(to_down, own_far, got_far)


def halves_sums(own_far, got_far, own_up, at_up, own_down, at_down, got):
    rows, width = own_far.shape
    step = min(rows // 2, 1024)
    blocks = rows // step
    low = blocks // 2

    def spec(index):
        return pl.BlockSpec((step, width), lambda t: (index(t), 0))

    here = spec(lambda t: t)
    return pl.pallas_call(
        functools.partial(halves_kernel, low),
        grid=(blocks,),
        in_specs=[
            here,
            here,
            spec(lambda t: jnp.maximum(t, low)),
            spec(lambda t: jnp.maximum(t, low) + at_up * blocks),
            spec(lambda t: jnp.minimum(t, low - 1)),
            spec(lambda t: jnp.minimum(t, low - 1) + at_down * blocks),
        ],
        out_specs=[here, here],
        out_shape=[jax.ShapeDtypeStruct((rows, width), BF16)] * 2,
        compiler_params=params(),
        cost_estimate=pl.CostEstimate(flops=2 * rows * width, bytes_accessed=12 * rows * width, transcendentals=0),
        name="halves_sums",
    )(own_far, got_far, own_up, got, own_down, got)


def joined_kernel(low_blocks, own, got, up_low, up_high, down_low, down_high, out):
    low = pl.program_id(0) < low_blocks

    def put(up, down):
        total = own[...].astype(F32) + got[...].astype(F32) + up[...].astype(F32) + down[...].astype(F32)
        out[...] = total.astype(BF16)

    @pl.when(low)
    def _():
        put(up_low, down_low)

    @pl.when(jnp.logical_not(low))
    def _():
        put(up_high, down_high)


def joined(own, got, at, up_low, up, down, down_high):
    rows, width = own.shape
    step = min(rows // 2, 1024)
    blocks = rows // step
    low = blocks // 2

    def spec(index):
        return pl.BlockSpec((step, width), lambda t: (index(t), 0))

    return pl.pallas_call(
        functools.partial(joined_kernel, low),
        grid=(blocks,),
        in_specs=[
            spec(lambda t: t),
            spec(lambda t: t + at * blocks),
            spec(lambda t: jnp.minimum(t, low - 1)),
            spec(lambda t: jnp.maximum(t, low)),
            spec(lambda t: jnp.minimum(t, low - 1)),
            spec(lambda t: jnp.maximum(t - low, 0)),
        ],
        out_specs=spec(lambda t: t),
        out_shape=jax.ShapeDtypeStruct((rows, width), BF16),
        compiler_params=params(),
        cost_estimate=pl.CostEstimate(flops=3 * rows * width, bytes_accessed=10 * rows * width, transcendentals=0),
        name="joined",
    )(own, got, up_low, up, down, down_high)


class Reduction:
    def __init__(self, ring, own_far, own_near, other_far, other_near):
        self.ring, self.middle = ring, ring.chips // 2
        self.near = [o for o in range(ring.chips) if o != self.middle]
        self.own_far, self.own_near, self.other_far, self.other_near = own_far, own_near, other_far, other_near
        self.rows = own_far.shape[0]

    def far_swap(self):
        return self.ring.sibling(self.other_far)

    def near_swap(self, after):
        return self.ring.sibling(lax.optimization_barrier((self.other_near, after))[0])

    def far_sums(self, got):
        half = self.rows // 2
        return [total_of(self.own_far[at : at + half], got[at : at + half]) for at in (0, half)]

    def hops(self, up, down):
        return self.ring.hop(up, 1), self.ring.hop(down, -1)

    def place(self, offset):
        return self.near.index(offset % self.ring.chips)

    def near_terms(self, offset, got):
        at = self.place(offset)
        return self.own_near[at], got[at * self.rows : (at + 1) * self.rows]

    def sums(self, step, got, up, down, kernel):
        if step < self.middle - 1:
            return total_of(*self.near_terms(step, got), up), total_of(*self.near_terms(-step, got), down)
        at_up, at_down = self.place(step), self.place(-step)
        if kernel:
            return step_sums(self.own_near[at_up], at_up, up, self.own_near[at_down], at_down, down, got)
        zeros = jnp.zeros_like(up)
        return (
            total_of(*self.near_terms(step, got), jnp.concatenate([up, zeros])),
            total_of(*self.near_terms(-step, got), jnp.concatenate([zeros, down])),
        )

    def halves(self, got_far, got):
        at_up, at_down = self.place(1), self.place(-1)
        return halves_sums(self.own_far, got_far, self.own_near[at_up], at_up, self.own_near[at_down], at_down, got)

    def other_halves(self, got, up, down):
        half = self.rows // 2
        (own_up, got_up), (own_down, got_down) = self.near_terms(1, got), self.near_terms(-1, got)
        return total_of(own_up[:half], got_up[:half], up[:half]), total_of(own_down[half:], got_down[half:], down[half:])

    def last(self, up, down):
        if self.middle > 1:
            return up, down
        return jnp.concatenate([up, jnp.zeros_like(up)]), jnp.concatenate([jnp.zeros_like(down), down])


def local(features, tiles, columns, counts, weight, cotangent):
    rows, f_wide = features.shape
    h_wide = cotangent.shape[1]
    row_size, parts = lax.axis_size("row"), lax.axis_size("rep")
    ring = Ring(row_size)
    rep = lax.axis_index("rep")
    chunks = f_wide // LANES if f_wide % LANES == 0 else 1
    width = f_wide // chunks
    half = rows // 2
    part_rows = rows // parts
    halves = 2
    half_rows = part_rows // halves
    middle = ring.chips // 2
    near = [o for o in range(ring.chips) if o != middle]
    ends, inner = shift_groups(parts)
    last = chunks - 1
    w = Waves()

    offsets = [(0, 0)] + [(o, 0) for step in range(1, middle) for o in (-step, step)] + [(middle, 0), (middle, half)]
    own_meta = [ring.device_at(o, False) * rows + at for o, at in offsets]
    other_meta = [ring.device_at(o, True) * rows + at for o, at in offsets]
    spmm_meta = jnp.stack([rep] + own_meta + other_meta).astype(jnp.int32)
    held = [1] + [1] * len(near) + [1, len(near)]
    order = [middle] + near
    terms_at = [ring.device_at(o, other) * rows for other in (False, True) for o in order]
    spmm_t_meta = jnp.stack([rep] + terms_at).astype(jnp.int32)
    dense_meta = rep[None].astype(jnp.int32)

    def part_of(x, u):
        return lax.dynamic_slice_in_dim(x, lax.rem(rep + u, parts) * part_rows, part_rows, 0)

    share = weight.shape[0] // row_size
    w_share = lax.dynamic_slice_in_dim(weight, lax.axis_index("row") * share, share, 0)

    cot_blocks = [part_of(cotangent, u) for u in range(parts)]
    xs = [features[:, c * width : (c + 1) * width] for c in range(chunks)]
    up = down = xs[0]
    got_own = {}
    got_other = {}
    mixed = {}

    def run_spmm(c, cut, skip):
        own = [got_own[c, i] for i in range(len(offsets))]
        other = [got_other[c, i] for i in range(len(offsets))]
        return spmm(tiles, columns, counts, spmm_meta, own + other, parts, cut, skip)

    cot_ends = send(cot_blocks, ends)
    own_other = ring.sibling(features)
    for c in range(chunks):
        got_own[c, 0] = xs[c]
        got_other[c, 0] = own_other[:, c * width : (c + 1) * width]
        for step in range(1, middle):
            name = f"{c}_{step}"
            w.go(**{"up" + name: ring.hop(up, 1), "down" + name: ring.hop(down, -1)})
            if c and step == 1:
                for i in range(1, len(offsets)):
                    got_other[c - 1, i] = ring.sibling(got_own[c - 1, i])
                w.go(**{f"mixed{c - 1}": run_spmm(c - 1, 1, 0)})
            if c == 0 and step == 1:
                w.go(metas=(spmm_meta, spmm_t_meta, dense_meta))
            w.close()
            up, down = w["up" + name], w["down" + name]
            got_own[c, 2 * step - 1], got_own[c, 2 * step] = up, down
        w.go(**{f"far_up{c}": ring.hop(up[:half], 1), f"far_down{c}": ring.hop(down[half:], -1)})
        if c == 0:
            w.go(cot_ends=cot_ends, own_other=own_other)
        seen = []
        if c == last:
            for step in range(1, middle):
                for i in (2 * step - 1, 2 * step):
                    got_other[c, i] = ring.sibling(got_own[c, i])
                    w.go(**{f"other{c}_{i}": got_other[c, i]})
                    seen.append(got_other[c, i])
        if c:
            mixed[c - 1] = w[f"mixed{c - 1}"]
            ready = [lax.optimization_barrier((b, *seen))[0] for b in mixed[c - 1]]
            w.go(**{f"mixed_ends{c - 1}": send(ready, ends)})
        w.close()
        if c == 0:
            spmm_meta, spmm_t_meta, dense_meta = w["metas"]
            w.go(cot_inner=send([w.gate(b) for b in cot_blocks], inner))
            w.go(shares=send([w.gate(w_share)] * parts, ends + inner))
        else:
            w.go(**{f"mixed_inner{c - 1}": send([w.gate(b) for b in mixed[c - 1]], inner)})
        got_own[c, len(offsets) - 2], got_own[c, len(offsets) - 1] = w[f"far_up{c}"], w[f"far_down{c}"]
        if c < last:
            up = down = w.gate(xs[c + 1])
    w_rows = jnp.concatenate(ordered(w_share, {**w.done, **w.pending}["shares"]), axis=1)
    w_full = lax.all_gather(w.gate(w_rows), "row", axis=0, tiled=True)
    for i in (-2, -1):
        got_other[last, len(offsets) + i] = ring.sibling(got_own[last, len(offsets) + i])

    for h in range(halves):
        w.go(**{f"half{h}": run_spmm(last, halves, h)})
        w.close()
        w.go(**{f"half_got{h}": send(w[f"half{h}"], ends + inner)})

    cot = ordered(cot_blocks[0], w["cot_ends"], w["cot_inner"])
    whole = [ordered(mixed[c][0], w[f"mixed_ends{c}"], w[f"mixed_inner{c}"]) for c in range(last)]
    earlier = ()
    for h in range(halves):
        part = ordered(w[f"half{h}"][0], w[f"half_got{h}"])
        blocks = [[(whole[c][u], h * half_rows) for c in range(last)] + [(part[u], 0)] for u in range(parts)]
        act, back, mixed_rows, grad_rows, earlier = dense(
            dense_meta, blocks, cot, w_full, half_rows, h * half_rows, earlier
        )
        w.go(**{f"back{h}": [b[0] for b in back]})
        if h == halves - 1:
            w.go(whole=(act, back, mixed_rows, grad_rows))
        w.close()
        w.go(**{f"back_got{h}": send(w[f"back{h}"], ends + inner)})
    act, back, mixed_rows, grad_rows = w["whole"]
    sums = lax.dot_general(grad_rows, mixed_rows, (((0,), (0,)), ((), ())), preferred_element_type=F32).astype(BF16)
    share = sums.shape[0] // row_size

    def sums_for(offset, other):
        return lax.dynamic_slice_in_dim(sums, ring.device_at(offset, other) * share, share, 0)

    wg = Reduction(
        ring,
        sums_for(middle, False),
        [sums_for(o, False) for o in near],
        sums_for(middle, True),
        jnp.concatenate([sums_for(o, True) for o in near]),
    )
    wg_far = wg.far_swap()
    w.go(wg_own=(wg.own_far, wg.own_near), wg_far=wg_far, wg_near=ring.sibling(wg.other_near))
    w.close()
    wg.own_far, wg.own_near = w["wg_own"]
    w.go(wg_up_down=wg.hops(*wg.far_sums(w["wg_far"])))

    def run_spmm_t(c, grads):
        return spmm_t(tiles, columns, counts, spmm_t_meta, grads, parts, held, rows, rows * row_size)

    parts_got = [ordered(w[f"back{h}"][0], w[f"back_got{h}"]) for h in range(halves)]
    w.go(terms0=run_spmm_t(0, [parts_got[h][u] for u in range(parts) for h in range(halves)]))
    for c in range(1, chunks):
        w.go(**{f"rest_got{c}": send([w.gate(b[c]) for b in back], ends + inner)})
    w.close()

    def wg_steps(first, until):
        up, down = w["wg_up_down"]
        for step in range(first, until, -1):
            up, down = wg.hops(*wg.sums(step, w["wg_near"], up, down, False))
        return up, down

    def send_act(shifts):
        return send([w.gate(a) for a in act], shifts)

    reductions = []
    for c in range(chunks):
        terms = w[f"terms{c}"]
        red = Reduction(ring, terms[0], terms[1:-2], terms[-2], terms[-1])
        reductions.append(red)
        combined = c < last and middle == 2
        got_far = red.far_swap()
        got_near = red.near_swap(got_far)
        if c == last and c:
            got_near, cuts = lax.optimization_barrier((got_near, cuts))
            w.go(cuts_got=send(cuts, ends + inner))
        sums = red.halves(got_far, got_near) if combined else red.far_sums(got_far)
        if c == 0:
            sums, wg_last = lax.optimization_barrier((sums, wg_steps(middle - 1, 0)))
        w.go(**{f"got_near{c}": got_near})
        if c < last:
            grads = ordered(back[0][c + 1], w[f"rest_got{c + 1}"])
            grads, sums = lax.optimization_barrier((grads, sums))
            w.go(**{f"terms{c + 1}": run_spmm_t(c + 1, grads)})
        w.go(**{f"sum{c}_{middle}": red.hops(*sums)})
        if c == 0:
            w.go(act_inner=send_act(inner))
        w.close()
        if c == 0:
            block = total_of(*wg.near_terms(0, w["wg_near"]), *wg.last(*wg_last))
            cuts = [
                w.gate(lax.dynamic_slice_in_dim(block, lax.rem(rep + u, parts) * f_wide, f_wide, 1))
                for u in range(parts)
            ]
        if combined:
            w.go(**{f"sum{c}_1": red.hops(*red.other_halves(w[f"got_near{c}"], *w[f"sum{c}_{middle}"]))})
            continue
        for step in range(middle - 1, 0, -1):
            to_up, to_down = red.sums(step, w[f"got_near{c}"], *w[f"sum{c}_{step + 1}"], True)
            if step == 1 and c == last:
                act, to_up, to_down = lax.optimization_barrier((act, to_up, to_down))
            w.go(**{f"sum{c}_{step}": red.hops(to_up, to_down)})
            if step > 1:
                w.close()
    w.go(act_ends=send(act, ends))
    if last == 0:
        w.go(cuts_got=send(cuts, ends + inner))
    got = {**w.done, **w.pending}
    cuts_got = got["cuts_got"]
    got["weight_grad"] = functools.reduce(lambda a, b: a + b, [v.astype(F32) for v in [cuts[0], *cuts_got.values()]])
    ready = []
    at = near.index(0)
    for c, red in enumerate(reductions[:-1]):
        up, down = got[f"sum{c}_1"]
        if middle == 2:
            whole_up, whole_down = got[f"sum{c}_2"]
            ready.append(joined(red.own_near[at], got[f"got_near{c}"], at, up, whole_up, whole_down, down))
        else:
            ready.append(total_of(*red.near_terms(0, got[f"got_near{c}"]), *red.last(up, down)))
    red = reductions[-1]
    feature_grad = result_of(ready, red.own_near[at], got[f"got_near{last}"], at, *red.last(*got[f"sum{last}_1"]))
    weight_grad = got["weight_grad"].T
    act = ordered(act[0], got["act_ends"], got["act_inner"])
    activations = jnp.zeros((rows, h_wide), BF16)
    for u in range(parts):
        activations = lax.dynamic_update_slice_in_dim(activations, act[u], lax.rem(rep + u, parts) * part_rows, 0)
    return (activations, feature_grad, weight_grad)


def solution(mesh):
    in_specs = (
        P("row", "rep"),
        P("row", None, None, None),
        P("row", None),
        P("row"),
        P(None, "rep"),
        P("row", "rep"),
    )
    out_specs = (P("row", "rep"), P("row", "rep"), P("rep", "row"))
    return jax.shard_map(local, mesh=mesh, in_specs=in_specs, out_specs=out_specs, check_vma=False)
```

```python
import functools
import jax
import jax.numpy as jnp
from jax import lax
from jax.experimental import pallas as pl
from jax.experimental.pallas import tpu as pltpu
from jax.sharding import PartitionSpec as P

BF16, F32 = jnp.bfloat16, jnp.float32
VMEM_LIMIT = 56 * 1024 * 1024
LANES = 128
CORES = 2


def params():
    return pltpu.CompilerParams(vmem_limit_bytes=VMEM_LIMIT)


def any_spec():
    return pl.BlockSpec(memory_space=pl.ANY)


class Ring:
    def __init__(self, devices):
        self.chips = devices // CORES
        half = self.chips // 2
        self.order = list(range(half)) + list(range(self.chips - 1, half - 1, -1))
        self.devices = devices

    def perm(self, step):
        pairs = []
        for place, chip in enumerate(self.order):
            to = self.order[(place + step) % self.chips]
            pairs += [(chip * CORES + core, to * CORES + core) for core in range(CORES)]
        return pairs

    def hop(self, value, step):
        return lax.ppermute(value, "row", self.perm(step))

    def sibling(self, value):
        return lax.ppermute(value, "row", [(d, d ^ 1) for d in range(self.devices)])

    def device_at(self, offset, other_core):
        me = lax.axis_index("row")
        order = jnp.array(self.order, jnp.int32)
        place_of = jnp.array([self.order.index(c) for c in range(self.chips)], jnp.int32)
        chip = order[(place_of[me // CORES] + offset) % self.chips]
        core = me % CORES
        return chip * CORES + (1 - core if other_core else core)


class Waves:
    def __init__(self):
        self.pending = {}
        self.done = {}
        self.token = None

    def go(self, **values):
        assert not set(values) & (set(self.pending) | set(self.done))
        self.pending.update(values)

    def close(self):
        names, values = list(self.pending), list(self.pending.values())
        flat, tree = jax.tree.flatten(values)
        flat = lax.optimization_barrier(flat)
        self.token = flat[0]
        self.done.update(zip(names, jax.tree.unflatten(tree, flat)))
        self.pending = {}

    def gate(self, value):
        if self.token is None:
            return value
        return lax.optimization_barrier((value, self.token))[0]

    def __getitem__(self, name):
        return self.done[name]


def shift_groups(size):
    ends = sorted({1, size - 1})
    return ends, [s for s in range(2, size - 1)]


def send(blocks, shifts):
    size = len(blocks)
    return {
        (size - s) % size: lax.ppermute(blocks[s], "rep", [(i, (i + s) % size) for i in range(size)]) for s in shifts
    }


def ordered(own, *groups):
    got = {0: own}
    for group in groups:
        got.update(group)
    return [got[u] for u in range(len(got))]


def masked_tiles(tiles, i, count):
    found = []
    for k in range(tiles.shape[1]):
        tile = tiles[i, k]
        found.append(jnp.where(k < count, tile, jnp.zeros_like(tile)))
    return jnp.concatenate(found, axis=1)


def step_spec(blocks, slots, tile_size, parts, per_step, skip):
    def index(t, cols, cnt, meta):
        return (lax.rem(meta[0] + t, parts) * (blocks // parts // per_step) + skip, 0, 0, 0)

    return pl.BlockSpec((per_step, slots, tile_size, tile_size), index)


def aligned(start, size, unit):
    return pl.ds(pl.multiple_of(start, unit), size)


def spmm_kernel(n_pieces, per_part, skip, cols, counts, meta, tiles, *refs):
    parts = pl.num_programs(0)
    n_outs = len(refs) - n_pieces - 3
    pieces, outs = refs[:n_pieces], refs[n_pieces : n_pieces + n_outs]
    source, result, sems = refs[n_pieces + n_outs :]
    t = pl.program_id(0)
    per_step, slots, tile_size, _ = tiles.shape

    @pl.when(t == 0)
    def _():
        copies = []
        for p, piece in enumerate(pieces):
            copies.append(
                pltpu.make_async_copy(piece, source.at[aligned(meta[1 + p], piece.shape[0], tile_size)], sems.at[p])
            )
            copies[-1].start()
        for copy in copies:
            copy.wait()

    for i in range(per_step):
        b = lax.rem(meta[0] + t, parts) * per_part + skip * per_step + i
        right = [source[aligned(cols[b, k] * tile_size, tile_size, tile_size), :] for k in range(slots)]
        product = jnp.dot(
            masked_tiles(tiles, i, counts[b]), jnp.concatenate(right, axis=0), preferred_element_type=F32
        )
        result[i * tile_size : (i + 1) * tile_size, :] = product.astype(BF16)

    for u in range(n_outs):

        @pl.when(t == u)
        def _():
            outs[u][...] = result[...]


def spmm(tiles, columns, counts, meta, pieces, parts, cut, skip):
    blocks, slots, tile_size, _ = tiles.shape
    width = pieces[0].shape[1]
    total_rows = sum(v.shape[0] for v in pieces)
    per_part = blocks // parts
    per_step = per_part // cut
    rows = per_step * tile_size
    return pl.pallas_call(
        functools.partial(spmm_kernel, len(pieces), per_part, skip),
        grid_spec=pltpu.PrefetchScalarGridSpec(
            num_scalar_prefetch=3,
            grid=(parts,),
            in_specs=[step_spec(blocks, slots, tile_size, parts, per_step, skip)] + [any_spec()] * len(pieces),
            out_specs=[pl.BlockSpec((rows, width), lambda t, cols, cnt, meta: (0, 0))] * parts,
            scratch_shapes=[
                pltpu.VMEM((total_rows, width), BF16),
                pltpu.VMEM((rows, width), BF16),
                pltpu.SemaphoreType.DMA((len(pieces),)),
            ],
        ),
        out_shape=[jax.ShapeDtypeStruct((rows, width), BF16)] * parts,
        compiler_params=params(),
        cost_estimate=pl.CostEstimate(
            flops=2 * parts * rows * slots * tile_size * width,
            bytes_accessed=2 * (tiles.size // cut + total_rows * width),
            transcendentals=0,
        ),
        name="spmm",
    )(columns, counts, meta, tiles, *pieces)


def spmm_t_kernel(n_grads, per_part, n_outs, terms, cols, counts, meta, tiles, *refs):
    parts = pl.num_programs(0)
    grads, outs = refs[:n_grads], refs[n_grads : n_grads + n_outs]
    total, grad, stage, in_sems, out_sems = refs[n_grads + n_outs :]
    t = pl.program_id(0)
    per_step, slots, tile_size, _ = tiles.shape
    width = grad.shape[1]
    rows = stage.shape[1]

    @pl.when(t == 0)
    def _():
        copies, start = [], 0
        for g, ref in enumerate(grads):
            copies.append(pltpu.make_async_copy(ref, grad.at[pl.ds(start, ref.shape[0])], in_sems.at[g]))
            copies[-1].start()
            start += ref.shape[0]

        @pl.loop(0, total.shape[0] // tile_size, unroll=8)
        def _(i):
            total[aligned(i * tile_size, tile_size, tile_size), :] = jnp.zeros((tile_size, width), F32)

        for copy in copies:
            copy.wait()

    for i in range(per_step):
        b = lax.rem(meta[0] + t, parts) * per_part + i
        block = grad[aligned((t * per_step + i) * tile_size, tile_size, tile_size), :]
        part = lax.dot_general(
            masked_tiles(tiles, i, counts[b]), block, (((0,), (0,)), ((), ())), preferred_element_type=F32
        )
        for k in range(slots):
            total[aligned(cols[b, k] * tile_size, tile_size, tile_size), :] += part[k * tile_size : (k + 1) * tile_size]

    @pl.when(t == parts - 1)
    def _():
        copies = []
        for o, (out, at) in enumerate(terms):
            slot = o % 2
            if o >= 2:
                copies[o - 2].wait()

            @pl.loop(0, rows // tile_size, unroll=4)
            def _(i):
                start = aligned(meta[1 + o] + i * tile_size, tile_size, tile_size)
                stage[slot, aligned(i * tile_size, tile_size, tile_size), :] = total[start, :].astype(BF16)

            copies.append(
                pltpu.make_async_copy(stage.at[slot], outs[out].at[pl.ds(at * rows, rows)], out_sems.at[o])
            )
            copies[o].start()
        for copy in copies[-2:]:
            copy.wait()


def spmm_t(tiles, columns, counts, meta, grads, parts, held, rows, total_rows):
    blocks, slots, tile_size, _ = tiles.shape
    width = grads[0].shape[1]
    per_part = blocks // parts
    flat = [(out, at) for out, many in enumerate(held) for at in range(many)]
    return pl.pallas_call(
        functools.partial(spmm_t_kernel, len(grads), per_part, len(held), flat),
        grid_spec=pltpu.PrefetchScalarGridSpec(
            num_scalar_prefetch=3,
            grid=(parts,),
            in_specs=[step_spec(blocks, slots, tile_size, parts, per_part, 0)] + [any_spec()] * len(grads),
            out_specs=[any_spec()] * len(held),
            scratch_shapes=[
                pltpu.VMEM((total_rows, width), F32),
                pltpu.VMEM((rows, width), BF16),
                pltpu.VMEM((2, rows, width), BF16),
                pltpu.SemaphoreType.DMA((len(grads),)),
                pltpu.SemaphoreType.DMA((len(flat),)),
            ],
        ),
        out_shape=[jax.ShapeDtypeStruct((many * rows, width), BF16) for many in held],
        compiler_params=params(),
        cost_estimate=pl.CostEstimate(
            flops=2 * blocks * slots * tile_size * tile_size * width,
            bytes_accessed=2 * (tiles.size + total_rows * width),
            transcendentals=0,
        ),
        name="spmm_t",
    )(columns, counts, meta, tiles, *grads)


def dense_kernel(parts, chunks, n_earlier, meta, *refs):
    n_mixed = parts * chunks
    mixed_refs, cot_refs, w_hbm = refs[:n_mixed], refs[n_mixed : n_mixed + parts], refs[n_mixed + parts]
    outs = refs[n_mixed + parts + 1 + n_earlier :]
    act_outs, mg_outs = outs[:parts], outs[parts : parts + n_mixed]
    mixed_out, grad_out, weight, sems = outs[parts + n_mixed :]
    f_wide, h_wide = weight.shape[0] // parts, weight.shape[1] // parts
    width = f_wide // chunks
    me = meta[0]

    def place(u):
        return lax.rem(me + u, parts)

    @pl.when(pl.program_id(0) == 0)
    def _():
        copies = []
        for i in range(parts):
            src = w_hbm.at[aligned(place(i) * f_wide, f_wide, f_wide)]
            copies.append(pltpu.make_async_copy(src, weight.at[pl.ds(i * f_wide, f_wide)], sems.at[i]))
            copies[-1].start()
        for copy in copies:
            copy.wait()

    mixed = jnp.concatenate([ref[...] for ref in mixed_refs], axis=1)
    for u in range(parts):
        at = pl.ds(pl.multiple_of(place(u) * f_wide, f_wide), f_wide)
        mixed_out[:, at] = mixed[:, u * f_wide : (u + 1) * f_wide]
    grads = []
    for u in range(parts):
        preact = jnp.dot(mixed, weight[:, u * h_wide : (u + 1) * h_wide], preferred_element_type=F32)
        sig = jax.nn.sigmoid(preact)
        act_outs[u][...] = (preact * sig).astype(BF16)
        grads.append((cot_refs[u][...].astype(F32) * sig * (1.0 + preact * (1.0 - sig))).astype(BF16))
        at = pl.ds(pl.multiple_of(place(u) * h_wide, h_wide), h_wide)
        grad_out[:, at] = grads[u]
    grad = jnp.concatenate(grads, axis=1)
    back = lax.dot_general(grad, weight[...], (((1,), (1,)), ((), ())), preferred_element_type=F32).astype(BF16)
    for i in range(n_mixed):
        mg_outs[i][...] = back[:, i * width : (i + 1) * width]


def dense(meta, mixed, cot, weight, rows, first, earlier):
    parts, chunks = len(mixed), len(mixed[0])
    width = mixed[0][0][0].shape[1]
    features, hidden = weight.shape
    h_wide = hidden // parts
    all_rows = cot[0].shape[0]
    step = min(rows, 256)
    flat = [m for row in mixed for m in row]
    earlier = list(earlier)

    def spec(w, start=0):
        return pl.BlockSpec((step, w), lambda t, meta: (t + start // step, 0))

    kinds = [(h_wide, True)] * parts + [(width, c > 0) for _ in range(parts) for c in range(chunks)]
    kinds += [(features, True), (hidden, True)]
    whole_at = [i for i, (_, whole) in enumerate(kinds) if whole]
    n_inputs = 1 + len(flat) + parts + 1
    outs = pl.pallas_call(
        functools.partial(dense_kernel, parts, chunks, len(earlier)),
        grid_spec=pltpu.PrefetchScalarGridSpec(
            num_scalar_prefetch=1,
            grid=(rows // step,),
            in_specs=[spec(width, at) for _, at in flat]
            + [spec(h_wide, first)] * parts
            + [any_spec()]
            + [any_spec()] * len(earlier),
            out_specs=[spec(w, first if whole else 0) for w, whole in kinds],
            scratch_shapes=[pltpu.VMEM((features, hidden), BF16), pltpu.SemaphoreType.DMA((parts,))],
        ),
        out_shape=[jax.ShapeDtypeStruct((all_rows if whole else rows, w), BF16) for w, whole in kinds],
        input_output_aliases={n_inputs + i: at for i, at in enumerate(whole_at)} if earlier else {},
        compiler_params=params(),
        cost_estimate=pl.CostEstimate(
            flops=4 * rows * features * hidden,
            bytes_accessed=2 * (features * hidden + 6 * rows * hidden),
            transcendentals=rows * hidden,
        ),
        name="dense",
    )(meta, *[m for m, _ in flat], *cot, weight, *earlier)
    n = parts * chunks
    act, back = outs[:parts], outs[parts : parts + n]
    return (
        act,
        [back[u * chunks : (u + 1) * chunks] for u in range(parts)],
        outs[-2],
        outs[-1],
        [outs[i] for i in whole_at],
    )


def total_of(*values):
    return functools.reduce(lambda a, b: a + b, [v.astype(F32) for v in values]).astype(BF16)


def step_kernel(low_blocks, own_up, got_up, up, own_down, got_down, down, to_up, to_down):
    low = pl.program_id(0) < low_blocks

    def put(out, own, got, more, with_more):
        both = own[...].astype(F32) + got[...].astype(F32)

        @pl.when(with_more)
        def _():
            out[...] = (both + more[...].astype(F32)).astype(BF16)

        @pl.when(jnp.logical_not(with_more))
        def _():
            out[...] = both.astype(BF16)

    put(to_up, own_up, got_up, up, low)
    put(to_down, own_down, got_down, down, jnp.logical_not(low))


def step_sums(own_up, at_up, up, own_down, at_down, down, got):
    rows, width = own_up.shape
    step = min(rows // 2, 1024)
    blocks = rows // step
    low = blocks // 2

    def spec(index):
        return pl.BlockSpec((step, width), lambda t: (index(t), 0))

    here = spec(lambda t: t)
    return pl.pallas_call(
        functools.partial(step_kernel, low),
        grid=(blocks,),
        in_specs=[
            here,
            spec(lambda t: t + at_up * blocks),
            spec(lambda t: jnp.minimum(t, low - 1)),
            here,
            spec(lambda t: t + at_down * blocks),
            spec(lambda t: jnp.maximum(t - low, 0)),
        ],
        out_specs=[here, here],
        out_shape=[jax.ShapeDtypeStruct((rows, width), BF16)] * 2,
        compiler_params=params(),
        cost_estimate=pl.CostEstimate(flops=4 * rows * width, bytes_accessed=14 * rows * width, transcendentals=0),
        name="step_sums",
    )(own_up, got, up, own_down, got, down)


def result_kernel(n_ready, *refs):
    ready, (own, got, up, down, out) = refs[:n_ready], refs[n_ready:]
    width = own.shape[1]
    for c, ref in enumerate(ready):
        out[:, c * width : (c + 1) * width] = ref[...]
    out[:, n_ready * width :] = (
        own[...].astype(F32) + got[...].astype(F32) + up[...].astype(F32) + down[...].astype(F32)
    ).astype(BF16)


def result_of(ready, own, got, at, up, down):
    rows, width = own.shape
    step = min(rows // 2, 1024)
    blocks = rows // step
    here = pl.BlockSpec((step, width), lambda t: (t, 0))
    there = pl.BlockSpec((step, width), lambda t: (t + at * blocks, 0))
    wide = width * (len(ready) + 1)
    return pl.pallas_call(
        functools.partial(result_kernel, len(ready)),
        grid=(blocks,),
        in_specs=[here] * (len(ready) + 1) + [there, here, here],
        out_specs=pl.BlockSpec((step, wide), lambda t: (t, 0)),
        out_shape=jax.ShapeDtypeStruct((rows, wide), BF16),
        compiler_params=params(),
        cost_estimate=pl.CostEstimate(flops=4 * rows * width, bytes_accessed=14 * rows * width, transcendentals=0),
        name="feature_grad",
    )(*ready, own, got, up, down)


def halves_kernel(low_blocks, own_far, got_far, own_up, got_up, own_down, got_down, to_up, to_down):
    low = pl.program_id(0) < low_blocks

    def put(out, own, got):
        out[...] = (own[...].astype(F32) + got[...].astype(F32)).astype(BF16)

    @pl.when(low)
    def _():
        put(to_up, own_far, got_far)
        put(to_down, own_down, got_down)

    @pl.when(jnp.logical_not(low))
    def _():
        put(to_up, own_up, got_up)
        put(to_down, own_far, got_far)


def halves_sums(own_far, got_far, own_up, at_up, own_down, at_down, got):
    rows, width = own_far.shape
    step = min(rows // 2, 1024)
    blocks = rows // step
    low = blocks // 2

    def spec(index):
        return pl.BlockSpec((step, width), lambda t: (index(t), 0))

    here = spec(lambda t: t)
    return pl.pallas_call(
        functools.partial(halves_kernel, low),
        grid=(blocks,),
        in_specs=[
            here,
            here,
            spec(lambda t: jnp.maximum(t, low)),
            spec(lambda t: jnp.maximum(t, low) + at_up * blocks),
            spec(lambda t: jnp.minimum(t, low - 1)),
            spec(lambda t: jnp.minimum(t, low - 1) + at_down * blocks),
        ],
        out_specs=[here, here],
        out_shape=[jax.ShapeDtypeStruct((rows, width), BF16)] * 2,
        compiler_params=params(),
        cost_estimate=pl.CostEstimate(flops=2 * rows * width, bytes_accessed=12 * rows * width, transcendentals=0),
        name="halves_sums",
    )(own_far, got_far, own_up, got, own_down, got)


def joined_kernel(low_blocks, own, got, up_low, up_high, down_low, down_high, out):
    low = pl.program_id(0) < low_blocks

    def put(up, down):
        total = own[...].astype(F32) + got[...].astype(F32) + up[...].astype(F32) + down[...].astype(F32)
        out[...] = total.astype(BF16)

    @pl.when(low)
    def _():
        put(up_low, down_low)

    @pl.when(jnp.logical_not(low))
    def _():
        put(up_high, down_high)


def joined(own, got, at, up_low, up, down, down_high):
    rows, width = own.shape
    step = min(rows // 2, 1024)
    blocks = rows // step
    low = blocks // 2

    def spec(index):
        return pl.BlockSpec((step, width), lambda t: (index(t), 0))

    return pl.pallas_call(
        functools.partial(joined_kernel, low),
        grid=(blocks,),
        in_specs=[
            spec(lambda t: t),
            spec(lambda t: t + at * blocks),
            spec(lambda t: jnp.minimum(t, low - 1)),
            spec(lambda t: jnp.maximum(t, low)),
            spec(lambda t: jnp.minimum(t, low - 1)),
            spec(lambda t: jnp.maximum(t - low, 0)),
        ],
        out_specs=spec(lambda t: t),
        out_shape=jax.ShapeDtypeStruct((rows, width), BF16),
        compiler_params=params(),
        cost_estimate=pl.CostEstimate(flops=3 * rows * width, bytes_accessed=10 * rows * width, transcendentals=0),
        name="joined",
    )(own, got, up_low, up, down, down_high)


class Reduction:
    def __init__(self, ring, own_far, own_near, other_far, other_near):
        self.ring, self.middle = ring, ring.chips // 2
        self.near = [o for o in range(ring.chips) if o != self.middle]
        self.own_far, self.own_near, self.other_far, self.other_near = own_far, own_near, other_far, other_near
        self.rows = own_far.shape[0]

    def far_swap(self):
        return self.ring.sibling(self.other_far)

    def near_swap(self, after):
        return self.ring.sibling(lax.optimization_barrier((self.other_near, after))[0])

    def far_sums(self, got):
        half = self.rows // 2
        return [total_of(self.own_far[at : at + half], got[at : at + half]) for at in (0, half)]

    def hops(self, up, down):
        return self.ring.hop(up, 1), self.ring.hop(down, -1)

    def place(self, offset):
        return self.near.index(offset % self.ring.chips)

    def near_terms(self, offset, got):
        at = self.place(offset)
        return self.own_near[at], got[at * self.rows : (at + 1) * self.rows]

    def sums(self, step, got, up, down, kernel):
        if step < self.middle - 1:
            return total_of(*self.near_terms(step, got), up), total_of(*self.near_terms(-step, got), down)
        at_up, at_down = self.place(step), self.place(-step)
        if kernel:
            return step_sums(self.own_near[at_up], at_up, up, self.own_near[at_down], at_down, down, got)
        zeros = jnp.zeros_like(up)
        return (
            total_of(*self.near_terms(step, got), jnp.concatenate([up, zeros])),
            total_of(*self.near_terms(-step, got), jnp.concatenate([zeros, down])),
        )

    def halves(self, got_far, got):
        at_up, at_down = self.place(1), self.place(-1)
        return halves_sums(self.own_far, got_far, self.own_near[at_up], at_up, self.own_near[at_down], at_down, got)

    def other_halves(self, got, up, down):
        half = self.rows // 2
        (own_up, got_up), (own_down, got_down) = self.near_terms(1, got), self.near_terms(-1, got)
        return total_of(own_up[:half], got_up[:half], up[:half]), total_of(own_down[half:], got_down[half:], down[half:])

    def last(self, up, down):
        if self.middle > 1:
            return up, down
        return jnp.concatenate([up, jnp.zeros_like(up)]), jnp.concatenate([jnp.zeros_like(down), down])


def local(features, tiles, columns, counts, weight, cotangent):
    rows, f_wide = features.shape
    h_wide = cotangent.shape[1]
    row_size, parts = lax.axis_size("row"), lax.axis_size("rep")
    ring = Ring(row_size)
    rep = lax.axis_index("rep")
    chunks = f_wide // LANES if f_wide % LANES == 0 else 1
    width = f_wide // chunks
    half = rows // 2
    part_rows = rows // parts
    halves = 2
    half_rows = part_rows // halves
    middle = ring.chips // 2
    near = [o for o in range(ring.chips) if o != middle]
    ends, inner = shift_groups(parts)
    last = chunks - 1
    w = Waves()

    offsets = [(0, 0)] + [(o, 0) for step in range(1, middle) for o in (-step, step)] + [(middle, 0), (middle, half)]
    own_meta = [ring.device_at(o, False) * rows + at for o, at in offsets]
    other_meta = [ring.device_at(o, True) * rows + at for o, at in offsets]
    spmm_meta = jnp.stack([rep] + own_meta + other_meta).astype(jnp.int32)
    held = [1] + [1] * len(near) + [1, len(near)]
    order = [middle] + near
    terms_at = [ring.device_at(o, other) * rows for other in (False, True) for o in order]
    spmm_t_meta = jnp.stack([rep] + terms_at).astype(jnp.int32)
    dense_meta = rep[None].astype(jnp.int32)

    def part_of(x, u):
        return lax.dynamic_slice_in_dim(x, lax.rem(rep + u, parts) * part_rows, part_rows, 0)

    share = weight.shape[0] // row_size
    w_share = lax.dynamic_slice_in_dim(weight, lax.axis_index("row") * share, share, 0)

    cot_blocks = [part_of(cotangent, u) for u in range(parts)]
    xs = [features[:, c * width : (c + 1) * width] for c in range(chunks)]
    up = down = xs[0]
    got_own = {}
    got_other = {}
    mixed = {}

    def run_spmm(c, cut, skip):
        own = [got_own[c, i] for i in range(len(offsets))]
        other = [got_other[c, i] for i in range(len(offsets))]
        return spmm(tiles, columns, counts, spmm_meta, own + other, parts, cut, skip)

    cot_ends = send(cot_blocks, ends)
    own_other = ring.sibling(features)
    for c in range(chunks):
        got_own[c, 0] = xs[c]
        got_other[c, 0] = own_other[:, c * width : (c + 1) * width]
        for step in range(1, middle):
            name = f"{c}_{step}"
            w.go(**{"up" + name: ring.hop(up, 1), "down" + name: ring.hop(down, -1)})
            if c and step == 1:
                for i in range(1, len(offsets)):
                    got_other[c - 1, i] = ring.sibling(got_own[c - 1, i])
                w.go(**{f"mixed{c - 1}": run_spmm(c - 1, 1, 0)})
            if c == 0 and step == 1:
                w.go(metas=(spmm_meta, spmm_t_meta, dense_meta))
            w.close()
            up, down = w["up" + name], w["down" + name]
            got_own[c, 2 * step - 1], got_own[c, 2 * step] = up, down
        w.go(**{f"far_up{c}": ring.hop(up[:half], 1), f"far_down{c}": ring.hop(down[half:], -1)})
        if c == 0:
            w.go(cot_ends=cot_ends, own_other=own_other)
        seen = []
        if c == last:
            for step in range(1, middle):
                for i in (2 * step - 1, 2 * step):
                    got_other[c, i] = ring.sibling(got_own[c, i])
                    w.go(**{f"other{c}_{i}": got_other[c, i]})
                    seen.append(got_other[c, i])
        if c:
            mixed[c - 1] = w[f"mixed{c - 1}"]
            ready = [lax.optimization_barrier((b, *seen))[0] for b in mixed[c - 1]]
            w.go(**{f"mixed_ends{c - 1}": send(ready, ends)})
        w.close()
        if c == 0:
            spmm_meta, spmm_t_meta, dense_meta = w["metas"]
            shares = send([w.gate(w_share)] * parts, ends + inner)
            blocks, shares = lax.optimization_barrier(([w.gate(b) for b in cot_blocks], shares))
            w.go(cot_inner=send(blocks, inner), shares=shares)
        else:
            w.go(**{f"mixed_inner{c - 1}": send([w.gate(b) for b in mixed[c - 1]], inner)})
        got_own[c, len(offsets) - 2], got_own[c, len(offsets) - 1] = w[f"far_up{c}"], w[f"far_down{c}"]
        if c < last:
            up = down = w.gate(xs[c + 1])
    w_rows = jnp.concatenate(ordered(w_share, {**w.done, **w.pending}["shares"]), axis=1)
    w_full = lax.all_gather(w.gate(w_rows), "row", axis=0, tiled=True)
    for i in (-2, -1):
        got_other[last, len(offsets) + i] = ring.sibling(got_own[last, len(offsets) + i])

    for h in range(halves):
        w.go(**{f"half{h}": run_spmm(last, halves, h)})
        w.close()
        w.go(**{f"half_got{h}": send(w[f"half{h}"], ends + inner)})

    cot = ordered(cot_blocks[0], w["cot_ends"], w["cot_inner"])
    whole = [ordered(mixed[c][0], w[f"mixed_ends{c}"], w[f"mixed_inner{c}"]) for c in range(last)]
    earlier = ()
    for h in range(halves):
        part = ordered(w[f"half{h}"][0], w[f"half_got{h}"])
        blocks = [[(whole[c][u], h * half_rows) for c in range(last)] + [(part[u], 0)] for u in range(parts)]
        act, back, mixed_rows, grad_rows, earlier = dense(
            dense_meta, blocks, cot, w_full, half_rows, h * half_rows, earlier
        )
        w.go(**{f"back{h}": [b[0] for b in back]})
        if h == halves - 1:
            w.go(whole=(act, back, mixed_rows, grad_rows))
        w.close()
        w.go(**{f"back_got{h}": send(w[f"back{h}"], ends + inner)})
    act, back, mixed_rows, grad_rows = w["whole"]
    sums = lax.dot_general(grad_rows, mixed_rows, (((0,), (0,)), ((), ())), preferred_element_type=F32).astype(BF16)
    share = sums.shape[0] // row_size

    def sums_for(offset, other):
        return lax.dynamic_slice_in_dim(sums, ring.device_at(offset, other) * share, share, 0)

    wg = Reduction(
        ring,
        sums_for(middle, False),
        [sums_for(o, False) for o in near],
        sums_for(middle, True),
        jnp.concatenate([sums_for(o, True) for o in near]),
    )
    wg_far = wg.far_swap()
    w.go(wg_own=(wg.own_far, wg.own_near), wg_far=wg_far, wg_near=ring.sibling(wg.other_near))
    w.close()
    wg.own_far, wg.own_near = w["wg_own"]
    w.go(wg_up_down=wg.hops(*wg.far_sums(w["wg_far"])))

    def run_spmm_t(c, grads):
        return spmm_t(tiles, columns, counts, spmm_t_meta, grads, parts, held, rows, rows * row_size)

    parts_got = [ordered(w[f"back{h}"][0], w[f"back_got{h}"]) for h in range(halves)]
    w.go(terms0=run_spmm_t(0, [parts_got[h][u] for u in range(parts) for h in range(halves)]))
    for c in range(1, chunks):
        w.go(**{f"rest_got{c}": send([w.gate(b[c]) for b in back], ends + inner)})
    w.close()

    def wg_steps(first, until):
        up, down = w["wg_up_down"]
        for step in range(first, until, -1):
            up, down = wg.hops(*wg.sums(step, w["wg_near"], up, down, False))
        return up, down

    def send_act(shifts):
        return send([w.gate(a) for a in act], shifts)

    reductions = []
    for c in range(chunks):
        terms = w[f"terms{c}"]
        red = Reduction(ring, terms[0], terms[1:-2], terms[-2], terms[-1])
        reductions.append(red)
        combined = c < last and middle == 2
        got_far = red.far_swap()
        got_near = red.near_swap(got_far)
        if c == last and c:
            got_near, cuts = lax.optimization_barrier((got_near, cuts))
            w.go(cuts_got=send(cuts, ends + inner))
        sums = red.halves(got_far, got_near) if combined else red.far_sums(got_far)
        if c == 0:
            sums, wg_last = lax.optimization_barrier((sums, wg_steps(middle - 1, 0)))
        w.go(**{f"got_near{c}": got_near})
        if c < last:
            grads = ordered(back[0][c + 1], w[f"rest_got{c + 1}"])
            grads, sums = lax.optimization_barrier((grads, sums))
            w.go(**{f"terms{c + 1}": run_spmm_t(c + 1, grads)})
        w.go(**{f"sum{c}_{middle}": red.hops(*sums)})
        if c == 0:
            w.go(act_inner=send_act(inner))
        w.close()
        if c == 0:
            block = total_of(*wg.near_terms(0, w["wg_near"]), *wg.last(*wg_last))
            cuts = [
                w.gate(lax.dynamic_slice_in_dim(block, lax.rem(rep + u, parts) * f_wide, f_wide, 1))
                for u in range(parts)
            ]
        if combined:
            w.go(**{f"sum{c}_1": red.hops(*red.other_halves(w[f"got_near{c}"], *w[f"sum{c}_{middle}"]))})
            continue
        for step in range(middle - 1, 0, -1):
            to_up, to_down = red.sums(step, w[f"got_near{c}"], *w[f"sum{c}_{step + 1}"], True)
            if step == 1 and c == last:
                act, to_up, to_down = lax.optimization_barrier((act, to_up, to_down))
            w.go(**{f"sum{c}_{step}": red.hops(to_up, to_down)})
            if step > 1:
                w.close()
    w.go(act_ends=send(act, ends))
    if last == 0:
        w.go(cuts_got=send(cuts, ends + inner))
    got = {**w.done, **w.pending}
    cuts_got = got["cuts_got"]
    got["weight_grad"] = functools.reduce(lambda a, b: a + b, [v.astype(F32) for v in [cuts[0], *cuts_got.values()]])
    ready = []
    at = near.index(0)
    for c, red in enumerate(reductions[:-1]):
        up, down = got[f"sum{c}_1"]
        if middle == 2:
            whole_up, whole_down = got[f"sum{c}_2"]
            ready.append(joined(red.own_near[at], got[f"got_near{c}"], at, up, whole_up, whole_down, down))
        else:
            ready.append(total_of(*red.near_terms(0, got[f"got_near{c}"]), *red.last(up, down)))
    red = reductions[-1]
    feature_grad = result_of(ready, red.own_near[at], got[f"got_near{last}"], at, *red.last(*got[f"sum{last}_1"]))
    weight_grad = got["weight_grad"].T
    act = ordered(act[0], got["act_ends"], got["act_inner"])
    activations = jnp.zeros((rows, h_wide), BF16)
    for u in range(parts):
        activations = lax.dynamic_update_slice_in_dim(activations, act[u], lax.rem(rep + u, parts) * part_rows, 0)
    return (activations, feature_grad, weight_grad)


def solution(mesh):
    in_specs = (
        P("row", "rep"),
        P("row", None, None, None),
        P("row", None),
        P("row"),
        P(None, "rep"),
        P("row", "rep"),
    )
    out_specs = (P("row", "rep"), P("row", "rep"), P("rep", "row"))
    return jax.shard_map(local, mesh=mesh, in_specs=in_specs, out_specs=out_specs, check_vma=False)
```
